32 devices in a mesh: members: 2 (over y), window: 4 (over z), space: 4 (over x, core).
Axes of the slice: x: 2, y: 2, z: 4, core: 2. Of those that a mesh axis runs over, the one named last changes fastest.
Arguments:
- trajectory: bfloat16 [8, 4, 5, 4, 32, 384], P('members', None, None, None, 'space', 'window'), parts along dimension 0, may hold values from -4 to 4
- dual_model: float32 [8, 5, 4, 32, 384], P(('members', 'window'), None, None, 'space'), parts along dimension 0, may hold values from -6 to 6
- increment: float32 [8, 5, 4, 32, 384], P(('members', 'window'), None, None, 'space'), parts along dimension 0, may hold values from -6 to 6
- model_rhs: float32 [8, 5, 4, 32, 384], P(('members', 'window'), None, None, 'space'), parts along dimension 0, may hold values from -6 to 6
- dual_obs: float32 [8, 4, 4, 32, 384], P(('members', 'window'), None, None, 'space'), parts along dimension 0, may hold values from -6 to 6
- innovation: float32 [8, 4, 4, 32, 384], P(('members', 'window'), None, None, 'space'), parts along dimension 0, may hold values from -6 to 6
- coupling: float32 [5, 5], replicated, may hold values from -2.5 to 2.5
- error_var: float32 [8, 5, 4], P(('members', 'window')), parts along dimension 0, may hold values from 0.25 to 4
- obs_var: float32 [8, 4, 4], P(('members', 'window')), parts along dimension 0, may hold values from 0.5 to 2
- obs_count: int32 [8], P(('members', 'window')), parts along dimension 0, may hold values from 1 to 4
Outputs:
- new_dual_model: float32 [8, 5, 4, 32, 384], P(('members', 'window'), None, None, 'space'), parts along dimension 0
- new_dual_obs: float32 [8, 4, 4, 32, 384], P(('members', 'window'), None, None, 'space'), parts along dimension 0
- new_increment: float32 [8, 5, 4, 32, 384], P(('members', 'window'), None, None, 'space'), parts along dimension 0
The draws below stay inside these ranges and needn't reach their ends.
There are 2 independent parts, one for each index of `members`. The reference program is written for one: setup_inputs(seed, part) draws one part's arguments, and reference() takes and returns one part's arrays. A program takes and returns all parts, laid end to end along the dimension named above; an argument that names none is the same for every part. Nothing has to cross between parts.
Inputs may be any that keep to these rules, and one draw needn't show every extreme that they name: `obs_count`: observed steps of a subwindow are its first ones.
All inputs are finite; a program needn't handle non-finite values.
Results may differ from the reference program's by a relative error of at most 0.00085.
Values may be sent and summed in bfloat16 or wider, within the bound.
No kernel may reach another device: no remote copies, remote signals or barrier semaphores. Data moves between devices by JAX's collectives and lax.ppermute only.
A program may use at most 64 MiB of HBM per device.

```python
import math
import jax
import jax.numpy as jnp
from jax import lax

V = 5
LEV = 4
STEPS = 4
NY = 384
NSUB = 4
NX = 32


def touch_ends(entries, own_key, low, high):
    spot = [jax.random.randint(jax.random.fold_in(own_key, axis), (), 0, length) for axis, length in enumerate(entries.shape)]
    main_axis = entries.shape.index(max(entries.shape))
    neighbour = spot[:main_axis] + [(spot[main_axis] + 1) % entries.shape[main_axis]] + spot[main_axis + 1:]
    return entries.at[tuple(spot)].set(low).at[tuple(neighbour)].set(high)


def steps_of(rng, shape, split, least, largest):
    level, own = 1.0, jax.random.fold_in(rng, 6)
    for axis_at, shards_of in split:
        draws = jnp.exp(jax.random.uniform(jax.random.fold_in(own, axis_at), (shards_of,), jnp.float32, least / len(split), largest / len(split)))
        level = level * jnp.repeat(draws, shape[axis_at] // shards_of).reshape([-1 if axis == axis_at else 1 for axis in range(len(shape))])
    return level


def gaussian(rng, dims, width, reach, split=(), held_as=jnp.bfloat16):
    array = width * jax.random.normal(rng, dims, jnp.float32)
    if split:
        array = array * steps_of(rng, dims, split, -0.22, 0.18)
    return jnp.clip(array, -reach, reach).astype(held_as)


def setup_inputs(seed: int = 0, part: int = 0) -> dict:
    arg_keys = jax.random.split(jax.random.key(seed), 11)
    own_keys = jax.random.split(jax.random.fold_in(arg_keys[10], part), 11)
    trajectory = gaussian(own_keys[0], (NSUB, STEPS, V, LEV, NX, NY), 1.0, 4.0, ((4, 4), (5, 4)))
    dual_model = gaussian(own_keys[1], (NSUB, V, LEV, NX, NY), 1.0, 6.0, ((0, 4), (3, 4)), jnp.float32)
    increment = gaussian(own_keys[2], (NSUB, V, LEV, NX, NY), 1.0, 6.0, ((0, 4), (3, 4)), jnp.float32)
    model_rhs = gaussian(own_keys[3], (NSUB, V, LEV, NX, NY), 1.0, 6.0, ((0, 4), (3, 4)), jnp.float32)
    dual_obs = gaussian(own_keys[4], (NSUB, STEPS, LEV, NX, NY), 1.0, 6.0, ((0, 4), (3, 4)), jnp.float32)
    innovation = gaussian(own_keys[5], (NSUB, STEPS, LEV, NX, NY), 1.0, 6.0, ((0, 4), (3, 4)), jnp.float32)
    coupling = gaussian(arg_keys[6], (V, V), V ** -0.5, 2.5, (), jnp.float32)
    error_var = jnp.clip(jnp.exp(math.log(4.0) - 2.7725887 * jax.random.uniform(own_keys[7], (NSUB, V, LEV), jnp.float32) ** steps_of(own_keys[7], (NSUB, V, LEV), ((0, 4),), -0.2, 0.2)), 0.25, 4.0)
    obs_var = jnp.clip(jnp.exp(math.log(2.0) - 1.3862944 * jax.random.uniform(own_keys[8], (NSUB, STEPS, LEV), jnp.float32) ** steps_of(own_keys[8], (NSUB, STEPS, LEV), ((0, 4),), -0.2, 0.2)), 0.5, 2.0)
    obs_count = touch_ends(jax.random.randint(own_keys[9], (NSUB,), 1, STEPS + 1), jax.random.fold_in(own_keys[9], 1), 1, STEPS).astype(jnp.int32)
    return {"trajectory": trajectory, "dual_model": dual_model, "increment": increment, "model_rhs": model_rhs, "dual_obs": dual_obs, "innovation": innovation, "coupling": coupling, "error_var": error_var, "obs_var": obs_var, "obs_count": obs_count}


diffusion = 0.2
advection = 0.2
coupling_gain = 0.5


def neighbours(field):
    padded = jnp.pad(field, ((0, 0), (0, 0), (1, 1), (1, 1)))
    east = padded[:, :, 2:, 1:-1]
    west = padded[:, :, :-2, 1:-1]
    north = padded[:, :, 1:-1, 2:]
    south = padded[:, :, 1:-1, :-2]
    return east, west, north, south


def tangent(state, traj, coupling):
    east, west, north, south = neighbours(state)
    laplace = east + west + north + south - 4.0 * state
    slope_x = 0.5 * (east - west)
    slope_y = 0.5 * (north - south)
    mixed = jnp.sum(coupling[:, :, None, None, None] * (traj * state)[None], axis=1)
    return state + diffusion * laplace - advection * (traj[0] * slope_x + traj[1] * slope_y) + coupling_gain * mixed


def adjoint(state, traj, coupling):
    east, west, north, south = neighbours(state)
    laplace = east + west + north + south - 4.0 * state
    east_x, west_x, north_x, south_x = neighbours(traj[0] * state)
    east_y, west_y, north_y, south_y = neighbours(traj[1] * state)
    mixed = traj * jnp.sum(coupling[:, :, None, None, None] * state[:, None], axis=0)
    return state + diffusion * laplace + advection * (0.5 * (east_x - west_x) + 0.5 * (north_y - south_y)) + coupling_gain * mixed


def reference(trajectory, dual_model, increment, model_rhs, dual_obs, innovation, coupling, error_var, obs_var, obs_count):
    steps_range = jnp.arange(STEPS, dtype=jnp.int32)
    observed = (steps_range[None, :] < obs_count[:, None]).astype(jnp.float32)

    def forward(items):
        state, traj = items
        traj = traj.astype(jnp.float32)
        seen = []
        for index in range(STEPS):
            seen.append(state[0])
            state = tangent(state, traj[index], coupling)
        return state, jnp.stack(seen)

    ends, images = lax.map(forward, (increment, trajectory))
    zero_state = jnp.zeros_like(ends[:1])
    before = jnp.concatenate([zero_state, ends[:-1]], 0)
    variance = error_var[:, :, :, None, None]
    model_res = model_rhs - variance * dual_model - (increment - before)
    weights = observed[:, :, None, None, None]
    noise = obs_var[:, :, :, None, None]
    new_dual_obs = weights * (innovation - noise * dual_obs - images) / noise
    after = jnp.concatenate([dual_model[1:], zero_state], 0)
    forcing = weights * dual_obs

    def backward(items):
        state, pulls, traj = items
        traj = traj.astype(jnp.float32)
        state = -state
        for index in reversed(range(STEPS)):
            state = adjoint(state, traj[index], coupling)
            state = state.at[0].add(pulls[index])
        return state

    pulled = lax.map(backward, (after, forcing, trajectory))
    state_res = -(dual_model + pulled)
    new_dual_model = jnp.flip(jnp.cumsum(jnp.flip(state_res, 0), 0), 0)
    new_increment = jnp.cumsum(model_res - variance * new_dual_model, 0)
    return new_dual_model, new_dual_obs, new_increment
```

```python
import jax
import jax.numpy as jnp
from jax import lax
from jax.experimental import pallas as pl
from jax.experimental.pallas import tpu as pltpu
from jax.sharding import PartitionSpec as P

LANES = 128
SUB = 8
CODE_MAX = 32766.0
ROUNDER = 12582912.0

diffusion = 0.2
advection = 0.2
coupling_gain = 0.5
keep = 1.0 - 4.0 * diffusion
half_adv = 0.5 * advection

VMEM = pl.BlockSpec(memory_space=pltpu.VMEM)
SMEM = pl.BlockSpec(memory_space=pltpu.SMEM)


def lane_pieces(src, first, width, target):
    out = []
    done = 0
    while done < width:
        a, b = first + done, target + done
        n = min(width - done, LANES - a % LANES, LANES - b % LANES)
        shift = (b - a) % LANES
        out.append((b // LANES, b % LANES, b % LANES + n, a // LANES, shift))
        done += n
    return out


def model_kernel(
    steps, nvar, windows, spaces, tiles, part,
    coupling_ref, var_ref, count_ref, traj_ref, fields_ref, after_ref,
    payload_ref, images_ref,
    x_ref, s_ref, a_ref, ends_ref, q_ref,
):
    rows = spaces * SUB
    me = lax.axis_index("window")
    level = lax.axis_index("space")
    lane = lax.broadcasted_iota(jnp.int32, (SUB, LANES), 1)
    zero = jnp.zeros((SUB, LANES), jnp.float32)
    cells = [(b, t) for b in range(spaces) for t in range(tiles)]

    for t in range(tiles):
        for edge in (0, SUB + rows):
            for v in range(nvar):
                for p in range(2):
                    s_ref[p, v, t, edge : edge + SUB, :] = zero
                    a_ref[p, v, t, edge : edge + SUB, :] = zero
            for j in range(steps):
                x_ref[j, 0, t, edge : edge + SUB, :] = zero

    def gather(b, carry):
        here = pl.ds(pl.multiple_of(SUB + b * SUB, SUB), SUB)
        for v in range(nvar):
            rolled = {}
            built = {}
            for w in range(windows):
                wide = traj_ref[w * spaces + b, v].astype(jnp.float32)
                total = wide.shape[1]
                short = -total % LANES
                if short:
                    wide = jnp.concatenate([wide, jnp.zeros((SUB, short), jnp.float32)], 1)
                for j in range(steps):
                    for tile, low, high, source, shift in lane_pieces(
                        None, j * part, part, w * part
                    ):
                        key = (w, source, shift)
                        if key not in rolled:
                            value = wide[:, source * LANES : (source + 1) * LANES]
                            rolled[key] = pltpu.roll(value, shift, 1) if shift else value
                        if low == 0:
                            old = built.get((j, tile), None)
                            built[j, tile] = (
                                rolled[key]
                                if old is None
                                else jnp.where(lane < high, rolled[key], old)
                            )
                        else:
                            old = built.get((j, tile), zero)
                            built[j, tile] = jnp.where(lane >= low, rolled[key], old)
            for (j, tile), value in built.items():
                x_ref[j, v, tile, here, :] = value
        for v in range(nvar):
            for t in range(tiles):
                cut = slice(t * LANES, (t + 1) * LANES)
                s_ref[0, v, t, here, :] = fields_ref[b, v, :, cut]
                a_ref[0, v, t, here, :] = -after_ref[b, v, :, cut]
        return carry

    lax.fori_loop(0, spaces, gather, 0)

    mix = [[coupling_gain * coupling_ref[v, u] for u in range(nvar)] for v in range(nvar)]

    def from_north(row):
        turned = [pltpu.roll(value, LANES - 1, 1) for value in row]
        return [
            jnp.where(lane < LANES - 1, turned[t], turned[(t + 1) % tiles]) for t in range(tiles)
        ]

    def from_south(row):
        turned = [pltpu.roll(value, 1, 1) for value in row]
        return [jnp.where(lane > 0, turned[t], turned[t - 1]) for t in range(tiles)]

    def masked_last(row):
        return row[:-1] + [jnp.where(lane < LANES - 1, row[-1], 0.0)]

    def masked_first(row):
        return [jnp.where(lane > 0, row[0], 0.0)] + row[1:]

    def tangent(j, carry):
        now = lax.rem(j, 2)

        def block(b, inner):
            first = pl.multiple_of(SUB + b * SUB, SUB)
            here = pl.ds(first, SUB)
            up, down = pl.ds(first + 1, SUB), pl.ds(first - 1, SUB)
            x = [[x_ref[j, u, t, here, :] for t in range(tiles)] for u in range(nvar)]
            ce = [diffusion - half_adv * value for value in x[0]]
            cw = [diffusion + half_adv * value for value in x[0]]
            cn = masked_last([diffusion - half_adv * value for value in x[1]])
            cs = masked_first([diffusion + half_adv * value for value in x[1]])
            s = [[s_ref[now, u, t, here, :] for t in range(tiles)] for u in range(nvar)]
            xs = [[x[u][t] * s[u][t] for t in range(tiles)] for u in range(nvar)]
            for v in range(nvar):
                north, south = from_north(s[v]), from_south(s[v])
                for t in range(tiles):
                    fresh = keep * s[v][t] + ce[t] * s_ref[now, v, t, up, :]
                    fresh = fresh + cw[t] * s_ref[now, v, t, down, :]
                    fresh = fresh + cn[t] * north[t] + cs[t] * south[t]
                    for u in range(nvar):
                        fresh = fresh + mix[v][u] * xs[u][t]
                    s_ref[1 - now, v, t, here, :] = fresh
            for t in range(tiles):
                images_ref[b, j, :, t * LANES : (t + 1) * LANES] = s[0][t]
            return inner

        return lax.fori_loop(0, spaces, block, carry)

    lax.fori_loop(0, steps, tangent, 0)

    def adjoint(turn, carry):
        now = lax.rem(turn, 2)
        j = steps - 1 - turn
        seen = jnp.where(j < count_ref[0], 1.0, 0.0)

        def block(b, inner):
            first = pl.multiple_of(SUB + b * SUB, SUB)
            here = pl.ds(first, SUB)
            up, down = pl.ds(first + 1, SUB), pl.ds(first - 1, SUB)
            x = [[x_ref[j, u, t, here, :] for t in range(tiles)] for u in range(nvar)]
            ce = [diffusion + half_adv * x_ref[j, 0, t, up, :] for t in range(tiles)]
            cw = [diffusion - half_adv * x_ref[j, 0, t, down, :] for t in range(tiles)]
            cn = masked_first([diffusion + half_adv * value for value in x[1]])
            cs = masked_last([diffusion - half_adv * value for value in x[1]])
            a = [[a_ref[now, u, t, here, :] for t in range(tiles)] for u in range(nvar)]
            for u in range(nvar):
                north = from_north([cn[t] * a[u][t] for t in range(tiles)])
                south = from_south([cs[t] * a[u][t] for t in range(tiles)])
                for t in range(tiles):
                    fresh = keep * a[u][t] + ce[t] * a_ref[now, u, t, up, :]
                    fresh = fresh + cw[t] * a_ref[now, u, t, down, :]
                    fresh = fresh + north[t] + south[t]
                    pull = mix[0][u] * a[0][t]
                    for v in range(1, nvar):
                        pull = pull + mix[v][u] * a[v][t]
                    fresh = fresh + x[u][t] * pull
                    if u == 0:
                        fresh = fresh + seen * fields_ref[
                            b, nvar + j, :, t * LANES : (t + 1) * LANES
                        ]
                    a_ref[1 - now, u, t, here, :] = fresh
            return inner

        return lax.fori_loop(0, spaces, block, carry)

    lax.fori_loop(0, steps, adjoint, 0)

    end = steps % 2
    total_var = []
    for v in range(nvar):
        total_var.append(
            lax.fori_loop(
                0, windows,
                lambda w, acc: acc + jnp.where(w <= me, var_ref[w, v, level], 0.0),
                jnp.float32(0.0),
            )
        )

    def coded(planes):
        scales = zero
        out = []
        for v in range(nvar):
            big = jnp.abs(planes[v][0])
            for t in range(1, tiles):
                big = jnp.maximum(big, jnp.abs(planes[v][t]))
            big = jnp.max(big, axis=1, keepdims=True)
            power = jnp.clip(jnp.ceil(jnp.log2(jnp.maximum(big, 1e-30))), -90.0, 126.0)
            scales = jnp.where(lane == v, power, scales)
            gain = CODE_MAX * jnp.exp2(-power)
            for t in range(tiles):
                scaled = jnp.clip(planes[v][t] * gain, -CODE_MAX, CODE_MAX)
                out.append((scaled + ROUNDER) - ROUNDER)
        out.append(scales)
        while len(out) % 2:
            out.append(zero)
        pairs = [jnp.concatenate(out[i : i + 2], 0) for i in range(0, len(out), 2)]
        return [pair.astype(jnp.int32).astype(jnp.int16) for pair in pairs]

    def finish(b, carry):
        first = pl.multiple_of(SUB + b * SUB, SUB)
        here = pl.ds(first, SUB)
        back, ahead = [], []
        for v in range(nvar):
            tv, gv = [], []
            for t in range(tiles):
                cut = slice(t * LANES, (t + 1) * LANES)
                term = a_ref[end, v, t, here, :] + after_ref[b, v, :, cut]
                given = fields_ref[b, nvar + steps + v, :, cut] - fields_ref[b, v, :, cut]
                tv.append(term)
                gv.append(given + s_ref[end, v, t, here, :] + total_var[v] * term)
            back.append(tv)
            ahead.append(gv)
        for kind, planes in ((0, back), (1, ahead)):
            for i, pair in enumerate(coded(planes)):
                q_ref[kind, b, i * 2 * SUB : (i + 1) * 2 * SUB, :] = pair
        return carry

    lax.fori_loop(0, spaces, finish, 0)

    def send(w, carry):
        kind = jnp.where(w <= me, 0, 1)
        for b in range(spaces):
            payload_ref[w * spaces + b] = q_ref[kind, b]
        return carry

    lax.fori_loop(0, windows, send, 0)


def final_kernel(
    steps, nvar, windows, spaces, tiles,
    var_ref, noise_ref, count_ref, codes_ref, images_ref, dual_ref, inc_ref, rhs_ref, dobs_ref, innov_ref,
    ndm_ref, ndo_ref, ninc_ref,
):
    me = lax.axis_index("window")
    for lev in range(spaces):
        empty = [jnp.zeros((SUB, LANES), jnp.float32)] * (2 * nvar * tiles)

        def add(w, sums):
            source = w * spaces + lev
            later = jnp.where(w >= me, 1.0 / CODE_MAX, 0.0)
            earlier = jnp.where(w < me, 1.0 / CODE_MAX, 0.0)
            parts = []
            for i in range(codes_ref.shape[1] // (2 * SUB)):
                pair = codes_ref[source, i * 2 * SUB : (i + 1) * 2 * SUB, :]
                pair = pair.astype(jnp.int32).astype(jnp.float32)
                parts += [pair[:SUB], pair[SUB:]]
            scales = jnp.exp2(parts[nvar * tiles])
            out = list(sums)
            for v in range(nvar):
                column = scales[:, v : v + 1]
                up, down = column * later, column * earlier
                for t in range(tiles):
                    i = v * tiles + t
                    out[i] = out[i] + up * parts[i]
                    out[nvar * tiles + i] = out[nvar * tiles + i] + down * parts[i]
            return tuple(out)

        sums = lax.fori_loop(0, windows, add, tuple(empty), unroll=windows <= 4)
        for v in range(nvar):
            total = lax.fori_loop(
                0, windows,
                lambda w, acc: acc + jnp.where(w <= me, var_ref[w, v, lev], 0.0),
                jnp.float32(0.0),
            )
            for t in range(tiles):
                cut = slice(t * LANES, (t + 1) * LANES)
                tail = sums[v * tiles + t]
                head = sums[(nvar + v) * tiles + t]
                ndm_ref[0, v, lev, :, cut] = -(dual_ref[0, v, lev, :, cut] + tail)
                given = rhs_ref[0, v, lev, :, cut] - inc_ref[0, v, lev, :, cut]
                ninc_ref[0, v, lev, :, cut] = head + given + total * tail
        for j in range(steps):
            seen = jnp.where(j < count_ref[0], 1.0, 0.0)
            noise = jnp.full((SUB, LANES), noise_ref[0, j, lev])
            inverse = seen / noise
            for t in range(tiles):
                cut = slice(t * LANES, (t + 1) * LANES)
                gap = innov_ref[0, j, lev, :, cut] - noise * dobs_ref[0, j, lev, :, cut]
                gap = gap - images_ref[lev, j, :, cut]
                ndo_ref[0, j, lev, :, cut] = gap * inverse


def shifted(block, axis, distance):
    devices = range(lax.axis_size(axis))
    route = [(i - distance, i) for i in devices if i - distance in devices]
    return lax.ppermute(block, axis, route)


def body(
    trajectory,
    dual_model,
    increment,
    model_rhs,
    dual_obs,
    innovation,
    coupling,
    error_var,
    obs_var,
    obs_count,
):
    windows, spaces = lax.axis_size("window"), lax.axis_size("space")
    _, steps, nvar, levels, rows, part = trajectory.shape
    columns = dual_model.shape[-1]
    tiles = columns // LANES
    assert trajectory.shape[0] == windows and levels == spaces and rows == SUB
    assert columns == tiles * LANES == windows * part

    after = shifted(dual_model[0], "window", -1)
    sending = trajectory.transpose(0, 3, 2, 4, 1, 5)
    sending = sending.reshape(windows * levels, nvar, rows, steps * part)
    traj = lax.all_to_all(sending, ("window", "space"), 0, 0, tiled=True)
    fields = jnp.concatenate([increment[0], dual_obs[0], model_rhs[0]], 0)
    fields = lax.all_to_all(fields.transpose(1, 0, 2, 3), "space", 0, 0, tiled=True)
    after = lax.all_to_all(after.transpose(1, 0, 2, 3), "space", 0, 0, tiled=True)
    variances = lax.all_gather(error_var[0], "window")

    code_rows = -(-(nvar * tiles + 1) // 2) * 2 * SUB
    padded = SUB + spaces * rows + SUB
    payload, images = pl.pallas_call(
        lambda *refs: model_kernel(steps, nvar, windows, spaces, tiles, part, *refs),
        out_shape=(
            jax.ShapeDtypeStruct((windows * spaces, code_rows, LANES), jnp.int16),
            jax.ShapeDtypeStruct((spaces, steps, rows, columns), jnp.float32),
        ),
        in_specs=[SMEM, SMEM, SMEM, VMEM, VMEM, VMEM],
        out_specs=(VMEM, VMEM),
        scratch_shapes=[
            pltpu.VMEM((steps, nvar, tiles, padded, LANES), jnp.float32),
            pltpu.VMEM((2, nvar, tiles, padded, LANES), jnp.float32),
            pltpu.VMEM((2, nvar, tiles, padded, LANES), jnp.float32),
            pltpu.VMEM((SUB, LANES), jnp.float32),
            pltpu.VMEM((2, spaces, code_rows, LANES), jnp.int16),
        ],
        compiler_params=pltpu.CompilerParams(vmem_limit_bytes=24 * 1024 * 1024),
    )(coupling, variances, obs_count, traj, fields, after)

    codes = lax.all_to_all(payload, ("window", "space"), 0, 0, tiled=True)
    images = lax.all_to_all(images, "space", 0, 0, tiled=True)

    shapes = [jax.ShapeDtypeStruct(a.shape, jnp.float32) for a in (dual_model, dual_obs, increment)]
    return pl.pallas_call(
        lambda *refs: final_kernel(steps, nvar, windows, spaces, tiles, *refs),
        out_shape=tuple(shapes),
        in_specs=[SMEM, SMEM, SMEM] + [VMEM] * 7,
        out_specs=(VMEM, VMEM, VMEM),
        compiler_params=pltpu.CompilerParams(vmem_limit_bytes=24 * 1024 * 1024),
    )(
        variances, obs_var, obs_count, codes, images,
        dual_model, increment, model_rhs, dual_obs, innovation,
    )


def solution(mesh):
    placed = (
        P("members", None, None, None, "space", "window"),
        P(("members", "window"), None, None, "space", None),
        P(("members", "window"), None, None, "space", None),
        P(("members", "window"), None, None, "space", None),
        P(("members", "window"), None, None, "space", None),
        P(("members", "window"), None, None, "space", None),
        P(),
        P(("members", "window"), None, None),
        P(("members", "window"), None, None),
        P(("members", "window")),
    )
    return jax.shard_map(
        body,
        mesh=mesh,
        in_specs=placed,
        out_specs=(
            P(("members", "window"), None, None, "space", None),
            P(("members", "window"), None, None, "space", None),
            P(("members", "window"), None, None, "space", None),
        ),
        check_vma=False,
    )
```

```python
import jax
import jax.numpy as jnp
from jax import lax
from jax.experimental import pallas as pl
from jax.experimental.pallas import tpu as pltpu
from jax.sharding import PartitionSpec as P

LANES = 128
SUB = 8
HALF = SUB // 2
CODE_MAX = 32766.0
ROUNDER = 12582912.0

diffusion = 0.2
advection = 0.2
coupling_gain = 0.5
keep = 1.0 - 4.0 * diffusion
half_adv = 0.5 * advection

VMEM = pl.BlockSpec(memory_space=pltpu.VMEM)
SMEM = pl.BlockSpec(memory_space=pltpu.SMEM)


def params(mib=24):
    return pltpu.CompilerParams(vmem_limit_bytes=mib * 1024 * 1024)


def lane_index():
    return lax.broadcasted_iota(jnp.int32, (SUB, LANES), 1)


def row_index():
    return lax.broadcasted_iota(jnp.int32, (SUB, LANES), 0)


def tiled(wide):
    short = -wide.shape[1] % LANES
    if short:
        wide = jnp.concatenate([wide, jnp.zeros((wide.shape[0], short), wide.dtype)], 1)
    return [wide[:, i : i + LANES] for i in range(0, wide.shape[1], LANES)]


def place(parts, rolled, lane):
    built = {}
    for key, tiles, first, width, target in parts:
        done = 0
        while done < width:
            a, b = first + done, target + done
            n = min(width - done, LANES - a % LANES, LANES - b % LANES)
            shift = (b - a) % LANES
            name = (key, a // LANES, shift)
            if name not in rolled:
                value = tiles[a // LANES]
                rolled[name] = pltpu.roll(value, shift, 1) if shift else value
            if b % LANES:
                built[b // LANES] = jnp.where(
                    lane >= b % LANES, rolled[name], built[b // LANES]
                )
            else:
                built[b // LANES] = rolled[name]
            done += n
    return [built[i] for i in range(len(built))]


def joined_halves(first, second):
    top = row_index()[:, :1] < HALF
    last = jnp.where(top, pltpu.roll(first, HALF, 0), second)
    start = jnp.where(top, first, pltpu.roll(second, HALF, 0))
    return last, start


def widened(own, low, high, odd):
    top = row_index() < HALF
    turned = pltpu.roll(own, HALF, 0)
    low = pltpu.roll(low, HALF, 0) if odd else low
    high = high if odd else pltpu.roll(high, HALF, 0)
    return jnp.where(top, low, turned), jnp.where(top, turned, high)


def row_codes(planes):
    lane = lax.broadcasted_iota(jnp.int32, planes[0][0].shape, 1)
    scales = jnp.zeros(planes[0][0].shape, jnp.float32)
    out = []
    for v, row in enumerate(planes):
        big = jnp.abs(row[0])
        for value in row[1:]:
            big = jnp.maximum(big, jnp.abs(value))
        big = jnp.max(big, axis=1, keepdims=True)
        power = jnp.clip(jnp.ceil(jnp.log2(jnp.maximum(big, 1e-30))), -90.0, 126.0)
        scales = jnp.where(lane == v, power, scales)
        gain = CODE_MAX * jnp.exp2(-power)
        for value in row:
            scaled = jnp.clip(value * gain, -CODE_MAX, CODE_MAX)
            out.append((scaled + ROUNDER) - ROUNDER)
    return out, scales


def shorts(value):
    return value.astype(jnp.int32).astype(jnp.int16)


def floats(value):
    return value.astype(jnp.int32).astype(jnp.float32)


def pack_kernel(windows, steps, nvar, levels, part, var_ref, traj_ref, *out_refs):
    me = lax.axis_index("window")
    lane, row = lane_index(), row_index()
    variance = jnp.zeros((SUB, LANES), jnp.float32)
    for v in range(nvar):
        for lev in range(levels):
            variance = jnp.where(lane == v * levels + lev, var_ref[0, v, lev], variance)
    high = variance.astype(jnp.bfloat16).astype(jnp.float32)
    middle = (variance - high).astype(jnp.bfloat16).astype(jnp.float32)
    low = variance - high - middle
    split = jnp.where(row == 0, high, jnp.where(row == 1, middle, jnp.where(row == 2, low, 0.0)))

    for d in range(windows):
        target = lax.rem(me + d, windows)

        def level(lev, carry, d=d, target=target):
            for v in range(nvar):
                pieces = [
                    tiled(traj_ref[target, j, v, lev].astype(jnp.float32)) for j in range(steps)
                ]
                parts = [(j, pieces[j], 0, part, j * part) for j in range(steps)]
                wide = jnp.concatenate(place(parts, {}, lane), 1)
                out_refs[d][v * levels + lev] = wide.astype(jnp.bfloat16)
            return carry

        lax.fori_loop(0, levels, level, 0)
        out_refs[d][nvar * levels, :, :LANES] = split.astype(jnp.bfloat16)


def field_halo_kernel(inc_ref, dobs_ref, dual_ref, low_ref, high_ref):
    base = 0
    tiles = inc_ref.shape[-1] // LANES
    for ref in (inc_ref, dobs_ref, dual_ref):
        count, pairs = ref.shape[1], ref.shape[2] // 2

        def field(f, carry, ref=ref, base=base, pairs=pairs):
            for i in range(pairs):
                for t in range(tiles):
                    cut = slice(t * LANES, (t + 1) * LANES)
                    last, start = joined_halves(
                        ref[0, f, 2 * i, :, cut], ref[0, f, 2 * i + 1, :, cut]
                    )
                    low_ref[base + f * pairs + i, :, cut] = last
                    high_ref[base + f * pairs + i, :, cut] = start
            return carry

        lax.fori_loop(0, count, field, 0)
        base += count * pairs


def dual_code_kernel(base, dual_ref, low_ref, high_ref, codes_ref):
    nvar, levels = dual_ref.shape[1:3]
    tiles = dual_ref.shape[-1] // LANES
    pairs = levels // 2

    def pair(i, carry):
        for odd in range(2):
            lev = 2 * i + odd
            planes = []
            for v in range(nvar):
                row = []
                for t in range(tiles):
                    cut = slice(t * LANES, (t + 1) * LANES)
                    halves = widened(
                        dual_ref[0, v, lev, :, cut],
                        low_ref[base + v * pairs + i, :, cut],
                        high_ref[base + v * pairs + i, :, cut],
                        odd,
                    )
                    row.append(jnp.concatenate(halves, 0))
                planes.append(row)
            values, scales = row_codes(planes)
            for n, value in enumerate(values + [scales]):
                codes_ref[lev, n] = shorts(value)
        return carry

    lax.fori_loop(0, pairs, pair, 0)


def assemble_kernel(windows, steps, nvar, levels, part, *refs):
    pieces = refs[:windows]
    own_ref, low_ref, high_ref, total_ref, stack_ref = refs[windows:]
    me = lax.axis_index("window")
    lane = lane_index()
    total = jnp.zeros((1, LANES), jnp.float32)
    for d in range(windows):
        source = lax.rem(me - d + windows, windows)
        stack_ref[source] = pieces[d][: nvar * levels]
        split = pieces[d][nvar * levels, :, :LANES].astype(jnp.float32)
        here = jnp.sum(split, axis=0, keepdims=True)
        total = total + jnp.where(source <= me, here, 0.0)
    for p in range(nvar * levels):
        total_ref[p] = jnp.broadcast_to(total[:, p : p + 1], (SUB, LANES))

    pairs = levels // 2

    def pair(n, carry):
        both = []
        for odd in range(2):
            plane = 2 * n + odd
            sources = [tiled(stack_ref[w, plane].astype(jnp.float32)) for w in range(windows)]
            rolled = {}
            built = []
            for j in range(steps):
                parts = [(w, sources[w], j * part, part, w * part) for w in range(windows)]
                built.append(place(parts, rolled, lane))
                own_ref[j, plane] = jnp.concatenate(built[j], 1).astype(jnp.bfloat16)
            both.append(built)
        for j in range(steps):
            halves = [joined_halves(a, b) for a, b in zip(both[0][j], both[1][j])]
            low_ref[j, n] = jnp.concatenate([h[0] for h in halves], 1).astype(jnp.bfloat16)
            high_ref[j, n] = jnp.concatenate([h[1] for h in halves], 1).astype(jnp.bfloat16)
        return carry

    lax.fori_loop(0, nvar * pairs, pair, 0)


def model_kernel(
    windows, spaces, steps, nvar, levels, tiles,
    coupling_ref, count_ref, noise_ref, total_ref, own_ref, low_ref, high_ref, after_ref,
    flow_ref, fhigh_ref, inc_ref, dobs_ref, rhs_ref, dual_ref, innov_ref,
    ndo_ref, ndm_ref, ninc_ref, *rest,
):
    payload_refs = rest[: windows - 1]
    x_ref, s_ref, a_ref, f_ref, keep_ref, q_ref = rest[windows - 1 :]
    me = lax.axis_index("window")
    place_x = lax.axis_index("space")
    lane, row = lane_index(), row_index()
    pairs = levels // 2
    zero = jnp.zeros((SUB, LANES), jnp.float32)
    blocks = [slice(SUB, 2 * SUB), slice(2 * SUB, 3 * SUB)]
    ups = [slice(b.start + 1, b.stop + 1) for b in blocks]
    downs = [slice(b.start - 1, b.stop - 1) for b in blocks]
    mine = slice(SUB + HALF, 2 * SUB + HALF)
    cuts = [slice(t * LANES, (t + 1) * LANES) for t in range(tiles)]
    mix = [[coupling_gain * coupling_ref[v, u] for u in range(nvar)] for v in range(nvar)]
    low_wall = jnp.where((row == HALF) & (place_x == 0), 0.0, 1.0)
    high_wall = jnp.where((row == HALF - 1) & (place_x == spaces - 1), 0.0, 1.0)

    def from_north(line):
        turned = [pltpu.roll(value, LANES - 1, 1) for value in line]
        return [
            jnp.where(lane < LANES - 1, turned[t], turned[(t + 1) % tiles]) for t in range(tiles)
        ]

    def from_south(line):
        turned = [pltpu.roll(value, 1, 1) for value in line]
        return [jnp.where(lane > 0, turned[t], turned[t - 1]) for t in range(tiles)]

    def masked_last(line):
        return line[:-1] + [jnp.where(lane < LANES - 1, line[-1], 0.0)]

    def masked_first(line):
        return [jnp.where(lane > 0, line[0], 0.0)] + line[1:]

    def walled(block, east, west):
        if block == 0:
            return east, [low_wall * value for value in west]
        return [high_wall * value for value in east], west

    def pair(i, outer):
        for odd in range(2):
            lev = 2 * i + odd

            def spread(j, carry, odd=odd, lev=lev):
                for v in range(nvar):
                    for t in range(tiles):
                        halves = widened(
                            own_ref[j, v * levels + lev, :, cuts[t]].astype(jnp.float32),
                            low_ref[j, v * pairs + i, :, cuts[t]].astype(jnp.float32),
                            high_ref[j, v * pairs + i, :, cuts[t]].astype(jnp.float32),
                            odd,
                        )
                        for b in range(2):
                            x_ref[odd, j, v, t, blocks[b], :] = halves[b]
                seen = jnp.where(j < count_ref[0], 1.0, 0.0)
                for t in range(tiles):
                    halves = widened(
                        dobs_ref[0, j, lev, :, cuts[t]],
                        flow_ref[(nvar + j) * pairs + i, :, cuts[t]],
                        fhigh_ref[(nvar + j) * pairs + i, :, cuts[t]],
                        odd,
                    )
                    for b in range(2):
                        f_ref[odd, j, t, b * SUB : (b + 1) * SUB, :] = seen * halves[b]
                return carry

            lax.fori_loop(0, steps, spread, 0)
            scales = jnp.exp2(floats(after_ref[lev, nvar * tiles])) * (1.0 / CODE_MAX)
            for v in range(nvar):
                for t in range(tiles):
                    halves = widened(
                        inc_ref[0, v, lev, :, cuts[t]],
                        flow_ref[v * pairs + i, :, cuts[t]],
                        fhigh_ref[v * pairs + i, :, cuts[t]],
                        odd,
                    )
                    for b in range(2):
                        s_ref[odd, 0, v, t, blocks[b], :] = halves[b]
                    later = floats(after_ref[lev, v * tiles + t]) * scales[:, v : v + 1]
                    a_ref[odd, 0, v, t, SUB : 3 * SUB, :] = -later
                    keep_ref[odd, v, t] = a_ref[odd, 0, v, t, mine, :]

        def tangent(j, carry):
            now = lax.rem(j, 2)
            seen = jnp.where(j < count_ref[0], 1.0, 0.0)
            for odd in range(2):
                lev = 2 * i + odd
                noise = jnp.full((SUB, LANES), noise_ref[0, j, lev])
                share = seen / noise
                for t in range(tiles):
                    gap = innov_ref[0, j, lev, :, cuts[t]] - noise * dobs_ref[0, j, lev, :, cuts[t]]
                    gap = gap - s_ref[odd, now, 0, t, mine, :]
                    ndo_ref[0, j, lev, :, cuts[t]] = gap * share
                for b in range(2):
                    here, up, down = blocks[b], ups[b], downs[b]
                    x = [[x_ref[odd, j, u, t, here, :] for t in range(tiles)] for u in range(nvar)]
                    ce = [diffusion - half_adv * value for value in x[0]]
                    cw = [diffusion + half_adv * value for value in x[0]]
                    ce, cw = walled(b, ce, cw)
                    cn = masked_last([diffusion - half_adv * value for value in x[1]])
                    cs = masked_first([diffusion + half_adv * value for value in x[1]])
                    s = [
                        [s_ref[odd, now, u, t, here, :] for t in range(tiles)] for u in range(nvar)
                    ]
                    xs = [[x[u][t] * s[u][t] for t in range(tiles)] for u in range(nvar)]
                    for v in range(nvar):
                        north, south = from_north(s[v]), from_south(s[v])
                        for t in range(tiles):
                            fresh = keep * s[v][t] + ce[t] * s_ref[odd, now, v, t, up, :]
                            fresh = fresh + cw[t] * s_ref[odd, now, v, t, down, :]
                            fresh = fresh + cn[t] * north[t] + cs[t] * south[t]
                            for u in range(nvar):
                                fresh = fresh + mix[v][u] * xs[u][t]
                            s_ref[odd, 1 - now, v, t, here, :] = fresh
            return carry

        lax.fori_loop(0, steps, tangent, 0)

        def adjoint(turn, carry):
            now = lax.rem(turn, 2)
            j = steps - 1 - turn
            for odd in range(2):
                for b in range(2):
                    here, up, down = blocks[b], ups[b], downs[b]
                    x = [[x_ref[odd, j, u, t, here, :] for t in range(tiles)] for u in range(nvar)]
                    ce = [
                        diffusion + half_adv * x_ref[odd, j, 0, t, up, :] for t in range(tiles)
                    ]
                    cw = [
                        diffusion - half_adv * x_ref[odd, j, 0, t, down, :] for t in range(tiles)
                    ]
                    ce, cw = walled(b, ce, cw)
                    cn = masked_first([diffusion + half_adv * value for value in x[1]])
                    cs = masked_last([diffusion - half_adv * value for value in x[1]])
                    a = [
                        [a_ref[odd, now, u, t, here, :] for t in range(tiles)] for u in range(nvar)
                    ]
                    for u in range(nvar):
                        north = from_north([cn[t] * a[u][t] for t in range(tiles)])
                        south = from_south([cs[t] * a[u][t] for t in range(tiles)])
                        for t in range(tiles):
                            fresh = keep * a[u][t] + ce[t] * a_ref[odd, now, u, t, up, :]
                            fresh = fresh + cw[t] * a_ref[odd, now, u, t, down, :]
                            fresh = fresh + north[t] + south[t]
                            pull = mix[0][u] * a[0][t]
                            for v in range(1, nvar):
                                pull = pull + mix[v][u] * a[v][t]
                            fresh = fresh + x[u][t] * pull
                            if u == 0:
                                fresh = fresh + f_ref[odd, j, t, b * SUB : (b + 1) * SUB, :]
                            a_ref[odd, 1 - now, u, t, here, :] = fresh
            return carry

        lax.fori_loop(0, steps, adjoint, 0)

        end = steps % 2
        coded = []
        for odd in range(2):
            lev = 2 * i + odd
            back, ahead = [], []
            for v in range(nvar):
                share = total_ref[v * levels + lev]
                tv, gv = [], []
                for t in range(tiles):
                    term = a_ref[odd, end, v, t, mine, :] - keep_ref[odd, v, t]
                    given = rhs_ref[0, v, lev, :, cuts[t]] - inc_ref[0, v, lev, :, cuts[t]]
                    given = given + share * term
                    ndm_ref[v, lev, :, cuts[t]] = -(dual_ref[0, v, lev, :, cuts[t]] + term)
                    ninc_ref[v, lev, :, cuts[t]] = given
                    tv.append(term)
                    gv.append(given + s_ref[odd, end, v, t, mine, :])
                back.append(tv)
                ahead.append(gv)
            coded.append((row_codes(back), row_codes(ahead)))
        for kind in range(2):
            first, second = coded[0][kind], coded[1][kind]
            for n, (a, b) in enumerate(zip(first[0] + [first[1]], second[0] + [second[1]])):
                q_ref[kind, i, n] = shorts(jnp.concatenate([a, b], 0))
        return outer

    lax.fori_loop(0, pairs, pair, 0)
    for d in range(1, windows):
        payload_refs[d - 1][...] = q_ref[jnp.where(me + d >= windows, 0, 1)]


def final_kernel(windows, nvar, levels, tiles, *refs):
    pieces = refs[: windows - 1]
    total_ref, base_dual_ref, base_inc_ref, ndm_ref, ninc_ref = refs[windows - 1 :]
    me = lax.axis_index("window")
    pairs = levels // 2
    cuts = [slice(t * LANES, (t + 1) * LANES) for t in range(tiles)]

    def pair(i, carry):
        tails = [None] * (nvar * tiles)
        heads = [None] * (nvar * tiles)
        for d in range(1, windows):
            piece = pieces[d - 1]
            scales = jnp.exp2(floats(piece[i, nvar * tiles])) * (1.0 / CODE_MAX)
            later = jnp.where(d > me, scales, 0.0)
            earlier = jnp.where(d > me, 0.0, scales)
            for v in range(nvar):
                for t in range(tiles):
                    n = v * tiles + t
                    value = floats(piece[i, n])
                    tail, head = value * later[:, v : v + 1], value * earlier[:, v : v + 1]
                    tails[n] = tail if d == 1 else tails[n] + tail
                    heads[n] = head if d == 1 else heads[n] + head
        for v in range(nvar):
            for odd in range(2):
                lev = 2 * i + odd
                share = total_ref[v * levels + lev]
                for t in range(tiles):
                    rows = slice(odd * SUB, (odd + 1) * SUB)
                    tail, head = tails[v * tiles + t][rows], heads[v * tiles + t][rows]
                    ndm_ref[0, v, lev, :, cuts[t]] = base_dual_ref[v, lev, :, cuts[t]] - tail
                    ninc_ref[0, v, lev, :, cuts[t]] = (
                        base_inc_ref[v, lev, :, cuts[t]] + head + share * tail
                    )
        return carry

    lax.fori_loop(0, pairs, pair, 0)


def moved(block, axis, distance, around=False):
    count = lax.axis_size(axis)
    route = [(i, (i + distance) % count) for i in range(count) if around or 0 <= i + distance < count]
    return lax.ppermute(block, axis, route)


def body(
    trajectory,
    dual_model,
    increment,
    model_rhs,
    dual_obs,
    innovation,
    coupling,
    error_var,
    obs_var,
    obs_count,
):
    windows, spaces = lax.axis_size("window"), lax.axis_size("space")
    _, steps, nvar, levels, rows, part = trajectory.shape
    columns = dual_model.shape[-1]
    tiles = columns // LANES
    assert trajectory.shape[0] == windows and windows > 1 and rows == SUB and steps == HALF
    assert columns == tiles * LANES == windows * part and levels % 2 == 0
    pairs = levels // 2
    wide = -(-steps * part // LANES) * LANES
    bf16, f32, i16 = jnp.bfloat16, jnp.float32, jnp.int16

    def shape(dims, dtype):
        return jax.ShapeDtypeStruct(dims, dtype)

    blocks = pl.pallas_call(
        lambda *refs: pack_kernel(windows, steps, nvar, levels, part, *refs),
        out_shape=[shape((nvar * levels + 1, rows, wide), bf16)] * windows,
        in_specs=[SMEM, VMEM],
        out_specs=[VMEM] * windows,
        compiler_params=params(),
    )(error_var, trajectory)
    order = sorted(range(1, windows), key=lambda d: -d * (windows - d))
    arrived = {0: blocks[0]}
    for d in order:
        arrived[d] = moved(blocks[d], "window", d, around=True)

    field_tiles = shape(((2 * nvar + steps) * pairs, rows, columns), f32)
    low, high = pl.pallas_call(
        field_halo_kernel,
        out_shape=[field_tiles, field_tiles],
        in_specs=[VMEM] * 3,
        out_specs=[VMEM] * 2,
        compiler_params=params(),
    )(increment, dual_obs, dual_model)
    low, high = moved(low, "space", 1), moved(high, "space", -1)

    after = pl.pallas_call(
        lambda *refs: dual_code_kernel((nvar + steps) * pairs, *refs),
        out_shape=shape((levels, nvar * tiles + 1, 2 * SUB, LANES), i16),
        in_specs=[VMEM] * 3,
        out_specs=VMEM,
        compiler_params=params(),
    )(dual_model, low, high)
    after = moved(after, "window", -1)

    own, traj_low, traj_high, totals = pl.pallas_call(
        lambda *refs: assemble_kernel(windows, steps, nvar, levels, part, *refs),
        out_shape=[
            shape((steps, nvar * levels, rows, columns), bf16),
            shape((steps, nvar * pairs, rows, columns), bf16),
            shape((steps, nvar * pairs, rows, columns), bf16),
            shape((nvar * levels, rows, LANES), f32),
        ],
        in_specs=[VMEM] * windows,
        out_specs=[VMEM] * 4,
        scratch_shapes=[pltpu.VMEM((windows, nvar * levels, rows, wide), bf16)],
        compiler_params=params(),
    )(*[arrived[d] for d in range(windows)])
    traj_low, traj_high = moved(traj_low, "space", 1), moved(traj_high, "space", -1)

    state = shape((nvar, levels, rows, columns), f32)
    payload = shape((pairs, nvar * tiles + 1, 2 * SUB, LANES), i16)
    new_dual_obs, base_dual, base_inc, *payloads = pl.pallas_call(
        lambda *refs: model_kernel(windows, spaces, steps, nvar, levels, tiles, *refs),
        out_shape=[shape(dual_obs.shape, f32), state, state] + [payload] * (windows - 1),
        in_specs=[SMEM] * 3 + [VMEM] * 12,
        out_specs=[VMEM] * (3 + windows - 1),
        scratch_shapes=[
            pltpu.VMEM((2, steps, nvar, tiles, 4 * SUB, LANES), f32),
            pltpu.VMEM((2, 2, nvar, tiles, 4 * SUB, LANES), f32),
            pltpu.VMEM((2, 2, nvar, tiles, 4 * SUB, LANES), f32),
            pltpu.VMEM((2, steps, tiles, 2 * SUB, LANES), f32),
            pltpu.VMEM((2, nvar, tiles, SUB, LANES), f32),
            pltpu.VMEM((2,) + payload.shape, i16),
        ],
        compiler_params=params(32),
    )(
        coupling, obs_count, obs_var, totals, own, traj_low, traj_high, after,
        low, high, increment, dual_obs, model_rhs, dual_model, innovation,
    )
    sent = {d: moved(payloads[d - 1], "window", d, around=True) for d in order}

    new_dual_model, new_increment = pl.pallas_call(
        lambda *refs: final_kernel(windows, nvar, levels, tiles, *refs),
        out_shape=[shape(dual_model.shape, f32), shape(increment.shape, f32)],
        in_specs=[VMEM] * (windows + 2),
        out_specs=[VMEM] * 2,
        compiler_params=params(),
    )(*[sent[d] for d in range(1, windows)], totals, base_dual, base_inc)
    return new_dual_model, new_dual_obs, new_increment


def solution(mesh):
    placed = (
        P("members", None, None, None, "space", "window"),
        P(("members", "window"), None, None, "space", None),
        P(("members", "window"), None, None, "space", None),
        P(("members", "window"), None, None, "space", None),
        P(("members", "window"), None, None, "space", None),
        P(("members", "window"), None, None, "space", None),
        P(),
        P(("members", "window"), None, None),
        P(("members", "window"), None, None),
        P(("members", "window")),
    )
    return jax.shard_map(
        body,
        mesh=mesh,
        in_specs=placed,
        out_specs=(
            P(("members", "window"), None, None, "space", None),
            P(("members", "window"), None, None, "space", None),
            P(("members", "window"), None, None, "space", None),
        ),
        check_vma=False,
    )
```

```python
import jax
import jax.numpy as jnp
from jax import lax
from jax.experimental import pallas as pl
from jax.experimental.pallas import tpu as pltpu
from jax.sharding import PartitionSpec as P

LANES = 128
SUB = 8
HALF = SUB // 2
CODE_MAX = 32766.0
ROUNDER = 12582912.0

diffusion = 0.2
advection = 0.2
coupling_gain = 0.5
keep = 1.0 - 4.0 * diffusion
half_adv = 0.5 * advection

VMEM = pl.BlockSpec(memory_space=pltpu.VMEM)
SMEM = pl.BlockSpec(memory_space=pltpu.SMEM)
ANY = pl.BlockSpec(memory_space=pl.ANY)


def params(mib=24):
    return pltpu.CompilerParams(vmem_limit_bytes=mib * 1024 * 1024)


def lane_index():
    return lax.broadcasted_iota(jnp.int32, (SUB, LANES), 1)


def row_index():
    return lax.broadcasted_iota(jnp.int32, (SUB, LANES), 0)


def tiled(wide):
    short = -wide.shape[1] % LANES
    if short:
        wide = jnp.concatenate([wide, jnp.zeros((wide.shape[0], short), wide.dtype)], 1)
    return [wide[:, i : i + LANES] for i in range(0, wide.shape[1], LANES)]


def place(parts, rolled, lane):
    built = {}
    for key, tiles, first, width, target in parts:
        done = 0
        while done < width:
            a, b = first + done, target + done
            n = min(width - done, LANES - a % LANES, LANES - b % LANES)
            shift = (b - a) % LANES
            name = (key, a // LANES, shift)
            if name not in rolled:
                value = tiles[a // LANES]
                rolled[name] = pltpu.roll(value, shift, 1) if shift else value
            if b % LANES:
                built[b // LANES] = jnp.where(
                    lane >= b % LANES, rolled[name], built[b // LANES]
                )
            else:
                built[b // LANES] = rolled[name]
            done += n
    return [built[i] for i in range(len(built))]


def joined_halves(first, second):
    top = row_index()[:, :1] < HALF
    last = jnp.where(top, pltpu.roll(first, HALF, 0), second)
    start = jnp.where(top, first, pltpu.roll(second, HALF, 0))
    return last, start


def widened(own, near, far, odd, even):
    top = row_index() < HALF
    low, high = jnp.where(even, far, near), jnp.where(even, near, far)
    turned = pltpu.roll(own, HALF, 0)
    low = pltpu.roll(low, HALF, 0) if odd else low
    high = high if odd else pltpu.roll(high, HALF, 0)
    return jnp.where(top, low, turned), jnp.where(top, turned, high)


def row_codes(planes):
    lane = lax.broadcasted_iota(jnp.int32, planes[0][0].shape, 1)
    scales = jnp.zeros(planes[0][0].shape, jnp.float32)
    out = []
    for v, row in enumerate(planes):
        big = jnp.abs(row[0])
        for value in row[1:]:
            big = jnp.maximum(big, jnp.abs(value))
        big = jnp.max(big, axis=1, keepdims=True)
        power = jnp.clip(jnp.ceil(jnp.log2(jnp.maximum(big, 1e-30))), -90.0, 126.0)
        scales = jnp.where(lane == v, power, scales)
        gain = CODE_MAX * jnp.exp2(-power)
        for value in row:
            scaled = jnp.clip(value * gain, -CODE_MAX, CODE_MAX)
            out.append((scaled + ROUNDER) - ROUNDER)
    return out, scales


def shorts(value):
    return value.astype(jnp.int32).astype(jnp.int16)


def floats(value):
    return value.astype(jnp.int32).astype(jnp.float32)


def pack_kernel(distances, windows, steps, nvar, levels, part, var_ref, traj_ref, *outs):
    me = lax.axis_index("window")
    lane, row = lane_index(), row_index()
    variance = jnp.zeros((SUB, LANES), jnp.float32)
    for v in range(nvar):
        for lev in range(levels):
            variance = jnp.where(lane == v * levels + lev, var_ref[0, v, lev], variance)
    high = variance.astype(jnp.bfloat16).astype(jnp.float32)
    middle = (variance - high).astype(jnp.bfloat16).astype(jnp.float32)
    low = variance - high - middle
    split = jnp.where(row == 0, high, jnp.where(row == 1, middle, jnp.where(row == 2, low, 0.0)))
    split = split.astype(jnp.bfloat16)

    for n, d in enumerate(distances):
        outs[n][nvar * levels, :, :LANES] = split
        target = lax.rem(me + d, windows)

        def variable(v, carry, n=n, target=target):
            for lev in range(levels):
                pieces = [
                    tiled(traj_ref[target, j, v, lev].astype(jnp.float32)) for j in range(steps)
                ]
                parts = [(j, pieces[j], 0, part, j * part) for j in range(steps)]
                wide = jnp.concatenate(place(parts, {}, lane), 1)
                outs[n][v * levels + lev] = wide.astype(jnp.bfloat16)
            return carry

        lax.fori_loop(0, nvar, variable, 0, unroll=len(distances) == 1)


def even_place():
    return lax.rem(lax.axis_index("space"), 2) == 0


def code_kernel(count, own_codes, *refs):
    sources, near_ref, far_ref = refs[:count], refs[count + 1], refs[count + 2]
    even = even_place()

    def pair(i, carry):
        near, far = [], []
        for ref in sources:
            coded = []
            for odd in range(2):
                planes = [
                    [ref[0, v, 2 * i + odd, :, t : t + LANES] for t in range(0, ref.shape[-1], LANES)]
                    for v in range(ref.shape[1])
                ]
                values, scales = row_codes(planes)
                coded.append(values + [scales])
            if own_codes:
                for n, (first, second) in enumerate(zip(*coded)):
                    refs[count + 3][i, n] = shorts(jnp.concatenate([first, second], 0))
            for first, second in zip(*coded):
                last, start = joined_halves(first, second)
                near.append(jnp.where(even, last, start))
                far.append(jnp.where(even, start, last))
            if len(near) % 2:
                near.append(jnp.zeros((SUB, LANES), jnp.float32))
                far.append(jnp.zeros((SUB, LANES), jnp.float32))
        for tiles, ref in ((near, near_ref), (far, far_ref)):
            for n in range(0, len(tiles), 2):
                ref[i, n // 2] = shorts(jnp.concatenate(tiles[n : n + 2], 0))
        return carry

    lax.fori_loop(0, near_ref.shape[0], pair, 0)


def decoded(ref, i, first, nvar, tiles):
    def tile(n):
        whole = floats(ref[i, n // 2])
        return whole[SUB:] if n % 2 else whole[:SUB]

    scales = jnp.exp2(tile(first + nvar * tiles)) * (1.0 / CODE_MAX)
    return [
        [tile(first + v * tiles + t) * scales[:, v : v + 1] for t in range(tiles)]
        for v in range(nvar)
    ]


def assemble_kernel(windows, steps, nvar, levels, part, *refs):
    pieces = refs[:windows]
    own_ref, far_ref, total_ref, stack_ref = refs[windows:]
    me = lax.axis_index("window")
    even = even_place()
    lane = lane_index()
    total = jnp.zeros((1, LANES), jnp.float32)
    for d in range(windows):
        source = lax.rem(me - d + windows, windows)
        stack_ref[source] = pieces[d][: nvar * levels]
        split = pieces[d][nvar * levels, :, :LANES].astype(jnp.float32)
        here = jnp.sum(split, axis=0, keepdims=True)
        total = total + jnp.where(source <= me, here, 0.0)
    for p in range(nvar * levels):
        total_ref[p] = jnp.broadcast_to(total[:, p : p + 1], (SUB, LANES))

    pairs = levels // 2

    def pair(n, carry):
        both = []
        for odd in range(2):
            plane = 2 * n + odd
            sources = [tiled(stack_ref[w, plane].astype(jnp.float32)) for w in range(windows)]
            rolled = {}
            built = []
            for j in range(steps):
                parts = [(w, sources[w], j * part, part, w * part) for w in range(windows)]
                built.append(place(parts, rolled, lane))
                own_ref[j, plane] = jnp.concatenate(built[j], 1).astype(jnp.bfloat16)
            both.append(built)
        for j in range(steps):
            halves = [joined_halves(a, b) for a, b in zip(both[0][j], both[1][j])]
            last, start = (jnp.concatenate([h[k] for h in halves], 1) for k in range(2))
            far_ref[j, n] = jnp.where(even, start, last).astype(jnp.bfloat16)
        return carry

    lax.fori_loop(0, nvar * pairs, pair, 0)


def near_kernel(own_ref, order_ref, near_ref):
    even = even_place()

    def pair(n, carry):
        for j in range(own_ref.shape[0]):
            for t in range(0, own_ref.shape[-1], LANES):
                cut = slice(t, t + LANES)
                first, second = (
                    own_ref[j, 2 * n + odd, :, cut].astype(jnp.float32) for odd in range(2)
                )
                last, start = joined_halves(first, second)
                near_ref[j, n, :, cut] = jnp.where(even, last, start).astype(jnp.bfloat16)
        return carry

    lax.fori_loop(0, near_ref.shape[1], pair, 0)


def prepare_kernel(
    steps, nvar, levels, tiles,
    count_ref, after_ref, anear_ref, afar_ref, fnear_ref, ffar_ref, inc_ref, dobs_ref,
    first_ref, last_ref, force_ref,
):
    even = even_place()
    blocks = [slice(0, SUB), slice(SUB, 2 * SUB)]
    cuts = [slice(t * LANES, (t + 1) * LANES) for t in range(tiles)]

    def pair(i, carry):
        offset = -(-(nvar * tiles + 1) // 2) * 2
        fields = [decoded(ref, i, 0, nvar, tiles) for ref in (fnear_ref, ffar_ref)]
        forces = [decoded(ref, i, offset, steps, tiles) for ref in (fnear_ref, ffar_ref)]
        afters = [decoded(ref, i, 0, nvar, tiles) for ref in (anear_ref, afar_ref)]
        scales = jnp.exp2(floats(after_ref[i, nvar * tiles])) * (1.0 / CODE_MAX)
        for odd in range(2):
            lev = 2 * i + odd
            rows = blocks[odd]
            for t in range(tiles):
                for v in range(nvar):
                    near, far = (side[v][t] for side in fields)
                    halves = widened(inc_ref[0, v, lev, :, cuts[t]], near, far, odd, even)
                    for b in range(2):
                        first_ref[lev, v, t, blocks[b], :] = halves[b]
                    near, far = (side[v][t] for side in afters)
                    own = floats(after_ref[i, v * tiles + t])[rows] * scales[rows, v : v + 1]
                    halves = widened(own, near, far, odd, even)
                    for b in range(2):
                        last_ref[lev, v, t, blocks[b], :] = -halves[b]
                for j in range(steps):
                    seen = jnp.where(j < count_ref[0], 1.0, 0.0)
                    near, far = (side[j][t] for side in forces)
                    halves = widened(dobs_ref[0, j, lev, :, cuts[t]], near, far, odd, even)
                    for b in range(2):
                        force_ref[lev, j, t, blocks[b], :] = seen * halves[b]
        return carry

    lax.fori_loop(0, levels // 2, pair, 0)


def model_kernel(
    windows, spaces, steps, nvar, levels, tiles,
    coupling_ref, count_ref, noise_ref, total_ref, own_ref, near_ref, far_ref,
    first_ref, last_ref, force_ref, inc_ref, dobs_ref, rhs_ref, dual_ref, innov_ref,
    ndo_ref, ndm_ref, ninc_ref, *rest,
):
    payload_refs = rest[: windows - 1]
    x_ref, s_ref, a_ref, q_ref = rest[windows - 1 :]
    me = lax.axis_index("window")
    place_x = lax.axis_index("space")
    even = even_place()
    lane, row = lane_index(), row_index()
    pairs = levels // 2
    zero = jnp.zeros((SUB, LANES), jnp.float32)
    blocks = [slice(SUB, 2 * SUB), slice(2 * SUB, 3 * SUB)]
    ups = [slice(b.start + 1, b.stop + 1) for b in blocks]
    downs = [slice(b.start - 1, b.stop - 1) for b in blocks]
    mine = slice(SUB + HALF, 2 * SUB + HALF)
    cuts = [slice(t * LANES, (t + 1) * LANES) for t in range(tiles)]
    mix = [[coupling_gain * coupling_ref[v, u] for u in range(nvar)] for v in range(nvar)]
    low_wall = jnp.where((row == HALF) & (place_x == 0), 0.0, 1.0)
    high_wall = jnp.where((row == HALF - 1) & (place_x == spaces - 1), 0.0, 1.0)

    def from_north(line):
        turned = [pltpu.roll(value, LANES - 1, 1) for value in line]
        return [
            jnp.where(lane < LANES - 1, turned[t], turned[(t + 1) % tiles]) for t in range(tiles)
        ]

    def from_south(line):
        turned = [pltpu.roll(value, 1, 1) for value in line]
        return [jnp.where(lane > 0, turned[t], turned[t - 1]) for t in range(tiles)]

    def masked_last(line):
        return line[:-1] + [jnp.where(lane < LANES - 1, line[-1], 0.0)]

    def masked_first(line):
        return [jnp.where(lane > 0, line[0], 0.0)] + line[1:]

    def walled(block, east, west):
        if block == 0:
            return east, [low_wall * value for value in west]
        return [high_wall * value for value in east], west

    def pair(i, outer):
        for odd in range(2):
            lev = 2 * i + odd

            def spread(j, carry, odd=odd, lev=lev):
                for v in range(nvar):
                    for t in range(tiles):
                        halves = widened(
                            own_ref[j, v * levels + lev, :, cuts[t]].astype(jnp.float32),
                            near_ref[j, v * pairs + i, :, cuts[t]].astype(jnp.float32),
                            far_ref[j, v * pairs + i, :, cuts[t]].astype(jnp.float32),
                            odd,
                            even,
                        )
                        for b in range(2):
                            x_ref[odd, j, v, t, blocks[b], :] = halves[b]
                return carry

            lax.fori_loop(0, steps, spread, 0)

            for v in range(nvar):
                for t in range(tiles):
                    s_ref[odd, 0, v, t, SUB : 3 * SUB, :] = first_ref[lev, v, t]
                    a_ref[odd, 0, v, t, SUB : 3 * SUB, :] = last_ref[lev, v, t]

        def tangent(j, carry):
            now = lax.rem(j, 2)
            seen = jnp.where(j < count_ref[0], 1.0, 0.0)
            for odd in range(2):
                lev = 2 * i + odd
                noise = jnp.full((SUB, LANES), noise_ref[0, j, lev])
                share = seen / noise
                for t in range(tiles):
                    gap = innov_ref[0, j, lev, :, cuts[t]] - noise * dobs_ref[0, j, lev, :, cuts[t]]
                    gap = gap - s_ref[odd, now, 0, t, mine, :]
                    ndo_ref[0, j, lev, :, cuts[t]] = gap * share
                for b in range(2):
                    here, up, down = blocks[b], ups[b], downs[b]
                    x = [[x_ref[odd, j, u, t, here, :] for t in range(tiles)] for u in range(nvar)]
                    ce = [diffusion - half_adv * value for value in x[0]]
                    cw = [diffusion + half_adv * value for value in x[0]]
                    ce, cw = walled(b, ce, cw)
                    cn = masked_last([diffusion - half_adv * value for value in x[1]])
                    cs = masked_first([diffusion + half_adv * value for value in x[1]])
                    s = [
                        [s_ref[odd, now, u, t, here, :] for t in range(tiles)] for u in range(nvar)
                    ]
                    xs = [[x[u][t] * s[u][t] for t in range(tiles)] for u in range(nvar)]
                    for v in range(nvar):
                        north, south = from_north(s[v]), from_south(s[v])
                        for t in range(tiles):
                            fresh = keep * s[v][t] + ce[t] * s_ref[odd, now, v, t, up, :]
                            fresh = fresh + cw[t] * s_ref[odd, now, v, t, down, :]
                            fresh = fresh + cn[t] * north[t] + cs[t] * south[t]
                            for u in range(nvar):
                                fresh = fresh + mix[v][u] * xs[u][t]
                            s_ref[odd, 1 - now, v, t, here, :] = fresh
            return carry

        lax.fori_loop(0, steps, tangent, 0)

        def adjoint(turn, carry):
            now = lax.rem(turn, 2)
            j = steps - 1 - turn
            for odd in range(2):
                for b in range(2):
                    here, up, down = blocks[b], ups[b], downs[b]
                    x = [[x_ref[odd, j, u, t, here, :] for t in range(tiles)] for u in range(nvar)]
                    ce = [
                        diffusion + half_adv * x_ref[odd, j, 0, t, up, :] for t in range(tiles)
                    ]
                    cw = [
                        diffusion - half_adv * x_ref[odd, j, 0, t, down, :] for t in range(tiles)
                    ]
                    ce, cw = walled(b, ce, cw)
                    cn = masked_first([diffusion + half_adv * value for value in x[1]])
                    cs = masked_last([diffusion - half_adv * value for value in x[1]])
                    a = [
                        [a_ref[odd, now, u, t, here, :] for t in range(tiles)] for u in range(nvar)
                    ]
                    for u in range(nvar):
                        north = from_north([cn[t] * a[u][t] for t in range(tiles)])
                        south = from_south([cs[t] * a[u][t] for t in range(tiles)])
                        for t in range(tiles):
                            fresh = keep * a[u][t] + ce[t] * a_ref[odd, now, u, t, up, :]
                            fresh = fresh + cw[t] * a_ref[odd, now, u, t, down, :]
                            fresh = fresh + north[t] + south[t]
                            pull = mix[0][u] * a[0][t]
                            for v in range(1, nvar):
                                pull = pull + mix[v][u] * a[v][t]
                            fresh = fresh + x[u][t] * pull
                            if u == 0:
                                fresh = fresh + force_ref[2 * i + odd, j, t, b * SUB : (b + 1) * SUB, :]
                            a_ref[odd, 1 - now, u, t, here, :] = fresh
            return carry

        lax.fori_loop(0, steps, adjoint, 0)

        end = steps % 2
        coded = []
        for odd in range(2):
            lev = 2 * i + odd
            back, ahead = [], []
            for v in range(nvar):
                share = total_ref[v * levels + lev]
                tv, gv = [], []
                for t in range(tiles):
                    term = a_ref[odd, end, v, t, mine, :] - last_ref[lev, v, t, HALF : HALF + SUB, :]
                    given = rhs_ref[0, v, lev, :, cuts[t]] - inc_ref[0, v, lev, :, cuts[t]]
                    given = given + share * term
                    ndm_ref[v, lev, :, cuts[t]] = -(dual_ref[0, v, lev, :, cuts[t]] + term)
                    ninc_ref[v, lev, :, cuts[t]] = given
                    tv.append(term)
                    gv.append(given + s_ref[odd, end, v, t, mine, :])
                back.append(tv)
                ahead.append(gv)
            coded.append((row_codes(back), row_codes(ahead)))
        for kind in range(2):
            first, second = coded[0][kind], coded[1][kind]
            for n, (a, b) in enumerate(zip(first[0] + [first[1]], second[0] + [second[1]])):
                q_ref[kind, i, n] = shorts(jnp.concatenate([a, b], 0))
        return outer

    lax.fori_loop(0, pairs, pair, 0)
    for d in range(1, windows):
        payload_refs[d - 1][...] = q_ref[jnp.where(me + d >= windows, 0, 1)]


def final_kernel(windows, nvar, levels, tiles, *refs):
    pieces = refs[: windows - 1]
    total_ref, base_dual_ref, base_inc_ref, ndm_ref, ninc_ref = refs[windows - 1 :]
    me = lax.axis_index("window")
    pairs = levels // 2
    cuts = [slice(t * LANES, (t + 1) * LANES) for t in range(tiles)]

    def pair(i, carry):
        tails = [None] * (nvar * tiles)
        heads = [None] * (nvar * tiles)
        for d in range(1, windows):
            piece = pieces[d - 1]
            scales = jnp.exp2(floats(piece[i, nvar * tiles])) * (1.0 / CODE_MAX)
            later = jnp.where(d > me, scales, 0.0)
            earlier = jnp.where(d > me, 0.0, scales)
            for v in range(nvar):
                for t in range(tiles):
                    n = v * tiles + t
                    value = floats(piece[i, n])
                    tail, head = value * later[:, v : v + 1], value * earlier[:, v : v + 1]
                    tails[n] = tail if d == 1 else tails[n] + tail
                    heads[n] = head if d == 1 else heads[n] + head
        for v in range(nvar):
            for odd in range(2):
                lev = 2 * i + odd
                share = total_ref[v * levels + lev]
                for t in range(tiles):
                    rows = slice(odd * SUB, (odd + 1) * SUB)
                    tail, head = tails[v * tiles + t][rows], heads[v * tiles + t][rows]
                    ndm_ref[0, v, lev, :, cuts[t]] = base_dual_ref[v, lev, :, cuts[t]] - tail
                    ninc_ref[0, v, lev, :, cuts[t]] = (
                        base_inc_ref[v, lev, :, cuts[t]] + head + share * tail
                    )
        return carry

    lax.fori_loop(0, pairs, pair, 0)


def moved(block, axis, distance, around=False):
    count = lax.axis_size(axis)
    route = [(i, (i + distance) % count) for i in range(count) if around or 0 <= i + distance < count]
    return lax.ppermute(block, axis, route)


def swaps(axis, first):
    route = []
    for i in range(first, lax.axis_size(axis) - 1, 2):
        route += [(i, i + 1), (i + 1, i)]
    return route


def swapped(block, axis, first):
    return lax.ppermute(block, axis, swaps(axis, first))


def swapped_back(block, first):
    windows, spaces = lax.axis_size("window"), lax.axis_size("space")
    route = [
        ((w + 1) * spaces + source, w * spaces + target)
        for w in range(windows - 1)
        for source, target in swaps("space", first)
    ]
    return lax.ppermute(block, ("window", "space"), route)


def body(
    trajectory,
    dual_model,
    increment,
    model_rhs,
    dual_obs,
    innovation,
    coupling,
    error_var,
    obs_var,
    obs_count,
):
    windows, spaces = lax.axis_size("window"), lax.axis_size("space")
    _, steps, nvar, levels, rows, part = trajectory.shape
    columns = dual_model.shape[-1]
    tiles = columns // LANES
    assert trajectory.shape[0] == windows and windows > 1 and rows == SUB and steps == HALF
    assert columns == tiles * LANES == windows * part and levels % 2 == 0
    pairs = levels // 2
    wide = -(-steps * part // LANES) * LANES
    bf16, f32, i16 = jnp.bfloat16, jnp.float32, jnp.int16

    def shape(dims, dtype):
        return jax.ShapeDtypeStruct(dims, dtype)

    light = pl.CostEstimate(flops=0, bytes_accessed=0, transcendentals=0)

    def packed(distances):
        return pl.pallas_call(
            lambda *refs: pack_kernel(distances, windows, steps, nvar, levels, part, *refs),
            out_shape=[shape((nvar * levels + 1, rows, wide), bf16)] * len(distances),
            in_specs=[SMEM, VMEM],
            out_specs=[VMEM] * len(distances),
            compiler_params=params(),
            cost_estimate=light,
        )(error_var, trajectory)

    order = sorted(range(1, windows), key=lambda d: -d * (windows - d))
    groups = [[d] for d in order] if windows <= 4 else [order]
    blocks = {}
    for group in groups:
        blocks.update(zip(group, packed(group)))
    arrived = {d: moved(blocks[d], "window", d, around=True) for d in order}
    arrived[0] = packed([0])[0]

    payload = shape((pairs, nvar * tiles + 1, 2 * SUB, LANES), i16)

    def half_tiles(*counts):
        total = sum(-(-(count * tiles + 1) // 2) for count in counts)
        return shape((pairs, total, 2 * SUB, LANES), i16)

    def coded(fields, own_codes):
        halves = half_tiles(*[field.shape[1] for field in fields])
        return pl.pallas_call(
            lambda *refs: code_kernel(len(fields), own_codes, *refs),
            out_shape=[halves, halves] + [payload] * own_codes,
            in_specs=[VMEM] * len(fields) + [ANY],
            out_specs=[VMEM] * (2 + own_codes),
            compiler_params=params(),
            cost_estimate=light,
        )(*fields, arrived[0])

    after_near, after_far, after = coded([dual_model], 1)
    after = moved(after, "window", -1)
    after_near, after_far = swapped_back(after_near, 0), swapped_back(after_far, 1)
    near, far = coded([increment, dual_obs], 0)
    far, near = swapped(far, "space", 1), swapped(near, "space", 0)

    own, traj_far, totals = pl.pallas_call(
        lambda *refs: assemble_kernel(windows, steps, nvar, levels, part, *refs),
        out_shape=[
            shape((steps, nvar * levels, rows, columns), bf16),
            shape((steps, nvar * pairs, rows, columns), bf16),
            shape((nvar * levels, rows, LANES), f32),
        ],
        in_specs=[VMEM] * windows,
        out_specs=[VMEM] * 3,
        scratch_shapes=[pltpu.VMEM((windows, nvar * levels, rows, wide), bf16)],
        compiler_params=params(),
    )(*[arrived[d] for d in range(windows)])
    traj_far = swapped(traj_far, "space", 1)

    state = shape((nvar, levels, rows, columns), f32)
    around = [shape((levels, n, tiles, 2 * SUB, LANES), f32) for n in (nvar, nvar, steps)]
    first, last, force = pl.pallas_call(
        lambda *refs: prepare_kernel(steps, nvar, levels, tiles, *refs),
        out_shape=around,
        in_specs=[SMEM] + [VMEM] * 7,
        out_specs=[VMEM] * 3,
        compiler_params=params(),
    )(obs_count, after, after_near, after_far, near, far, increment, dual_obs)
    traj_near = pl.pallas_call(
        near_kernel,
        out_shape=shape((steps, nvar * pairs, rows, columns), bf16),
        in_specs=[VMEM, ANY],
        out_specs=VMEM,
        compiler_params=params(),
    )(own, force)
    traj_near = swapped(traj_near, "space", 0)
    new_dual_obs, base_dual, base_inc, *payloads = pl.pallas_call(
        lambda *refs: model_kernel(windows, spaces, steps, nvar, levels, tiles, *refs),
        out_shape=[shape(dual_obs.shape, f32), state, state] + [payload] * (windows - 1),
        in_specs=[SMEM] * 3 + [VMEM] * 12,
        out_specs=[VMEM] * (3 + windows - 1),
        scratch_shapes=[
            pltpu.VMEM((2, steps, nvar, tiles, 4 * SUB, LANES), f32),
            pltpu.VMEM((2, 2, nvar, tiles, 4 * SUB, LANES), f32),
            pltpu.VMEM((2, 2, nvar, tiles, 4 * SUB, LANES), f32),
            pltpu.VMEM((2,) + payload.shape, i16),
        ],
        compiler_params=params(32),
    )(
        coupling, obs_count, obs_var, totals, own, traj_near, traj_far,
        first, last, force, increment, dual_obs, model_rhs, dual_model, innovation,
    )
    sent = {d: moved(payloads[d - 1], "window", d, around=True) for d in order}

    new_dual_model, new_increment = pl.pallas_call(
        lambda *refs: final_kernel(windows, nvar, levels, tiles, *refs),
        out_shape=[shape(dual_model.shape, f32), shape(increment.shape, f32)],
        in_specs=[VMEM] * (windows + 2),
        out_specs=[VMEM] * 2,
        compiler_params=params(),
    )(*[sent[d] for d in range(1, windows)], totals, base_dual, base_inc)
    return new_dual_model, new_dual_obs, new_increment


def solution(mesh):
    placed = (
        P("members", None, None, None, "space", "window"),
        P(("members", "window"), None, None, "space", None),
        P(("members", "window"), None, None, "space", None),
        P(("members", "window"), None, None, "space", None),
        P(("members", "window"), None, None, "space", None),
        P(("members", "window"), None, None, "space", None),
        P(),
        P(("members", "window"), None, None),
        P(("members", "window"), None, None),
        P(("members", "window")),
    )
    return jax.shard_map(
        body,
        mesh=mesh,
        in_specs=placed,
        out_specs=(
            P(("members", "window"), None, None, "space", None),
            P(("members", "window"), None, None, "space", None),
            P(("members", "window"), None, None, "space", None),
        ),
        check_vma=False,
    )
```

```python
import jax
import jax.numpy as jnp
from jax import lax
from jax.experimental import pallas as pl
from jax.experimental.pallas import tpu as pltpu
from jax.sharding import PartitionSpec as P

LANES = 128
SUB = 8
HALF = SUB // 2
CODE_MAX = 32766.0
ROUNDER = 12582912.0

diffusion = 0.2
advection = 0.2
coupling_gain = 0.5
keep = 1.0 - 4.0 * diffusion
half_adv = 0.5 * advection

VMEM = pl.BlockSpec(memory_space=pltpu.VMEM)
SMEM = pl.BlockSpec(memory_space=pltpu.SMEM)
ANY = pl.BlockSpec(memory_space=pl.ANY)


def params(mib=24):
    return pltpu.CompilerParams(vmem_limit_bytes=mib * 1024 * 1024)


def lane_index():
    return lax.broadcasted_iota(jnp.int32, (SUB, LANES), 1)


def row_index():
    return lax.broadcasted_iota(jnp.int32, (SUB, LANES), 0)


def tiled(wide):
    short = -wide.shape[1] % LANES
    if short:
        wide = jnp.concatenate([wide, jnp.zeros((wide.shape[0], short), wide.dtype)], 1)
    return [wide[:, i : i + LANES] for i in range(0, wide.shape[1], LANES)]


def place(parts, rolled, lane):
    built = {}
    for key, tiles, first, width, target in parts:
        done = 0
        while done < width:
            a, b = first + done, target + done
            n = min(width - done, LANES - a % LANES, LANES - b % LANES)
            shift = (b - a) % LANES
            name = (key, a // LANES, shift)
            if name not in rolled:
                value = tiles[a // LANES]
                rolled[name] = pltpu.roll(value, shift, 1) if shift else value
            if b % LANES:
                built[b // LANES] = jnp.where(
                    lane >= b % LANES, rolled[name], built[b // LANES]
                )
            else:
                built[b // LANES] = rolled[name]
            done += n
    return [built[i] for i in range(len(built))]


def joined_halves(first, second):
    top = row_index()[:, :1] < HALF
    last = jnp.where(top, pltpu.roll(first, HALF, 0), second)
    start = jnp.where(top, first, pltpu.roll(second, HALF, 0))
    return last, start


def widened(own, near, far, odd, even):
    top = row_index() < HALF
    low, high = jnp.where(even, far, near), jnp.where(even, near, far)
    turned = pltpu.roll(own, HALF, 0)
    low = pltpu.roll(low, HALF, 0) if odd else low
    high = high if odd else pltpu.roll(high, HALF, 0)
    return jnp.where(top, low, turned), jnp.where(top, turned, high)


def row_codes(planes):
    lane = lax.broadcasted_iota(jnp.int32, planes[0][0].shape, 1)
    scales = jnp.zeros(planes[0][0].shape, jnp.float32)
    out = []
    for v, row in enumerate(planes):
        big = jnp.abs(row[0])
        for value in row[1:]:
            big = jnp.maximum(big, jnp.abs(value))
        big = jnp.max(big, axis=1, keepdims=True)
        power = jnp.clip(jnp.ceil(jnp.log2(jnp.maximum(big, 1e-30))), -90.0, 126.0)
        scales = jnp.where(lane == v, power, scales)
        gain = CODE_MAX * jnp.exp2(-power)
        for value in row:
            scaled = jnp.clip(value * gain, -CODE_MAX, CODE_MAX)
            out.append((scaled + ROUNDER) - ROUNDER)
    return out, scales


def shorts(value):
    return value.astype(jnp.int32).astype(jnp.int16)


def floats(value):
    return value.astype(jnp.int32).astype(jnp.float32)


def pack_kernel(distances, windows, steps, nvar, levels, part, var_ref, traj_ref, *rest):
    outs, wide_ref = rest[:-1], rest[-1]
    me = lax.axis_index("window")
    lane = lane_index()
    wide_ref[...] = jnp.zeros((SUB, LANES), jnp.float32)
    wide_ref[:levels, :nvar] = var_ref[0]
    variance = wide_ref[...]
    high = variance.astype(jnp.bfloat16).astype(jnp.float32)
    middle = (variance - high).astype(jnp.bfloat16).astype(jnp.float32)
    low = variance - high - middle
    split = high + pltpu.roll(middle, HALF, 0) + pltpu.roll(low, LANES // 2, 1)
    split = split.astype(jnp.bfloat16)

    for n, d in enumerate(distances):
        outs[n][nvar * levels, :, :LANES] = split
        target = lax.rem(me + d, windows)

        def variable(v, carry, n=n, target=target):
            for lev in range(levels):
                pieces = [
                    tiled(traj_ref[target, j, v, lev].astype(jnp.float32)) for j in range(steps)
                ]
                parts = [(j, pieces[j], 0, part, j * part) for j in range(steps)]
                wide = jnp.concatenate(place(parts, {}, lane), 1)
                outs[n][v * levels + lev] = wide.astype(jnp.bfloat16)
            return carry

        lax.fori_loop(0, nvar, variable, 0, unroll=len(distances) == 1)


def even_place():
    return lax.rem(lax.axis_index("space"), 2) == 0


def level_codes(ref, lev):
    planes = [
        [ref[0, v, lev, :, t : t + LANES] for t in range(0, ref.shape[-1], LANES)]
        for v in range(ref.shape[1])
    ]
    values, scales = row_codes(planes)
    return values + [scales]


def own_code_kernel(field_ref, out_ref):
    def pair(i, carry):
        coded = [level_codes(field_ref, 2 * i + odd) for odd in range(2)]
        for n, (first, second) in enumerate(zip(*coded)):
            out_ref[i, n] = shorts(jnp.concatenate([first, second], 0))
        return carry

    lax.fori_loop(0, out_ref.shape[0], pair, 0)


def half_code_kernel(*refs):
    sources, (near_ref, far_ref) = refs[:-2], refs[-2:]
    even = even_place()

    def pair(i, carry):
        groups = []
        for ref in sources:
            if ref.dtype == jnp.int16:
                whole = [floats(ref[i, n]) for n in range(ref.shape[1])]
                groups.append([[tile[:SUB] for tile in whole], [tile[SUB:] for tile in whole]])
            else:
                groups.append([level_codes(ref, 2 * i + odd) for odd in range(2)])
        near, far = [], []
        for coded in groups:
            for first, second in zip(*coded):
                last, start = joined_halves(first, second)
                near.append(jnp.where(even, last, start))
                far.append(jnp.where(even, start, last))
            if len(near) % 2:
                near.append(jnp.zeros((SUB, LANES), jnp.float32))
                far.append(jnp.zeros((SUB, LANES), jnp.float32))
        for tiles, ref in ((near, near_ref), (far, far_ref)):
            for n in range(0, len(tiles), 2):
                ref[i, n // 2] = shorts(jnp.concatenate(tiles[n : n + 2], 0))
        return carry

    lax.fori_loop(0, near_ref.shape[0], pair, 0)


def half_tile(ref, i, n):
    whole = floats(ref[i, n // 2])
    return whole[SUB:] if n % 2 else whole[:SUB]


def decoded(ref, i, first, nvar, tiles):
    scales = jnp.exp2(half_tile(ref, i, first + nvar * tiles)) * (1.0 / CODE_MAX)
    return [
        [half_tile(ref, i, first + v * tiles + t) * scales[:, v : v + 1] for t in range(tiles)]
        for v in range(nvar)
    ]


def assemble_kernel(windows, steps, nvar, levels, part, *refs):
    pieces = refs[:windows]
    own_ref, far_ref, total_ref, stack_ref = refs[windows:]
    me = lax.axis_index("window")
    even = even_place()
    lane = lane_index()
    total = jnp.zeros((SUB, LANES), jnp.float32)
    for d in range(windows):
        source = lax.rem(me - d + windows, windows)
        stack_ref[source] = pieces[d][: nvar * levels]
        split = pieces[d][nvar * levels, :, :LANES].astype(jnp.float32)
        here = split + pltpu.roll(split, HALF, 0) + pltpu.roll(split, LANES // 2, 1)
        total = total + jnp.where(source <= me, here, 0.0)
    for v in range(nvar):
        for lev in range(levels):
            one = total[lev : lev + 1, v : v + 1]
            total_ref[v * levels + lev] = jnp.broadcast_to(one, (SUB, LANES))

    pairs = levels // 2

    def pair(n, carry):
        both = []
        for odd in range(2):
            plane = 2 * n + odd
            sources = [tiled(stack_ref[w, plane].astype(jnp.float32)) for w in range(windows)]
            rolled = {}
            built = []
            for j in range(steps):
                parts = [(w, sources[w], j * part, part, w * part) for w in range(windows)]
                built.append(place(parts, rolled, lane))
                own_ref[j, plane] = jnp.concatenate(built[j], 1).astype(jnp.bfloat16)
            both.append(built)
        for j in range(steps):
            halves = [joined_halves(a, b) for a, b in zip(both[0][j], both[1][j])]
            last, start = (jnp.concatenate([h[k] for h in halves], 1) for k in range(2))
            far_ref[j, n] = jnp.where(even, start, last).astype(jnp.bfloat16)
        return carry

    lax.fori_loop(0, nvar * pairs, pair, 0)


def near_kernel(own_ref, *refs):
    near_ref = refs[-1]
    even = even_place()

    def pair(n, carry):
        for j in range(own_ref.shape[0]):
            for t in range(0, own_ref.shape[-1], LANES):
                cut = slice(t, t + LANES)
                first, second = (
                    own_ref[j, 2 * n + odd, :, cut].astype(jnp.float32) for odd in range(2)
                )
                last, start = joined_halves(first, second)
                near_ref[j, n, :, cut] = jnp.where(even, last, start).astype(jnp.bfloat16)
        return carry

    lax.fori_loop(0, near_ref.shape[1], pair, 0)


def prepare_kernel(
    steps, nvar, levels, tiles,
    count_ref, after_ref, anear_ref, afar_ref, near_ref, far_ref, inc_ref, dobs_ref,
    first_ref, last_ref, force_ref,
):
    even = even_place()
    blocks = [slice(0, SUB), slice(SUB, 2 * SUB)]
    cuts = [slice(t * LANES, (t + 1) * LANES) for t in range(tiles)]

    def pair(i, carry):
        offset = -(-(nvar * tiles + 1) // 2) * 2
        fields = [decoded(ref, i, 0, nvar, tiles) for ref in (near_ref, far_ref)]
        forces = [decoded(ref, i, offset, steps, tiles) for ref in (near_ref, far_ref)]
        afters = [decoded(ref, i, 0, nvar, tiles) for ref in (anear_ref, afar_ref)]
        scales = jnp.exp2(floats(after_ref[i, nvar * tiles])) * (1.0 / CODE_MAX)
        for odd in range(2):
            lev = 2 * i + odd
            rows = blocks[odd]
            for t in range(tiles):
                for v in range(nvar):
                    near, far = (side[v][t] for side in fields)
                    halves = widened(inc_ref[0, v, lev, :, cuts[t]], near, far, odd, even)
                    for b in range(2):
                        first_ref[lev, v, t, blocks[b], :] = halves[b]
                    near, far = (side[v][t] for side in afters)
                    own = floats(after_ref[i, v * tiles + t])[rows] * scales[rows, v : v + 1]
                    halves = widened(own, near, far, odd, even)
                    for b in range(2):
                        last_ref[lev, v, t, blocks[b], :] = -halves[b]
                for j in range(steps):
                    seen = jnp.where(j < count_ref[0], 1.0, 0.0)
                    near, far = (side[j][t] for side in forces)
                    halves = widened(dobs_ref[0, j, lev, :, cuts[t]], near, far, odd, even)
                    for b in range(2):
                        force_ref[lev, j, t, blocks[b], :] = seen * halves[b]
        return carry

    lax.fori_loop(0, levels // 2, pair, 0)


def model_kernel(
    windows, spaces, steps, nvar, levels, tiles,
    coupling_ref, count_ref, noise_ref, total_ref, own_ref, near_ref, far_ref,
    first_ref, last_ref, force_ref, inc_ref, dobs_ref, rhs_ref, dual_ref, innov_ref,
    ndo_ref, ndm_ref, ninc_ref, *rest,
):
    payload_refs = rest[: windows - 1]
    x_ref, s_ref, a_ref, q_ref = rest[windows - 1 :]
    me = lax.axis_index("window")
    place_x = lax.axis_index("space")
    even = even_place()
    lane, row = lane_index(), row_index()
    pairs = levels // 2
    zero = jnp.zeros((SUB, LANES), jnp.float32)
    blocks = [slice(SUB, 2 * SUB), slice(2 * SUB, 3 * SUB)]
    ups = [slice(b.start + 1, b.stop + 1) for b in blocks]
    downs = [slice(b.start - 1, b.stop - 1) for b in blocks]
    mine = slice(SUB + HALF, 2 * SUB + HALF)
    cuts = [slice(t * LANES, (t + 1) * LANES) for t in range(tiles)]
    mix = [[coupling_gain * coupling_ref[v, u] for u in range(nvar)] for v in range(nvar)]
    low_wall = jnp.where((row == HALF) & (place_x == 0), 0.0, 1.0)
    high_wall = jnp.where((row == HALF - 1) & (place_x == spaces - 1), 0.0, 1.0)

    def from_north(line):
        turned = [pltpu.roll(value, LANES - 1, 1) for value in line]
        return [
            jnp.where(lane < LANES - 1, turned[t], turned[(t + 1) % tiles]) for t in range(tiles)
        ]

    def from_south(line):
        turned = [pltpu.roll(value, 1, 1) for value in line]
        return [jnp.where(lane > 0, turned[t], turned[t - 1]) for t in range(tiles)]

    def masked_last(line):
        return line[:-1] + [jnp.where(lane < LANES - 1, line[-1], 0.0)]

    def masked_first(line):
        return [jnp.where(lane > 0, line[0], 0.0)] + line[1:]

    def walled(block, east, west):
        if block == 0:
            return east, [low_wall * value for value in west]
        return [high_wall * value for value in east], west

    def pair(i, outer):
        for odd in range(2):
            lev = 2 * i + odd

            def spread(j, carry, odd=odd, lev=lev):
                for v in range(nvar):
                    for t in range(tiles):
                        halves = widened(
                            own_ref[j, v * levels + lev, :, cuts[t]].astype(jnp.float32),
                            near_ref[j, v * pairs + i, :, cuts[t]].astype(jnp.float32),
                            far_ref[j, v * pairs + i, :, cuts[t]].astype(jnp.float32),
                            odd,
                            even,
                        )
                        for b in range(2):
                            x_ref[odd, j, v, t, blocks[b], :] = halves[b]
                return carry

            lax.fori_loop(0, steps, spread, 0)

            for v in range(nvar):
                for t in range(tiles):
                    s_ref[odd, 0, v, t, SUB : 3 * SUB, :] = first_ref[lev, v, t]
                    a_ref[odd, 0, v, t, SUB : 3 * SUB, :] = last_ref[lev, v, t]

        def tangent(j, carry):
            now = lax.rem(j, 2)
            seen = jnp.where(j < count_ref[0], 1.0, 0.0)
            for odd in range(2):
                lev = 2 * i + odd
                noise = jnp.full((SUB, LANES), noise_ref[0, j, lev])
                share = seen / noise
                for t in range(tiles):
                    gap = innov_ref[0, j, lev, :, cuts[t]] - noise * dobs_ref[0, j, lev, :, cuts[t]]
                    gap = gap - s_ref[odd, now, 0, t, mine, :]
                    ndo_ref[0, j, lev, :, cuts[t]] = gap * share
                for b in range(2):
                    here, up, down = blocks[b], ups[b], downs[b]
                    x = [[x_ref[odd, j, u, t, here, :] for t in range(tiles)] for u in range(nvar)]
                    ce = [diffusion - half_adv * value for value in x[0]]
                    cw = [diffusion + half_adv * value for value in x[0]]
                    ce, cw = walled(b, ce, cw)
                    cn = masked_last([diffusion - half_adv * value for value in x[1]])
                    cs = masked_first([diffusion + half_adv * value for value in x[1]])
                    s = [
                        [s_ref[odd, now, u, t, here, :] for t in range(tiles)] for u in range(nvar)
                    ]
                    xs = [[x[u][t] * s[u][t] for t in range(tiles)] for u in range(nvar)]
                    for v in range(nvar):
                        north, south = from_north(s[v]), from_south(s[v])
                        for t in range(tiles):
                            fresh = keep * s[v][t] + ce[t] * s_ref[odd, now, v, t, up, :]
                            fresh = fresh + cw[t] * s_ref[odd, now, v, t, down, :]
                            fresh = fresh + cn[t] * north[t] + cs[t] * south[t]
                            for u in range(nvar):
                                fresh = fresh + mix[v][u] * xs[u][t]
                            s_ref[odd, 1 - now, v, t, here, :] = fresh
            return carry

        lax.fori_loop(0, steps, tangent, 0)

        def adjoint(turn, carry):
            now = lax.rem(turn, 2)
            j = steps - 1 - turn
            for odd in range(2):
                for b in range(2):
                    here, up, down = blocks[b], ups[b], downs[b]
                    x = [[x_ref[odd, j, u, t, here, :] for t in range(tiles)] for u in range(nvar)]
                    ce = [
                        diffusion + half_adv * x_ref[odd, j, 0, t, up, :] for t in range(tiles)
                    ]
                    cw = [
                        diffusion - half_adv * x_ref[odd, j, 0, t, down, :] for t in range(tiles)
                    ]
                    ce, cw = walled(b, ce, cw)
                    cn = masked_first([diffusion + half_adv * value for value in x[1]])
                    cs = masked_last([diffusion - half_adv * value for value in x[1]])
                    a = [
                        [a_ref[odd, now, u, t, here, :] for t in range(tiles)] for u in range(nvar)
                    ]
                    for u in range(nvar):
                        north = from_north([cn[t] * a[u][t] for t in range(tiles)])
                        south = from_south([cs[t] * a[u][t] for t in range(tiles)])
                        for t in range(tiles):
                            fresh = keep * a[u][t] + ce[t] * a_ref[odd, now, u, t, up, :]
                            fresh = fresh + cw[t] * a_ref[odd, now, u, t, down, :]
                            fresh = fresh + north[t] + south[t]
                            pull = mix[0][u] * a[0][t]
                            for v in range(1, nvar):
                                pull = pull + mix[v][u] * a[v][t]
                            fresh = fresh + x[u][t] * pull
                            if u == 0:
                                fresh = fresh + force_ref[2 * i + odd, j, t, b * SUB : (b + 1) * SUB, :]
                            a_ref[odd, 1 - now, u, t, here, :] = fresh
            return carry

        lax.fori_loop(0, steps, adjoint, 0)

        end = steps % 2
        coded = []
        for odd in range(2):
            lev = 2 * i + odd
            back, ahead = [], []
            for v in range(nvar):
                share = total_ref[v * levels + lev]
                tv, gv = [], []
                for t in range(tiles):
                    term = a_ref[odd, end, v, t, mine, :] - last_ref[lev, v, t, HALF : HALF + SUB, :]
                    given = rhs_ref[0, v, lev, :, cuts[t]] - inc_ref[0, v, lev, :, cuts[t]]
                    given = given + share * term
                    ndm_ref[v, lev, :, cuts[t]] = -(dual_ref[0, v, lev, :, cuts[t]] + term)
                    ninc_ref[v, lev, :, cuts[t]] = given
                    tv.append(term)
                    gv.append(given + s_ref[odd, end, v, t, mine, :])
                back.append(tv)
                ahead.append(gv)
            coded.append((row_codes(back), row_codes(ahead)))
        for kind in range(2):
            first, second = coded[0][kind], coded[1][kind]
            for n, (a, b) in enumerate(zip(first[0] + [first[1]], second[0] + [second[1]])):
                q_ref[kind, i, n] = shorts(jnp.concatenate([a, b], 0))
        return outer

    lax.fori_loop(0, pairs, pair, 0)
    for d in range(1, windows):
        payload_refs[d - 1][...] = q_ref[jnp.where(me + d >= windows, 0, 1)]


def final_kernel(windows, nvar, levels, tiles, *refs):
    pieces = refs[: windows - 1]
    total_ref, base_dual_ref, base_inc_ref, ndm_ref, ninc_ref = refs[windows - 1 :]
    me = lax.axis_index("window")
    pairs = levels // 2
    cuts = [slice(t * LANES, (t + 1) * LANES) for t in range(tiles)]

    def pair(i, carry):
        tails = [None] * (nvar * tiles)
        heads = [None] * (nvar * tiles)
        for d in range(1, windows):
            piece = pieces[d - 1]
            scales = jnp.exp2(floats(piece[i, nvar * tiles])) * (1.0 / CODE_MAX)
            later = jnp.where(d > me, scales, 0.0)
            earlier = jnp.where(d > me, 0.0, scales)
            for v in range(nvar):
                for t in range(tiles):
                    n = v * tiles + t
                    value = floats(piece[i, n])
                    tail, head = value * later[:, v : v + 1], value * earlier[:, v : v + 1]
                    tails[n] = tail if d == 1 else tails[n] + tail
                    heads[n] = head if d == 1 else heads[n] + head
        for v in range(nvar):
            for odd in range(2):
                lev = 2 * i + odd
                share = total_ref[v * levels + lev]
                for t in range(tiles):
                    rows = slice(odd * SUB, (odd + 1) * SUB)
                    tail, head = tails[v * tiles + t][rows], heads[v * tiles + t][rows]
                    ndm_ref[0, v, lev, :, cuts[t]] = base_dual_ref[v, lev, :, cuts[t]] - tail
                    ninc_ref[0, v, lev, :, cuts[t]] = (
                        base_inc_ref[v, lev, :, cuts[t]] + head + share * tail
                    )
        return carry

    lax.fori_loop(0, pairs, pair, 0)


def moved(block, axis, distance, around=False):
    count = lax.axis_size(axis)
    route = [(i, (i + distance) % count) for i in range(count) if around or 0 <= i + distance < count]
    return lax.ppermute(block, axis, route)


def swaps(axis, first):
    route = []
    for i in range(first, lax.axis_size(axis) - 1, 2):
        route += [(i, i + 1), (i + 1, i)]
    return route


def swapped(block, axis, first):
    return lax.ppermute(block, axis, swaps(axis, first))


def body(
    trajectory,
    dual_model,
    increment,
    model_rhs,
    dual_obs,
    innovation,
    coupling,
    error_var,
    obs_var,
    obs_count,
):
    windows, spaces = lax.axis_size("window"), lax.axis_size("space")
    _, steps, nvar, levels, rows, part = trajectory.shape
    columns = dual_model.shape[-1]
    tiles = columns // LANES
    assert trajectory.shape[0] == windows and windows > 1 and rows == SUB and steps == HALF
    assert columns == tiles * LANES == windows * part and levels % 2 == 0
    pairs = levels // 2
    wide = -(-steps * part // LANES) * LANES
    bf16, f32, i16 = jnp.bfloat16, jnp.float32, jnp.int16

    def shape(dims, dtype):
        return jax.ShapeDtypeStruct(dims, dtype)

    def packed(distances):
        return pl.pallas_call(
            lambda *refs: pack_kernel(distances, windows, steps, nvar, levels, part, *refs),
            out_shape=[shape((nvar * levels + 1, rows, wide), bf16)] * len(distances),
            in_specs=[VMEM, VMEM],
            out_specs=[VMEM] * len(distances),
            scratch_shapes=[pltpu.VMEM((SUB, LANES), f32)],
            compiler_params=params(),
        )(error_var.transpose(0, 2, 1), trajectory)

    order = sorted(range(1, windows), key=lambda d: -d * (windows - d))
    groups = [[d] for d in order] if windows <= 4 else [order]
    blocks = {}
    for group in groups:
        blocks.update(zip(group, packed(group)))
    arrived = {d: moved(blocks[d], "window", d, around=True) for d in order}
    arrived[0] = packed([0])[0]

    payload = shape((pairs, nvar * tiles + 1, 2 * SUB, LANES), i16)

    after = pl.pallas_call(
        own_code_kernel,
        out_shape=payload,
        in_specs=[VMEM],
        out_specs=VMEM,
        compiler_params=params(),
    )(dual_model)
    after = moved(after, "window", -1)

    def half_coded(counts, fields):
        total = sum(-(-(count * tiles + 1) // 2) for count in counts)
        halves = shape((pairs, total, 2 * SUB, LANES), i16)
        near, far = pl.pallas_call(
            half_code_kernel,
            out_shape=[halves, halves],
            in_specs=[VMEM] * len(fields),
            out_specs=[VMEM] * 2,
            compiler_params=params(),
        )(*fields)
        far = swapped(far, "space", 1)
        return swapped(near, "space", 0), far

    near, far = half_coded([nvar, steps], [increment, dual_obs])
    after_near, after_far = half_coded([nvar], [after])

    own, traj_far, totals = pl.pallas_call(
        lambda *refs: assemble_kernel(windows, steps, nvar, levels, part, *refs),
        out_shape=[
            shape((steps, nvar * levels, rows, columns), bf16),
            shape((steps, nvar * pairs, rows, columns), bf16),
            shape((nvar * levels, rows, LANES), f32),
        ],
        in_specs=[VMEM] * windows,
        out_specs=[VMEM] * 3,
        scratch_shapes=[pltpu.VMEM((windows, nvar * levels, rows, wide), bf16)],
        compiler_params=params(),
    )(*[arrived[d] for d in range(windows)])
    traj_far = swapped(traj_far, "space", 1)
    traj_near = pl.pallas_call(
        near_kernel,
        out_shape=shape((steps, nvar * pairs, rows, columns), bf16),
        in_specs=[VMEM] + [ANY] * 3,
        out_specs=VMEM,
        compiler_params=params(),
    )(own, after, near, far)
    traj_near = swapped(traj_near, "space", 0)

    state = shape((nvar, levels, rows, columns), f32)
    around = [shape((levels, n, tiles, 2 * SUB, LANES), f32) for n in (nvar, nvar, steps)]
    first, last, force = pl.pallas_call(
        lambda *refs: prepare_kernel(steps, nvar, levels, tiles, *refs),
        out_shape=around,
        in_specs=[SMEM] + [VMEM] * 7,
        out_specs=[VMEM] * 3,
        compiler_params=params(),
    )(obs_count, after, after_near, after_far, near, far, increment, dual_obs)
    new_dual_obs, base_dual, base_inc, *payloads = pl.pallas_call(
        lambda *refs: model_kernel(windows, spaces, steps, nvar, levels, tiles, *refs),
        out_shape=[shape(dual_obs.shape, f32), state, state] + [payload] * (windows - 1),
        in_specs=[SMEM] * 3 + [VMEM] * 12,
        out_specs=[VMEM] * (3 + windows - 1),
        scratch_shapes=[
            pltpu.VMEM((2, steps, nvar, tiles, 4 * SUB, LANES), f32),
            pltpu.VMEM((2, 2, nvar, tiles, 4 * SUB, LANES), f32),
            pltpu.VMEM((2, 2, nvar, tiles, 4 * SUB, LANES), f32),
            pltpu.VMEM((2,) + payload.shape, i16),
        ],
        compiler_params=params(32),
    )(
        coupling, obs_count, obs_var, totals, own, traj_near, traj_far,
        first, last, force, increment, dual_obs, model_rhs, dual_model, innovation,
    )
    sent = {d: moved(payloads[d - 1], "window", d, around=True) for d in order}

    new_dual_model, new_increment = pl.pallas_call(
        lambda *refs: final_kernel(windows, nvar, levels, tiles, *refs),
        out_shape=[shape(dual_model.shape, f32), shape(increment.shape, f32)],
        in_specs=[VMEM] * (windows + 2),
        out_specs=[VMEM] * 2,
        compiler_params=params(),
    )(*[sent[d] for d in range(1, windows)], totals, base_dual, base_inc)
    return new_dual_model, new_dual_obs, new_increment


def solution(mesh):
    placed = (
        P("members", None, None, None, "space", "window"),
        P(("members", "window"), None, None, "space", None),
        P(("members", "window"), None, None, "space", None),
        P(("members", "window"), None, None, "space", None),
        P(("members", "window"), None, None, "space", None),
        P(("members", "window"), None, None, "space", None),
        P(),
        P(("members", "window"), None, None),
        P(("members", "window"), None, None),
        P(("members", "window")),
    )
    return jax.shard_map(
        body,
        mesh=mesh,
        in_specs=placed,
        out_specs=(
            P(("members", "window"), None, None, "space", None),
            P(("members", "window"), None, None, "space", None),
            P(("members", "window"), None, None, "space", None),
        ),
        check_vma=False,
    )
```

```python
import jax
import jax.numpy as jnp
from jax import lax
from jax.experimental import pallas as pl
from jax.experimental.pallas import tpu as pltpu
from jax.sharding import PartitionSpec as P

LANES = 128
SUB = 8
HALF = SUB // 2
CODE_MAX = 32766.0
ROUNDER = 12582912.0

diffusion = 0.2
advection = 0.2
coupling_gain = 0.5
keep = 1.0 - 4.0 * diffusion
half_adv = 0.5 * advection

VMEM = pl.BlockSpec(memory_space=pltpu.VMEM)
SMEM = pl.BlockSpec(memory_space=pltpu.SMEM)


def params(mib=24):
    return pltpu.CompilerParams(vmem_limit_bytes=mib * 1024 * 1024)


def lane_index():
    return lax.broadcasted_iota(jnp.int32, (SUB, LANES), 1)


def row_index():
    return lax.broadcasted_iota(jnp.int32, (SUB, LANES), 0)


def tiled(wide):
    short = -wide.shape[1] % LANES
    if short:
        wide = jnp.concatenate([wide, jnp.zeros((wide.shape[0], short), wide.dtype)], 1)
    return [wide[:, i : i + LANES] for i in range(0, wide.shape[1], LANES)]


def place(parts, rolled, lane):
    built = {}
    for key, tiles, first, width, target in parts:
        done = 0
        while done < width:
            a, b = first + done, target + done
            n = min(width - done, LANES - a % LANES, LANES - b % LANES)
            shift = (b - a) % LANES
            name = (key, a // LANES, shift)
            if name not in rolled:
                value = tiles[a // LANES]
                rolled[name] = pltpu.roll(value, shift, 1) if shift else value
            if b % LANES:
                built[b // LANES] = jnp.where(
                    lane >= b % LANES, rolled[name], built[b // LANES]
                )
            else:
                built[b // LANES] = rolled[name]
            done += n
    return [built[i] for i in range(len(built))]


def joined_halves(first, second):
    top = row_index()[:, :1] < HALF
    last = jnp.where(top, pltpu.roll(first, HALF, 0), second)
    start = jnp.where(top, first, pltpu.roll(second, HALF, 0))
    return last, start


def widened(own, near, far, odd, even):
    top = row_index() < HALF
    low, high = jnp.where(even, far, near), jnp.where(even, near, far)
    turned = pltpu.roll(own, HALF, 0)
    low = pltpu.roll(low, HALF, 0) if odd else low
    high = high if odd else pltpu.roll(high, HALF, 0)
    return jnp.where(top, low, turned), jnp.where(top, turned, high)


def row_codes(planes):
    lane = lax.broadcasted_iota(jnp.int32, planes[0][0].shape, 1)
    scales = jnp.zeros(planes[0][0].shape, jnp.float32)
    out = []
    for v, row in enumerate(planes):
        big = jnp.abs(row[0])
        for value in row[1:]:
            big = jnp.maximum(big, jnp.abs(value))
        big = jnp.max(big, axis=1, keepdims=True)
        power = jnp.clip(jnp.ceil(jnp.log2(jnp.maximum(big, 1e-30))), -90.0, 126.0)
        scales = jnp.where(lane == v, power, scales)
        gain = CODE_MAX * jnp.exp2(-power)
        for value in row:
            scaled = jnp.clip(value * gain, -CODE_MAX, CODE_MAX)
            out.append((scaled + ROUNDER) - ROUNDER)
    return out, scales


def shorts(value):
    return value.astype(jnp.int32).astype(jnp.int16)


def floats(value):
    return value.astype(jnp.int32).astype(jnp.float32)


def pack_kernel(distances, windows, steps, nvar, levels, part, var_ref, traj_ref, *rest):
    outs, wide_ref = rest[:-1], rest[-1]
    me = lax.axis_index("window")
    lane = lane_index()
    wide_ref[...] = jnp.zeros((SUB, LANES), jnp.float32)
    wide_ref[:levels, :nvar] = var_ref[0]
    variance = wide_ref[...]
    high = variance.astype(jnp.bfloat16).astype(jnp.float32)
    middle = (variance - high).astype(jnp.bfloat16).astype(jnp.float32)
    low = variance - high - middle
    split = high + pltpu.roll(middle, HALF, 0) + pltpu.roll(low, LANES // 2, 1)
    split = split.astype(jnp.bfloat16)

    for n, d in enumerate(distances):
        outs[n][nvar * levels, :, :LANES] = split
        target = lax.rem(me + d, windows)

        def variable(v, carry, n=n, target=target):
            for lev in range(levels):
                pieces = [
                    tiled(traj_ref[target, j, v, lev].astype(jnp.float32)) for j in range(steps)
                ]
                parts = [(j, pieces[j], 0, part, j * part) for j in range(steps)]
                wide = jnp.concatenate(place(parts, {}, lane), 1)
                outs[n][v * levels + lev] = wide.astype(jnp.bfloat16)
            return carry

        lax.fori_loop(0, nvar, variable, 0, unroll=len(distances) == 1)


def even_place():
    return lax.rem(lax.axis_index("space"), 2) == 0


def level_codes(ref, lev):
    planes = [
        [ref[0, v, lev, :, t : t + LANES] for t in range(0, ref.shape[-1], LANES)]
        for v in range(ref.shape[1])
    ]
    values, scales = row_codes(planes)
    return values + [scales]


def half_code_kernel(*refs):
    sources, (near_ref, far_ref, own_ref) = refs[:-3], refs[-3:]
    even = even_place()

    def pair(i, carry):
        near, far = [], []
        for k, ref in enumerate(sources):
            coded = [level_codes(ref, 2 * i + odd) for odd in range(2)]
            for n, (first, second) in enumerate(zip(*coded)):
                if k == 0:
                    own_ref[i, n] = shorts(jnp.concatenate([first, second], 0))
                last, start = joined_halves(first, second)
                near.append(jnp.where(even, last, start))
                far.append(jnp.where(even, start, last))
            if len(near) % 2:
                near.append(jnp.zeros((SUB, LANES), jnp.float32))
                far.append(jnp.zeros((SUB, LANES), jnp.float32))
        for tiles, ref in ((near, near_ref), (far, far_ref)):
            for n in range(0, len(tiles), 2):
                ref[i, n // 2] = shorts(jnp.concatenate(tiles[n : n + 2], 0))
        return carry

    lax.fori_loop(0, near_ref.shape[0], pair, 0)


def half_tile(ref, i, n):
    whole = floats(ref[i, n // 2])
    return whole[SUB:] if n % 2 else whole[:SUB]


def around_kernel(windows, nvar, levels, *refs):
    pieces, (own_ref, near_ref, far_ref) = refs[:windows], refs[windows : windows + 3]
    outs, total_ref = refs[windows + 3 : -1], refs[-1]
    me = lax.axis_index("window")
    even = even_place()
    total = jnp.zeros((SUB, LANES), jnp.float32)
    for d in range(windows):
        split = pieces[d][nvar * levels, :, :LANES].astype(jnp.float32)
        here = split + pltpu.roll(split, HALF, 0) + pltpu.roll(split, LANES // 2, 1)
        total = total + jnp.where(lax.rem(me - d + windows, windows) <= me, here, 0.0)
    for v in range(nvar):
        for lev in range(levels):
            one = total[lev : lev + 1, v : v + 1]
            total_ref[v * levels + lev] = jnp.broadcast_to(one, (SUB, LANES))
    for i, out_ref in enumerate(outs):
        for n in range(own_ref.shape[1]):
            own = floats(own_ref[i, n])
            near, far = half_tile(near_ref, i, n), half_tile(far_ref, i, n)
            for odd in range(2):
                halves = widened(own[odd * SUB : (odd + 1) * SUB], near, far, odd, even)
                out_ref[odd, n] = shorts(jnp.concatenate(halves, 0))


def decoded(ref, i, first, nvar, tiles):
    scales = jnp.exp2(half_tile(ref, i, first + nvar * tiles)) * (1.0 / CODE_MAX)
    return [
        [half_tile(ref, i, first + v * tiles + t) * scales[:, v : v + 1] for t in range(tiles)]
        for v in range(nvar)
    ]


def assemble_kernel(windows, steps, nvar, levels, part, *refs):
    pieces = refs[:windows]
    own_ref, near_ref, early_ref, late_ref, stack_ref = refs[windows:]
    me = lax.axis_index("window")
    even = even_place()
    lane = lane_index()
    for d in range(windows):
        source = lax.rem(me - d + windows, windows)
        stack_ref[source] = pieces[d][: nvar * levels]

    pairs = levels // 2

    def pair(n):
        both = []
        for odd in range(2):
            plane = 2 * n + odd
            sources = [tiled(stack_ref[w, plane].astype(jnp.float32)) for w in range(windows)]
            rolled = {}
            built = []
            for j in range(steps):
                parts = [(w, sources[w], j * part, part, w * part) for w in range(windows)]
                built.append(place(parts, rolled, lane))
                own_ref[j, plane] = jnp.concatenate(built[j], 1).astype(jnp.bfloat16)
            both.append(built)
        for j in range(steps):
            halves = [joined_halves(a, b) for a, b in zip(both[0][j], both[1][j])]
            last, start = (jnp.concatenate([h[k] for h in halves], 1) for k in range(2))
            near_ref[j, n] = jnp.where(even, last, start).astype(jnp.bfloat16)
            far = jnp.where(even, start, last).astype(jnp.bfloat16)
            if j < steps // 2:
                early_ref[j, n] = far
            else:
                late_ref[j - steps // 2, n] = far

    def variable(v, carry):
        for i in range(pairs):
            pair(v * pairs + i)
        return carry

    lax.fori_loop(0, nvar, variable, 0)


def prepare_kernel(
    steps, nvar, levels, tiles,
    count_ref, noise_ref, coupling_ref, near_ref, far_ref, inc_ref, dobs_ref, innov_ref, *refs,
):
    after_refs = refs[: levels // 2]
    first_ref, last_ref, force_ref, obs_ref, share_ref, mix_ref = refs[levels // 2 :]
    even = even_place()
    blocks = [slice(0, SUB), slice(SUB, 2 * SUB)]
    cuts = [slice(t * LANES, (t + 1) * LANES) for t in range(tiles)]
    for v in range(nvar):
        for u in range(nvar):
            one = coupling_gain * coupling_ref[v : v + 1, u : u + 1]
            mix_ref[v, u] = jnp.broadcast_to(one, (SUB, LANES))
    seen = [jnp.where(j < count_ref[0], 1.0, 0.0) for j in range(steps)]
    offset = -(-(nvar * tiles + 1) // 2) * 2
    for i, after_ref in enumerate(after_refs):
        fields = [decoded(ref, i, offset, nvar, tiles) for ref in (near_ref, far_ref)]
        forces = [decoded(ref, i, 2 * offset, steps, tiles) for ref in (near_ref, far_ref)]
        for odd in range(2):
            lev = 2 * i + odd
            scales = jnp.exp2(floats(after_ref[odd, nvar * tiles])) * (-1.0 / CODE_MAX)
            for t in range(tiles):
                for v in range(nvar):
                    near, far = (side[v][t] for side in fields)
                    halves = widened(inc_ref[0, v, lev, :, cuts[t]], near, far, odd, even)
                    for b in range(2):
                        first_ref[lev, v, t, blocks[b], :] = halves[b]
                    value = floats(after_ref[odd, v * tiles + t])
                    last_ref[lev, v, t] = value * scales[:, v : v + 1]
                for j in range(steps):
                    near, far = (side[j][t] for side in forces)
                    halves = widened(dobs_ref[0, j, lev, :, cuts[t]], near, far, odd, even)
                    for b in range(2):
                        force_ref[lev, j, t, blocks[b], :] = seen[j] * halves[b]
            for j in range(steps):
                noise = jnp.full((SUB, LANES), noise_ref[0, j, lev])
                share = seen[j] / noise
                share_ref[lev, j] = share
                for t in range(tiles):
                    gap = innov_ref[0, j, lev, :, cuts[t]] - noise * dobs_ref[0, j, lev, :, cuts[t]]
                    obs_ref[lev, j, t] = gap * share


def model_kernel(
    windows, spaces, steps, nvar, levels, tiles,
    mix_ref, share_ref, obs_ref, total_ref, own_ref, near_ref, early_ref, late_ref,
    first_ref, last_ref, force_ref, inc_ref, rhs_ref, dual_ref,
    ndo_ref, ndm_ref, ninc_ref, *rest,
):
    payload_refs = rest[: windows - 1]
    x_ref, s_ref, a_ref, q_ref = rest[windows - 1 :]
    me = lax.axis_index("window")
    place_x = lax.axis_index("space")
    even = even_place()
    lane, row = lane_index(), row_index()
    pairs = levels // 2
    zero = jnp.zeros((SUB, LANES), jnp.float32)
    blocks = [slice(SUB, 2 * SUB), slice(2 * SUB, 3 * SUB)]
    ups = [slice(b.start + 1, b.stop + 1) for b in blocks]
    downs = [slice(b.start - 1, b.stop - 1) for b in blocks]
    mine = slice(SUB + HALF, 2 * SUB + HALF)
    cuts = [slice(t * LANES, (t + 1) * LANES) for t in range(tiles)]
    low_wall = jnp.where((row == HALF) & (place_x == 0), 0.0, 1.0)
    high_wall = jnp.where((row == HALF - 1) & (place_x == spaces - 1), 0.0, 1.0)

    def from_north(line):
        turned = [pltpu.roll(value, LANES - 1, 1) for value in line]
        return [
            jnp.where(lane < LANES - 1, turned[t], turned[(t + 1) % tiles]) for t in range(tiles)
        ]

    def from_south(line):
        turned = [pltpu.roll(value, 1, 1) for value in line]
        return [jnp.where(lane > 0, turned[t], turned[t - 1]) for t in range(tiles)]

    def masked_last(line):
        return line[:-1] + [jnp.where(lane < LANES - 1, line[-1], 0.0)]

    def masked_first(line):
        return [jnp.where(lane > 0, line[0], 0.0)] + line[1:]

    def walled(block, east, west):
        if block == 0:
            return east, [low_wall * value for value in west]
        return [high_wall * value for value in east], west

    def pair(i, outer):
        for odd in range(2):
            lev = 2 * i + odd

            for j in range(steps):
                far_ref = early_ref if j < steps // 2 else late_ref
                for v in range(nvar):
                    for t in range(tiles):
                        halves = widened(
                            own_ref[j, v * levels + lev, :, cuts[t]].astype(jnp.float32),
                            near_ref[j, v * pairs + i, :, cuts[t]].astype(jnp.float32),
                            far_ref[j % (steps // 2), v * pairs + i, :, cuts[t]].astype(jnp.float32),
                            odd,
                            even,
                        )
                        for b in range(2):
                            x_ref[odd, j, v, t, blocks[b], :] = halves[b]
            for v in range(nvar):
                for t in range(tiles):
                    s_ref[odd, 0, v, t, SUB : 3 * SUB, :] = first_ref[lev, v, t]
                    a_ref[odd, 0, v, t, SUB : 3 * SUB, :] = last_ref[lev, v, t]

        def tangent(j, carry):
            now = lax.rem(j, 2)
            for odd in range(2):
                lev = 2 * i + odd
                for t in range(tiles):
                    image = share_ref[lev, j] * s_ref[odd, now, 0, t, mine, :]
                    ndo_ref[0, j, lev, :, cuts[t]] = obs_ref[lev, j, t] - image
                for b in range(2):
                    here, up, down = blocks[b], ups[b], downs[b]
                    x = [[x_ref[odd, j, u, t, here, :] for t in range(tiles)] for u in range(nvar)]
                    ce = [diffusion - half_adv * value for value in x[0]]
                    cw = [diffusion + half_adv * value for value in x[0]]
                    ce, cw = walled(b, ce, cw)
                    cn = masked_last([diffusion - half_adv * value for value in x[1]])
                    cs = masked_first([diffusion + half_adv * value for value in x[1]])
                    s = [
                        [s_ref[odd, now, u, t, here, :] for t in range(tiles)] for u in range(nvar)
                    ]
                    xs = [[x[u][t] * s[u][t] for t in range(tiles)] for u in range(nvar)]
                    for v in range(nvar):
                        north, south = from_north(s[v]), from_south(s[v])
                        for t in range(tiles):
                            fresh = keep * s[v][t] + ce[t] * s_ref[odd, now, v, t, up, :]
                            fresh = fresh + cw[t] * s_ref[odd, now, v, t, down, :]
                            fresh = fresh + cn[t] * north[t] + cs[t] * south[t]
                            for u in range(nvar):
                                fresh = fresh + mix_ref[v, u] * xs[u][t]
                            s_ref[odd, 1 - now, v, t, here, :] = fresh
            return carry

        lax.fori_loop(0, steps, tangent, 0)

        def adjoint(turn, carry):
            now = lax.rem(turn, 2)
            j = steps - 1 - turn
            for odd in range(2):
                for b in range(2):
                    here, up, down = blocks[b], ups[b], downs[b]
                    x = [[x_ref[odd, j, u, t, here, :] for t in range(tiles)] for u in range(nvar)]
                    ce = [
                        diffusion + half_adv * x_ref[odd, j, 0, t, up, :] for t in range(tiles)
                    ]
                    cw = [
                        diffusion - half_adv * x_ref[odd, j, 0, t, down, :] for t in range(tiles)
                    ]
                    ce, cw = walled(b, ce, cw)
                    cn = masked_first([diffusion + half_adv * value for value in x[1]])
                    cs = masked_last([diffusion - half_adv * value for value in x[1]])
                    a = [
                        [a_ref[odd, now, u, t, here, :] for t in range(tiles)] for u in range(nvar)
                    ]
                    for u in range(nvar):
                        north = from_north([cn[t] * a[u][t] for t in range(tiles)])
                        south = from_south([cs[t] * a[u][t] for t in range(tiles)])
                        for t in range(tiles):
                            fresh = keep * a[u][t] + ce[t] * a_ref[odd, now, u, t, up, :]
                            fresh = fresh + cw[t] * a_ref[odd, now, u, t, down, :]
                            fresh = fresh + north[t] + south[t]
                            pull = mix_ref[0, u] * a[0][t]
                            for v in range(1, nvar):
                                pull = pull + mix_ref[v, u] * a[v][t]
                            fresh = fresh + x[u][t] * pull
                            if u == 0:
                                fresh = fresh + force_ref[2 * i + odd, j, t, b * SUB : (b + 1) * SUB, :]
                            a_ref[odd, 1 - now, u, t, here, :] = fresh
            return carry

        lax.fori_loop(0, steps, adjoint, 0)

        end = steps % 2
        coded = []
        for odd in range(2):
            lev = 2 * i + odd
            back, ahead = [], []
            for v in range(nvar):
                share = total_ref[v * levels + lev]
                tv, gv = [], []
                for t in range(tiles):
                    term = a_ref[odd, end, v, t, mine, :] - last_ref[lev, v, t, HALF : HALF + SUB, :]
                    given = rhs_ref[0, v, lev, :, cuts[t]] - inc_ref[0, v, lev, :, cuts[t]]
                    given = given + share * term
                    ndm_ref[v, lev, :, cuts[t]] = -(dual_ref[0, v, lev, :, cuts[t]] + term)
                    ninc_ref[v, lev, :, cuts[t]] = given
                    tv.append(term)
                    gv.append(given + s_ref[odd, end, v, t, mine, :])
                back.append(tv)
                ahead.append(gv)
            coded.append((row_codes(back), row_codes(ahead)))
        for kind in range(2):
            first, second = coded[0][kind], coded[1][kind]
            for n, (a, b) in enumerate(zip(first[0] + [first[1]], second[0] + [second[1]])):
                q_ref[kind, i, n] = shorts(jnp.concatenate([a, b], 0))
        return outer

    lax.fori_loop(0, pairs, pair, 0)
    for d in range(1, windows):
        payload_refs[d - 1][...] = q_ref[jnp.where(me + d >= windows, 0, 1)]


def final_kernel(windows, nvar, levels, tiles, *refs):
    pieces = refs[: windows - 1]
    total_ref, base_dual_ref, base_inc_ref, ndm_ref, ninc_ref = refs[windows - 1 :]
    me = lax.axis_index("window")
    pairs = levels // 2
    cuts = [slice(t * LANES, (t + 1) * LANES) for t in range(tiles)]

    def pair(i, carry):
        tails = [None] * (nvar * tiles)
        heads = [None] * (nvar * tiles)
        for d in range(1, windows):
            piece = pieces[d - 1]
            scales = jnp.exp2(floats(piece[i, nvar * tiles])) * (1.0 / CODE_MAX)
            later = jnp.where(d > me, scales, 0.0)
            earlier = jnp.where(d > me, 0.0, scales)
            for v in range(nvar):
                for t in range(tiles):
                    n = v * tiles + t
                    value = floats(piece[i, n])
                    tail, head = value * later[:, v : v + 1], value * earlier[:, v : v + 1]
                    tails[n] = tail if d == 1 else tails[n] + tail
                    heads[n] = head if d == 1 else heads[n] + head
        for v in range(nvar):
            for odd in range(2):
                lev = 2 * i + odd
                share = total_ref[v * levels + lev]
                for t in range(tiles):
                    rows = slice(odd * SUB, (odd + 1) * SUB)
                    tail, head = tails[v * tiles + t][rows], heads[v * tiles + t][rows]
                    ndm_ref[0, v, lev, :, cuts[t]] = base_dual_ref[v, lev, :, cuts[t]] - tail
                    ninc_ref[0, v, lev, :, cuts[t]] = (
                        base_inc_ref[v, lev, :, cuts[t]] + head + share * tail
                    )
        return carry

    lax.fori_loop(0, pairs, pair, 0)


def moved(block, axis, distance, around=False):
    count = lax.axis_size(axis)
    route = [(i, (i + distance) % count) for i in range(count) if around or 0 <= i + distance < count]
    return lax.ppermute(block, axis, route)


def swaps(axis, first):
    route = []
    for i in range(first, lax.axis_size(axis) - 1, 2):
        route += [(i, i + 1), (i + 1, i)]
    return route


def swapped(block, axis, first):
    return lax.ppermute(block, axis, swaps(axis, first))


def body(
    trajectory,
    dual_model,
    increment,
    model_rhs,
    dual_obs,
    innovation,
    coupling,
    error_var,
    obs_var,
    obs_count,
):
    windows, spaces = lax.axis_size("window"), lax.axis_size("space")
    _, steps, nvar, levels, rows, part = trajectory.shape
    columns = dual_model.shape[-1]
    tiles = columns // LANES
    assert trajectory.shape[0] == windows and windows > 1 and rows == SUB and steps == HALF
    assert columns == tiles * LANES == windows * part and levels % 2 == 0
    pairs = levels // 2
    wide = -(-steps * part // LANES) * LANES
    bf16, f32, i16 = jnp.bfloat16, jnp.float32, jnp.int16

    def shape(dims, dtype):
        return jax.ShapeDtypeStruct(dims, dtype)

    def packed(distances):
        return pl.pallas_call(
            lambda *refs: pack_kernel(distances, windows, steps, nvar, levels, part, *refs),
            out_shape=[shape((nvar * levels + 1, rows, wide), bf16)] * len(distances),
            in_specs=[VMEM, VMEM],
            out_specs=[VMEM] * len(distances),
            scratch_shapes=[pltpu.VMEM((SUB, LANES), f32)],
            compiler_params=params(),
        )(error_var.transpose(0, 2, 1), trajectory)

    order = sorted(range(1, windows), key=lambda d: -d * (windows - d))
    groups = [[d] for d in order] if windows <= 4 else [order]
    blocks = {}
    for group in groups:
        blocks.update(zip(group, packed(group)))
    arrived = {d: moved(blocks[d], "window", d, around=True) for d in order}
    arrived[0] = packed([0])[0]

    payload = shape((pairs, nvar * tiles + 1, 2 * SUB, LANES), i16)

    counts = [nvar, nvar, steps]
    half_tiles = sum(-(-(count * tiles + 1) // 2) for count in counts)
    halves = shape((pairs, half_tiles, 2 * SUB, LANES), i16)
    near, far, dual = pl.pallas_call(
        half_code_kernel,
        out_shape=[halves, halves, payload],
        in_specs=[VMEM] * 3,
        out_specs=[VMEM] * 3,
        compiler_params=params(),
    )(dual_model, increment, dual_obs)
    far, near = swapped(far, "space", 1), swapped(near, "space", 0)

    blocks_here = [arrived[d] for d in range(windows)]
    around = shape((2,) + payload.shape[1:], i16)
    *after, totals = pl.pallas_call(
        lambda *refs: around_kernel(windows, nvar, levels, *refs),
        out_shape=[around] * pairs + [shape((nvar * levels, rows, LANES), f32)],
        in_specs=[VMEM] * (windows + 3),
        out_specs=[VMEM] * (pairs + 1),
        compiler_params=params(),
    )(*blocks_here, dual, near, far)
    after = [moved(piece, "window", -1) for piece in after]

    half_steps = shape((steps // 2, nvar * pairs, rows, columns), bf16)
    own, traj_near, traj_early, traj_late = pl.pallas_call(
        lambda *refs: assemble_kernel(windows, steps, nvar, levels, part, *refs),
        out_shape=[
            shape((steps, nvar * levels, rows, columns), bf16),
            shape((steps, nvar * pairs, rows, columns), bf16),
            half_steps,
            half_steps,
        ],
        in_specs=[VMEM] * windows,
        out_specs=[VMEM] * 4,
        scratch_shapes=[pltpu.VMEM((windows, nvar * levels, rows, wide), bf16)],
        compiler_params=params(),
    )(*blocks_here)
    traj_early = swapped(traj_early, "space", 1)
    traj_late = swapped(traj_late, "space", 1)
    traj_near = swapped(traj_near, "space", 0)

    first, last, force, obs, share, mix = pl.pallas_call(
        lambda *refs: prepare_kernel(steps, nvar, levels, tiles, *refs),
        out_shape=[
            *[shape((levels, n, tiles, 2 * SUB, LANES), f32) for n in (nvar, nvar, steps)],
            shape((levels, steps, tiles, SUB, LANES), f32),
            shape((levels, steps, SUB, LANES), f32),
            shape((nvar, nvar, SUB, LANES), f32),
        ],
        in_specs=[SMEM] * 2 + [VMEM] * (6 + pairs),
        out_specs=[VMEM] * 6,
        compiler_params=params(),
    )(obs_count, obs_var, coupling, near, far, increment, dual_obs, innovation, *after)
    state = shape((nvar, levels, rows, columns), f32)
    new_dual_obs, base_dual, base_inc, *payloads = pl.pallas_call(
        lambda *refs: model_kernel(windows, spaces, steps, nvar, levels, tiles, *refs),
        out_shape=[shape(dual_obs.shape, f32), state, state] + [payload] * (windows - 1),
        in_specs=[VMEM] * 14,
        out_specs=[VMEM] * (3 + windows - 1),
        scratch_shapes=[
            pltpu.VMEM((2, steps, nvar, tiles, 4 * SUB, LANES), f32),
            pltpu.VMEM((2, 2, nvar, tiles, 4 * SUB, LANES), f32),
            pltpu.VMEM((2, 2, nvar, tiles, 4 * SUB, LANES), f32),
            pltpu.VMEM((2,) + payload.shape, i16),
        ],
        compiler_params=params(32),
    )(
        mix, share, obs, totals, own, traj_near, traj_early, traj_late,
        first, last, force, increment, model_rhs, dual_model,
    )
    sent = {d: moved(payloads[d - 1], "window", d, around=True) for d in order}

    new_dual_model, new_increment = pl.pallas_call(
        lambda *refs: final_kernel(windows, nvar, levels, tiles, *refs),
        out_shape=[shape(dual_model.shape, f32), shape(increment.shape, f32)],
        in_specs=[VMEM] * (windows + 2),
        out_specs=[VMEM] * 2,
        compiler_params=params(),
    )(*[sent[d] for d in range(1, windows)], totals, base_dual, base_inc)
    return new_dual_model, new_dual_obs, new_increment


def solution(mesh):
    placed = (
        P("members", None, None, None, "space", "window"),
        P(("members", "window"), None, None, "space", None),
        P(("members", "window"), None, None, "space", None),
        P(("members", "window"), None, None, "space", None),
        P(("members", "window"), None, None, "space", None),
        P(("members", "window"), None, None, "space", None),
        P(),
        P(("members", "window"), None, None),
        P(("members", "window"), None, None),
        P(("members", "window")),
    )
    return jax.shard_map(
        body,
        mesh=mesh,
        in_specs=placed,
        out_specs=(
            P(("members", "window"), None, None, "space", None),
            P(("members", "window"), None, None, "space", None),
            P(("members", "window"), None, None, "space", None),
        ),
        check_vma=False,
    )
```

```python
import jax
import jax.numpy as jnp
from jax import lax
from jax.experimental import pallas as pl
from jax.experimental.pallas import tpu as pltpu
from jax.sharding import PartitionSpec as P

LANES = 128
SUB = 8
HALF = SUB // 2
CODE_MAX = 32766.0
ROUNDER = 12582912.0

diffusion = 0.2
advection = 0.2
coupling_gain = 0.5
keep = 1.0 - 4.0 * diffusion
half_adv = 0.5 * advection

VMEM = pl.BlockSpec(memory_space=pltpu.VMEM)
SMEM = pl.BlockSpec(memory_space=pltpu.SMEM)


def params(mib=24):
    return pltpu.CompilerParams(vmem_limit_bytes=mib * 1024 * 1024)


def lane_index():
    return lax.broadcasted_iota(jnp.int32, (SUB, LANES), 1)


def row_index():
    return lax.broadcasted_iota(jnp.int32, (SUB, LANES), 0)


def tiled(wide):
    short = -wide.shape[1] % LANES
    if short:
        wide = jnp.concatenate([wide, jnp.zeros((wide.shape[0], short), wide.dtype)], 1)
    return [wide[:, i : i + LANES] for i in range(0, wide.shape[1], LANES)]


def place(parts, rolled, lane):
    built = {}
    for key, tiles, first, width, target in parts:
        done = 0
        while done < width:
            a, b = first + done, target + done
            n = min(width - done, LANES - a % LANES, LANES - b % LANES)
            shift = (b - a) % LANES
            name = (key, a // LANES, shift)
            if name not in rolled:
                value = tiles[a // LANES]
                rolled[name] = pltpu.roll(value, shift, 1) if shift else value
            if b % LANES:
                built[b // LANES] = jnp.where(
                    lane >= b % LANES, rolled[name], built[b // LANES]
                )
            else:
                built[b // LANES] = rolled[name]
            done += n
    return [built[i] for i in range(len(built))]


def joined_halves(first, second):
    top = row_index()[:, :1] < HALF
    last = jnp.where(top, pltpu.roll(first, HALF, 0), second)
    start = jnp.where(top, first, pltpu.roll(second, HALF, 0))
    return last, start


def widened(own, near, far, odd, even):
    top = row_index() < HALF
    low, high = jnp.where(even, far, near), jnp.where(even, near, far)
    turned = pltpu.roll(own, HALF, 0)
    low = pltpu.roll(low, HALF, 0) if odd else low
    high = high if odd else pltpu.roll(high, HALF, 0)
    return jnp.where(top, low, turned), jnp.where(top, turned, high)


def row_codes(planes):
    lane = lax.broadcasted_iota(jnp.int32, planes[0][0].shape, 1)
    scales = jnp.zeros(planes[0][0].shape, jnp.float32)
    out = []
    for v, row in enumerate(planes):
        big = jnp.abs(row[0])
        for value in row[1:]:
            big = jnp.maximum(big, jnp.abs(value))
        big = jnp.max(big, axis=1, keepdims=True)
        power = jnp.clip(jnp.ceil(jnp.log2(jnp.maximum(big, 1e-30))), -90.0, 126.0)
        scales = jnp.where(lane == v, power, scales)
        gain = CODE_MAX * jnp.exp2(-power)
        for value in row:
            out.append((value * gain + ROUNDER) - ROUNDER)
    return out, scales


def shorts(value):
    return value.astype(jnp.int32).astype(jnp.int16)


def floats(value):
    return value.astype(jnp.int32).astype(jnp.float32)


def pack_kernel(distances, windows, steps, nvar, levels, part, var_ref, traj_ref, *outs):
    me = lax.axis_index("window")
    lane = lane_index()
    variance = var_ref[...]
    high = variance.astype(jnp.bfloat16).astype(jnp.float32)
    middle = (variance - high).astype(jnp.bfloat16).astype(jnp.float32)
    low = variance - high - middle
    split = high + pltpu.roll(middle, HALF, 0) + pltpu.roll(low, LANES // 2, 1)
    split = split.astype(jnp.bfloat16)

    for n, d in enumerate(distances):
        outs[n][outs[n].shape[0] - 1] = split
        target = lax.rem(me + d, windows)

        def variable(v, carry, n=n, target=target):
            for lev in range(levels):
                pieces = [
                    tiled(traj_ref[target, j, v, lev].astype(jnp.float32)) for j in range(steps)
                ]
                parts = [(j, pieces[j], 0, part, j * part) for j in range(steps)]
                placed = place(parts, {}, lane)
                for t, value in enumerate(placed):
                    outs[n][(v * levels + lev) * len(placed) + t] = value.astype(jnp.bfloat16)
            return carry

        lax.fori_loop(0, nvar, variable, 0, unroll=len(distances) == 1)


def even_place():
    return lax.rem(lax.axis_index("space"), 2) == 0


def level_codes(ref, lev, first=0):
    planes = [
        [ref[0, v, lev, :, t : t + LANES] for t in range(0, ref.shape[-1], LANES)]
        for v in range(first, ref.shape[1])
    ]
    values, scales = row_codes(planes)
    return values + [scales]


def half_code_kernel(*refs):
    sources, (near_ref, far_ref, own_ref) = refs[:-3], refs[-3:]
    even = even_place()

    def pair(i, carry):
        near, far = [], []
        for k, ref in enumerate(sources):
            skip = int(k == len(sources) - 1)
            coded = [level_codes(ref, 2 * i + odd, skip) for odd in range(2)]
            for n, (first, second) in enumerate(zip(*coded)):
                if k == 0:
                    own_ref[i, n] = shorts(jnp.concatenate([first, second], 0))
                last, start = joined_halves(first, second)
                near.append(jnp.where(even, last, start))
                far.append(jnp.where(even, start, last))
            if len(near) % 2:
                near.append(jnp.zeros((SUB, LANES), jnp.float32))
                far.append(jnp.zeros((SUB, LANES), jnp.float32))
        for tiles, ref in ((near, near_ref), (far, far_ref)):
            for n in range(0, len(tiles), 2):
                ref[i, n // 2] = shorts(jnp.concatenate(tiles[n : n + 2], 0))
        return carry

    lax.fori_loop(0, near_ref.shape[0], pair, 0)


def half_tile(ref, i, n):
    whole = floats(ref[i, n // 2])
    return whole[SUB:] if n % 2 else whole[:SUB]


def around_kernel(windows, nvar, levels, *refs):
    pieces, (own_ref, near_ref, far_ref) = refs[:windows], refs[windows : windows + 3]
    outs, total_ref = refs[windows + 3 : -1], refs[-1]
    me = lax.axis_index("window")
    even = even_place()
    total = jnp.zeros((SUB, LANES), jnp.float32)
    for d in range(windows):
        split = pieces[d][pieces[d].shape[0] - 1].astype(jnp.float32)
        here = split + pltpu.roll(split, HALF, 0) + pltpu.roll(split, LANES // 2, 1)
        total = total + jnp.where(lax.rem(me - d + windows, windows) <= me, here, 0.0)
    for v in range(nvar):
        for lev in range(levels):
            one = total[lev : lev + 1, v : v + 1]
            total_ref[v * levels + lev] = jnp.broadcast_to(one, (SUB, LANES))
    for i, out_ref in enumerate(outs):
        for n in range(own_ref.shape[1]):
            own = floats(own_ref[i, n])
            near, far = half_tile(near_ref, i, n), half_tile(far_ref, i, n)
            for odd in range(2):
                halves = widened(own[odd * SUB : (odd + 1) * SUB], near, far, odd, even)
                out_ref[odd, n] = shorts(jnp.concatenate(halves, 0))


def decoded(ref, i, first, nvar, tiles):
    scales = jnp.exp2(half_tile(ref, i, first + nvar * tiles)) * (1.0 / CODE_MAX)
    return [
        [half_tile(ref, i, first + v * tiles + t) * scales[:, v : v + 1] for t in range(tiles)]
        for v in range(nvar)
    ]


def is_quarter(j, v, steps):
    return 0 < j < steps - 1 and not (v == 0 and j + 1 > HALF // 2)


def far_base(steps, nvar, levels):
    base, total = {}, 0
    for j in range(steps):
        for v in range(nvar):
            base[j, v] = total
            total += levels // (4 if is_quarter(j, v, steps) else 2)
    return base, total


def joined_quarters(four):
    slot = row_index() // 2
    last, start = pltpu.roll(four[0], 2, 0), four[0]
    for n in range(1, 4):
        last = jnp.where(slot == n, pltpu.roll(four[n], (2 * n + 2) % SUB, 0), last)
        start = jnp.where(slot == n, pltpu.roll(four[n], 2 * n, 0), start)
    return last, start


def assemble_kernel(windows, steps, nvar, levels, part, *refs):
    pieces = refs[:windows]
    own_ref, early_ref, late_ref, far_ref, stack_ref = refs[windows:]
    me = lax.axis_index("window")
    even = even_place()
    lane = lane_index()
    count = stack_ref.shape[1]
    packed_tiles = count // (nvar * levels)
    for d in range(windows):
        source = lax.rem(me - d + windows, windows)
        stack_ref[source] = pieces[d][:count]

    pairs = levels // 2
    base, _ = far_base(steps, nvar, levels)

    def variable(v):
        built = {}
        for lev in range(levels):
            plane = v * levels + lev
            sources = [
                [
                    stack_ref[w, plane * packed_tiles + t].astype(jnp.float32)
                    for t in range(packed_tiles)
                ]
                for w in range(windows)
            ]
            rolled = {}
            for j in range(steps):
                parts = [(w, sources[w], j * part, part, w * part) for w in range(windows)]
                built[j, lev] = place(parts, rolled, lane)
                own_ref[j, plane] = jnp.concatenate(built[j, lev], 1).astype(jnp.bfloat16)
        for j in range(steps):
            for i in range(pairs):
                halves = [joined_halves(a, b) for a, b in zip(built[j, 2 * i], built[j, 2 * i + 1])]
                last, start = (jnp.concatenate([h[k] for h in halves], 1) for k in range(2))
                near = jnp.where(even, last, start).astype(jnp.bfloat16)
                if j < steps // 2:
                    early_ref[j, v * pairs + i] = near
                else:
                    late_ref[j - steps // 2, v * pairs + i] = near
                if not is_quarter(j, v, steps):
                    far_ref[base[j, v] + i] = jnp.where(even, start, last).astype(jnp.bfloat16)
            if is_quarter(j, v, steps):
                for q in range(levels // 4):
                    four = zip(*[built[j, 4 * q + n] for n in range(4)])
                    ends = [joined_quarters(tiles) for tiles in four]
                    last, start = (jnp.concatenate([e[k] for e in ends], 1) for k in range(2))
                    far_ref[base[j, v] + q] = jnp.where(even, start, last).astype(jnp.bfloat16)

    for v in range(nvar):
        variable(v)


def prepare_tangent_kernel(
    steps, nvar, levels, tiles,
    count_ref, noise_ref, coupling_ref, near_ref, far_ref, inc_ref, dobs_ref, innov_ref,
    first_ref, obs_ref, share_ref, mix_ref,
):
    even = even_place()
    blocks = [slice(0, SUB), slice(SUB, 2 * SUB)]
    cuts = [slice(t * LANES, (t + 1) * LANES) for t in range(tiles)]
    for v in range(nvar):
        for u in range(nvar):
            one = coupling_gain * coupling_ref[v : v + 1, u : u + 1]
            mix_ref[v, u] = jnp.broadcast_to(one, (SUB, LANES))
    offset = -(-(nvar * tiles + 1) // 2) * 2
    for i in range(levels // 2):
        fields = [decoded(ref, i, offset, nvar, tiles) for ref in (near_ref, far_ref)]
        for odd in range(2):
            lev = 2 * i + odd
            for t in range(tiles):
                for v in range(nvar):
                    near, far = (side[v][t] for side in fields)
                    halves = widened(inc_ref[0, v, lev, :, cuts[t]], near, far, odd, even)
                    for b in range(2):
                        first_ref[lev, v, t, blocks[b], :] = halves[b]
            for j in range(steps):
                noise = jnp.full((SUB, LANES), noise_ref[0, j, lev])
                share = jnp.where(j < count_ref[0], 1.0, 0.0) / noise
                share_ref[lev, j] = share
                for t in range(tiles):
                    gap = innov_ref[0, j, lev, :, cuts[t]] - noise * dobs_ref[0, j, lev, :, cuts[t]]
                    obs_ref[lev, j, t] = gap * share


def prepare_adjoint_kernel(
    steps, nvar, levels, tiles, count_ref, near_ref, far_ref, dobs_ref, *refs
):
    after_refs, (last_ref, force_ref) = refs[: levels // 2], refs[levels // 2 + 1 :]
    even = even_place()
    blocks = [slice(0, SUB), slice(SUB, 2 * SUB)]
    cuts = [slice(t * LANES, (t + 1) * LANES) for t in range(tiles)]
    seen = [jnp.where(j < count_ref[0], 1.0, 0.0) for j in range(steps)]
    offset = -(-(nvar * tiles + 1) // 2) * 2
    none = [[jnp.zeros((SUB, LANES), jnp.float32)] * tiles]
    for i, after_ref in enumerate(after_refs):
        forces = [
            none + decoded(ref, i, 2 * offset, steps - 1, tiles) for ref in (near_ref, far_ref)
        ]
        for odd in range(2):
            lev = 2 * i + odd
            scales = jnp.exp2(floats(after_ref[odd, nvar * tiles])) * (-1.0 / CODE_MAX)
            for t in range(tiles):
                for v in range(nvar):
                    value = floats(after_ref[odd, v * tiles + t])
                    last_ref[lev, v, t] = value * scales[:, v : v + 1]
                for j in range(steps):
                    near, far = (side[j][t] for side in forces)
                    halves = widened(dobs_ref[0, j, lev, :, cuts[t]], near, far, odd, even)
                    for b in range(2):
                        force_ref[lev, j, t, blocks[b], :] = seen[j] * halves[b]


def from_north(line, lane):
    turned = [pltpu.roll(value, LANES - 1, 1) for value in line] * 2
    return [jnp.where(lane < LANES - 1, turned[t], turned[t + 1]) for t in range(len(line))]


def from_south(line, lane):
    turned = [pltpu.roll(value, 1, 1) for value in line]
    return [jnp.where(lane > 0, turned[t], turned[t - 1]) for t in range(len(line))]


def masked_last(line, lane):
    return line[:-1] + [jnp.where(lane < LANES - 1, line[-1], 0.0)]


def masked_first(line, lane):
    return [jnp.where(lane > 0, line[0], 0.0)] + line[1:]


def walls(spaces):
    row, place_x = row_index(), lax.axis_index("space")
    low = jnp.where((row == HALF) & (place_x == 0), 0.0, 1.0)
    high = jnp.where((row == HALF - 1) & (place_x == spaces - 1), 0.0, 1.0)

    def walled(block, east, west):
        if block == 0:
            return east, [low * value for value in west]
        return [high * value for value in east], west

    return walled


BLOCKS = [slice(SUB, 2 * SUB), slice(2 * SUB, 3 * SUB)]
UPS = [slice(b.start + 1, b.stop + 1) for b in BLOCKS]
DOWNS = [slice(b.start - 1, b.stop - 1) for b in BLOCKS]
MINE = slice(SUB + HALF, 2 * SUB + HALF)


def tangent_kernel(
    spaces, steps, nvar, levels, tiles,
    mix_ref, share_ref, obs_ref, own_ref, early_ref, late_ref, far_ref, first_ref,
    ndo_ref, ends_ref, x_ref, s_ref,
):
    lane, row = lane_index(), row_index()
    even = even_place()
    top = row < HALF
    walled = walls(spaces)
    pairs = levels // 2
    cuts = [slice(t * LANES, (t + 1) * LANES) for t in range(tiles)]
    base, _ = far_base(steps, nvar, levels)

    for lev in range(levels):
        i, odd = lev // 2, lev % 2
        for j in range(steps):
            near_ref = early_ref if j < steps // 2 else late_ref
            for v in range(nvar):
                for t in range(tiles):
                    own = own_ref[j, v * levels + lev, :, cuts[t]].astype(jnp.float32)
                    near = near_ref[j % (steps // 2), v * pairs + i, :, cuts[t]].astype(jnp.float32)
                    quarter = is_quarter(j, v, steps)
                    far = far_ref[base[j, v] + lev // (4 if quarter else 2), :, cuts[t]]
                    far = far.astype(jnp.float32)
                    if quarter:
                        slot = 2 * (lev % 4)
                        low_far = pltpu.roll(far, (HALF - 2 - slot) % SUB, 0)
                        high_far = pltpu.roll(far, (HALF - slot) % SUB, 0)
                    else:
                        low_far = pltpu.roll(far, HALF, 0) if odd else far
                        high_far = far if odd else pltpu.roll(far, HALF, 0)
                    low_near = pltpu.roll(near, HALF, 0) if odd else near
                    high_near = near if odd else pltpu.roll(near, HALF, 0)
                    turned = pltpu.roll(own, HALF, 0)
                    low = jnp.where(even, low_far, low_near)
                    high = jnp.where(even, high_near, high_far)
                    x_ref[lev, j, v, t, :SUB, :] = jnp.where(top, low, turned)
                    x_ref[lev, j, v, t, SUB:, :] = jnp.where(top, turned, high)

    def pair(i, outer):
        for odd in range(2):
            for v in range(nvar):
                for t in range(tiles):
                    s_ref[odd, 0, v, t, SUB : 3 * SUB, :] = first_ref[2 * i + odd, v, t]

        def step(j, carry):
            now = lax.rem(j, 2)
            for odd in range(2):
                lev = 2 * i + odd
                for t in range(tiles):
                    image = share_ref[lev, j] * s_ref[odd, now, 0, t, MINE, :]
                    ndo_ref[0, j, lev, :, cuts[t]] = obs_ref[lev, j, t] - image
                for b in range(2):
                    part = slice(b * SUB, (b + 1) * SUB)
                    here, up, down = BLOCKS[b], UPS[b], DOWNS[b]
                    x = [[x_ref[lev, j, u, t, part, :] for t in range(tiles)] for u in range(nvar)]
                    ce = [diffusion - half_adv * value for value in x[0]]
                    cw = [diffusion + half_adv * value for value in x[0]]
                    ce, cw = walled(b, ce, cw)
                    cn = masked_last([diffusion - half_adv * value for value in x[1]], lane)
                    cs = masked_first([diffusion + half_adv * value for value in x[1]], lane)
                    s = [
                        [s_ref[odd, now, u, t, here, :] for t in range(tiles)] for u in range(nvar)
                    ]
                    xs = [[x[u][t] * s[u][t] for t in range(tiles)] for u in range(nvar)]
                    for v in range(nvar):
                        north, south = from_north(s[v], lane), from_south(s[v], lane)
                        for t in range(tiles):
                            fresh = keep * s[v][t] + ce[t] * s_ref[odd, now, v, t, up, :]
                            fresh = fresh + cw[t] * s_ref[odd, now, v, t, down, :]
                            fresh = fresh + cn[t] * north[t] + cs[t] * south[t]
                            for u in range(nvar):
                                fresh = fresh + mix_ref[v, u] * xs[u][t]
                            s_ref[odd, 1 - now, v, t, here, :] = fresh
            return carry

        lax.fori_loop(0, steps, step, 0)
        for odd in range(2):
            for v in range(nvar):
                for t in range(tiles):
                    ends_ref[2 * i + odd, v, t] = s_ref[odd, steps % 2, v, t, MINE, :]
        return outer

    lax.fori_loop(0, pairs, pair, 0)


def adjoint_kernel(
    windows, spaces, steps, nvar, levels, tiles,
    mix_ref, total_ref, x_ref, last_ref, force_ref, ends_ref, inc_ref, rhs_ref, dual_ref,
    ndm_ref, ninc_ref, *rest,
):
    payload_refs = rest[: windows - 1]
    x0_ref, a_ref, q_ref = rest[windows - 1 :]
    me = lax.axis_index("window")
    lane = lane_index()
    walled = walls(spaces)
    pairs = levels // 2
    cuts = [slice(t * LANES, (t + 1) * LANES) for t in range(tiles)]

    def pair(i, outer):
        for odd in range(2):
            lev = 2 * i + odd
            for t in range(tiles):
                for j in range(steps):
                    x0_ref[odd, j, t, SUB : 3 * SUB, :] = x_ref[lev, j, 0, t]
                for v in range(nvar):
                    a_ref[odd, 0, v, t, SUB : 3 * SUB, :] = last_ref[lev, v, t]

        def step(turn, carry):
            now = lax.rem(turn, 2)
            j = steps - 1 - turn
            for odd in range(2):
                lev = 2 * i + odd
                for b in range(2):
                    part = slice(b * SUB, (b + 1) * SUB)
                    here, up, down = BLOCKS[b], UPS[b], DOWNS[b]
                    x = [[x_ref[lev, j, u, t, part, :] for t in range(tiles)] for u in range(nvar)]
                    ce = [diffusion + half_adv * x0_ref[odd, j, t, up, :] for t in range(tiles)]
                    cw = [diffusion - half_adv * x0_ref[odd, j, t, down, :] for t in range(tiles)]
                    ce, cw = walled(b, ce, cw)
                    cn = masked_first([diffusion + half_adv * value for value in x[1]], lane)
                    cs = masked_last([diffusion - half_adv * value for value in x[1]], lane)
                    a = [
                        [a_ref[odd, now, u, t, here, :] for t in range(tiles)] for u in range(nvar)
                    ]
                    for u in range(nvar):
                        north = from_north([cn[t] * a[u][t] for t in range(tiles)], lane)
                        south = from_south([cs[t] * a[u][t] for t in range(tiles)], lane)
                        for t in range(tiles):
                            fresh = keep * a[u][t] + ce[t] * a_ref[odd, now, u, t, up, :]
                            fresh = fresh + cw[t] * a_ref[odd, now, u, t, down, :]
                            fresh = fresh + north[t] + south[t]
                            pull = mix_ref[0, u] * a[0][t]
                            for v in range(1, nvar):
                                pull = pull + mix_ref[v, u] * a[v][t]
                            fresh = fresh + x[u][t] * pull
                            if u == 0:
                                fresh = fresh + force_ref[lev, j, t, part, :]
                            a_ref[odd, 1 - now, u, t, here, :] = fresh
            return carry

        lax.fori_loop(0, steps, step, 0)

        end = steps % 2
        coded = []
        for odd in range(2):
            lev = 2 * i + odd
            back, ahead = [], []
            for v in range(nvar):
                share = total_ref[v * levels + lev]
                tv, gv = [], []
                for t in range(tiles):
                    term = a_ref[odd, end, v, t, MINE, :] - last_ref[lev, v, t, HALF : HALF + SUB, :]
                    given = rhs_ref[0, v, lev, :, cuts[t]] - inc_ref[0, v, lev, :, cuts[t]]
                    given = given + share * term
                    ndm_ref[v, lev, :, cuts[t]] = -(dual_ref[0, v, lev, :, cuts[t]] + term)
                    ninc_ref[v, lev, :, cuts[t]] = given
                    tv.append(term)
                    gv.append(given + ends_ref[lev, v, t])
                back.append(tv)
                ahead.append(gv)
            coded.append((row_codes(back), row_codes(ahead)))
        for kind in range(2):
            first, second = coded[0][kind], coded[1][kind]
            for n, (a, b) in enumerate(zip(first[0] + [first[1]], second[0] + [second[1]])):
                q_ref[kind, i, n] = shorts(jnp.concatenate([a, b], 0))
        return outer

    lax.fori_loop(0, pairs, pair, 0)
    for d in range(1, windows):
        payload_refs[d - 1][...] = q_ref[jnp.where(me + d >= windows, 0, 1)]


def final_kernel(windows, nvar, levels, tiles, *refs):
    pieces = refs[: windows - 1]
    total_ref, base_dual_ref, base_inc_ref, ndm_ref, ninc_ref = refs[windows - 1 :]
    me = lax.axis_index("window")
    pairs = levels // 2
    cuts = [slice(t * LANES, (t + 1) * LANES) for t in range(tiles)]

    def pair(i, carry):
        tails = [None] * (nvar * tiles)
        heads = [None] * (nvar * tiles)
        for d in range(1, windows):
            piece = pieces[d - 1]
            scales = jnp.exp2(floats(piece[i, nvar * tiles])) * (1.0 / CODE_MAX)
            later = jnp.where(d > me, scales, 0.0)
            earlier = jnp.where(d > me, 0.0, scales)
            for v in range(nvar):
                for t in range(tiles):
                    n = v * tiles + t
                    value = floats(piece[i, n])
                    tail, head = value * later[:, v : v + 1], value * earlier[:, v : v + 1]
                    tails[n] = tail if d == 1 else tails[n] + tail
                    heads[n] = head if d == 1 else heads[n] + head
        for v in range(nvar):
            for odd in range(2):
                lev = 2 * i + odd
                share = total_ref[v * levels + lev]
                for t in range(tiles):
                    rows = slice(odd * SUB, (odd + 1) * SUB)
                    tail, head = tails[v * tiles + t][rows], heads[v * tiles + t][rows]
                    ndm_ref[0, v, lev, :, cuts[t]] = base_dual_ref[v, lev, :, cuts[t]] - tail
                    ninc_ref[0, v, lev, :, cuts[t]] = (
                        base_inc_ref[v, lev, :, cuts[t]] + head + share * tail
                    )
        return carry

    lax.fori_loop(0, pairs, pair, 0)


def moved(block, axis, distance, around=False):
    count = lax.axis_size(axis)
    route = [(i, (i + distance) % count) for i in range(count) if around or 0 <= i + distance < count]
    return lax.ppermute(block, axis, route)


def swaps(axis, first):
    route = []
    for i in range(first, lax.axis_size(axis) - 1, 2):
        route += [(i, i + 1), (i + 1, i)]
    return route


def swapped(block, axis, first):
    return lax.ppermute(block, axis, swaps(axis, first))


def body(
    trajectory,
    dual_model,
    increment,
    model_rhs,
    dual_obs,
    innovation,
    coupling,
    error_var,
    obs_var,
    obs_count,
):
    windows, spaces = lax.axis_size("window"), lax.axis_size("space")
    _, steps, nvar, levels, rows, part = trajectory.shape
    columns = dual_model.shape[-1]
    tiles = columns // LANES
    assert trajectory.shape[0] == windows and windows > 1 and rows == SUB and steps == HALF
    assert columns == tiles * LANES == windows * part and levels % 4 == 0
    pairs = levels // 2
    wide = -(-steps * part // LANES) * LANES
    bf16, f32, i16 = jnp.bfloat16, jnp.float32, jnp.int16

    def shape(dims, dtype):
        return jax.ShapeDtypeStruct(dims, dtype)

    block = shape((nvar * levels * wide // LANES + 1, rows, LANES), bf16)
    variances = jnp.pad(error_var[0].T, ((0, SUB - levels), (0, LANES - nvar)))

    def packed(distances):
        return pl.pallas_call(
            lambda *refs: pack_kernel(distances, windows, steps, nvar, levels, part, *refs),
            out_shape=[block] * len(distances),
            in_specs=[VMEM, VMEM],
            out_specs=[VMEM] * len(distances),
            compiler_params=params(),
        )(variances, trajectory)

    order = sorted(range(1, windows), key=lambda d: -d * (windows - d))
    groups = [[d] for d in order] if windows <= 4 else [order]
    blocks = {}
    for group in groups:
        blocks.update(zip(group, packed(group)))
    arrived = {d: moved(blocks[d], "window", d, around=True) for d in order}
    arrived[0] = packed([0])[0]

    payload = shape((pairs, nvar * tiles + 1, 2 * SUB, LANES), i16)

    counts = [nvar, nvar, steps - 1]
    half_tiles = sum(-(-(count * tiles + 1) // 2) for count in counts)
    halves = shape((pairs, half_tiles, 2 * SUB, LANES), i16)
    near, far, dual = pl.pallas_call(
        half_code_kernel,
        out_shape=[halves, halves, payload],
        in_specs=[VMEM] * 3,
        out_specs=[VMEM] * 3,
        compiler_params=params(),
    )(dual_model, increment, dual_obs)
    far, near = swapped(far, "space", 1), swapped(near, "space", 0)

    blocks_here = [arrived[d] for d in range(windows)]
    around = shape((2,) + payload.shape[1:], i16)
    *after, totals = pl.pallas_call(
        lambda *refs: around_kernel(windows, nvar, levels, *refs),
        out_shape=[around] * pairs + [shape((nvar * levels, rows, LANES), f32)],
        in_specs=[VMEM] * (windows + 3),
        out_specs=[VMEM] * (pairs + 1),
        compiler_params=params(),
    )(*blocks_here, dual, near, far)
    after = [moved(piece, "window", -1) for piece in after]

    half_steps = shape((steps // 2, nvar * pairs, rows, columns), bf16)
    own, traj_early, traj_late, traj_far = pl.pallas_call(
        lambda *refs: assemble_kernel(windows, steps, nvar, levels, part, *refs),
        out_shape=[
            shape((steps, nvar * levels, rows, columns), bf16),
            half_steps,
            half_steps,
            shape((far_base(steps, nvar, levels)[1], rows, columns), bf16),
        ],
        in_specs=[VMEM] * windows,
        out_specs=[VMEM] * 4,
        scratch_shapes=[pltpu.VMEM((windows, block.shape[0] - 1, rows, LANES), bf16)],
        compiler_params=params(),
    )(*blocks_here)
    traj_far = swapped(traj_far, "space", 1)
    traj_early, traj_late = swapped(traj_early, "space", 0), swapped(traj_late, "space", 0)

    first, obs, share, mix = pl.pallas_call(
        lambda *refs: prepare_tangent_kernel(steps, nvar, levels, tiles, *refs),
        out_shape=[
            shape((levels, nvar, tiles, 2 * SUB, LANES), f32),
            shape((levels, steps, tiles, SUB, LANES), f32),
            shape((levels, steps, SUB, LANES), f32),
            shape((nvar, nvar, SUB, LANES), f32),
        ],
        in_specs=[SMEM] * 2 + [VMEM] * 6,
        out_specs=[VMEM] * 4,
        compiler_params=params(),
    )(obs_count, obs_var, coupling, near, far, increment, dual_obs, innovation)
    new_dual_obs, ends, wide_traj = pl.pallas_call(
        lambda *refs: tangent_kernel(spaces, steps, nvar, levels, tiles, *refs),
        out_shape=[
            shape(dual_obs.shape, f32),
            shape((levels, nvar, tiles, SUB, LANES), f32),
            shape((levels, steps, nvar, tiles, 2 * SUB, LANES), f32),
        ],
        in_specs=[VMEM] * 8,
        out_specs=[VMEM] * 3,
        scratch_shapes=[pltpu.VMEM((2, 2, nvar, tiles, 4 * SUB, LANES), f32)],
        compiler_params=params(),
    )(mix, share, obs, own, traj_early, traj_late, traj_far, first)

    last, force = pl.pallas_call(
        lambda *refs: prepare_adjoint_kernel(steps, nvar, levels, tiles, *refs),
        out_shape=[shape((levels, n, tiles, 2 * SUB, LANES), f32) for n in (nvar, steps)],
        in_specs=[SMEM] + [VMEM] * (3 + pairs) + [pl.BlockSpec(memory_space=pl.ANY)],
        out_specs=[VMEM] * 2,
        compiler_params=params(),
    )(obs_count, near, far, dual_obs, *after, ends)
    state = shape((nvar, levels, rows, columns), f32)
    base_dual, base_inc, *payloads = pl.pallas_call(
        lambda *refs: adjoint_kernel(windows, spaces, steps, nvar, levels, tiles, *refs),
        out_shape=[state, state] + [payload] * (windows - 1),
        in_specs=[VMEM] * 9,
        out_specs=[VMEM] * (2 + windows - 1),
        scratch_shapes=[
            pltpu.VMEM((2, steps, tiles, 4 * SUB, LANES), f32),
            pltpu.VMEM((2, 2, nvar, tiles, 4 * SUB, LANES), f32),
            pltpu.VMEM((2,) + payload.shape, i16),
        ],
        compiler_params=params(),
    )(mix, totals, wide_traj, last, force, ends, increment, model_rhs, dual_model)
    sent = {d: moved(payloads[d - 1], "window", d, around=True) for d in order}

    new_dual_model, new_increment = pl.pallas_call(
        lambda *refs: final_kernel(windows, nvar, levels, tiles, *refs),
        out_shape=[shape(dual_model.shape, f32), shape(increment.shape, f32)],
        in_specs=[VMEM] * (windows + 2),
        out_specs=[VMEM] * 2,
        compiler_params=params(),
    )(*[sent[d] for d in range(1, windows)], totals, base_dual, base_inc)
    return new_dual_model, new_dual_obs, new_increment


def solution(mesh):
    placed = (
        P("members", None, None, None, "space", "window"),
        P(("members", "window"), None, None, "space", None),
        P(("members", "window"), None, None, "space", None),
        P(("members", "window"), None, None, "space", None),
        P(("members", "window"), None, None, "space", None),
        P(("members", "window"), None, None, "space", None),
        P(),
        P(("members", "window"), None, None),
        P(("members", "window"), None, None),
        P(("members", "window")),
    )
    return jax.shard_map(
        body,
        mesh=mesh,
        in_specs=placed,
        out_specs=(
            P(("members", "window"), None, None, "space", None),
            P(("members", "window"), None, None, "space", None),
            P(("members", "window"), None, None, "space", None),
        ),
        check_vma=False,
    )
```

```python
import jax
import jax.numpy as jnp
from jax import lax
from jax.experimental import pallas as pl
from jax.experimental.pallas import tpu as pltpu
from jax.sharding import PartitionSpec as P

LANES = 128
SUB = 8
HALF = SUB // 2
CODE_MAX = 32766.0
ROUNDER = 12582912.0

diffusion = 0.2
advection = 0.2
coupling_gain = 0.5
keep = 1.0 - 4.0 * diffusion
half_adv = 0.5 * advection

VMEM = pl.BlockSpec(memory_space=pltpu.VMEM)
SMEM = pl.BlockSpec(memory_space=pltpu.SMEM)
ANY = pl.BlockSpec(memory_space=pl.ANY)


def params(mib=24):
    return pltpu.CompilerParams(vmem_limit_bytes=mib * 1024 * 1024)


def lane_index():
    return lax.broadcasted_iota(jnp.int32, (SUB, LANES), 1)


def row_index():
    return lax.broadcasted_iota(jnp.int32, (SUB, LANES), 0)


def tiled(wide):
    short = -wide.shape[1] % LANES
    if short:
        wide = jnp.concatenate([wide, jnp.zeros((wide.shape[0], short), wide.dtype)], 1)
    return [wide[:, i : i + LANES] for i in range(0, wide.shape[1], LANES)]


def place(parts, rolled, lane):
    built = {}
    for key, tiles, first, width, target in parts:
        done = 0
        while done < width:
            a, b = first + done, target + done
            n = min(width - done, LANES - a % LANES, LANES - b % LANES)
            shift = (b - a) % LANES
            name = (key, a // LANES, shift)
            if name not in rolled:
                value = tiles[a // LANES]
                rolled[name] = pltpu.roll(value, shift, 1) if shift else value
            if b % LANES:
                built[b // LANES] = jnp.where(
                    lane >= b % LANES, rolled[name], built[b // LANES]
                )
            else:
                built[b // LANES] = rolled[name]
            done += n
    return [built[i] for i in range(len(built))]


def joined_halves(first, second):
    top = row_index()[:, :1] < HALF
    last = jnp.where(top, pltpu.roll(first, HALF, 0), second)
    start = jnp.where(top, first, pltpu.roll(second, HALF, 0))
    return last, start


def widened(own, near, far, odd, even):
    top = row_index() < HALF
    low, high = jnp.where(even, far, near), jnp.where(even, near, far)
    turned = pltpu.roll(own, HALF, 0)
    low = pltpu.roll(low, HALF, 0) if odd else low
    high = high if odd else pltpu.roll(high, HALF, 0)
    return jnp.where(top, low, turned), jnp.where(top, turned, high)


def row_codes(planes):
    lane = lax.broadcasted_iota(jnp.int32, planes[0][0].shape, 1)
    scales = jnp.zeros(planes[0][0].shape, jnp.float32)
    out = []
    for v, row in enumerate(planes):
        big = jnp.abs(row[0])
        for value in row[1:]:
            big = jnp.maximum(big, jnp.abs(value))
        big = jnp.max(big, axis=1, keepdims=True)
        power = jnp.clip(jnp.ceil(jnp.log2(jnp.maximum(big, 1e-30))), -90.0, 126.0)
        scales = jnp.where(lane == v, power, scales)
        gain = CODE_MAX * jnp.exp2(-power)
        for value in row:
            out.append((value * gain + ROUNDER) - ROUNDER)
    return out, scales


def shorts(value):
    return value.astype(jnp.int32).astype(jnp.int16)


def floats(value):
    return value.astype(jnp.int32).astype(jnp.float32)


def pack_kernel(distances, windows, steps, nvar, levels, part, var_ref, traj_ref, *outs):
    me = lax.axis_index("window")
    lane = lane_index()
    variance = var_ref[...]
    high = variance.astype(jnp.bfloat16).astype(jnp.float32)
    middle = (variance - high).astype(jnp.bfloat16).astype(jnp.float32)
    low = variance - high - middle
    split = high + pltpu.roll(middle, HALF, 0) + pltpu.roll(low, LANES // 2, 1)
    split = split.astype(jnp.bfloat16)

    for n, d in enumerate(distances):
        outs[n][outs[n].shape[0] - 1] = split
        target = lax.rem(me + d, windows)

        def variable(v, carry, n=n, target=target):
            for lev in range(levels):
                pieces = [
                    tiled(traj_ref[target, j, v, lev].astype(jnp.float32)) for j in range(steps)
                ]
                parts = [(j, pieces[j], 0, part, j * part) for j in range(steps)]
                placed = place(parts, {}, lane)
                for t, value in enumerate(placed):
                    outs[n][(v * levels + lev) * len(placed) + t] = value.astype(jnp.bfloat16)
            return carry

        lax.fori_loop(0, nvar, variable, 0, unroll=len(distances) == 1)


def even_place():
    return lax.rem(lax.axis_index("space"), 2) == 0


def level_codes(ref, lev, first=0):
    planes = [
        [ref[0, v, lev, :, t : t + LANES] for t in range(0, ref.shape[-1], LANES)]
        for v in range(first, ref.shape[1])
    ]
    values, scales = row_codes(planes)
    return values + [scales]


def half_code_kernel(*refs):
    sources, (near_ref, far_ref, own_ref) = refs[:-3], refs[-3:]
    even = even_place()

    def pair(i, carry):
        near, far = [], []
        for k, ref in enumerate(sources):
            skip = int(k == len(sources) - 1)
            coded = [level_codes(ref, 2 * i + odd, skip) for odd in range(2)]
            for n, (first, second) in enumerate(zip(*coded)):
                if k == 0:
                    own_ref[i, n] = shorts(jnp.concatenate([first, second], 0))
                last, start = joined_halves(first, second)
                near.append(jnp.where(even, last, start))
                far.append(jnp.where(even, start, last))
            if len(near) % 2:
                near.append(jnp.zeros((SUB, LANES), jnp.float32))
                far.append(jnp.zeros((SUB, LANES), jnp.float32))
        for tiles, ref in ((near, near_ref), (far, far_ref)):
            for n in range(0, len(tiles), 2):
                ref[i, n // 2] = shorts(jnp.concatenate(tiles[n : n + 2], 0))
        return carry

    lax.fori_loop(0, near_ref.shape[0], pair, 0)


def half_tile(ref, i, n):
    whole = floats(ref[i, n // 2])
    return whole[SUB:] if n % 2 else whole[:SUB]


def around_kernel(windows, nvar, levels, *refs):
    pieces, (own_ref, near_ref, far_ref) = refs[:windows], refs[windows : windows + 3]
    outs, total_ref = refs[windows + 3 : -1], refs[-1]
    me = lax.axis_index("window")
    even = even_place()
    total = jnp.zeros((SUB, LANES), jnp.float32)
    for d in range(windows):
        split = pieces[d][pieces[d].shape[0] - 1].astype(jnp.float32)
        here = split + pltpu.roll(split, HALF, 0) + pltpu.roll(split, LANES // 2, 1)
        total = total + jnp.where(lax.rem(me - d + windows, windows) <= me, here, 0.0)
    for v in range(nvar):
        for lev in range(levels):
            one = total[lev : lev + 1, v : v + 1]
            total_ref[v * levels + lev] = jnp.broadcast_to(one, (SUB, LANES))
    for i, out_ref in enumerate(outs):
        for n in range(own_ref.shape[1]):
            own = floats(own_ref[i, n])
            near, far = half_tile(near_ref, i, n), half_tile(far_ref, i, n)
            for odd in range(2):
                halves = widened(own[odd * SUB : (odd + 1) * SUB], near, far, odd, even)
                out_ref[odd, n] = shorts(jnp.concatenate(halves, 0))


def decoded(ref, i, first, nvar, tiles):
    scales = jnp.exp2(half_tile(ref, i, first + nvar * tiles)) * (1.0 / CODE_MAX)
    return [
        [half_tile(ref, i, first + v * tiles + t) * scales[:, v : v + 1] for t in range(tiles)]
        for v in range(nvar)
    ]


def is_quarter(j, v, steps):
    return 0 < j < steps - 1 and not (v == 0 and j + 1 > HALF // 2)


def far_base(steps, nvar, levels):
    base, total = {}, 0
    for j in range(steps):
        for v in range(nvar):
            base[j, v] = total
            total += levels // (4 if is_quarter(j, v, steps) else 2)
    return base, total


def joined_quarters(four):
    slot = row_index() // 2
    last, start = pltpu.roll(four[0], 2, 0), four[0]
    for n in range(1, 4):
        last = jnp.where(slot == n, pltpu.roll(four[n], (2 * n + 2) % SUB, 0), last)
        start = jnp.where(slot == n, pltpu.roll(four[n], 2 * n, 0), start)
    return last, start


def assemble_kernel(windows, steps, nvar, levels, part, *refs):
    pieces = refs[:windows]
    own_ref, early_ref, late_ref, far_ref, stack_ref = refs[windows + 1 :]
    me = lax.axis_index("window")
    even = even_place()
    lane = lane_index()
    count = stack_ref.shape[1]
    packed_tiles = count // (nvar * levels)
    for d in range(windows):
        source = lax.rem(me - d + windows, windows)
        stack_ref[source] = pieces[d][:count]

    pairs = levels // 2
    base, _ = far_base(steps, nvar, levels)

    def variable(v):
        built = {}
        for lev in range(levels):
            plane = v * levels + lev
            sources = [
                [
                    stack_ref[w, plane * packed_tiles + t].astype(jnp.float32)
                    for t in range(packed_tiles)
                ]
                for w in range(windows)
            ]
            rolled = {}
            for j in range(steps):
                parts = [(w, sources[w], j * part, part, w * part) for w in range(windows)]
                built[j, lev] = place(parts, rolled, lane)
                own_ref[j, plane] = jnp.concatenate(built[j, lev], 1).astype(jnp.bfloat16)
        for j in range(steps):
            for i in range(pairs):
                halves = [joined_halves(a, b) for a, b in zip(built[j, 2 * i], built[j, 2 * i + 1])]
                last, start = (jnp.concatenate([h[k] for h in halves], 1) for k in range(2))
                near = jnp.where(even, last, start).astype(jnp.bfloat16)
                if j < steps // 2:
                    early_ref[j, v * pairs + i] = near
                else:
                    late_ref[j - steps // 2, v * pairs + i] = near
                if not is_quarter(j, v, steps):
                    far_ref[base[j, v] + i] = jnp.where(even, start, last).astype(jnp.bfloat16)
            if is_quarter(j, v, steps):
                for q in range(levels // 4):
                    four = zip(*[built[j, 4 * q + n] for n in range(4)])
                    ends = [joined_quarters(tiles) for tiles in four]
                    last, start = (jnp.concatenate([e[k] for e in ends], 1) for k in range(2))
                    far_ref[base[j, v] + q] = jnp.where(even, start, last).astype(jnp.bfloat16)

    for v in range(nvar):
        variable(v)


def prepare_factor_kernel(
    steps, nvar, levels, tiles,
    count_ref, noise_ref, coupling_ref, dobs_ref, innov_ref, obs_ref, share_ref, mix_ref,
):
    cuts = [slice(t * LANES, (t + 1) * LANES) for t in range(tiles)]
    for v in range(nvar):
        for u in range(nvar):
            one = coupling_gain * coupling_ref[v : v + 1, u : u + 1]
            mix_ref[v, u] = jnp.broadcast_to(one, (SUB, LANES))
    for lev in range(levels):
        for j in range(steps):
            noise = jnp.full((SUB, LANES), noise_ref[0, j, lev])
            share = jnp.where(j < count_ref[0], 1.0, 0.0) / noise
            share_ref[lev, j] = share
            for t in range(tiles):
                gap = innov_ref[0, j, lev, :, cuts[t]] - noise * dobs_ref[0, j, lev, :, cuts[t]]
                obs_ref[lev, j, t] = gap * share


def prepare_tangent_kernel(nvar, levels, tiles, near_ref, far_ref, inc_ref, first_ref):
    even = even_place()
    blocks = [slice(0, SUB), slice(SUB, 2 * SUB)]
    cuts = [slice(t * LANES, (t + 1) * LANES) for t in range(tiles)]
    offset = -(-(nvar * tiles + 1) // 2) * 2
    for i in range(levels // 2):
        fields = [decoded(ref, i, offset, nvar, tiles) for ref in (near_ref, far_ref)]
        for odd in range(2):
            lev = 2 * i + odd
            for t in range(tiles):
                for v in range(nvar):
                    near, far = (side[v][t] for side in fields)
                    halves = widened(inc_ref[0, v, lev, :, cuts[t]], near, far, odd, even)
                    for b in range(2):
                        first_ref[lev, v, t, blocks[b], :] = halves[b]


def prepare_adjoint_kernel(
    steps, nvar, levels, tiles, count_ref, near_ref, far_ref, dobs_ref, *refs
):
    after_refs, (last_ref, force_ref) = refs[: levels // 2], refs[levels // 2 + 1 :]
    even = even_place()
    blocks = [slice(0, SUB), slice(SUB, 2 * SUB)]
    cuts = [slice(t * LANES, (t + 1) * LANES) for t in range(tiles)]
    seen = [jnp.where(j < count_ref[0], 1.0, 0.0) for j in range(steps)]
    offset = -(-(nvar * tiles + 1) // 2) * 2
    none = [[jnp.zeros((SUB, LANES), jnp.float32)] * tiles]
    for i, after_ref in enumerate(after_refs):
        forces = [
            none + decoded(ref, i, 2 * offset, steps - 1, tiles) for ref in (near_ref, far_ref)
        ]
        for odd in range(2):
            lev = 2 * i + odd
            scales = jnp.exp2(floats(after_ref[odd, nvar * tiles])) * (-1.0 / CODE_MAX)
            for t in range(tiles):
                for v in range(nvar):
                    value = floats(after_ref[odd, v * tiles + t])
                    last_ref[lev, v, t] = value * scales[:, v : v + 1]
                for j in range(steps):
                    near, far = (side[j][t] for side in forces)
                    halves = widened(dobs_ref[0, j, lev, :, cuts[t]], near, far, odd, even)
                    for b in range(2):
                        force_ref[lev, j, t, blocks[b], :] = seen[j] * halves[b]


def from_north(line, lane):
    turned = [pltpu.roll(value, LANES - 1, 1) for value in line] * 2
    return [jnp.where(lane < LANES - 1, turned[t], turned[t + 1]) for t in range(len(line))]


def from_south(line, lane):
    turned = [pltpu.roll(value, 1, 1) for value in line]
    return [jnp.where(lane > 0, turned[t], turned[t - 1]) for t in range(len(line))]


def masked_last(line, lane):
    return line[:-1] + [jnp.where(lane < LANES - 1, line[-1], 0.0)]


def masked_first(line, lane):
    return [jnp.where(lane > 0, line[0], 0.0)] + line[1:]


def walls(spaces):
    row, place_x = row_index(), lax.axis_index("space")
    low = jnp.where((row == HALF) & (place_x == 0), 0.0, 1.0)
    high = jnp.where((row == HALF - 1) & (place_x == spaces - 1), 0.0, 1.0)

    def walled(block, east, west):
        if block == 0:
            return east, [low * value for value in west]
        return [high * value for value in east], west

    return walled


BLOCKS = [slice(SUB, 2 * SUB), slice(2 * SUB, 3 * SUB)]
UPS = [slice(b.start + 1, b.stop + 1) for b in BLOCKS]
DOWNS = [slice(b.start - 1, b.stop - 1) for b in BLOCKS]
MINE = slice(SUB + HALF, 2 * SUB + HALF)


def tangent_kernel(
    spaces, steps, nvar, levels, tiles,
    mix_ref, share_ref, obs_ref, own_ref, early_ref, late_ref, far_ref, first_ref,
    ndo_ref, ends_ref, x_ref, s_ref,
):
    lane, row = lane_index(), row_index()
    even = even_place()
    top = row < HALF
    walled = walls(spaces)
    pairs = levels // 2
    cuts = [slice(t * LANES, (t + 1) * LANES) for t in range(tiles)]
    base, _ = far_base(steps, nvar, levels)

    for lev in range(levels):
        i, odd = lev // 2, lev % 2
        for j in range(steps):
            near_ref = early_ref if j < steps // 2 else late_ref
            for v in range(nvar):
                for t in range(tiles):
                    own = own_ref[j, v * levels + lev, :, cuts[t]].astype(jnp.float32)
                    near = near_ref[j % (steps // 2), v * pairs + i, :, cuts[t]].astype(jnp.float32)
                    quarter = is_quarter(j, v, steps)
                    far = far_ref[base[j, v] + lev // (4 if quarter else 2), :, cuts[t]]
                    far = far.astype(jnp.float32)
                    if quarter:
                        slot = 2 * (lev % 4)
                        low_far = pltpu.roll(far, (HALF - 2 - slot) % SUB, 0)
                        high_far = pltpu.roll(far, (HALF - slot) % SUB, 0)
                    else:
                        low_far = pltpu.roll(far, HALF, 0) if odd else far
                        high_far = far if odd else pltpu.roll(far, HALF, 0)
                    low_near = pltpu.roll(near, HALF, 0) if odd else near
                    high_near = near if odd else pltpu.roll(near, HALF, 0)
                    turned = pltpu.roll(own, HALF, 0)
                    low = jnp.where(even, low_far, low_near)
                    high = jnp.where(even, high_near, high_far)
                    x_ref[lev, j, v, t, :SUB, :] = jnp.where(top, low, turned)
                    x_ref[lev, j, v, t, SUB:, :] = jnp.where(top, turned, high)

    def pair(i, outer):
        for odd in range(2):
            for v in range(nvar):
                for t in range(tiles):
                    s_ref[odd, 0, v, t, SUB : 3 * SUB, :] = first_ref[2 * i + odd, v, t]

        def step(j, carry):
            now = lax.rem(j, 2)
            for odd in range(2):
                lev = 2 * i + odd
                for t in range(tiles):
                    image = share_ref[lev, j] * s_ref[odd, now, 0, t, MINE, :]
                    ndo_ref[0, j, lev, :, cuts[t]] = obs_ref[lev, j, t] - image
                for b in range(2):
                    part = slice(b * SUB, (b + 1) * SUB)
                    here, up, down = BLOCKS[b], UPS[b], DOWNS[b]
                    x = [[x_ref[lev, j, u, t, part, :] for t in range(tiles)] for u in range(nvar)]
                    ce = [diffusion - half_adv * value for value in x[0]]
                    cw = [diffusion + half_adv * value for value in x[0]]
                    ce, cw = walled(b, ce, cw)
                    cn = masked_last([diffusion - half_adv * value for value in x[1]], lane)
                    cs = masked_first([diffusion + half_adv * value for value in x[1]], lane)
                    s = [
                        [s_ref[odd, now, u, t, here, :] for t in range(tiles)] for u in range(nvar)
                    ]
                    xs = [[x[u][t] * s[u][t] for t in range(tiles)] for u in range(nvar)]
                    for v in range(nvar):
                        north, south = from_north(s[v], lane), from_south(s[v], lane)
                        for t in range(tiles):
                            fresh = keep * s[v][t] + ce[t] * s_ref[odd, now, v, t, up, :]
                            fresh = fresh + cw[t] * s_ref[odd, now, v, t, down, :]
                            fresh = fresh + cn[t] * north[t] + cs[t] * south[t]
                            for u in range(nvar):
                                fresh = fresh + mix_ref[v, u] * xs[u][t]
                            s_ref[odd, 1 - now, v, t, here, :] = fresh
            return carry

        lax.fori_loop(0, steps, step, 0)
        for odd in range(2):
            for v in range(nvar):
                for t in range(tiles):
                    ends_ref[2 * i + odd, v, t] = s_ref[odd, steps % 2, v, t, MINE, :]
        return outer

    lax.fori_loop(0, pairs, pair, 0)


def adjoint_kernel(
    windows, spaces, steps, nvar, levels, tiles,
    mix_ref, total_ref, x_ref, last_ref, force_ref, ends_ref, inc_ref, rhs_ref, dual_ref,
    ndm_ref, ninc_ref, *rest,
):
    payload_refs = rest[: windows - 1]
    x0_ref, a_ref, q_ref = rest[windows - 1 :]
    me = lax.axis_index("window")
    lane = lane_index()
    walled = walls(spaces)
    pairs = levels // 2
    cuts = [slice(t * LANES, (t + 1) * LANES) for t in range(tiles)]

    def pair(i, outer):
        for odd in range(2):
            lev = 2 * i + odd
            for t in range(tiles):
                for j in range(steps):
                    x0_ref[odd, j, t, SUB : 3 * SUB, :] = x_ref[lev, j, 0, t]
                for v in range(nvar):
                    a_ref[odd, 0, v, t, SUB : 3 * SUB, :] = last_ref[lev, v, t]

        def step(turn, carry):
            now = lax.rem(turn, 2)
            j = steps - 1 - turn
            for odd in range(2):
                lev = 2 * i + odd
                for b in range(2):
                    part = slice(b * SUB, (b + 1) * SUB)
                    here, up, down = BLOCKS[b], UPS[b], DOWNS[b]
                    x = [[x_ref[lev, j, u, t, part, :] for t in range(tiles)] for u in range(nvar)]
                    ce = [diffusion + half_adv * x0_ref[odd, j, t, up, :] for t in range(tiles)]
                    cw = [diffusion - half_adv * x0_ref[odd, j, t, down, :] for t in range(tiles)]
                    ce, cw = walled(b, ce, cw)
                    cn = masked_first([diffusion + half_adv * value for value in x[1]], lane)
                    cs = masked_last([diffusion - half_adv * value for value in x[1]], lane)
                    a = [
                        [a_ref[odd, now, u, t, here, :] for t in range(tiles)] for u in range(nvar)
                    ]
                    for u in range(nvar):
                        north = from_north([cn[t] * a[u][t] for t in range(tiles)], lane)
                        south = from_south([cs[t] * a[u][t] for t in range(tiles)], lane)
                        for t in range(tiles):
                            fresh = keep * a[u][t] + ce[t] * a_ref[odd, now, u, t, up, :]
                            fresh = fresh + cw[t] * a_ref[odd, now, u, t, down, :]
                            fresh = fresh + north[t] + south[t]
                            pull = mix_ref[0, u] * a[0][t]
                            for v in range(1, nvar):
                                pull = pull + mix_ref[v, u] * a[v][t]
                            fresh = fresh + x[u][t] * pull
                            if u == 0:
                                fresh = fresh + force_ref[lev, j, t, part, :]
                            a_ref[odd, 1 - now, u, t, here, :] = fresh
            return carry

        lax.fori_loop(0, steps, step, 0)

        end = steps % 2
        coded = []
        for odd in range(2):
            lev = 2 * i + odd
            back, ahead = [], []
            for v in range(nvar):
                share = total_ref[v * levels + lev]
                tv, gv = [], []
                for t in range(tiles):
                    term = a_ref[odd, end, v, t, MINE, :] - last_ref[lev, v, t, HALF : HALF + SUB, :]
                    given = rhs_ref[0, v, lev, :, cuts[t]] - inc_ref[0, v, lev, :, cuts[t]]
                    given = given + share * term
                    ndm_ref[v, lev, :, cuts[t]] = -(dual_ref[0, v, lev, :, cuts[t]] + term)
                    ninc_ref[v, lev, :, cuts[t]] = given
                    tv.append(term)
                    gv.append(given + ends_ref[lev, v, t])
                back.append(tv)
                ahead.append(gv)
            coded.append((row_codes(back), row_codes(ahead)))
        for kind in range(2):
            first, second = coded[0][kind], coded[1][kind]
            for n, (a, b) in enumerate(zip(first[0] + [first[1]], second[0] + [second[1]])):
                q_ref[kind, i, n] = shorts(jnp.concatenate([a, b], 0))
        return outer

    lax.fori_loop(0, pairs, pair, 0)
    if windows == 4:
        later_ref, earlier_ref, over_ref = payload_refs
        later_ref[...] = q_ref[1]
        earlier_ref[...] = q_ref[0]
        over_ref[...] = q_ref[jnp.where(me == 0, 1, 0)]
    else:
        for d in range(1, windows):
            payload_refs[d - 1][...] = q_ref[jnp.where(me + d >= windows, 0, 1)]


def join_kernel(nvar, tiles, right_ref, left_ref, later_ref, earlier_ref, out_ref):
    upward = lax.axis_index("window") == 1

    def pair(i, carry):
        def summed(ref, other_ref):
            codes = [
                jnp.where(upward, floats(ref[i, n]), floats(other_ref[i, n]))
                for n in range(nvar * tiles + 1)
            ]
            scales = jnp.exp2(codes[-1]) * (1.0 / CODE_MAX)
            return [
                [codes[v * tiles + t] * scales[:, v : v + 1] for t in range(tiles)]
                for v in range(nvar)
            ]

        mine, other = summed(later_ref, earlier_ref), summed(right_ref, left_ref)
        planes = [[a + b for a, b in zip(x, y)] for x, y in zip(mine, other)]
        values, scales = row_codes(planes)
        for n, value in enumerate(values + [scales]):
            out_ref[i, n] = shorts(value)
        return carry

    lax.fori_loop(0, out_ref.shape[0], pair, 0)


def final_kernel(windows, nvar, levels, tiles, *refs):
    pieces, refs = refs[:-5], refs[-5:]
    total_ref, base_dual_ref, base_inc_ref, ndm_ref, ninc_ref = refs
    me = lax.axis_index("window")
    pairs = levels // 2
    cuts = [slice(t * LANES, (t + 1) * LANES) for t in range(tiles)]
    if windows == 4:
        from_later = [False, True, me < 2, me < 2]
    else:
        from_later = [d > me for d in range(1, windows)]

    def pair(i, carry):
        tails = [None] * (nvar * tiles)
        heads = [None] * (nvar * tiles)

        def add(sums, n, value):
            sums[n] = value if sums[n] is None else sums[n] + value

        for piece, later in zip(pieces, from_later):
            scales = jnp.exp2(floats(piece[i, nvar * tiles])) * (1.0 / CODE_MAX)
            for v in range(nvar):
                scale = scales[:, v : v + 1]
                for t in range(tiles):
                    n = v * tiles + t
                    value = floats(piece[i, n]) * scale
                    if later is True:
                        add(tails, n, value)
                    elif later is False:
                        add(heads, n, value)
                    else:
                        add(tails, n, jnp.where(later, value, 0.0))
                        add(heads, n, jnp.where(later, 0.0, value))
        for v in range(nvar):
            for odd in range(2):
                lev = 2 * i + odd
                share = total_ref[v * levels + lev]
                for t in range(tiles):
                    rows = slice(odd * SUB, (odd + 1) * SUB)
                    tail, head = tails[v * tiles + t][rows], heads[v * tiles + t][rows]
                    ndm_ref[0, v, lev, :, cuts[t]] = base_dual_ref[v, lev, :, cuts[t]] - tail
                    ninc_ref[0, v, lev, :, cuts[t]] = (
                        base_inc_ref[v, lev, :, cuts[t]] + head + share * tail
                    )
        return carry

    lax.fori_loop(0, pairs, pair, 0)


def moved(block, axis, distance, around=False):
    count = lax.axis_size(axis)
    route = [(i, (i + distance) % count) for i in range(count) if around or 0 <= i + distance < count]
    return lax.ppermute(block, axis, route)


def swaps(axis, first):
    route = []
    for i in range(first, lax.axis_size(axis) - 1, 2):
        route += [(i, i + 1), (i + 1, i)]
    return route


def swapped(block, axis, first):
    return lax.ppermute(block, axis, swaps(axis, first))


def body(
    trajectory,
    dual_model,
    increment,
    model_rhs,
    dual_obs,
    innovation,
    coupling,
    error_var,
    obs_var,
    obs_count,
):
    windows, spaces = lax.axis_size("window"), lax.axis_size("space")
    _, steps, nvar, levels, rows, part = trajectory.shape
    columns = dual_model.shape[-1]
    tiles = columns // LANES
    assert trajectory.shape[0] == windows and windows > 1 and rows == SUB and steps == HALF
    assert columns == tiles * LANES == windows * part and levels % 4 == 0
    pairs = levels // 2
    wide = -(-steps * part // LANES) * LANES
    bf16, f32, i16 = jnp.bfloat16, jnp.float32, jnp.int16

    def shape(dims, dtype):
        return jax.ShapeDtypeStruct(dims, dtype)

    block = shape((nvar * levels * wide // LANES + 1, rows, LANES), bf16)
    variances = jnp.pad(error_var[0].T, ((0, SUB - levels), (0, LANES - nvar)))

    def packed(distances):
        return pl.pallas_call(
            lambda *refs: pack_kernel(distances, windows, steps, nvar, levels, part, *refs),
            out_shape=[block] * len(distances),
            in_specs=[VMEM, VMEM],
            out_specs=[VMEM] * len(distances),
            compiler_params=params(),
        )(variances, trajectory)

    order = sorted(range(1, windows), key=lambda d: -d * (windows - d))
    groups = [[d] for d in order] if windows <= 4 else [order]
    blocks = {}
    for group in groups:
        blocks.update(zip(group, packed(group)))
    arrived = {d: moved(blocks[d], "window", d, around=True) for d in order}
    arrived[0] = packed([0])[0]

    payload = shape((pairs, nvar * tiles + 1, 2 * SUB, LANES), i16)

    counts = [nvar, nvar, steps - 1]
    half_tiles = sum(-(-(count * tiles + 1) // 2) for count in counts)
    halves = shape((pairs, half_tiles, 2 * SUB, LANES), i16)
    near, far, dual = pl.pallas_call(
        half_code_kernel,
        out_shape=[halves, halves, payload],
        in_specs=[VMEM] * 3,
        out_specs=[VMEM] * 3,
        compiler_params=params(),
    )(dual_model, increment, dual_obs)
    far, near = swapped(far, "space", 1), swapped(near, "space", 0)

    blocks_here = [arrived[d] for d in range(windows)]
    *after, totals = pl.pallas_call(
        lambda *refs: around_kernel(windows, nvar, levels, *refs),
        out_shape=[shape((2,) + payload.shape[1:], i16)] * pairs
        + [shape((nvar * levels, rows, LANES), f32)],
        in_specs=[VMEM] * (windows + 3),
        out_specs=[VMEM] * (pairs + 1),
        compiler_params=params(),
    )(*blocks_here, dual, near, far)
    after = [moved(piece, "window", -1) for piece in after]

    obs, share, mix = pl.pallas_call(
        lambda *refs: prepare_factor_kernel(steps, nvar, levels, tiles, *refs),
        out_shape=[
            shape((levels, steps, tiles, SUB, LANES), f32),
            shape((levels, steps, SUB, LANES), f32),
            shape((nvar, nvar, SUB, LANES), f32),
        ],
        in_specs=[SMEM] * 2 + [VMEM] * 3,
        out_specs=[VMEM] * 3,
        compiler_params=params(),
    )(obs_count, obs_var, coupling, dual_obs, innovation)

    half_steps = shape((steps // 2, nvar * pairs, rows, columns), bf16)
    own, traj_early, traj_late, traj_far = pl.pallas_call(
        lambda *refs: assemble_kernel(windows, steps, nvar, levels, part, *refs),
        out_shape=[
            shape((steps, nvar * levels, rows, columns), bf16),
            half_steps,
            half_steps,
            shape((far_base(steps, nvar, levels)[1], rows, columns), bf16),
        ],
        in_specs=[VMEM] * windows + [ANY],
        out_specs=[VMEM] * 4,
        scratch_shapes=[pltpu.VMEM((windows, block.shape[0] - 1, rows, LANES), bf16)],
        compiler_params=params(),
    )(*blocks_here, mix)
    traj_far = swapped(traj_far, "space", 1)
    traj_early, traj_late = swapped(traj_early, "space", 0), swapped(traj_late, "space", 0)

    first = pl.pallas_call(
        lambda *refs: prepare_tangent_kernel(nvar, levels, tiles, *refs),
        out_shape=shape((levels, nvar, tiles, 2 * SUB, LANES), f32),
        in_specs=[VMEM] * 3,
        out_specs=VMEM,
        compiler_params=params(),
    )(near, far, increment)
    new_dual_obs, ends, wide_traj = pl.pallas_call(
        lambda *refs: tangent_kernel(spaces, steps, nvar, levels, tiles, *refs),
        out_shape=[
            shape(dual_obs.shape, f32),
            shape((levels, nvar, tiles, SUB, LANES), f32),
            shape((levels, steps, nvar, tiles, 2 * SUB, LANES), f32),
        ],
        in_specs=[VMEM] * 8,
        out_specs=[VMEM] * 3,
        scratch_shapes=[pltpu.VMEM((2, 2, nvar, tiles, 4 * SUB, LANES), f32)],
        compiler_params=params(),
    )(mix, share, obs, own, traj_early, traj_late, traj_far, first)

    last, force = pl.pallas_call(
        lambda *refs: prepare_adjoint_kernel(steps, nvar, levels, tiles, *refs),
        out_shape=[shape((levels, n, tiles, 2 * SUB, LANES), f32) for n in (nvar, steps)],
        in_specs=[SMEM] + [VMEM] * (3 + pairs) + [ANY],
        out_specs=[VMEM] * 2,
        compiler_params=params(),
    )(obs_count, near, far, dual_obs, *after, ends)
    state = shape((nvar, levels, rows, columns), f32)
    base_dual, base_inc, *payloads = pl.pallas_call(
        lambda *refs: adjoint_kernel(windows, spaces, steps, nvar, levels, tiles, *refs),
        out_shape=[state, state] + [payload] * (windows - 1),
        in_specs=[VMEM] * 9,
        out_specs=[VMEM] * (2 + windows - 1),
        scratch_shapes=[
            pltpu.VMEM((2, steps, tiles, 4 * SUB, LANES), f32),
            pltpu.VMEM((2, 2, nvar, tiles, 4 * SUB, LANES), f32),
            pltpu.VMEM((2,) + payload.shape, i16),
        ],
        compiler_params=params(),
    )(mix, totals, wide_traj, last, force, ends, increment, model_rhs, dual_model)
    if windows == 4:
        later, earlier, over = payloads
        right, left = moved(later, "window", 1), moved(earlier, "window", -1)
        over = lax.ppermute(over, "window", [(0, 2), (3, 1)])
        both = pl.pallas_call(
            lambda *refs: join_kernel(nvar, tiles, *refs),
            out_shape=payload,
            in_specs=[VMEM] * 4,
            out_specs=VMEM,
            compiler_params=params(),
        )(right, left, later, earlier)
        both = lax.ppermute(both, "window", [(1, 3), (2, 0)])
        sent = [right, left, over, both]
    else:
        sent = [moved(payloads[d - 1], "window", d, around=True) for d in range(1, windows)]

    new_dual_model, new_increment = pl.pallas_call(
        lambda *refs: final_kernel(windows, nvar, levels, tiles, *refs),
        out_shape=[shape(dual_model.shape, f32), shape(increment.shape, f32)],
        in_specs=[VMEM] * (len(sent) + 3),
        out_specs=[VMEM] * 2,
        compiler_params=params(),
    )(*sent, totals, base_dual, base_inc)
    return new_dual_model, new_dual_obs, new_increment


def solution(mesh):
    placed = (
        P("members", None, None, None, "space", "window"),
        P(("members", "window"), None, None, "space", None),
        P(("members", "window"), None, None, "space", None),
        P(("members", "window"), None, None, "space", None),
        P(("members", "window"), None, None, "space", None),
        P(("members", "window"), None, None, "space", None),
        P(),
        P(("members", "window"), None, None),
        P(("members", "window"), None, None),
        P(("members", "window")),
    )
    return jax.shard_map(
        body,
        mesh=mesh,
        in_specs=placed,
        out_specs=(
            P(("members", "window"), None, None, "space", None),
            P(("members", "window"), None, None, "space", None),
            P(("members", "window"), None, None, "space", None),
        ),
        check_vma=False,
    )
```

```python
import jax
import jax.numpy as jnp
from jax import lax
from jax.experimental import pallas as pl
from jax.experimental.pallas import tpu as pltpu
from jax.sharding import PartitionSpec as P

LANES = 128
SUB = 8
HALF = SUB // 2
CODE_MAX = 32766.0
ROUNDER = 12582912.0

diffusion = 0.2
advection = 0.2
coupling_gain = 0.5
keep = 1.0 - 4.0 * diffusion
half_adv = 0.5 * advection

VMEM = pl.BlockSpec(memory_space=pltpu.VMEM)
SMEM = pl.BlockSpec(memory_space=pltpu.SMEM)
ANY = pl.BlockSpec(memory_space=pl.ANY)


def params(mib=24):
    return pltpu.CompilerParams(vmem_limit_bytes=mib * 1024 * 1024)


def lane_index():
    return lax.broadcasted_iota(jnp.int32, (SUB, LANES), 1)


def row_index():
    return lax.broadcasted_iota(jnp.int32, (SUB, LANES), 0)


def tiled(wide):
    short = -wide.shape[1] % LANES
    if short:
        wide = jnp.concatenate([wide, jnp.zeros((wide.shape[0], short), wide.dtype)], 1)
    return [wide[:, i : i + LANES] for i in range(0, wide.shape[1], LANES)]


def place(parts, rolled, lane):
    built = {}
    for key, tiles, first, width, target in parts:
        done = 0
        while done < width:
            a, b = first + done, target + done
            n = min(width - done, LANES - a % LANES, LANES - b % LANES)
            shift = (b - a) % LANES
            name = (key, a // LANES, shift)
            if name not in rolled:
                value = tiles[a // LANES]
                rolled[name] = pltpu.roll(value, shift, 1) if shift else value
            if b % LANES:
                built[b // LANES] = jnp.where(
                    lane >= b % LANES, rolled[name], built[b // LANES]
                )
            else:
                built[b // LANES] = rolled[name]
            done += n
    return [built[i] for i in range(len(built))]


def joined_halves(first, second):
    top = row_index()[:, :1] < HALF
    last = jnp.where(top, pltpu.roll(first, HALF, 0), second)
    start = jnp.where(top, first, pltpu.roll(second, HALF, 0))
    return last, start


def widened(own, near, far, odd, even):
    top = row_index() < HALF
    low, high = jnp.where(even, far, near), jnp.where(even, near, far)
    turned = pltpu.roll(own, HALF, 0)
    low = pltpu.roll(low, HALF, 0) if odd else low
    high = high if odd else pltpu.roll(high, HALF, 0)
    return jnp.where(top, low, turned), jnp.where(top, turned, high)


def row_codes(planes):
    lane = lax.broadcasted_iota(jnp.int32, planes[0][0].shape, 1)
    scales = jnp.zeros(planes[0][0].shape, jnp.float32)
    out = []
    for v, row in enumerate(planes):
        big = jnp.abs(row[0])
        for value in row[1:]:
            big = jnp.maximum(big, jnp.abs(value))
        big = jnp.max(big, axis=1, keepdims=True)
        power = jnp.clip(jnp.ceil(jnp.log2(jnp.maximum(big, 1e-30))), -90.0, 126.0)
        scales = jnp.where(lane == v, power, scales)
        gain = CODE_MAX * jnp.exp2(-power)
        for value in row:
            out.append((value * gain + ROUNDER) - ROUNDER)
    return out, scales


def shorts(value):
    return value.astype(jnp.int32).astype(jnp.int16)


def floats(value):
    return value.astype(jnp.int32).astype(jnp.float32)


def pack_kernel(distances, windows, steps, nvar, levels, part, var_ref, traj_ref, *outs):
    me = lax.axis_index("window")
    lane = lane_index()
    variance = var_ref[...]
    high = variance.astype(jnp.bfloat16).astype(jnp.float32)
    middle = (variance - high).astype(jnp.bfloat16).astype(jnp.float32)
    low = variance - high - middle
    split = high + pltpu.roll(middle, HALF, 0) + pltpu.roll(low, LANES // 2, 1)
    split = split.astype(jnp.bfloat16)

    for n, d in enumerate(distances):
        outs[n][outs[n].shape[0] - 1] = split
        target = lax.rem(me + d, windows)

        def variable(v, carry, n=n, target=target):
            for lev in range(levels):
                pieces = [
                    tiled(traj_ref[target, j, v, lev].astype(jnp.float32)) for j in range(steps)
                ]
                parts = [(j, pieces[j], 0, part, j * part) for j in range(steps)]
                placed = place(parts, {}, lane)
                for t, value in enumerate(placed):
                    outs[n][(v * levels + lev) * len(placed) + t] = value.astype(jnp.bfloat16)
            return carry

        lax.fori_loop(0, nvar, variable, 0, unroll=len(distances) == 1)


def even_place():
    return lax.rem(lax.axis_index("space"), 2) == 0


def level_codes(ref, lev, first=0):
    planes = [
        [ref[0, v, lev, :, t : t + LANES] for t in range(0, ref.shape[-1], LANES)]
        for v in range(first, ref.shape[1])
    ]
    values, scales = row_codes(planes)
    return values + [scales]


def half_code_kernel(*refs):
    sources, (near_ref, far_ref, own_ref) = refs[:-3], refs[-3:]
    even = even_place()

    def pair(i, carry):
        near, far = [], []
        for k, ref in enumerate(sources):
            skip = int(k == len(sources) - 1)
            coded = [level_codes(ref, 2 * i + odd, skip) for odd in range(2)]
            for n, (first, second) in enumerate(zip(*coded)):
                if k == 0:
                    own_ref[i, n] = shorts(jnp.concatenate([first, second], 0))
                last, start = joined_halves(first, second)
                near.append(jnp.where(even, last, start))
                far.append(jnp.where(even, start, last))
            if len(near) % 2:
                near.append(jnp.zeros((SUB, LANES), jnp.float32))
                far.append(jnp.zeros((SUB, LANES), jnp.float32))
        for tiles, ref in ((near, near_ref), (far, far_ref)):
            for n in range(0, len(tiles), 2):
                ref[i, n // 2] = shorts(jnp.concatenate(tiles[n : n + 2], 0))
        return carry

    lax.fori_loop(0, near_ref.shape[0], pair, 0)


def half_tile(ref, i, n):
    whole = floats(ref[i, n // 2])
    return whole[SUB:] if n % 2 else whole[:SUB]


def around_kernel(windows, nvar, levels, *refs):
    pieces, (own_ref, near_ref, far_ref) = refs[:windows], refs[windows : windows + 3]
    outs, total_ref = refs[windows + 3 : -1], refs[-1]
    me = lax.axis_index("window")
    even = even_place()
    total = jnp.zeros((SUB, LANES), jnp.float32)
    for d in range(windows):
        split = pieces[d][pieces[d].shape[0] - 1].astype(jnp.float32)
        here = split + pltpu.roll(split, HALF, 0) + pltpu.roll(split, LANES // 2, 1)
        total = total + jnp.where(lax.rem(me - d + windows, windows) <= me, here, 0.0)
    for v in range(nvar):
        for lev in range(levels):
            one = total[lev : lev + 1, v : v + 1]
            total_ref[v * levels + lev] = jnp.broadcast_to(one, (SUB, LANES))
    for i, out_ref in enumerate(outs):
        for n in range(own_ref.shape[1]):
            own = floats(own_ref[i, n])
            near, far = half_tile(near_ref, i, n), half_tile(far_ref, i, n)
            for odd in range(2):
                halves = widened(own[odd * SUB : (odd + 1) * SUB], near, far, odd, even)
                out_ref[odd, n] = shorts(jnp.concatenate(halves, 0))


def decoded(ref, i, first, nvar, tiles):
    scales = jnp.exp2(half_tile(ref, i, first + nvar * tiles)) * (1.0 / CODE_MAX)
    return [
        [half_tile(ref, i, first + v * tiles + t) * scales[:, v : v + 1] for t in range(tiles)]
        for v in range(nvar)
    ]


def is_quarter(j, v, steps):
    return 0 < j < steps - 1 and not (v == 0 and j + 1 > HALF // 2)


def far_base(steps, nvar, levels):
    base, total = {}, 0
    for j in range(steps):
        for v in range(nvar):
            base[j, v] = total
            total += levels // (4 if is_quarter(j, v, steps) else 2)
    return base, total


def joined_quarters(four):
    slot = row_index() // 2
    last, start = pltpu.roll(four[0], 2, 0), four[0]
    for n in range(1, 4):
        last = jnp.where(slot == n, pltpu.roll(four[n], (2 * n + 2) % SUB, 0), last)
        start = jnp.where(slot == n, pltpu.roll(four[n], 2 * n, 0), start)
    return last, start


def assemble_kernel(windows, steps, nvar, levels, part, *refs):
    pieces = refs[:windows]
    own_ref, near_ref, far_ref, stack_ref = refs[windows + 1 :]
    me = lax.axis_index("window")
    even = even_place()
    lane = lane_index()
    count = stack_ref.shape[1]
    packed_tiles = count // (nvar * levels)
    for d in range(windows):
        source = lax.rem(me - d + windows, windows)
        stack_ref[source] = pieces[d][:count]

    pairs = levels // 2
    base, _ = far_base(steps, nvar, levels)

    def variable(v):
        built = {}
        for lev in range(levels):
            plane = v * levels + lev
            sources = [
                [
                    stack_ref[w, plane * packed_tiles + t].astype(jnp.float32)
                    for t in range(packed_tiles)
                ]
                for w in range(windows)
            ]
            rolled = {}
            for j in range(steps):
                parts = [(w, sources[w], j * part, part, w * part) for w in range(windows)]
                built[j, lev] = place(parts, rolled, lane)
                own_ref[j, plane] = jnp.concatenate(built[j, lev], 1).astype(jnp.bfloat16)
        for j in range(steps):
            for i in range(pairs):
                halves = [joined_halves(a, b) for a, b in zip(built[j, 2 * i], built[j, 2 * i + 1])]
                last, start = (jnp.concatenate([h[k] for h in halves], 1) for k in range(2))
                near_ref[j, v * pairs + i] = jnp.where(even, last, start).astype(jnp.bfloat16)
                if not is_quarter(j, v, steps):
                    far_ref[base[j, v] + i] = jnp.where(even, start, last).astype(jnp.bfloat16)
            if is_quarter(j, v, steps):
                for q in range(levels // 4):
                    four = zip(*[built[j, 4 * q + n] for n in range(4)])
                    ends = [joined_quarters(tiles) for tiles in four]
                    last, start = (jnp.concatenate([e[k] for e in ends], 1) for k in range(2))
                    far_ref[base[j, v] + q] = jnp.where(even, start, last).astype(jnp.bfloat16)

    for v in range(nvar):
        variable(v)


def prepare_factor_kernel(
    steps, nvar, levels, tiles,
    count_ref, noise_ref, coupling_ref, dobs_ref, innov_ref, obs_ref, share_ref, mix_ref,
):
    cuts = [slice(t * LANES, (t + 1) * LANES) for t in range(tiles)]
    for v in range(nvar):
        for u in range(nvar):
            one = coupling_gain * coupling_ref[v : v + 1, u : u + 1]
            mix_ref[v, u] = jnp.broadcast_to(one, (SUB, LANES))
    for lev in range(levels):
        for j in range(steps):
            noise = jnp.full((SUB, LANES), noise_ref[0, j, lev])
            share = jnp.where(j < count_ref[0], 1.0, 0.0) / noise
            share_ref[lev, j] = share
            for t in range(tiles):
                gap = innov_ref[0, j, lev, :, cuts[t]] - noise * dobs_ref[0, j, lev, :, cuts[t]]
                obs_ref[lev, j, t] = gap * share


def prepare_tangent_kernel(nvar, levels, tiles, near_ref, far_ref, inc_ref, first_ref):
    even = even_place()
    blocks = [slice(0, SUB), slice(SUB, 2 * SUB)]
    cuts = [slice(t * LANES, (t + 1) * LANES) for t in range(tiles)]
    offset = -(-(nvar * tiles + 1) // 2) * 2
    for i in range(levels // 2):
        fields = [decoded(ref, i, offset, nvar, tiles) for ref in (near_ref, far_ref)]
        for odd in range(2):
            lev = 2 * i + odd
            for t in range(tiles):
                for v in range(nvar):
                    near, far = (side[v][t] for side in fields)
                    halves = widened(inc_ref[0, v, lev, :, cuts[t]], near, far, odd, even)
                    for b in range(2):
                        first_ref[lev, v, t, blocks[b], :] = halves[b]


def prepare_adjoint_kernel(
    steps, nvar, levels, tiles, count_ref, near_ref, far_ref, dobs_ref, *refs
):
    after_refs, (last_ref, force_ref) = refs[: levels // 2], refs[levels // 2 + 1 :]
    even = even_place()
    blocks = [slice(0, SUB), slice(SUB, 2 * SUB)]
    cuts = [slice(t * LANES, (t + 1) * LANES) for t in range(tiles)]
    seen = [jnp.where(j < count_ref[0], 1.0, 0.0) for j in range(steps)]
    offset = -(-(nvar * tiles + 1) // 2) * 2
    none = [[jnp.zeros((SUB, LANES), jnp.float32)] * tiles]
    for i, after_ref in enumerate(after_refs):
        forces = [
            none + decoded(ref, i, 2 * offset, steps - 1, tiles) for ref in (near_ref, far_ref)
        ]
        for odd in range(2):
            lev = 2 * i + odd
            scales = jnp.exp2(floats(after_ref[odd, nvar * tiles])) * (-1.0 / CODE_MAX)
            for t in range(tiles):
                for v in range(nvar):
                    value = floats(after_ref[odd, v * tiles + t])
                    last_ref[lev, v, t] = value * scales[:, v : v + 1]
                for j in range(steps):
                    near, far = (side[j][t] for side in forces)
                    halves = widened(dobs_ref[0, j, lev, :, cuts[t]], near, far, odd, even)
                    for b in range(2):
                        force_ref[lev, j, t, blocks[b], :] = seen[j] * halves[b]


def from_north(line, lane):
    turned = [pltpu.roll(value, LANES - 1, 1) for value in line] * 2
    return [jnp.where(lane < LANES - 1, turned[t], turned[t + 1]) for t in range(len(line))]


def from_south(line, lane):
    turned = [pltpu.roll(value, 1, 1) for value in line]
    return [jnp.where(lane > 0, turned[t], turned[t - 1]) for t in range(len(line))]


def masked_last(line, lane):
    return line[:-1] + [jnp.where(lane < LANES - 1, line[-1], 0.0)]


def masked_first(line, lane):
    return [jnp.where(lane > 0, line[0], 0.0)] + line[1:]


def walls(spaces):
    row, place_x = row_index(), lax.axis_index("space")
    low = jnp.where((row == HALF) & (place_x == 0), 0.0, 1.0)
    high = jnp.where((row == HALF - 1) & (place_x == spaces - 1), 0.0, 1.0)

    def walled(block, east, west):
        if block == 0:
            return east, [low * value for value in west]
        return [high * value for value in east], west

    return walled


BLOCKS = [slice(SUB, 2 * SUB), slice(2 * SUB, 3 * SUB)]
UPS = [slice(b.start + 1, b.stop + 1) for b in BLOCKS]
DOWNS = [slice(b.start - 1, b.stop - 1) for b in BLOCKS]
MINE = slice(SUB + HALF, 2 * SUB + HALF)


def tangent_kernel(
    spaces, steps, nvar, levels, tiles,
    mix_ref, share_ref, obs_ref, own_ref, near_ref, far_ref, first_ref,
    ndo_ref, ends_ref, x_ref, s_ref,
):
    lane, row = lane_index(), row_index()
    even = even_place()
    top = row < HALF
    walled = walls(spaces)
    pairs = levels // 2
    cuts = [slice(t * LANES, (t + 1) * LANES) for t in range(tiles)]
    base, _ = far_base(steps, nvar, levels)

    for lev in range(levels):
        i, odd = lev // 2, lev % 2
        for j in range(steps):
            for v in range(nvar):
                for t in range(tiles):
                    own = own_ref[j, v * levels + lev, :, cuts[t]].astype(jnp.float32)
                    near = near_ref[j, v * pairs + i, :, cuts[t]].astype(jnp.float32)
                    quarter = is_quarter(j, v, steps)
                    far = far_ref[base[j, v] + lev // (4 if quarter else 2), :, cuts[t]]
                    far = far.astype(jnp.float32)
                    if quarter:
                        slot = 2 * (lev % 4)
                        low_far = pltpu.roll(far, (HALF - 2 - slot) % SUB, 0)
                        high_far = pltpu.roll(far, (HALF - slot) % SUB, 0)
                    else:
                        low_far = pltpu.roll(far, HALF, 0) if odd else far
                        high_far = far if odd else pltpu.roll(far, HALF, 0)
                    low_near = pltpu.roll(near, HALF, 0) if odd else near
                    high_near = near if odd else pltpu.roll(near, HALF, 0)
                    turned = pltpu.roll(own, HALF, 0)
                    low = jnp.where(even, low_far, low_near)
                    high = jnp.where(even, high_near, high_far)
                    x_ref[lev, j, v, t, :SUB, :] = jnp.where(top, low, turned)
                    x_ref[lev, j, v, t, SUB:, :] = jnp.where(top, turned, high)

    def pair(i, outer):
        for odd in range(2):
            for v in range(nvar):
                for t in range(tiles):
                    s_ref[odd, 0, v, t, SUB : 3 * SUB, :] = first_ref[2 * i + odd, v, t]

        def step(j, carry):
            now = lax.rem(j, 2)
            for odd in range(2):
                lev = 2 * i + odd
                for t in range(tiles):
                    image = share_ref[lev, j] * s_ref[odd, now, 0, t, MINE, :]
                    ndo_ref[0, j, lev, :, cuts[t]] = obs_ref[lev, j, t] - image
                for b in range(2):
                    part = slice(b * SUB, (b + 1) * SUB)
                    here, up, down = BLOCKS[b], UPS[b], DOWNS[b]
                    x = [[x_ref[lev, j, u, t, part, :] for t in range(tiles)] for u in range(nvar)]
                    ce = [diffusion - half_adv * value for value in x[0]]
                    cw = [diffusion + half_adv * value for value in x[0]]
                    ce, cw = walled(b, ce, cw)
                    cn = masked_last([diffusion - half_adv * value for value in x[1]], lane)
                    cs = masked_first([diffusion + half_adv * value for value in x[1]], lane)
                    s = [
                        [s_ref[odd, now, u, t, here, :] for t in range(tiles)] for u in range(nvar)
                    ]
                    xs = [[x[u][t] * s[u][t] for t in range(tiles)] for u in range(nvar)]
                    for v in range(nvar):
                        north, south = from_north(s[v], lane), from_south(s[v], lane)
                        for t in range(tiles):
                            fresh = keep * s[v][t] + ce[t] * s_ref[odd, now, v, t, up, :]
                            fresh = fresh + cw[t] * s_ref[odd, now, v, t, down, :]
                            fresh = fresh + cn[t] * north[t] + cs[t] * south[t]
                            for u in range(nvar):
                                fresh = fresh + mix_ref[v, u] * xs[u][t]
                            s_ref[odd, 1 - now, v, t, here, :] = fresh
            return carry

        lax.fori_loop(0, steps, step, 0)
        for odd in range(2):
            for v in range(nvar):
                for t in range(tiles):
                    ends_ref[2 * i + odd, v, t] = s_ref[odd, steps % 2, v, t, MINE, :]
        return outer

    lax.fori_loop(0, pairs, pair, 0)


def adjoint_kernel(
    windows, spaces, steps, nvar, levels, tiles,
    mix_ref, total_ref, x_ref, last_ref, force_ref, ends_ref, inc_ref, rhs_ref, dual_ref,
    ndm_ref, ninc_ref, *rest,
):
    payload_refs = rest[: windows - 1]
    x0_ref, a_ref, q_ref = rest[windows - 1 :]
    me = lax.axis_index("window")
    lane = lane_index()
    walled = walls(spaces)
    pairs = levels // 2
    cuts = [slice(t * LANES, (t + 1) * LANES) for t in range(tiles)]

    def pair(i, outer):
        for odd in range(2):
            lev = 2 * i + odd
            for t in range(tiles):
                for j in range(steps):
                    x0_ref[odd, j, t, SUB : 3 * SUB, :] = x_ref[lev, j, 0, t]
                for v in range(nvar):
                    a_ref[odd, 0, v, t, SUB : 3 * SUB, :] = last_ref[lev, v, t]

        def step(turn, carry):
            now = lax.rem(turn, 2)
            j = steps - 1 - turn
            for odd in range(2):
                lev = 2 * i + odd
                for b in range(2):
                    part = slice(b * SUB, (b + 1) * SUB)
                    here, up, down = BLOCKS[b], UPS[b], DOWNS[b]
                    x = [[x_ref[lev, j, u, t, part, :] for t in range(tiles)] for u in range(nvar)]
                    ce = [diffusion + half_adv * x0_ref[odd, j, t, up, :] for t in range(tiles)]
                    cw = [diffusion - half_adv * x0_ref[odd, j, t, down, :] for t in range(tiles)]
                    ce, cw = walled(b, ce, cw)
                    cn = masked_first([diffusion + half_adv * value for value in x[1]], lane)
                    cs = masked_last([diffusion - half_adv * value for value in x[1]], lane)
                    a = [
                        [a_ref[odd, now, u, t, here, :] for t in range(tiles)] for u in range(nvar)
                    ]
                    for u in range(nvar):
                        north = from_north([cn[t] * a[u][t] for t in range(tiles)], lane)
                        south = from_south([cs[t] * a[u][t] for t in range(tiles)], lane)
                        for t in range(tiles):
                            fresh = keep * a[u][t] + ce[t] * a_ref[odd, now, u, t, up, :]
                            fresh = fresh + cw[t] * a_ref[odd, now, u, t, down, :]
                            fresh = fresh + north[t] + south[t]
                            pull = mix_ref[0, u] * a[0][t]
                            for v in range(1, nvar):
                                pull = pull + mix_ref[v, u] * a[v][t]
                            fresh = fresh + x[u][t] * pull
                            if u == 0:
                                fresh = fresh + force_ref[lev, j, t, part, :]
                            a_ref[odd, 1 - now, u, t, here, :] = fresh
            return carry

        lax.fori_loop(0, steps, step, 0)

        end = steps % 2
        coded = []
        for odd in range(2):
            lev = 2 * i + odd
            back, ahead = [], []
            for v in range(nvar):
                share = total_ref[v * levels + lev]
                tv, gv = [], []
                for t in range(tiles):
                    term = a_ref[odd, end, v, t, MINE, :] - last_ref[lev, v, t, HALF : HALF + SUB, :]
                    given = rhs_ref[0, v, lev, :, cuts[t]] - inc_ref[0, v, lev, :, cuts[t]]
                    given = given + share * term
                    ndm_ref[v, lev, :, cuts[t]] = -(dual_ref[0, v, lev, :, cuts[t]] + term)
                    ninc_ref[v, lev, :, cuts[t]] = given
                    tv.append(term)
                    gv.append(given + ends_ref[lev, v, t])
                back.append(tv)
                ahead.append(gv)
            coded.append((row_codes(back), row_codes(ahead)))
        for kind in range(2):
            first, second = coded[0][kind], coded[1][kind]
            for n, (a, b) in enumerate(zip(first[0] + [first[1]], second[0] + [second[1]])):
                q_ref[kind, i, n] = shorts(jnp.concatenate([a, b], 0))
        return outer

    lax.fori_loop(0, pairs, pair, 0)
    for d in range(1, windows):
        payload_refs[d - 1][...] = q_ref[jnp.where(me + d >= windows, 0, 1)]


def final_kernel(windows, nvar, levels, tiles, *refs):
    pieces, refs = refs[:-5], refs[-5:]
    total_ref, base_dual_ref, base_inc_ref, ndm_ref, ninc_ref = refs
    me = lax.axis_index("window")
    pairs = levels // 2
    cuts = [slice(t * LANES, (t + 1) * LANES) for t in range(tiles)]
    from_later = [d > me for d in range(1, windows)]

    def pair(i, carry):
        tails = [None] * (nvar * tiles)
        heads = [None] * (nvar * tiles)

        def add(sums, n, value):
            sums[n] = value if sums[n] is None else sums[n] + value

        for piece, later in zip(pieces, from_later):
            scales = jnp.exp2(floats(piece[i, nvar * tiles])) * (1.0 / CODE_MAX)
            for v in range(nvar):
                scale = scales[:, v : v + 1]
                for t in range(tiles):
                    n = v * tiles + t
                    value = floats(piece[i, n]) * scale
                    add(tails, n, jnp.where(later, value, 0.0))
                    add(heads, n, jnp.where(later, 0.0, value))
        for v in range(nvar):
            for odd in range(2):
                lev = 2 * i + odd
                share = total_ref[v * levels + lev]
                for t in range(tiles):
                    rows = slice(odd * SUB, (odd + 1) * SUB)
                    tail, head = tails[v * tiles + t][rows], heads[v * tiles + t][rows]
                    ndm_ref[0, v, lev, :, cuts[t]] = base_dual_ref[v, lev, :, cuts[t]] - tail
                    ninc_ref[0, v, lev, :, cuts[t]] = (
                        base_inc_ref[v, lev, :, cuts[t]] + head + share * tail
                    )
        return carry

    lax.fori_loop(0, pairs, pair, 0)


def moved(block, axis, distance, around=False):
    count = lax.axis_size(axis)
    route = [(i, (i + distance) % count) for i in range(count) if around or 0 <= i + distance < count]
    return lax.ppermute(block, axis, route)


def swaps(axis, first):
    route = []
    for i in range(first, lax.axis_size(axis) - 1, 2):
        route += [(i, i + 1), (i + 1, i)]
    return route


def swapped(block, axis, first):
    return lax.ppermute(block, axis, swaps(axis, first))


def body(
    trajectory,
    dual_model,
    increment,
    model_rhs,
    dual_obs,
    innovation,
    coupling,
    error_var,
    obs_var,
    obs_count,
):
    windows, spaces = lax.axis_size("window"), lax.axis_size("space")
    _, steps, nvar, levels, rows, part = trajectory.shape
    columns = dual_model.shape[-1]
    tiles = columns // LANES
    assert trajectory.shape[0] == windows and windows > 1 and rows == SUB and steps == HALF
    assert columns == tiles * LANES == windows * part and levels % 4 == 0
    pairs = levels // 2
    wide = -(-steps * part // LANES) * LANES
    bf16, f32, i16 = jnp.bfloat16, jnp.float32, jnp.int16

    def shape(dims, dtype):
        return jax.ShapeDtypeStruct(dims, dtype)

    block = shape((nvar * levels * wide // LANES + 1, rows, LANES), bf16)
    variances = jnp.pad(error_var[0].T, ((0, SUB - levels), (0, LANES - nvar)))

    def packed(distances):
        return pl.pallas_call(
            lambda *refs: pack_kernel(distances, windows, steps, nvar, levels, part, *refs),
            out_shape=[block] * len(distances),
            in_specs=[VMEM, VMEM],
            out_specs=[VMEM] * len(distances),
            compiler_params=params(),
        )(variances, trajectory)

    order = sorted(range(1, windows), key=lambda d: -d * (windows - d))
    groups = [[d] for d in order] if windows <= 4 else [order]
    blocks = {}
    for group in groups:
        blocks.update(zip(group, packed(group)))
    arrived = {d: moved(blocks[d], "window", d, around=True) for d in order}
    arrived[0] = packed([0])[0]

    payload = shape((pairs, nvar * tiles + 1, 2 * SUB, LANES), i16)

    counts = [nvar, nvar, steps - 1]
    half_tiles = sum(-(-(count * tiles + 1) // 2) for count in counts)
    halves = shape((pairs, half_tiles, 2 * SUB, LANES), i16)
    near, far, dual = pl.pallas_call(
        half_code_kernel,
        out_shape=[halves, halves, payload],
        in_specs=[VMEM] * 3,
        out_specs=[VMEM] * 3,
        compiler_params=params(),
    )(dual_model, increment, dual_obs)
    far, near = swapped(far, "space", 1), swapped(near, "space", 0)

    blocks_here = [arrived[d] for d in range(windows)]
    *after, totals = pl.pallas_call(
        lambda *refs: around_kernel(windows, nvar, levels, *refs),
        out_shape=[shape((2,) + payload.shape[1:], i16)] * pairs
        + [shape((nvar * levels, rows, LANES), f32)],
        in_specs=[VMEM] * (windows + 3),
        out_specs=[VMEM] * (pairs + 1),
        compiler_params=params(),
    )(*blocks_here, dual, near, far)
    after = [moved(piece, "window", -1) for piece in after]

    obs, share, mix = pl.pallas_call(
        lambda *refs: prepare_factor_kernel(steps, nvar, levels, tiles, *refs),
        out_shape=[
            shape((levels, steps, tiles, SUB, LANES), f32),
            shape((levels, steps, SUB, LANES), f32),
            shape((nvar, nvar, SUB, LANES), f32),
        ],
        in_specs=[SMEM] * 2 + [VMEM] * 3,
        out_specs=[VMEM] * 3,
        compiler_params=params(),
    )(obs_count, obs_var, coupling, dual_obs, innovation)

    own, traj_near, traj_far = pl.pallas_call(
        lambda *refs: assemble_kernel(windows, steps, nvar, levels, part, *refs),
        out_shape=[
            shape((steps, nvar * levels, rows, columns), bf16),
            shape((steps, nvar * pairs, rows, columns), bf16),
            shape((far_base(steps, nvar, levels)[1], rows, columns), bf16),
        ],
        in_specs=[VMEM] * windows + [ANY],
        out_specs=[VMEM] * 3,
        scratch_shapes=[pltpu.VMEM((windows, block.shape[0] - 1, rows, LANES), bf16)],
        compiler_params=params(),
    )(*blocks_here, mix)
    traj_near, traj_far = swapped(traj_near, "space", 0), swapped(traj_far, "space", 1)

    first = pl.pallas_call(
        lambda *refs: prepare_tangent_kernel(nvar, levels, tiles, *refs),
        out_shape=shape((levels, nvar, tiles, 2 * SUB, LANES), f32),
        in_specs=[VMEM] * 3,
        out_specs=VMEM,
        compiler_params=params(),
    )(near, far, increment)
    new_dual_obs, ends, wide_traj = pl.pallas_call(
        lambda *refs: tangent_kernel(spaces, steps, nvar, levels, tiles, *refs),
        out_shape=[
            shape(dual_obs.shape, f32),
            shape((levels, nvar, tiles, SUB, LANES), f32),
            shape((levels, steps, nvar, tiles, 2 * SUB, LANES), f32),
        ],
        in_specs=[VMEM] * 7,
        out_specs=[VMEM] * 3,
        scratch_shapes=[pltpu.VMEM((2, 2, nvar, tiles, 4 * SUB, LANES), f32)],
        compiler_params=params(),
    )(mix, share, obs, own, traj_near, traj_far, first)

    last, force = pl.pallas_call(
        lambda *refs: prepare_adjoint_kernel(steps, nvar, levels, tiles, *refs),
        out_shape=[shape((levels, n, tiles, 2 * SUB, LANES), f32) for n in (nvar, steps)],
        in_specs=[SMEM] + [VMEM] * (3 + pairs) + [ANY],
        out_specs=[VMEM] * 2,
        compiler_params=params(),
    )(obs_count, near, far, dual_obs, *after, ends)
    state = shape((nvar, levels, rows, columns), f32)
    base_dual, base_inc, *payloads = pl.pallas_call(
        lambda *refs: adjoint_kernel(windows, spaces, steps, nvar, levels, tiles, *refs),
        out_shape=[state, state] + [payload] * (windows - 1),
        in_specs=[VMEM] * 9,
        out_specs=[VMEM] * (2 + windows - 1),
        scratch_shapes=[
            pltpu.VMEM((2, steps, tiles, 4 * SUB, LANES), f32),
            pltpu.VMEM((2, 2, nvar, tiles, 4 * SUB, LANES), f32),
            pltpu.VMEM((2,) + payload.shape, i16),
        ],
        compiler_params=params(),
    )(mix, totals, wide_traj, last, force, ends, increment, model_rhs, dual_model)
    sent = {d: moved(payloads[d - 1], "window", d, around=True) for d in order}
    sent = [sent[d] for d in range(1, windows)]

    new_dual_model, new_increment = pl.pallas_call(
        lambda *refs: final_kernel(windows, nvar, levels, tiles, *refs),
        out_shape=[shape(dual_model.shape, f32), shape(increment.shape, f32)],
        in_specs=[VMEM] * (len(sent) + 3),
        out_specs=[VMEM] * 2,
        compiler_params=params(),
    )(*sent, totals, base_dual, base_inc)
    return new_dual_model, new_dual_obs, new_increment


def solution(mesh):
    placed = (
        P("members", None, None, None, "space", "window"),
        P(("members", "window"), None, None, "space", None),
        P(("members", "window"), None, None, "space", None),
        P(("members", "window"), None, None, "space", None),
        P(("members", "window"), None, None, "space", None),
        P(("members", "window"), None, None, "space", None),
        P(),
        P(("members", "window"), None, None),
        P(("members", "window"), None, None),
        P(("members", "window")),
    )
    return jax.shard_map(
        body,
        mesh=mesh,
        in_specs=placed,
        out_specs=(
            P(("members", "window"), None, None, "space", None),
            P(("members", "window"), None, None, "space", None),
            P(("members", "window"), None, None, "space", None),
        ),
        check_vma=False,
    )
```

```python
import jax
import jax.numpy as jnp
from jax import lax
from jax.experimental import pallas as pl
from jax.experimental.pallas import tpu as pltpu
from jax.sharding import PartitionSpec as P

LANES = 128
SUB = 8
HALF = SUB // 2
CODE_MAX = 32766.0
ROUNDER = 12582912.0

diffusion = 0.2
advection = 0.2
coupling_gain = 0.5
keep = 1.0 - 4.0 * diffusion
half_adv = 0.5 * advection

VMEM = pl.BlockSpec(memory_space=pltpu.VMEM)
SMEM = pl.BlockSpec(memory_space=pltpu.SMEM)
ANY = pl.BlockSpec(memory_space=pl.ANY)


def params(mib=24):
    return pltpu.CompilerParams(vmem_limit_bytes=mib * 1024 * 1024)


def lane_index():
    return lax.broadcasted_iota(jnp.int32, (SUB, LANES), 1)


def row_index():
    return lax.broadcasted_iota(jnp.int32, (SUB, LANES), 0)


def tiled(wide):
    short = -wide.shape[1] % LANES
    if short:
        wide = jnp.concatenate([wide, jnp.zeros((wide.shape[0], short), wide.dtype)], 1)
    return [wide[:, i : i + LANES] for i in range(0, wide.shape[1], LANES)]


def place(parts, rolled, lane):
    built = {}
    for key, tiles, first, width, target in parts:
        done = 0
        while done < width:
            a, b = first + done, target + done
            n = min(width - done, LANES - a % LANES, LANES - b % LANES)
            shift = (b - a) % LANES
            name = (key, a // LANES, shift)
            if name not in rolled:
                value = tiles[a // LANES]
                rolled[name] = pltpu.roll(value, shift, 1) if shift else value
            if b % LANES:
                built[b // LANES] = jnp.where(
                    lane >= b % LANES, rolled[name], built[b // LANES]
                )
            else:
                built[b // LANES] = rolled[name]
            done += n
    return [built[i] for i in range(len(built))]


def joined_halves(first, second):
    top = row_index()[:, :1] < HALF
    last = jnp.where(top, pltpu.roll(first, HALF, 0), second)
    start = jnp.where(top, first, pltpu.roll(second, HALF, 0))
    return last, start


def widened(own, near, far, odd, even):
    top = row_index() < HALF
    low, high = jnp.where(even, far, near), jnp.where(even, near, far)
    turned = pltpu.roll(own, HALF, 0)
    low = pltpu.roll(low, HALF, 0) if odd else low
    high = high if odd else pltpu.roll(high, HALF, 0)
    return jnp.where(top, low, turned), jnp.where(top, turned, high)


def row_codes(planes):
    lane = lax.broadcasted_iota(jnp.int32, planes[0][0].shape, 1)
    scales = jnp.zeros(planes[0][0].shape, jnp.float32)
    out = []
    for v, row in enumerate(planes):
        big = jnp.abs(row[0])
        for value in row[1:]:
            big = jnp.maximum(big, jnp.abs(value))
        big = jnp.max(big, axis=1, keepdims=True)
        power = jnp.clip(jnp.ceil(jnp.log2(jnp.maximum(big, 1e-30))), -90.0, 126.0)
        scales = jnp.where(lane == v, power, scales)
        gain = CODE_MAX * jnp.exp2(-power)
        for value in row:
            out.append((value * gain + ROUNDER) - ROUNDER)
    return out, scales


def shorts(value):
    return value.astype(jnp.int32).astype(jnp.int16)


def floats(value):
    return value.astype(jnp.int32).astype(jnp.float32)


def pack_kernel(distances, windows, steps, nvar, levels, part, var_ref, traj_ref, *outs):
    me = lax.axis_index("window")
    lane = lane_index()
    variance = var_ref[...]
    high = variance.astype(jnp.bfloat16).astype(jnp.float32)
    middle = (variance - high).astype(jnp.bfloat16).astype(jnp.float32)
    low = variance - high - middle
    split = high + pltpu.roll(middle, HALF, 0) + pltpu.roll(low, LANES // 2, 1)
    split = split.astype(jnp.bfloat16)

    for n, d in enumerate(distances):
        outs[n][outs[n].shape[0] - 1] = split
        target = lax.rem(me + d, windows)

        def variable(v, carry, n=n, target=target):
            for lev in range(levels):
                pieces = [
                    tiled(traj_ref[target, j, v, lev].astype(jnp.float32)) for j in range(steps)
                ]
                parts = [(j, pieces[j], 0, part, j * part) for j in range(steps)]
                placed = place(parts, {}, lane)
                for t, value in enumerate(placed):
                    outs[n][(v * levels + lev) * len(placed) + t] = value.astype(jnp.bfloat16)
            return carry

        lax.fori_loop(0, nvar, variable, 0, unroll=len(distances) == 1)


def even_place():
    return lax.rem(lax.axis_index("space"), 2) == 0


def level_codes(ref, lev, first=0):
    planes = [
        [ref[0, v, lev, :, t : t + LANES] for t in range(0, ref.shape[-1], LANES)]
        for v in range(first, ref.shape[1])
    ]
    values, scales = row_codes(planes)
    return values + [scales]


def own_code_kernel(field_ref, out_ref):
    def pair(i, carry):
        coded = [level_codes(field_ref, 2 * i + odd) for odd in range(2)]
        for n, (first, second) in enumerate(zip(*coded)):
            out_ref[i, n] = shorts(jnp.concatenate([first, second], 0))
        return carry

    lax.fori_loop(0, out_ref.shape[0], pair, 0)


def write_halves(i, groups, near_ref, far_ref):
    even = even_place()
    near, far = [], []
    for coded in groups:
        for first, second in zip(*coded):
            last, start = joined_halves(first, second)
            near.append(jnp.where(even, last, start))
            far.append(jnp.where(even, start, last))
        if len(near) % 2:
            near.append(jnp.zeros((SUB, LANES), jnp.float32))
            far.append(jnp.zeros((SUB, LANES), jnp.float32))
    for tiles, ref in ((near, near_ref), (far, far_ref)):
        for n in range(0, len(tiles), 2):
            ref[i, n // 2] = shorts(jnp.concatenate(tiles[n : n + 2], 0))


def field_half_kernel(inc_ref, dobs_ref, near_ref, far_ref):
    def pair(i, carry):
        groups = [
            [level_codes(ref, 2 * i + odd, skip) for odd in range(2)]
            for ref, skip in ((inc_ref, 0), (dobs_ref, 1))
        ]
        write_halves(i, groups, near_ref, far_ref)
        return carry

    lax.fori_loop(0, near_ref.shape[0], pair, 0)


def dual_half_kernel(windows, nvar, levels, *refs):
    pieces, (coded_ref, near_ref, far_ref, total_ref) = refs[:windows], refs[windows:]
    me = lax.axis_index("window")
    total = jnp.zeros((SUB, LANES), jnp.float32)
    for d in range(windows):
        split = pieces[d][pieces[d].shape[0] - 1].astype(jnp.float32)
        here = split + pltpu.roll(split, HALF, 0) + pltpu.roll(split, LANES // 2, 1)
        total = total + jnp.where(lax.rem(me - d + windows, windows) <= me, here, 0.0)
    for v in range(nvar):
        for lev in range(levels):
            one = total[lev : lev + 1, v : v + 1]
            total_ref[v * levels + lev] = jnp.broadcast_to(one, (SUB, LANES))
    for i in range(levels // 2):
        whole = [floats(coded_ref[i, n]) for n in range(coded_ref.shape[1])]
        groups = [[[tile[:SUB] for tile in whole], [tile[SUB:] for tile in whole]]]
        write_halves(i, groups, near_ref, far_ref)


def half_tile(ref, i, n):
    whole = floats(ref[i, n // 2])
    return whole[SUB:] if n % 2 else whole[:SUB]


def decoded(ref, i, first, nvar, tiles):
    scales = jnp.exp2(half_tile(ref, i, first + nvar * tiles)) * (1.0 / CODE_MAX)
    return [
        [half_tile(ref, i, first + v * tiles + t) * scales[:, v : v + 1] for t in range(tiles)]
        for v in range(nvar)
    ]


def is_quarter(j, v, steps):
    return 0 < j < steps - 1 and not (v == 0 and j + 1 > HALF // 2)


def far_base(steps, nvar, levels):
    base, total = {}, 0
    for j in range(steps):
        for v in range(nvar):
            base[j, v] = total
            total += levels // (4 if is_quarter(j, v, steps) else 2)
    return base, total


def joined_quarters(four):
    slot = row_index() // 2
    last, start = pltpu.roll(four[0], 2, 0), four[0]
    for n in range(1, 4):
        last = jnp.where(slot == n, pltpu.roll(four[n], (2 * n + 2) % SUB, 0), last)
        start = jnp.where(slot == n, pltpu.roll(four[n], 2 * n, 0), start)
    return last, start


def assemble_kernel(windows, steps, nvar, levels, part, *refs):
    pieces, codes_ref = refs[:windows], refs[windows]
    own_ref, near_ref, far_ref, out_ref, stack_ref = refs[windows + 4 :]
    out_ref[...] = codes_ref[...]
    me = lax.axis_index("window")
    even = even_place()
    lane = lane_index()
    count = stack_ref.shape[1]
    packed_tiles = count // (nvar * levels)
    for d in range(windows):
        source = lax.rem(me - d + windows, windows)
        stack_ref[source] = pieces[d][:count]

    pairs = levels // 2
    base, _ = far_base(steps, nvar, levels)

    def variable(v):
        built = {}
        for lev in range(levels):
            plane = v * levels + lev
            sources = [
                [
                    stack_ref[w, plane * packed_tiles + t].astype(jnp.float32)
                    for t in range(packed_tiles)
                ]
                for w in range(windows)
            ]
            rolled = {}
            for j in range(steps):
                parts = [(w, sources[w], j * part, part, w * part) for w in range(windows)]
                built[j, lev] = place(parts, rolled, lane)
                own_ref[j, plane] = jnp.concatenate(built[j, lev], 1).astype(jnp.bfloat16)
        for j in range(steps):
            for i in range(pairs):
                halves = [joined_halves(a, b) for a, b in zip(built[j, 2 * i], built[j, 2 * i + 1])]
                last, start = (jnp.concatenate([h[k] for h in halves], 1) for k in range(2))
                near_ref[j, v * pairs + i] = jnp.where(even, last, start).astype(jnp.bfloat16)
                if not is_quarter(j, v, steps):
                    far_ref[base[j, v] + i] = jnp.where(even, start, last).astype(jnp.bfloat16)
            if is_quarter(j, v, steps):
                for q in range(levels // 4):
                    four = zip(*[built[j, 4 * q + n] for n in range(4)])
                    ends = [joined_quarters(tiles) for tiles in four]
                    last, start = (jnp.concatenate([e[k] for e in ends], 1) for k in range(2))
                    far_ref[base[j, v] + q] = jnp.where(even, start, last).astype(jnp.bfloat16)

    for v in range(nvar):
        variable(v)


def prepare_factor_kernel(
    steps, nvar, levels, tiles,
    count_ref, noise_ref, coupling_ref, dobs_ref, innov_ref, obs_ref, share_ref, mix_ref,
):
    cuts = [slice(t * LANES, (t + 1) * LANES) for t in range(tiles)]
    for v in range(nvar):
        for u in range(nvar):
            one = coupling_gain * coupling_ref[v : v + 1, u : u + 1]
            mix_ref[v, u] = jnp.broadcast_to(one, (SUB, LANES))
    for lev in range(levels):
        for j in range(steps):
            noise = jnp.full((SUB, LANES), noise_ref[0, j, lev])
            share = jnp.where(j < count_ref[0], 1.0, 0.0) / noise
            share_ref[lev, j] = share
            for t in range(tiles):
                gap = innov_ref[0, j, lev, :, cuts[t]] - noise * dobs_ref[0, j, lev, :, cuts[t]]
                obs_ref[lev, j, t] = gap * share


def prepare_tangent_kernel(nvar, levels, tiles, near_ref, far_ref, inc_ref, first_ref):
    even = even_place()
    blocks = [slice(0, SUB), slice(SUB, 2 * SUB)]
    cuts = [slice(t * LANES, (t + 1) * LANES) for t in range(tiles)]
    for i in range(levels // 2):
        fields = [decoded(ref, i, 0, nvar, tiles) for ref in (near_ref, far_ref)]
        for odd in range(2):
            lev = 2 * i + odd
            for t in range(tiles):
                for v in range(nvar):
                    near, far = (side[v][t] for side in fields)
                    halves = widened(inc_ref[0, v, lev, :, cuts[t]], near, far, odd, even)
                    for b in range(2):
                        first_ref[lev, v, t, blocks[b], :] = halves[b]


def prepare_adjoint_kernel(
    steps, nvar, levels, tiles,
    count_ref, near_ref, far_ref, dobs_ref, after_ref, anear_ref, afar_ref, order_ref,
    last_ref, force_ref,
):
    even = even_place()
    blocks = [slice(0, SUB), slice(SUB, 2 * SUB)]
    cuts = [slice(t * LANES, (t + 1) * LANES) for t in range(tiles)]
    seen = [jnp.where(j < count_ref[0], 1.0, 0.0) for j in range(steps)]
    offset = -(-(nvar * tiles + 1) // 2) * 2
    none = [[jnp.zeros((SUB, LANES), jnp.float32)] * tiles]
    for i in range(levels // 2):
        forces = [none + decoded(ref, i, offset, steps - 1, tiles) for ref in (near_ref, far_ref)]
        afters = [decoded(ref, i, 0, nvar, tiles) for ref in (anear_ref, afar_ref)]
        scales = jnp.exp2(floats(after_ref[i, nvar * tiles])) * (1.0 / CODE_MAX)
        for odd in range(2):
            lev = 2 * i + odd
            rows = blocks[odd]
            for t in range(tiles):
                for v in range(nvar):
                    near, far = (side[v][t] for side in afters)
                    own = floats(after_ref[i, v * tiles + t])[rows] * scales[rows, v : v + 1]
                    halves = widened(own, near, far, odd, even)
                    for b in range(2):
                        last_ref[lev, v, t, blocks[b], :] = -halves[b]
                for j in range(steps):
                    near, far = (side[j][t] for side in forces)
                    halves = widened(dobs_ref[0, j, lev, :, cuts[t]], near, far, odd, even)
                    for b in range(2):
                        force_ref[lev, j, t, blocks[b], :] = seen[j] * halves[b]


def from_north(line, lane):
    turned = [pltpu.roll(value, LANES - 1, 1) for value in line] * 2
    return [jnp.where(lane < LANES - 1, turned[t], turned[t + 1]) for t in range(len(line))]


def from_south(line, lane):
    turned = [pltpu.roll(value, 1, 1) for value in line]
    return [jnp.where(lane > 0, turned[t], turned[t - 1]) for t in range(len(line))]


def masked_last(line, lane):
    return line[:-1] + [jnp.where(lane < LANES - 1, line[-1], 0.0)]


def masked_first(line, lane):
    return [jnp.where(lane > 0, line[0], 0.0)] + line[1:]


def walls(spaces):
    row, place_x = row_index(), lax.axis_index("space")
    low = jnp.where((row == HALF) & (place_x == 0), 0.0, 1.0)
    high = jnp.where((row == HALF - 1) & (place_x == spaces - 1), 0.0, 1.0)

    def walled(block, east, west):
        if block == 0:
            return east, [low * value for value in west]
        return [high * value for value in east], west

    return walled


BLOCKS = [slice(SUB, 2 * SUB), slice(2 * SUB, 3 * SUB)]
UPS = [slice(b.start + 1, b.stop + 1) for b in BLOCKS]
DOWNS = [slice(b.start - 1, b.stop - 1) for b in BLOCKS]
MINE = slice(SUB + HALF, 2 * SUB + HALF)


def tangent_kernel(
    spaces, steps, nvar, levels, tiles,
    mix_ref, share_ref, obs_ref, own_ref, near_ref, far_ref, first_ref,
    ndo_ref, ends_ref, x_ref, s_ref,
):
    lane, row = lane_index(), row_index()
    even = even_place()
    top = row < HALF
    walled = walls(spaces)
    pairs = levels // 2
    cuts = [slice(t * LANES, (t + 1) * LANES) for t in range(tiles)]
    base, _ = far_base(steps, nvar, levels)

    for lev in range(levels):
        i, odd = lev // 2, lev % 2
        for j in range(steps):
            for v in range(nvar):
                for t in range(tiles):
                    own = own_ref[j, v * levels + lev, :, cuts[t]].astype(jnp.float32)
                    near = near_ref[j, v * pairs + i, :, cuts[t]].astype(jnp.float32)
                    quarter = is_quarter(j, v, steps)
                    far = far_ref[base[j, v] + lev // (4 if quarter else 2), :, cuts[t]]
                    far = far.astype(jnp.float32)
                    if quarter:
                        slot = 2 * (lev % 4)
                        low_far = pltpu.roll(far, (HALF - 2 - slot) % SUB, 0)
                        high_far = pltpu.roll(far, (HALF - slot) % SUB, 0)
                    else:
                        low_far = pltpu.roll(far, HALF, 0) if odd else far
                        high_far = far if odd else pltpu.roll(far, HALF, 0)
                    low_near = pltpu.roll(near, HALF, 0) if odd else near
                    high_near = near if odd else pltpu.roll(near, HALF, 0)
                    turned = pltpu.roll(own, HALF, 0)
                    low = jnp.where(even, low_far, low_near)
                    high = jnp.where(even, high_near, high_far)
                    x_ref[lev, j, v, t, :SUB, :] = jnp.where(top, low, turned)
                    x_ref[lev, j, v, t, SUB:, :] = jnp.where(top, turned, high)

    def pair(i, outer):
        for odd in range(2):
            for v in range(nvar):
                for t in range(tiles):
                    s_ref[odd, 0, v, t, SUB : 3 * SUB, :] = first_ref[2 * i + odd, v, t]

        def step(j, carry):
            now = lax.rem(j, 2)
            for odd in range(2):
                lev = 2 * i + odd
                for t in range(tiles):
                    image = share_ref[lev, j] * s_ref[odd, now, 0, t, MINE, :]
                    ndo_ref[0, j, lev, :, cuts[t]] = obs_ref[lev, j, t] - image
                for b in range(2):
                    part = slice(b * SUB, (b + 1) * SUB)
                    here, up, down = BLOCKS[b], UPS[b], DOWNS[b]
                    x = [[x_ref[lev, j, u, t, part, :] for t in range(tiles)] for u in range(nvar)]
                    ce = [diffusion - half_adv * value for value in x[0]]
                    cw = [diffusion + half_adv * value for value in x[0]]
                    ce, cw = walled(b, ce, cw)
                    cn = masked_last([diffusion - half_adv * value for value in x[1]], lane)
                    cs = masked_first([diffusion + half_adv * value for value in x[1]], lane)
                    s = [
                        [s_ref[odd, now, u, t, here, :] for t in range(tiles)] for u in range(nvar)
                    ]
                    xs = [[x[u][t] * s[u][t] for t in range(tiles)] for u in range(nvar)]
                    for v in range(nvar):
                        north, south = from_north(s[v], lane), from_south(s[v], lane)
                        for t in range(tiles):
                            fresh = keep * s[v][t] + ce[t] * s_ref[odd, now, v, t, up, :]
                            fresh = fresh + cw[t] * s_ref[odd, now, v, t, down, :]
                            fresh = fresh + cn[t] * north[t] + cs[t] * south[t]
                            for u in range(nvar):
                                fresh = fresh + mix_ref[v, u] * xs[u][t]
                            s_ref[odd, 1 - now, v, t, here, :] = fresh
            return carry

        lax.fori_loop(0, steps, step, 0)
        for odd in range(2):
            for v in range(nvar):
                for t in range(tiles):
                    ends_ref[2 * i + odd, v, t] = s_ref[odd, steps % 2, v, t, MINE, :]
        return outer

    lax.fori_loop(0, pairs, pair, 0)


def adjoint_kernel(
    windows, spaces, steps, nvar, levels, tiles,
    mix_ref, total_ref, x_ref, last_ref, force_ref, ends_ref, inc_ref, rhs_ref, dual_ref,
    ndm_ref, ninc_ref, *rest,
):
    payload_refs = rest[: windows - 1]
    x0_ref, a_ref, q_ref = rest[windows - 1 :]
    me = lax.axis_index("window")
    lane = lane_index()
    walled = walls(spaces)
    pairs = levels // 2
    cuts = [slice(t * LANES, (t + 1) * LANES) for t in range(tiles)]

    def pair(i, outer):
        for odd in range(2):
            lev = 2 * i + odd
            for t in range(tiles):
                for j in range(steps):
                    x0_ref[odd, j, t, SUB : 3 * SUB, :] = x_ref[lev, j, 0, t]
                for v in range(nvar):
                    a_ref[odd, 0, v, t, SUB : 3 * SUB, :] = last_ref[lev, v, t]

        def step(turn, carry):
            now = lax.rem(turn, 2)
            j = steps - 1 - turn
            for odd in range(2):
                lev = 2 * i + odd
                for b in range(2):
                    part = slice(b * SUB, (b + 1) * SUB)
                    here, up, down = BLOCKS[b], UPS[b], DOWNS[b]
                    x = [[x_ref[lev, j, u, t, part, :] for t in range(tiles)] for u in range(nvar)]
                    ce = [diffusion + half_adv * x0_ref[odd, j, t, up, :] for t in range(tiles)]
                    cw = [diffusion - half_adv * x0_ref[odd, j, t, down, :] for t in range(tiles)]
                    ce, cw = walled(b, ce, cw)
                    cn = masked_first([diffusion + half_adv * value for value in x[1]], lane)
                    cs = masked_last([diffusion - half_adv * value for value in x[1]], lane)
                    a = [
                        [a_ref[odd, now, u, t, here, :] for t in range(tiles)] for u in range(nvar)
                    ]
                    for u in range(nvar):
                        north = from_north([cn[t] * a[u][t] for t in range(tiles)], lane)
                        south = from_south([cs[t] * a[u][t] for t in range(tiles)], lane)
                        for t in range(tiles):
                            fresh = keep * a[u][t] + ce[t] * a_ref[odd, now, u, t, up, :]
                            fresh = fresh + cw[t] * a_ref[odd, now, u, t, down, :]
                            fresh = fresh + north[t] + south[t]
                            pull = mix_ref[0, u] * a[0][t]
                            for v in range(1, nvar):
                                pull = pull + mix_ref[v, u] * a[v][t]
                            fresh = fresh + x[u][t] * pull
                            if u == 0:
                                fresh = fresh + force_ref[lev, j, t, part, :]
                            a_ref[odd, 1 - now, u, t, here, :] = fresh
            return carry

        lax.fori_loop(0, steps, step, 0)

        end = steps % 2
        coded = []
        for odd in range(2):
            lev = 2 * i + odd
            back, ahead = [], []
            for v in range(nvar):
                share = total_ref[v * levels + lev]
                tv, gv = [], []
                for t in range(tiles):
                    term = a_ref[odd, end, v, t, MINE, :] - last_ref[lev, v, t, HALF : HALF + SUB, :]
                    given = rhs_ref[0, v, lev, :, cuts[t]] - inc_ref[0, v, lev, :, cuts[t]]
                    given = given + share * term
                    ndm_ref[v, lev, :, cuts[t]] = -(dual_ref[0, v, lev, :, cuts[t]] + term)
                    ninc_ref[v, lev, :, cuts[t]] = given
                    tv.append(term)
                    gv.append(given + ends_ref[lev, v, t])
                back.append(tv)
                ahead.append(gv)
            coded.append((row_codes(back), row_codes(ahead)))
        for kind in range(2):
            first, second = coded[0][kind], coded[1][kind]
            for n, (a, b) in enumerate(zip(first[0] + [first[1]], second[0] + [second[1]])):
                q_ref[kind, i, n] = shorts(jnp.concatenate([a, b], 0))
        return outer

    lax.fori_loop(0, pairs, pair, 0)
    for d in range(1, windows):
        payload_refs[d - 1][...] = q_ref[jnp.where(me + d >= windows, 0, 1)]


def final_kernel(windows, nvar, levels, tiles, *refs):
    pieces, refs = refs[:-5], refs[-5:]
    total_ref, base_dual_ref, base_inc_ref, ndm_ref, ninc_ref = refs
    me = lax.axis_index("window")
    pairs = levels // 2
    cuts = [slice(t * LANES, (t + 1) * LANES) for t in range(tiles)]
    from_later = [d > me for d in range(1, windows)]

    def pair(i, carry):
        tails = [None] * (nvar * tiles)
        heads = [None] * (nvar * tiles)

        def add(sums, n, value):
            sums[n] = value if sums[n] is None else sums[n] + value

        for piece, later in zip(pieces, from_later):
            scales = jnp.exp2(floats(piece[i, nvar * tiles])) * (1.0 / CODE_MAX)
            for v in range(nvar):
                scale = scales[:, v : v + 1]
                for t in range(tiles):
                    n = v * tiles + t
                    value = floats(piece[i, n]) * scale
                    add(tails, n, jnp.where(later, value, 0.0))
                    add(heads, n, jnp.where(later, 0.0, value))
        for v in range(nvar):
            for odd in range(2):
                lev = 2 * i + odd
                share = total_ref[v * levels + lev]
                for t in range(tiles):
                    rows = slice(odd * SUB, (odd + 1) * SUB)
                    tail, head = tails[v * tiles + t][rows], heads[v * tiles + t][rows]
                    ndm_ref[0, v, lev, :, cuts[t]] = base_dual_ref[v, lev, :, cuts[t]] - tail
                    ninc_ref[0, v, lev, :, cuts[t]] = (
                        base_inc_ref[v, lev, :, cuts[t]] + head + share * tail
                    )
        return carry

    lax.fori_loop(0, pairs, pair, 0)


def moved(block, axis, distance, around=False):
    count = lax.axis_size(axis)
    route = [(i, (i + distance) % count) for i in range(count) if around or 0 <= i + distance < count]
    return lax.ppermute(block, axis, route)


def swaps(axis, first):
    route = []
    for i in range(first, lax.axis_size(axis) - 1, 2):
        route += [(i, i + 1), (i + 1, i)]
    return route


def swapped(block, axis, first):
    return lax.ppermute(block, axis, swaps(axis, first))


def body(
    trajectory,
    dual_model,
    increment,
    model_rhs,
    dual_obs,
    innovation,
    coupling,
    error_var,
    obs_var,
    obs_count,
):
    windows, spaces = lax.axis_size("window"), lax.axis_size("space")
    _, steps, nvar, levels, rows, part = trajectory.shape
    columns = dual_model.shape[-1]
    tiles = columns // LANES
    assert trajectory.shape[0] == windows and windows > 1 and rows == SUB and steps == HALF
    assert columns == tiles * LANES == windows * part and levels % 4 == 0
    pairs = levels // 2
    wide = -(-steps * part // LANES) * LANES
    bf16, f32, i16 = jnp.bfloat16, jnp.float32, jnp.int16

    def shape(dims, dtype):
        return jax.ShapeDtypeStruct(dims, dtype)

    block = shape((nvar * levels * wide // LANES + 1, rows, LANES), bf16)
    variances = jnp.pad(error_var[0].T, ((0, SUB - levels), (0, LANES - nvar)))

    def packed(distances):
        return pl.pallas_call(
            lambda *refs: pack_kernel(distances, windows, steps, nvar, levels, part, *refs),
            out_shape=[block] * len(distances),
            in_specs=[VMEM, VMEM],
            out_specs=[VMEM] * len(distances),
            compiler_params=params(),
        )(variances, trajectory)

    order = sorted(range(1, windows), key=lambda d: -d * (windows - d))
    groups = [[d] for d in order] if windows <= 4 else [order]
    blocks = {}
    for group in groups:
        blocks.update(zip(group, packed(group)))
    arrived = {d: moved(blocks[d], "window", d, around=True) for d in order}
    arrived[0] = packed([0])[0]

    payload = shape((pairs, nvar * tiles + 1, 2 * SUB, LANES), i16)

    def half_shape(*counts):
        total = sum(-(-(count * tiles + 1) // 2) for count in counts)
        return shape((pairs, total, 2 * SUB, LANES), i16)

    near, far = pl.pallas_call(
        field_half_kernel,
        out_shape=[half_shape(nvar, steps - 1)] * 2,
        in_specs=[VMEM] * 2,
        out_specs=[VMEM] * 2,
        compiler_params=params(),
    )(increment, dual_obs)
    far, near = swapped(far, "space", 1), swapped(near, "space", 0)
    dual = pl.pallas_call(
        own_code_kernel,
        out_shape=payload,
        in_specs=[VMEM],
        out_specs=VMEM,
        compiler_params=params(),
    )(dual_model)
    blocks_here = [arrived[d] for d in range(windows)]

    obs, share, mix = pl.pallas_call(
        lambda *refs: prepare_factor_kernel(steps, nvar, levels, tiles, *refs),
        out_shape=[
            shape((levels, steps, tiles, SUB, LANES), f32),
            shape((levels, steps, SUB, LANES), f32),
            shape((nvar, nvar, SUB, LANES), f32),
        ],
        in_specs=[SMEM] * 2 + [VMEM] * 3,
        out_specs=[VMEM] * 3,
        compiler_params=params(),
    )(obs_count, obs_var, coupling, dual_obs, innovation)

    own, traj_near, traj_far, dual = pl.pallas_call(
        lambda *refs: assemble_kernel(windows, steps, nvar, levels, part, *refs),
        out_shape=[
            shape((steps, nvar * levels, rows, columns), bf16),
            shape((steps, nvar * pairs, rows, columns), bf16),
            shape((far_base(steps, nvar, levels)[1], rows, columns), bf16),
            payload,
        ],
        in_specs=[VMEM] * (windows + 1) + [ANY] * 3,
        out_specs=[VMEM] * 4,
        scratch_shapes=[pltpu.VMEM((windows, block.shape[0] - 1, rows, LANES), bf16)],
        compiler_params=params(),
    )(*blocks_here, dual, mix, near, far)
    traj_near, traj_far = swapped(traj_near, "space", 0), swapped(traj_far, "space", 1)
    after = moved(dual, "window", -1)
    after_near, after_far, totals = pl.pallas_call(
        lambda *refs: dual_half_kernel(windows, nvar, levels, *refs),
        out_shape=[half_shape(nvar)] * 2 + [shape((nvar * levels, rows, LANES), f32)],
        in_specs=[VMEM] * (windows + 1),
        out_specs=[VMEM] * 3,
        compiler_params=params(),
    )(*blocks_here, after)
    after_near, after_far = swapped(after_near, "space", 0), swapped(after_far, "space", 1)

    first = pl.pallas_call(
        lambda *refs: prepare_tangent_kernel(nvar, levels, tiles, *refs),
        out_shape=shape((levels, nvar, tiles, 2 * SUB, LANES), f32),
        in_specs=[VMEM] * 3,
        out_specs=VMEM,
        compiler_params=params(),
    )(near, far, increment)
    new_dual_obs, ends, wide_traj = pl.pallas_call(
        lambda *refs: tangent_kernel(spaces, steps, nvar, levels, tiles, *refs),
        out_shape=[
            shape(dual_obs.shape, f32),
            shape((levels, nvar, tiles, SUB, LANES), f32),
            shape((levels, steps, nvar, tiles, 2 * SUB, LANES), f32),
        ],
        in_specs=[VMEM] * 7,
        out_specs=[VMEM] * 3,
        scratch_shapes=[pltpu.VMEM((2, 2, nvar, tiles, 4 * SUB, LANES), f32)],
        compiler_params=params(),
    )(mix, share, obs, own, traj_near, traj_far, first)

    last, force = pl.pallas_call(
        lambda *refs: prepare_adjoint_kernel(steps, nvar, levels, tiles, *refs),
        out_shape=[shape((levels, n, tiles, 2 * SUB, LANES), f32) for n in (nvar, steps)],
        in_specs=[SMEM] + [VMEM] * 6 + [ANY],
        out_specs=[VMEM] * 2,
        compiler_params=params(),
    )(obs_count, near, far, dual_obs, after, after_near, after_far, ends)
    state = shape((nvar, levels, rows, columns), f32)
    base_dual, base_inc, *payloads = pl.pallas_call(
        lambda *refs: adjoint_kernel(windows, spaces, steps, nvar, levels, tiles, *refs),
        out_shape=[state, state] + [payload] * (windows - 1),
        in_specs=[VMEM] * 9,
        out_specs=[VMEM] * (2 + windows - 1),
        scratch_shapes=[
            pltpu.VMEM((2, steps, tiles, 4 * SUB, LANES), f32),
            pltpu.VMEM((2, 2, nvar, tiles, 4 * SUB, LANES), f32),
            pltpu.VMEM((2,) + payload.shape, i16),
        ],
        compiler_params=params(),
    )(mix, totals, wide_traj, last, force, ends, increment, model_rhs, dual_model)
    sent = {d: moved(payloads[d - 1], "window", d, around=True) for d in order}
    sent = [sent[d] for d in range(1, windows)]

    new_dual_model, new_increment = pl.pallas_call(
        lambda *refs: final_kernel(windows, nvar, levels, tiles, *refs),
        out_shape=[shape(dual_model.shape, f32), shape(increment.shape, f32)],
        in_specs=[VMEM] * (len(sent) + 3),
        out_specs=[VMEM] * 2,
        compiler_params=params(),
    )(*sent, totals, base_dual, base_inc)
    return new_dual_model, new_dual_obs, new_increment


def solution(mesh):
    placed = (
        P("members", None, None, None, "space", "window"),
        P(("members", "window"), None, None, "space", None),
        P(("members", "window"), None, None, "space", None),
        P(("members", "window"), None, None, "space", None),
        P(("members", "window"), None, None, "space", None),
        P(("members", "window"), None, None, "space", None),
        P(),
        P(("members", "window"), None, None),
        P(("members", "window"), None, None),
        P(("members", "window")),
    )
    return jax.shard_map(
        body,
        mesh=mesh,
        in_specs=placed,
        out_specs=(
            P(("members", "window"), None, None, "space", None),
            P(("members", "window"), None, None, "space", None),
            P(("members", "window"), None, None, "space", None),
        ),
        check_vma=False,
    )
```

```python
import jax
import jax.numpy as jnp
from jax import lax
from jax.experimental import pallas as pl
from jax.experimental.pallas import tpu as pltpu
from jax.sharding import PartitionSpec as P

LANES = 128
SUB = 8
HALF = SUB // 2
CODE_MAX = 32766.0
ROUNDER = 12582912.0

diffusion = 0.2
advection = 0.2
coupling_gain = 0.5
keep = 1.0 - 4.0 * diffusion
half_adv = 0.5 * advection

VMEM = pl.BlockSpec(memory_space=pltpu.VMEM)
SMEM = pl.BlockSpec(memory_space=pltpu.SMEM)
ANY = pl.BlockSpec(memory_space=pl.ANY)


def params(mib=24):
    return pltpu.CompilerParams(vmem_limit_bytes=mib * 1024 * 1024)


def lane_index():
    return lax.broadcasted_iota(jnp.int32, (SUB, LANES), 1)


def row_index():
    return lax.broadcasted_iota(jnp.int32, (SUB, LANES), 0)


def tiled(wide):
    short = -wide.shape[1] % LANES
    if short:
        wide = jnp.concatenate([wide, jnp.zeros((wide.shape[0], short), wide.dtype)], 1)
    return [wide[:, i : i + LANES] for i in range(0, wide.shape[1], LANES)]


def place(parts, rolled, lane):
    built = {}
    for key, tiles, first, width, target in parts:
        done = 0
        while done < width:
            a, b = first + done, target + done
            n = min(width - done, LANES - a % LANES, LANES - b % LANES)
            shift = (b - a) % LANES
            name = (key, a // LANES, shift)
            if name not in rolled:
                value = tiles[a // LANES]
                rolled[name] = pltpu.roll(value, shift, 1) if shift else value
            if b % LANES:
                built[b // LANES] = jnp.where(
                    lane >= b % LANES, rolled[name], built[b // LANES]
                )
            else:
                built[b // LANES] = rolled[name]
            done += n
    return [built[i] for i in range(len(built))]


def joined_halves(first, second):
    top = row_index()[:, :1] < HALF
    last = jnp.where(top, pltpu.roll(first, HALF, 0), second)
    start = jnp.where(top, first, pltpu.roll(second, HALF, 0))
    return last, start


def widened(own, near, far, odd, even):
    top = row_index() < HALF
    low, high = jnp.where(even, far, near), jnp.where(even, near, far)
    turned = pltpu.roll(own, HALF, 0)
    low = pltpu.roll(low, HALF, 0) if odd else low
    high = high if odd else pltpu.roll(high, HALF, 0)
    return jnp.where(top, low, turned), jnp.where(top, turned, high)


def row_codes(planes):
    lane = lax.broadcasted_iota(jnp.int32, planes[0][0].shape, 1)
    scales = jnp.zeros(planes[0][0].shape, jnp.float32)
    out = []
    for v, row in enumerate(planes):
        big = jnp.abs(row[0])
        for value in row[1:]:
            big = jnp.maximum(big, jnp.abs(value))
        big = jnp.max(big, axis=1, keepdims=True)
        power = jnp.clip(jnp.ceil(jnp.log2(jnp.maximum(big, 1e-30))), -90.0, 126.0)
        scales = jnp.where(lane == v, power, scales)
        gain = CODE_MAX * jnp.exp2(-power)
        for value in row:
            out.append((value * gain + ROUNDER) - ROUNDER)
    return out, scales


def shorts(value):
    return value.astype(jnp.int32).astype(jnp.int16)


def floats(value):
    return value.astype(jnp.int32).astype(jnp.float32)


def pack_kernel(distances, windows, steps, nvar, levels, part, var_ref, traj_ref, *outs):
    me = lax.axis_index("window")
    lane = lane_index()
    variance = var_ref[...]
    high = variance.astype(jnp.bfloat16).astype(jnp.float32)
    middle = (variance - high).astype(jnp.bfloat16).astype(jnp.float32)
    low = variance - high - middle
    split = high + pltpu.roll(middle, HALF, 0) + pltpu.roll(low, LANES // 2, 1)
    split = split.astype(jnp.bfloat16)

    for n, d in enumerate(distances):
        outs[n][outs[n].shape[0] - 1] = split
        target = lax.rem(me + d, windows)

        def variable(v, carry, n=n, target=target):
            for lev in range(levels):
                pieces = [
                    tiled(traj_ref[target, j, v, lev].astype(jnp.float32)) for j in range(steps)
                ]
                parts = [(j, pieces[j], 0, part, j * part) for j in range(steps)]
                placed = place(parts, {}, lane)
                for t, value in enumerate(placed):
                    outs[n][(v * levels + lev) * len(placed) + t] = value.astype(jnp.bfloat16)
            return carry

        lax.fori_loop(0, nvar, variable, 0, unroll=len(distances) == 1)


def even_place():
    return lax.rem(lax.axis_index("space"), 2) == 0


def level_codes(ref, lev, first=0):
    planes = [
        [ref[0, v, lev, :, t : t + LANES] for t in range(0, ref.shape[-1], LANES)]
        for v in range(first, ref.shape[1])
    ]
    values, scales = row_codes(planes)
    return values + [scales]


def half_code_kernel(*refs):
    sources, (near_ref, far_ref, own_ref) = refs[:-3], refs[-3:]
    even = even_place()

    def pair(i, carry):
        near, far = [], []
        for k, ref in enumerate(sources):
            skip = int(k == len(sources) - 1)
            coded = [level_codes(ref, 2 * i + odd, skip) for odd in range(2)]
            for n, (first, second) in enumerate(zip(*coded)):
                if k == 0:
                    own_ref[i, n] = shorts(jnp.concatenate([first, second], 0))
                last, start = joined_halves(first, second)
                near.append(jnp.where(even, last, start))
                far.append(jnp.where(even, start, last))
            if len(near) % 2:
                near.append(jnp.zeros((SUB, LANES), jnp.float32))
                far.append(jnp.zeros((SUB, LANES), jnp.float32))
        for tiles, ref in ((near, near_ref), (far, far_ref)):
            for n in range(0, len(tiles), 2):
                ref[i, n // 2] = shorts(jnp.concatenate(tiles[n : n + 2], 0))
        return carry

    lax.fori_loop(0, near_ref.shape[0], pair, 0)


def half_tile(ref, i, n):
    whole = floats(ref[i, n // 2])
    return whole[SUB:] if n % 2 else whole[:SUB]


def around_kernel(windows, nvar, levels, *refs):
    pieces, (own_ref, near_ref, far_ref) = refs[:windows], refs[windows : windows + 3]
    outs, total_ref = refs[windows + 3 : -1], refs[-1]
    me = lax.axis_index("window")
    even = even_place()
    total = jnp.zeros((SUB, LANES), jnp.float32)
    for d in range(windows):
        split = pieces[d][pieces[d].shape[0] - 1].astype(jnp.float32)
        here = split + pltpu.roll(split, HALF, 0) + pltpu.roll(split, LANES // 2, 1)
        total = total + jnp.where(lax.rem(me - d + windows, windows) <= me, here, 0.0)
    for v in range(nvar):
        for lev in range(levels):
            one = total[lev : lev + 1, v : v + 1]
            total_ref[v * levels + lev] = jnp.broadcast_to(one, (SUB, LANES))
    for i, out_ref in enumerate(outs):
        for n in range(own_ref.shape[1]):
            own = floats(own_ref[i, n])
            near, far = half_tile(near_ref, i, n), half_tile(far_ref, i, n)
            for odd in range(2):
                halves = widened(own[odd * SUB : (odd + 1) * SUB], near, far, odd, even)
                out_ref[odd, n] = shorts(jnp.concatenate(halves, 0))


def decoded(ref, i, first, nvar, tiles):
    scales = jnp.exp2(half_tile(ref, i, first + nvar * tiles)) * (1.0 / CODE_MAX)
    return [
        [half_tile(ref, i, first + v * tiles + t) * scales[:, v : v + 1] for t in range(tiles)]
        for v in range(nvar)
    ]


def is_quarter(j, v, steps):
    return 0 < j < steps - 1 and not (v == 0 and j + 1 > HALF // 2)


def far_base(steps, nvar, levels):
    base, total = {}, 0
    for j in range(steps):
        for v in range(nvar):
            base[j, v] = total
            total += levels // (4 if is_quarter(j, v, steps) else 2)
    return base, total


def joined_quarters(four):
    slot = row_index() // 2
    last, start = pltpu.roll(four[0], 2, 0), four[0]
    for n in range(1, 4):
        last = jnp.where(slot == n, pltpu.roll(four[n], (2 * n + 2) % SUB, 0), last)
        start = jnp.where(slot == n, pltpu.roll(four[n], 2 * n, 0), start)
    return last, start


def assemble_kernel(windows, steps, nvar, levels, part, *refs):
    pieces = refs[:windows]
    own_ref, near_ref, far_ref, stack_ref = refs[windows + 1 :]
    me = lax.axis_index("window")
    even = even_place()
    lane = lane_index()
    count = stack_ref.shape[1]
    packed_tiles = count // (nvar * levels)
    for d in range(windows):
        source = lax.rem(me - d + windows, windows)
        stack_ref[source] = pieces[d][:count]

    pairs = levels // 2
    base, _ = far_base(steps, nvar, levels)

    def variable(v):
        built = {}
        for lev in range(levels):
            plane = v * levels + lev
            sources = [
                [
                    stack_ref[w, plane * packed_tiles + t].astype(jnp.float32)
                    for t in range(packed_tiles)
                ]
                for w in range(windows)
            ]
            rolled = {}
            for j in range(steps):
                parts = [(w, sources[w], j * part, part, w * part) for w in range(windows)]
                built[j, lev] = place(parts, rolled, lane)
                own_ref[j, plane] = jnp.concatenate(built[j, lev], 1).astype(jnp.bfloat16)
        for j in range(steps):
            for i in range(pairs):
                halves = [joined_halves(a, b) for a, b in zip(built[j, 2 * i], built[j, 2 * i + 1])]
                last, start = (jnp.concatenate([h[k] for h in halves], 1) for k in range(2))
                near_ref[j, v * pairs + i] = jnp.where(even, last, start).astype(jnp.bfloat16)
                if not is_quarter(j, v, steps):
                    far_ref[base[j, v] + i] = jnp.where(even, start, last).astype(jnp.bfloat16)
            if is_quarter(j, v, steps):
                for q in range(levels // 4):
                    four = zip(*[built[j, 4 * q + n] for n in range(4)])
                    ends = [joined_quarters(tiles) for tiles in four]
                    last, start = (jnp.concatenate([e[k] for e in ends], 1) for k in range(2))
                    far_ref[base[j, v] + q] = jnp.where(even, start, last).astype(jnp.bfloat16)

    for v in range(nvar):
        variable(v)


def prepare_factor_kernel(
    steps, nvar, levels, tiles,
    count_ref, noise_ref, coupling_ref, dobs_ref, innov_ref, obs_ref, share_ref, mix_ref,
):
    cuts = [slice(t * LANES, (t + 1) * LANES) for t in range(tiles)]
    for v in range(nvar):
        for u in range(nvar):
            one = coupling_gain * coupling_ref[v : v + 1, u : u + 1]
            mix_ref[v, u] = jnp.broadcast_to(one, (SUB, LANES))
    for lev in range(levels):
        for j in range(steps):
            noise = jnp.full((SUB, LANES), noise_ref[0, j, lev])
            share = jnp.where(j < count_ref[0], 1.0, 0.0) / noise
            share_ref[lev, j] = share
            for t in range(tiles):
                gap = innov_ref[0, j, lev, :, cuts[t]] - noise * dobs_ref[0, j, lev, :, cuts[t]]
                obs_ref[lev, j, t] = gap * share


def prepare_tangent_kernel(nvar, levels, tiles, near_ref, far_ref, inc_ref, first_ref):
    even = even_place()
    blocks = [slice(0, SUB), slice(SUB, 2 * SUB)]
    cuts = [slice(t * LANES, (t + 1) * LANES) for t in range(tiles)]
    offset = -(-(nvar * tiles + 1) // 2) * 2
    for i in range(levels // 2):
        fields = [decoded(ref, i, offset, nvar, tiles) for ref in (near_ref, far_ref)]
        for odd in range(2):
            lev = 2 * i + odd
            for t in range(tiles):
                for v in range(nvar):
                    near, far = (side[v][t] for side in fields)
                    halves = widened(inc_ref[0, v, lev, :, cuts[t]], near, far, odd, even)
                    for b in range(2):
                        first_ref[lev, v, t, blocks[b], :] = halves[b]


def prepare_adjoint_kernel(
    i, steps, nvar, tiles, count_ref, near_ref, far_ref, dobs_ref, after_ref, *refs
):
    _, last_ref, force_ref = refs
    even = even_place()
    blocks = [slice(0, SUB), slice(SUB, 2 * SUB)]
    cuts = [slice(t * LANES, (t + 1) * LANES) for t in range(tiles)]
    seen = [jnp.where(j < count_ref[0], 1.0, 0.0) for j in range(steps)]
    offset = -(-(nvar * tiles + 1) // 2) * 2
    none = [[jnp.zeros((SUB, LANES), jnp.float32)] * tiles]
    forces = [none + decoded(ref, i, 2 * offset, steps - 1, tiles) for ref in (near_ref, far_ref)]
    for odd in range(2):
        scales = jnp.exp2(floats(after_ref[odd, nvar * tiles])) * (-1.0 / CODE_MAX)
        for t in range(tiles):
            for v in range(nvar):
                value = floats(after_ref[odd, v * tiles + t])
                last_ref[odd, v, t] = value * scales[:, v : v + 1]
            for j in range(steps):
                near, far = (side[j][t] for side in forces)
                halves = widened(dobs_ref[0, j, 2 * i + odd, :, cuts[t]], near, far, odd, even)
                for b in range(2):
                    force_ref[odd, j, t, blocks[b], :] = seen[j] * halves[b]


def from_north(line, lane):
    turned = [pltpu.roll(value, LANES - 1, 1) for value in line] * 2
    return [jnp.where(lane < LANES - 1, turned[t], turned[t + 1]) for t in range(len(line))]


def from_south(line, lane):
    turned = [pltpu.roll(value, 1, 1) for value in line]
    return [jnp.where(lane > 0, turned[t], turned[t - 1]) for t in range(len(line))]


def masked_last(line, lane):
    return line[:-1] + [jnp.where(lane < LANES - 1, line[-1], 0.0)]


def masked_first(line, lane):
    return [jnp.where(lane > 0, line[0], 0.0)] + line[1:]


def walls(spaces):
    row, place_x = row_index(), lax.axis_index("space")
    low = jnp.where((row == HALF) & (place_x == 0), 0.0, 1.0)
    high = jnp.where((row == HALF - 1) & (place_x == spaces - 1), 0.0, 1.0)

    def walled(block, east, west):
        if block == 0:
            return east, [low * value for value in west]
        return [high * value for value in east], west

    return walled


BLOCKS = [slice(SUB, 2 * SUB), slice(2 * SUB, 3 * SUB)]
UPS = [slice(b.start + 1, b.stop + 1) for b in BLOCKS]
DOWNS = [slice(b.start - 1, b.stop - 1) for b in BLOCKS]
MINE = slice(SUB + HALF, 2 * SUB + HALF)


def tangent_kernel(
    spaces, steps, nvar, levels, tiles,
    mix_ref, share_ref, obs_ref, own_ref, near_ref, far_ref, first_ref,
    ndo_ref, ends_ref, x_ref, s_ref,
):
    lane, row = lane_index(), row_index()
    even = even_place()
    top = row < HALF
    walled = walls(spaces)
    pairs = levels // 2
    cuts = [slice(t * LANES, (t + 1) * LANES) for t in range(tiles)]
    base, _ = far_base(steps, nvar, levels)

    for lev in range(levels):
        i, odd = lev // 2, lev % 2
        for j in range(steps):
            for v in range(nvar):
                for t in range(tiles):
                    own = own_ref[j, v * levels + lev, :, cuts[t]].astype(jnp.float32)
                    near = near_ref[j, v * pairs + i, :, cuts[t]].astype(jnp.float32)
                    quarter = is_quarter(j, v, steps)
                    far = far_ref[base[j, v] + lev // (4 if quarter else 2), :, cuts[t]]
                    far = far.astype(jnp.float32)
                    if quarter:
                        slot = 2 * (lev % 4)
                        low_far = pltpu.roll(far, (HALF - 2 - slot) % SUB, 0)
                        high_far = pltpu.roll(far, (HALF - slot) % SUB, 0)
                    else:
                        low_far = pltpu.roll(far, HALF, 0) if odd else far
                        high_far = far if odd else pltpu.roll(far, HALF, 0)
                    low_near = pltpu.roll(near, HALF, 0) if odd else near
                    high_near = near if odd else pltpu.roll(near, HALF, 0)
                    turned = pltpu.roll(own, HALF, 0)
                    low = jnp.where(even, low_far, low_near)
                    high = jnp.where(even, high_near, high_far)
                    x_ref[lev, j, v, t, :SUB, :] = jnp.where(top, low, turned)
                    x_ref[lev, j, v, t, SUB:, :] = jnp.where(top, turned, high)

    def pair(i, outer):
        for odd in range(2):
            for v in range(nvar):
                for t in range(tiles):
                    s_ref[odd, 0, v, t, SUB : 3 * SUB, :] = first_ref[2 * i + odd, v, t]

        def step(j, carry):
            now = lax.rem(j, 2)
            for odd in range(2):
                lev = 2 * i + odd
                for t in range(tiles):
                    image = share_ref[lev, j] * s_ref[odd, now, 0, t, MINE, :]
                    ndo_ref[0, j, lev, :, cuts[t]] = obs_ref[lev, j, t] - image
                for b in range(2):
                    part = slice(b * SUB, (b + 1) * SUB)
                    here, up, down = BLOCKS[b], UPS[b], DOWNS[b]
                    x = [[x_ref[lev, j, u, t, part, :] for t in range(tiles)] for u in range(nvar)]
                    ce = [diffusion - half_adv * value for value in x[0]]
                    cw = [diffusion + half_adv * value for value in x[0]]
                    ce, cw = walled(b, ce, cw)
                    cn = masked_last([diffusion - half_adv * value for value in x[1]], lane)
                    cs = masked_first([diffusion + half_adv * value for value in x[1]], lane)
                    s = [
                        [s_ref[odd, now, u, t, here, :] for t in range(tiles)] for u in range(nvar)
                    ]
                    xs = [[x[u][t] * s[u][t] for t in range(tiles)] for u in range(nvar)]
                    for v in range(nvar):
                        north, south = from_north(s[v], lane), from_south(s[v], lane)
                        for t in range(tiles):
                            fresh = keep * s[v][t] + ce[t] * s_ref[odd, now, v, t, up, :]
                            fresh = fresh + cw[t] * s_ref[odd, now, v, t, down, :]
                            fresh = fresh + cn[t] * north[t] + cs[t] * south[t]
                            for u in range(nvar):
                                fresh = fresh + mix_ref[v, u] * xs[u][t]
                            s_ref[odd, 1 - now, v, t, here, :] = fresh
            return carry

        lax.fori_loop(0, steps, step, 0)
        for odd in range(2):
            for v in range(nvar):
                for t in range(tiles):
                    ends_ref[2 * i + odd, v, t] = s_ref[odd, steps % 2, v, t, MINE, :]
        return outer

    lax.fori_loop(0, pairs, pair, 0)


def adjoint_kernel(
    i, windows, spaces, steps, nvar, levels, tiles,
    mix_ref, total_ref, x_ref, last_ref, force_ref, ends_ref, inc_ref, rhs_ref, dual_ref,
    ndm_ref, ninc_ref, *rest,
):
    payload_refs = rest[: windows - 1]
    x0_ref, a_ref, q_ref = rest[windows - 1 :]
    me = lax.axis_index("window")
    lane = lane_index()
    walled = walls(spaces)
    cuts = [slice(t * LANES, (t + 1) * LANES) for t in range(tiles)]

    for odd in range(2):
        lev = 2 * i + odd
        for t in range(tiles):
            for j in range(steps):
                x0_ref[odd, j, t, SUB : 3 * SUB, :] = x_ref[lev, j, 0, t]
            for v in range(nvar):
                a_ref[odd, 0, v, t, SUB : 3 * SUB, :] = last_ref[odd, v, t]

    def step(turn, carry):
        now = lax.rem(turn, 2)
        j = steps - 1 - turn
        for odd in range(2):
            lev = 2 * i + odd
            for b in range(2):
                part = slice(b * SUB, (b + 1) * SUB)
                here, up, down = BLOCKS[b], UPS[b], DOWNS[b]
                x = [[x_ref[lev, j, u, t, part, :] for t in range(tiles)] for u in range(nvar)]
                ce = [diffusion + half_adv * x0_ref[odd, j, t, up, :] for t in range(tiles)]
                cw = [diffusion - half_adv * x0_ref[odd, j, t, down, :] for t in range(tiles)]
                ce, cw = walled(b, ce, cw)
                cn = masked_first([diffusion + half_adv * value for value in x[1]], lane)
                cs = masked_last([diffusion - half_adv * value for value in x[1]], lane)
                a = [
                    [a_ref[odd, now, u, t, here, :] for t in range(tiles)] for u in range(nvar)
                ]
                for u in range(nvar):
                    north = from_north([cn[t] * a[u][t] for t in range(tiles)], lane)
                    south = from_south([cs[t] * a[u][t] for t in range(tiles)], lane)
                    for t in range(tiles):
                        fresh = keep * a[u][t] + ce[t] * a_ref[odd, now, u, t, up, :]
                        fresh = fresh + cw[t] * a_ref[odd, now, u, t, down, :]
                        fresh = fresh + north[t] + south[t]
                        pull = mix_ref[0, u] * a[0][t]
                        for v in range(1, nvar):
                            pull = pull + mix_ref[v, u] * a[v][t]
                        fresh = fresh + x[u][t] * pull
                        if u == 0:
                            fresh = fresh + force_ref[odd, j, t, part, :]
                        a_ref[odd, 1 - now, u, t, here, :] = fresh
        return carry

    lax.fori_loop(0, steps, step, 0)

    end = steps % 2
    coded = []
    for odd in range(2):
        lev = 2 * i + odd
        back, ahead = [], []
        for v in range(nvar):
            share = total_ref[v * levels + lev]
            tv, gv = [], []
            for t in range(tiles):
                term = a_ref[odd, end, v, t, MINE, :] - last_ref[odd, v, t, HALF : HALF + SUB, :]
                given = rhs_ref[0, v, lev, :, cuts[t]] - inc_ref[0, v, lev, :, cuts[t]]
                given = given + share * term
                ndm_ref[v, odd, :, cuts[t]] = -(dual_ref[0, v, lev, :, cuts[t]] + term)
                ninc_ref[v, odd, :, cuts[t]] = given
                tv.append(term)
                gv.append(given + ends_ref[lev, v, t])
            back.append(tv)
            ahead.append(gv)
        coded.append((row_codes(back), row_codes(ahead)))
    for kind in range(2):
        first, second = coded[0][kind], coded[1][kind]
        for n, (a, b) in enumerate(zip(first[0] + [first[1]], second[0] + [second[1]])):
            q_ref[kind, n] = shorts(jnp.concatenate([a, b], 0))
    for d in range(1, windows):
        payload_refs[d - 1][...] = q_ref[jnp.where(me + d >= windows, 0, 1)]


def final_kernel(windows, nvar, levels, tiles, *refs):
    pairs = levels // 2
    cut = pairs * (windows - 1)
    pieces, base_duals, base_incs = refs[:cut], refs[cut : cut + pairs], refs[cut + pairs : -3]
    total_ref, ndm_ref, ninc_ref = refs[-3:]
    me = lax.axis_index("window")
    cuts = [slice(t * LANES, (t + 1) * LANES) for t in range(tiles)]

    for i in range(pairs):
        tails = [None] * (nvar * tiles)
        heads = [None] * (nvar * tiles)
        for d in range(1, windows):
            piece = pieces[i * (windows - 1) + d - 1]
            later = d > me
            scales = jnp.exp2(floats(piece[nvar * tiles])) * (1.0 / CODE_MAX)
            for v in range(nvar):
                scale = scales[:, v : v + 1]
                for t in range(tiles):
                    n = v * tiles + t
                    value = floats(piece[n]) * scale
                    tail, head = jnp.where(later, value, 0.0), jnp.where(later, 0.0, value)
                    tails[n] = tail if d == 1 else tails[n] + tail
                    heads[n] = head if d == 1 else heads[n] + head
        for v in range(nvar):
            for odd in range(2):
                lev = 2 * i + odd
                share = total_ref[v * levels + lev]
                for t in range(tiles):
                    rows = slice(odd * SUB, (odd + 1) * SUB)
                    tail, head = tails[v * tiles + t][rows], heads[v * tiles + t][rows]
                    ndm_ref[0, v, lev, :, cuts[t]] = base_duals[i][v, odd, :, cuts[t]] - tail
                    ninc_ref[0, v, lev, :, cuts[t]] = (
                        base_incs[i][v, odd, :, cuts[t]] + head + share * tail
                    )


def moved(block, axis, distance, around=False):
    count = lax.axis_size(axis)
    route = [(i, (i + distance) % count) for i in range(count) if around or 0 <= i + distance < count]
    return lax.ppermute(block, axis, route)


def swaps(axis, first):
    route = []
    for i in range(first, lax.axis_size(axis) - 1, 2):
        route += [(i, i + 1), (i + 1, i)]
    return route


def swapped(block, axis, first):
    return lax.ppermute(block, axis, swaps(axis, first))


def body(
    trajectory,
    dual_model,
    increment,
    model_rhs,
    dual_obs,
    innovation,
    coupling,
    error_var,
    obs_var,
    obs_count,
):
    windows, spaces = lax.axis_size("window"), lax.axis_size("space")
    _, steps, nvar, levels, rows, part = trajectory.shape
    columns = dual_model.shape[-1]
    tiles = columns // LANES
    assert trajectory.shape[0] == windows and windows > 1 and rows == SUB and steps == HALF
    assert columns == tiles * LANES == windows * part and levels % 4 == 0
    pairs = levels // 2
    wide = -(-steps * part // LANES) * LANES
    bf16, f32, i16 = jnp.bfloat16, jnp.float32, jnp.int16

    def shape(dims, dtype):
        return jax.ShapeDtypeStruct(dims, dtype)

    block = shape((nvar * levels * wide // LANES + 1, rows, LANES), bf16)
    variances = jnp.pad(error_var[0].T, ((0, SUB - levels), (0, LANES - nvar)))

    def packed(distances):
        return pl.pallas_call(
            lambda *refs: pack_kernel(distances, windows, steps, nvar, levels, part, *refs),
            out_shape=[block] * len(distances),
            in_specs=[VMEM, VMEM],
            out_specs=[VMEM] * len(distances),
            compiler_params=params(),
        )(variances, trajectory)

    order = sorted(range(1, windows), key=lambda d: -d * (windows - d))
    groups = [[d] for d in order] if windows <= 4 else [order]
    blocks = {}
    for group in groups:
        blocks.update(zip(group, packed(group)))
    arrived = {d: moved(blocks[d], "window", d, around=True) for d in order}
    arrived[0] = packed([0])[0]

    payload = shape((pairs, nvar * tiles + 1, 2 * SUB, LANES), i16)

    counts = [nvar, nvar, steps - 1]
    half_tiles = sum(-(-(count * tiles + 1) // 2) for count in counts)
    halves = shape((pairs, half_tiles, 2 * SUB, LANES), i16)
    near, far, dual = pl.pallas_call(
        half_code_kernel,
        out_shape=[halves, halves, payload],
        in_specs=[VMEM] * 3,
        out_specs=[VMEM] * 3,
        compiler_params=params(),
    )(dual_model, increment, dual_obs)
    far, near = swapped(far, "space", 1), swapped(near, "space", 0)

    blocks_here = [arrived[d] for d in range(windows)]
    *after, totals = pl.pallas_call(
        lambda *refs: around_kernel(windows, nvar, levels, *refs),
        out_shape=[shape((2,) + payload.shape[1:], i16)] * pairs
        + [shape((nvar * levels, rows, LANES), f32)],
        in_specs=[VMEM] * (windows + 3),
        out_specs=[VMEM] * (pairs + 1),
        compiler_params=params(),
    )(*blocks_here, dual, near, far)
    after = [moved(piece, "window", -1) for piece in after]

    obs, share, mix = pl.pallas_call(
        lambda *refs: prepare_factor_kernel(steps, nvar, levels, tiles, *refs),
        out_shape=[
            shape((levels, steps, tiles, SUB, LANES), f32),
            shape((levels, steps, SUB, LANES), f32),
            shape((nvar, nvar, SUB, LANES), f32),
        ],
        in_specs=[SMEM] * 2 + [VMEM] * 3,
        out_specs=[VMEM] * 3,
        compiler_params=params(),
    )(obs_count, obs_var, coupling, dual_obs, innovation)

    own, traj_near, traj_far = pl.pallas_call(
        lambda *refs: assemble_kernel(windows, steps, nvar, levels, part, *refs),
        out_shape=[
            shape((steps, nvar * levels, rows, columns), bf16),
            shape((steps, nvar * pairs, rows, columns), bf16),
            shape((far_base(steps, nvar, levels)[1], rows, columns), bf16),
        ],
        in_specs=[VMEM] * windows + [ANY],
        out_specs=[VMEM] * 3,
        scratch_shapes=[pltpu.VMEM((windows, block.shape[0] - 1, rows, LANES), bf16)],
        compiler_params=params(),
    )(*blocks_here, mix)
    traj_near, traj_far = swapped(traj_near, "space", 0), swapped(traj_far, "space", 1)

    first = pl.pallas_call(
        lambda *refs: prepare_tangent_kernel(nvar, levels, tiles, *refs),
        out_shape=shape((levels, nvar, tiles, 2 * SUB, LANES), f32),
        in_specs=[VMEM] * 3,
        out_specs=VMEM,
        compiler_params=params(),
    )(near, far, increment)
    new_dual_obs, ends, wide_traj = pl.pallas_call(
        lambda *refs: tangent_kernel(spaces, steps, nvar, levels, tiles, *refs),
        out_shape=[
            shape(dual_obs.shape, f32),
            shape((levels, nvar, tiles, SUB, LANES), f32),
            shape((levels, steps, nvar, tiles, 2 * SUB, LANES), f32),
        ],
        in_specs=[VMEM] * 7,
        out_specs=[VMEM] * 3,
        scratch_shapes=[pltpu.VMEM((2, 2, nvar, tiles, 4 * SUB, LANES), f32)],
        compiler_params=params(),
    )(mix, share, obs, own, traj_near, traj_far, first)

    state = shape((nvar, 2, rows, columns), f32)
    coded = shape((nvar * tiles + 1, 2 * SUB, LANES), i16)
    base_duals, base_incs, sent = [], [], []
    before = ends
    for i in range(pairs):
        last, force = pl.pallas_call(
            lambda *refs, i=i: prepare_adjoint_kernel(i, steps, nvar, tiles, *refs),
            out_shape=[shape((2, n, tiles, 2 * SUB, LANES), f32) for n in (nvar, steps)],
            in_specs=[SMEM] + [VMEM] * 4 + [ANY],
            out_specs=[VMEM] * 2,
            compiler_params=params(),
        )(obs_count, near, far, dual_obs, after[i], before)
        base_dual, base_inc, *payloads = pl.pallas_call(
            lambda *refs, i=i: adjoint_kernel(
                i, windows, spaces, steps, nvar, levels, tiles, *refs
            ),
            out_shape=[state, state] + [coded] * (windows - 1),
            in_specs=[VMEM] * 9,
            out_specs=[VMEM] * (2 + windows - 1),
            scratch_shapes=[
                pltpu.VMEM((2, steps, tiles, 4 * SUB, LANES), f32),
                pltpu.VMEM((2, 2, nvar, tiles, 4 * SUB, LANES), f32),
                pltpu.VMEM((2,) + coded.shape, i16),
            ],
            compiler_params=params(),
        )(mix, totals, wide_traj, last, force, ends, increment, model_rhs, dual_model)
        before = base_dual
        base_duals.append(base_dual)
        base_incs.append(base_inc)
        moving = {d: moved(payloads[d - 1], "window", d, around=True) for d in order}
        sent += [moving[d] for d in range(1, windows)]

    new_dual_model, new_increment = pl.pallas_call(
        lambda *refs: final_kernel(windows, nvar, levels, tiles, *refs),
        out_shape=[shape(dual_model.shape, f32), shape(increment.shape, f32)],
        in_specs=[VMEM] * (len(sent) + 2 * pairs + 1),
        out_specs=[VMEM] * 2,
        compiler_params=params(),
    )(*sent, *base_duals, *base_incs, totals)
    return new_dual_model, new_dual_obs, new_increment


def solution(mesh):
    placed = (
        P("members", None, None, None, "space", "window"),
        P(("members", "window"), None, None, "space", None),
        P(("members", "window"), None, None, "space", None),
        P(("members", "window"), None, None, "space", None),
        P(("members", "window"), None, None, "space", None),
        P(("members", "window"), None, None, "space", None),
        P(),
        P(("members", "window"), None, None),
        P(("members", "window"), None, None),
        P(("members", "window")),
    )
    return jax.shard_map(
        body,
        mesh=mesh,
        in_specs=placed,
        out_specs=(
            P(("members", "window"), None, None, "space", None),
            P(("members", "window"), None, None, "space", None),
            P(("members", "window"), None, None, "space", None),
        ),
        check_vma=False,
    )
```

```python
import jax
import jax.numpy as jnp
from jax import lax
from jax.experimental import pallas as pl
from jax.experimental.pallas import tpu as pltpu
from jax.sharding import PartitionSpec as P

LANES = 128
SUB = 8
HALF = SUB // 2
CODE_MAX = 32766.0
ROUNDER = 12582912.0

diffusion = 0.2
advection = 0.2
coupling_gain = 0.5
keep = 1.0 - 4.0 * diffusion
half_adv = 0.5 * advection

VMEM = pl.BlockSpec(memory_space=pltpu.VMEM)
SMEM = pl.BlockSpec(memory_space=pltpu.SMEM)
ANY = pl.BlockSpec(memory_space=pl.ANY)


def params(mib=24):
    return pltpu.CompilerParams(vmem_limit_bytes=mib * 1024 * 1024)


def lane_index():
    return lax.broadcasted_iota(jnp.int32, (SUB, LANES), 1)


def row_index():
    return lax.broadcasted_iota(jnp.int32, (SUB, LANES), 0)


def tiled(wide):
    short = -wide.shape[1] % LANES
    if short:
        wide = jnp.concatenate([wide, jnp.zeros((wide.shape[0], short), wide.dtype)], 1)
    return [wide[:, i : i + LANES] for i in range(0, wide.shape[1], LANES)]


def place(parts, rolled, lane):
    built = {}
    for key, tiles, first, width, target in parts:
        done = 0
        while done < width:
            a, b = first + done, target + done
            n = min(width - done, LANES - a % LANES, LANES - b % LANES)
            shift = (b - a) % LANES
            name = (key, a // LANES, shift)
            if name not in rolled:
                value = tiles[a // LANES]
                rolled[name] = pltpu.roll(value, shift, 1) if shift else value
            if b % LANES:
                built[b // LANES] = jnp.where(
                    lane >= b % LANES, rolled[name], built[b // LANES]
                )
            else:
                built[b // LANES] = rolled[name]
            done += n
    return [built[i] for i in range(len(built))]


def joined_halves(first, second):
    top = row_index()[:, :1] < HALF
    last = jnp.where(top, pltpu.roll(first, HALF, 0), second)
    start = jnp.where(top, first, pltpu.roll(second, HALF, 0))
    return last, start


def widened(own, near, far, odd, even):
    top = row_index() < HALF
    low, high = jnp.where(even, far, near), jnp.where(even, near, far)
    turned = pltpu.roll(own, HALF, 0)
    low = pltpu.roll(low, HALF, 0) if odd else low
    high = high if odd else pltpu.roll(high, HALF, 0)
    return jnp.where(top, low, turned), jnp.where(top, turned, high)


def row_codes(planes):
    lane = lax.broadcasted_iota(jnp.int32, planes[0][0].shape, 1)
    scales = jnp.zeros(planes[0][0].shape, jnp.float32)
    out = []
    for v, row in enumerate(planes):
        big = jnp.abs(row[0])
        for value in row[1:]:
            big = jnp.maximum(big, jnp.abs(value))
        big = jnp.max(big, axis=1, keepdims=True)
        power = jnp.clip(jnp.ceil(jnp.log2(jnp.maximum(big, 1e-30))), -90.0, 126.0)
        scales = jnp.where(lane == v, power, scales)
        gain = CODE_MAX * jnp.exp2(-power)
        for value in row:
            out.append((value * gain + ROUNDER) - ROUNDER)
    return out, scales


def shorts(value):
    return value.astype(jnp.int32).astype(jnp.int16)


def floats(value):
    return value.astype(jnp.int32).astype(jnp.float32)


def pack_kernel(steps, nvar, levels, part, var_ref, traj_ref, out_ref):
    lane = lane_index()
    variance = var_ref[...]
    high = variance.astype(jnp.bfloat16).astype(jnp.float32)
    middle = (variance - high).astype(jnp.bfloat16).astype(jnp.float32)
    low = variance - high - middle
    split = high + pltpu.roll(middle, HALF, 0) + pltpu.roll(low, LANES // 2, 1)
    split = split.astype(jnp.bfloat16)

    def window(w, carry):
        out_ref[w, out_ref.shape[1] - 1] = split
        for v in range(nvar):
            for lev in range(levels):
                pieces = [tiled(traj_ref[w, j, v, lev].astype(jnp.float32)) for j in range(steps)]
                parts = [(j, pieces[j], 0, part, j * part) for j in range(steps)]
                placed = place(parts, {}, lane)
                for t, value in enumerate(placed):
                    out_ref[w, (v * levels + lev) * len(placed) + t] = value.astype(jnp.bfloat16)
        return carry

    lax.fori_loop(0, out_ref.shape[0], window, 0)


def even_place():
    return lax.rem(lax.axis_index("space"), 2) == 0


def level_codes(ref, lev, first=0):
    planes = [
        [ref[0, v, lev, :, t : t + LANES] for t in range(0, ref.shape[-1], LANES)]
        for v in range(first, ref.shape[1])
    ]
    values, scales = row_codes(planes)
    return values + [scales]


def half_code_kernel(*refs):
    sources, (near_ref, far_ref, own_ref) = refs[:-4], refs[-3:]
    even = even_place()

    def pair(i, carry):
        near, far = [], []
        for k, ref in enumerate(sources):
            skip = int(k == len(sources) - 1)
            coded = [level_codes(ref, 2 * i + odd, skip) for odd in range(2)]
            for n, (first, second) in enumerate(zip(*coded)):
                if k == 0:
                    own_ref[i, n] = shorts(jnp.concatenate([first, second], 0))
                last, start = joined_halves(first, second)
                near.append(jnp.where(even, last, start))
                far.append(jnp.where(even, start, last))
            if len(near) % 2:
                near.append(jnp.zeros((SUB, LANES), jnp.float32))
                far.append(jnp.zeros((SUB, LANES), jnp.float32))
        for tiles, ref in ((near, near_ref), (far, far_ref)):
            for n in range(0, len(tiles), 2):
                ref[i, n // 2] = shorts(jnp.concatenate(tiles[n : n + 2], 0))
        return carry

    lax.fori_loop(0, near_ref.shape[0], pair, 0)


def half_tile(ref, i, n):
    whole = floats(ref[i, n // 2])
    return whole[SUB:] if n % 2 else whole[:SUB]


def around_kernel(windows, nvar, levels, *refs):
    blocks_ref, own_ref, near_ref, far_ref = refs[:4]
    outs, total_ref = refs[4:-1], refs[-1]
    me = lax.axis_index("window")
    even = even_place()
    total = jnp.zeros((SUB, LANES), jnp.float32)
    for w in range(windows):
        split = blocks_ref[w, blocks_ref.shape[1] - 1].astype(jnp.float32)
        here = split + pltpu.roll(split, HALF, 0) + pltpu.roll(split, LANES // 2, 1)
        total = total + jnp.where(w <= me, here, 0.0)
    for v in range(nvar):
        for lev in range(levels):
            one = total[lev : lev + 1, v : v + 1]
            total_ref[v * levels + lev] = jnp.broadcast_to(one, (SUB, LANES))
    for i, out_ref in enumerate(outs):
        for n in range(own_ref.shape[1]):
            own = floats(own_ref[i, n])
            near, far = half_tile(near_ref, i, n), half_tile(far_ref, i, n)
            for odd in range(2):
                halves = widened(own[odd * SUB : (odd + 1) * SUB], near, far, odd, even)
                out_ref[odd, n] = shorts(jnp.concatenate(halves, 0))


def decoded(ref, i, first, nvar, tiles):
    scales = jnp.exp2(half_tile(ref, i, first + nvar * tiles)) * (1.0 / CODE_MAX)
    return [
        [half_tile(ref, i, first + v * tiles + t) * scales[:, v : v + 1] for t in range(tiles)]
        for v in range(nvar)
    ]


def is_quarter(j, v, steps):
    return 0 < j < steps - 1 and not (v == 0 and j + 1 > HALF // 2)


def far_base(steps, nvar, levels):
    base, total = {}, 0
    for j in range(steps):
        for v in range(nvar):
            base[j, v] = total
            total += levels // (4 if is_quarter(j, v, steps) else 2)
    return base, total


def joined_quarters(four):
    slot = row_index() // 2
    last, start = pltpu.roll(four[0], 2, 0), four[0]
    for n in range(1, 4):
        last = jnp.where(slot == n, pltpu.roll(four[n], (2 * n + 2) % SUB, 0), last)
        start = jnp.where(slot == n, pltpu.roll(four[n], 2 * n, 0), start)
    return last, start


def assemble_kernel(windows, steps, nvar, levels, part, *refs):
    blocks_ref, _, own_ref, near_ref, far_ref = refs
    even = even_place()
    lane = lane_index()
    packed_tiles = blocks_ref.shape[1] // (nvar * levels)

    pairs = levels // 2
    base, _ = far_base(steps, nvar, levels)

    def variable(v):
        built = {}
        for lev in range(levels):
            plane = v * levels + lev
            sources = [
                [
                    blocks_ref[w, plane * packed_tiles + t].astype(jnp.float32)
                    for t in range(packed_tiles)
                ]
                for w in range(windows)
            ]
            rolled = {}
            for j in range(steps):
                parts = [(w, sources[w], j * part, part, w * part) for w in range(windows)]
                built[j, lev] = place(parts, rolled, lane)
                own_ref[j, plane] = jnp.concatenate(built[j, lev], 1).astype(jnp.bfloat16)
        for j in range(steps):
            for i in range(pairs):
                halves = [joined_halves(a, b) for a, b in zip(built[j, 2 * i], built[j, 2 * i + 1])]
                last, start = (jnp.concatenate([h[k] for h in halves], 1) for k in range(2))
                near_ref[j, v * pairs + i] = jnp.where(even, last, start).astype(jnp.bfloat16)
                if not is_quarter(j, v, steps):
                    far_ref[base[j, v] + i] = jnp.where(even, start, last).astype(jnp.bfloat16)
            if is_quarter(j, v, steps):
                for q in range(levels // 4):
                    four = zip(*[built[j, 4 * q + n] for n in range(4)])
                    ends = [joined_quarters(tiles) for tiles in four]
                    last, start = (jnp.concatenate([e[k] for e in ends], 1) for k in range(2))
                    far_ref[base[j, v] + q] = jnp.where(even, start, last).astype(jnp.bfloat16)

    for v in range(nvar):
        variable(v)


def prepare_factor_kernel(
    steps, nvar, levels, tiles,
    count_ref, noise_ref, coupling_ref, dobs_ref, innov_ref, obs_ref, share_ref, mix_ref,
):
    cuts = [slice(t * LANES, (t + 1) * LANES) for t in range(tiles)]
    for v in range(nvar):
        for u in range(nvar):
            one = coupling_gain * coupling_ref[v : v + 1, u : u + 1]
            mix_ref[v, u] = jnp.broadcast_to(one, (SUB, LANES))
    for lev in range(levels):
        for j in range(steps):
            noise = jnp.full((SUB, LANES), noise_ref[0, j, lev])
            share = jnp.where(j < count_ref[0], 1.0, 0.0) / noise
            share_ref[lev, j] = share
            for t in range(tiles):
                gap = innov_ref[0, j, lev, :, cuts[t]] - noise * dobs_ref[0, j, lev, :, cuts[t]]
                obs_ref[lev, j, t] = gap * share


def prepare_tangent_kernel(nvar, levels, tiles, near_ref, far_ref, inc_ref, first_ref):
    even = even_place()
    blocks = [slice(0, SUB), slice(SUB, 2 * SUB)]
    cuts = [slice(t * LANES, (t + 1) * LANES) for t in range(tiles)]
    offset = -(-(nvar * tiles + 1) // 2) * 2
    for i in range(levels // 2):
        fields = [decoded(ref, i, offset, nvar, tiles) for ref in (near_ref, far_ref)]
        for odd in range(2):
            lev = 2 * i + odd
            for t in range(tiles):
                for v in range(nvar):
                    near, far = (side[v][t] for side in fields)
                    halves = widened(inc_ref[0, v, lev, :, cuts[t]], near, far, odd, even)
                    for b in range(2):
                        first_ref[lev, v, t, blocks[b], :] = halves[b]


def prepare_adjoint_kernel(
    i, steps, nvar, tiles, count_ref, near_ref, far_ref, dobs_ref, after_ref, *refs
):
    _, last_ref, force_ref = refs
    even = even_place()
    blocks = [slice(0, SUB), slice(SUB, 2 * SUB)]
    cuts = [slice(t * LANES, (t + 1) * LANES) for t in range(tiles)]
    seen = [jnp.where(j < count_ref[0], 1.0, 0.0) for j in range(steps)]
    offset = -(-(nvar * tiles + 1) // 2) * 2
    none = [[jnp.zeros((SUB, LANES), jnp.float32)] * tiles]
    forces = [none + decoded(ref, i, 2 * offset, steps - 1, tiles) for ref in (near_ref, far_ref)]
    for odd in range(2):
        scales = jnp.exp2(floats(after_ref[odd, nvar * tiles])) * (-1.0 / CODE_MAX)
        for t in range(tiles):
            for v in range(nvar):
                value = floats(after_ref[odd, v * tiles + t])
                last_ref[odd, v, t] = value * scales[:, v : v + 1]
            for j in range(steps):
                near, far = (side[j][t] for side in forces)
                halves = widened(dobs_ref[0, j, 2 * i + odd, :, cuts[t]], near, far, odd, even)
                for b in range(2):
                    force_ref[odd, j, t, blocks[b], :] = seen[j] * halves[b]


def from_north(line, lane):
    turned = [pltpu.roll(value, LANES - 1, 1) for value in line] * 2
    return [jnp.where(lane < LANES - 1, turned[t], turned[t + 1]) for t in range(len(line))]


def from_south(line, lane):
    turned = [pltpu.roll(value, 1, 1) for value in line]
    return [jnp.where(lane > 0, turned[t], turned[t - 1]) for t in range(len(line))]


def masked_last(line, lane):
    return line[:-1] + [jnp.where(lane < LANES - 1, line[-1], 0.0)]


def masked_first(line, lane):
    return [jnp.where(lane > 0, line[0], 0.0)] + line[1:]


def walls(spaces):
    row, place_x = row_index(), lax.axis_index("space")
    low = jnp.where((row == HALF) & (place_x == 0), 0.0, 1.0)
    high = jnp.where((row == HALF - 1) & (place_x == spaces - 1), 0.0, 1.0)

    def walled(block, east, west):
        if block == 0:
            return east, [low * value for value in west]
        return [high * value for value in east], west

    return walled


BLOCKS = [slice(SUB, 2 * SUB), slice(2 * SUB, 3 * SUB)]
UPS = [slice(b.start + 1, b.stop + 1) for b in BLOCKS]
DOWNS = [slice(b.start - 1, b.stop - 1) for b in BLOCKS]
MINE = slice(SUB + HALF, 2 * SUB + HALF)


def tangent_kernel(
    spaces, steps, nvar, levels, tiles,
    mix_ref, share_ref, obs_ref, own_ref, near_ref, far_ref, first_ref,
    ndo_ref, ends_ref, x_ref, s_ref,
):
    lane, row = lane_index(), row_index()
    even = even_place()
    top = row < HALF
    walled = walls(spaces)
    pairs = levels // 2
    cuts = [slice(t * LANES, (t + 1) * LANES) for t in range(tiles)]
    base, _ = far_base(steps, nvar, levels)

    for lev in range(levels):
        i, odd = lev // 2, lev % 2
        for j in range(steps):
            for v in range(nvar):
                for t in range(tiles):
                    own = own_ref[j, v * levels + lev, :, cuts[t]].astype(jnp.float32)
                    near = near_ref[j, v * pairs + i, :, cuts[t]].astype(jnp.float32)
                    quarter = is_quarter(j, v, steps)
                    far = far_ref[base[j, v] + lev // (4 if quarter else 2), :, cuts[t]]
                    far = far.astype(jnp.float32)
                    if quarter:
                        slot = 2 * (lev % 4)
                        low_far = pltpu.roll(far, (HALF - 2 - slot) % SUB, 0)
                        high_far = pltpu.roll(far, (HALF - slot) % SUB, 0)
                    else:
                        low_far = pltpu.roll(far, HALF, 0) if odd else far
                        high_far = far if odd else pltpu.roll(far, HALF, 0)
                    low_near = pltpu.roll(near, HALF, 0) if odd else near
                    high_near = near if odd else pltpu.roll(near, HALF, 0)
                    turned = pltpu.roll(own, HALF, 0)
                    low = jnp.where(even, low_far, low_near)
                    high = jnp.where(even, high_near, high_far)
                    x_ref[lev, j, v, t, :SUB, :] = jnp.where(top, low, turned)
                    x_ref[lev, j, v, t, SUB:, :] = jnp.where(top, turned, high)

    def pair(i, outer):
        for odd in range(2):
            for v in range(nvar):
                for t in range(tiles):
                    s_ref[odd, 0, v, t, SUB : 3 * SUB, :] = first_ref[2 * i + odd, v, t]

        def step(j, carry):
            now = lax.rem(j, 2)
            for odd in range(2):
                lev = 2 * i + odd
                for t in range(tiles):
                    image = share_ref[lev, j] * s_ref[odd, now, 0, t, MINE, :]
                    ndo_ref[0, j, lev, :, cuts[t]] = obs_ref[lev, j, t] - image
                for b in range(2):
                    part = slice(b * SUB, (b + 1) * SUB)
                    here, up, down = BLOCKS[b], UPS[b], DOWNS[b]
                    x = [[x_ref[lev, j, u, t, part, :] for t in range(tiles)] for u in range(nvar)]
                    ce = [diffusion - half_adv * value for value in x[0]]
                    cw = [diffusion + half_adv * value for value in x[0]]
                    ce, cw = walled(b, ce, cw)
                    cn = masked_last([diffusion - half_adv * value for value in x[1]], lane)
                    cs = masked_first([diffusion + half_adv * value for value in x[1]], lane)
                    s = [
                        [s_ref[odd, now, u, t, here, :] for t in range(tiles)] for u in range(nvar)
                    ]
                    xs = [[x[u][t] * s[u][t] for t in range(tiles)] for u in range(nvar)]
                    for v in range(nvar):
                        north, south = from_north(s[v], lane), from_south(s[v], lane)
                        for t in range(tiles):
                            fresh = keep * s[v][t] + ce[t] * s_ref[odd, now, v, t, up, :]
                            fresh = fresh + cw[t] * s_ref[odd, now, v, t, down, :]
                            fresh = fresh + cn[t] * north[t] + cs[t] * south[t]
                            for u in range(nvar):
                                fresh = fresh + mix_ref[v, u] * xs[u][t]
                            s_ref[odd, 1 - now, v, t, here, :] = fresh
            return carry

        lax.fori_loop(0, steps, step, 0)
        for odd in range(2):
            for v in range(nvar):
                for t in range(tiles):
                    ends_ref[2 * i + odd, v, t] = s_ref[odd, steps % 2, v, t, MINE, :]
        return outer

    lax.fori_loop(0, pairs, pair, 0)


def adjoint_kernel(
    i, windows, spaces, steps, nvar, levels, tiles,
    mix_ref, total_ref, x_ref, last_ref, force_ref, ends_ref, inc_ref, rhs_ref, dual_ref,
    ndm_ref, ninc_ref, *rest,
):
    payload_refs = rest[: windows - 1]
    x0_ref, a_ref, q_ref = rest[windows - 1 :]
    me = lax.axis_index("window")
    lane = lane_index()
    walled = walls(spaces)
    cuts = [slice(t * LANES, (t + 1) * LANES) for t in range(tiles)]

    for odd in range(2):
        lev = 2 * i + odd
        for t in range(tiles):
            for j in range(steps):
                x0_ref[odd, j, t, SUB : 3 * SUB, :] = x_ref[lev, j, 0, t]
            for v in range(nvar):
                a_ref[odd, 0, v, t, SUB : 3 * SUB, :] = last_ref[odd, v, t]

    def step(turn, carry):
        now = lax.rem(turn, 2)
        j = steps - 1 - turn
        for odd in range(2):
            lev = 2 * i + odd
            for b in range(2):
                part = slice(b * SUB, (b + 1) * SUB)
                here, up, down = BLOCKS[b], UPS[b], DOWNS[b]
                x = [[x_ref[lev, j, u, t, part, :] for t in range(tiles)] for u in range(nvar)]
                ce = [diffusion + half_adv * x0_ref[odd, j, t, up, :] for t in range(tiles)]
                cw = [diffusion - half_adv * x0_ref[odd, j, t, down, :] for t in range(tiles)]
                ce, cw = walled(b, ce, cw)
                cn = masked_first([diffusion + half_adv * value for value in x[1]], lane)
                cs = masked_last([diffusion - half_adv * value for value in x[1]], lane)
                a = [
                    [a_ref[odd, now, u, t, here, :] for t in range(tiles)] for u in range(nvar)
                ]
                for u in range(nvar):
                    north = from_north([cn[t] * a[u][t] for t in range(tiles)], lane)
                    south = from_south([cs[t] * a[u][t] for t in range(tiles)], lane)
                    for t in range(tiles):
                        fresh = keep * a[u][t] + ce[t] * a_ref[odd, now, u, t, up, :]
                        fresh = fresh + cw[t] * a_ref[odd, now, u, t, down, :]
                        fresh = fresh + north[t] + south[t]
                        pull = mix_ref[0, u] * a[0][t]
                        for v in range(1, nvar):
                            pull = pull + mix_ref[v, u] * a[v][t]
                        fresh = fresh + x[u][t] * pull
                        if u == 0:
                            fresh = fresh + force_ref[odd, j, t, part, :]
                        a_ref[odd, 1 - now, u, t, here, :] = fresh
        return carry

    lax.fori_loop(0, steps, step, 0)

    end = steps % 2
    coded = []
    for odd in range(2):
        lev = 2 * i + odd
        back, ahead = [], []
        for v in range(nvar):
            share = total_ref[v * levels + lev]
            tv, gv = [], []
            for t in range(tiles):
                term = a_ref[odd, end, v, t, MINE, :] - last_ref[odd, v, t, HALF : HALF + SUB, :]
                given = rhs_ref[0, v, lev, :, cuts[t]] - inc_ref[0, v, lev, :, cuts[t]]
                given = given + share * term
                ndm_ref[v, odd, :, cuts[t]] = -(dual_ref[0, v, lev, :, cuts[t]] + term)
                ninc_ref[v, odd, :, cuts[t]] = given
                tv.append(term)
                gv.append(given + ends_ref[lev, v, t])
            back.append(tv)
            ahead.append(gv)
        coded.append((row_codes(back), row_codes(ahead)))
    for kind in range(2):
        first, second = coded[0][kind], coded[1][kind]
        for n, (a, b) in enumerate(zip(first[0] + [first[1]], second[0] + [second[1]])):
            q_ref[kind, n] = shorts(jnp.concatenate([a, b], 0))
    for d in range(1, windows):
        payload_refs[d - 1][...] = q_ref[jnp.where(me + d >= windows, 0, 1)]


def final_kernel(windows, nvar, levels, tiles, *refs):
    pairs = levels // 2
    cut = pairs * (windows - 1)
    pieces, base_duals, base_incs = refs[:cut], refs[cut : cut + pairs], refs[cut + pairs : -3]
    total_ref, ndm_ref, ninc_ref = refs[-3:]
    me = lax.axis_index("window")
    cuts = [slice(t * LANES, (t + 1) * LANES) for t in range(tiles)]

    for i in range(pairs):
        tails = [None] * (nvar * tiles)
        heads = [None] * (nvar * tiles)
        for d in range(1, windows):
            piece = pieces[i * (windows - 1) + d - 1]
            later = d > me
            scales = jnp.exp2(floats(piece[nvar * tiles])) * (1.0 / CODE_MAX)
            for v in range(nvar):
                scale = scales[:, v : v + 1]
                for t in range(tiles):
                    n = v * tiles + t
                    value = floats(piece[n]) * scale
                    tail, head = jnp.where(later, value, 0.0), jnp.where(later, 0.0, value)
                    tails[n] = tail if d == 1 else tails[n] + tail
                    heads[n] = head if d == 1 else heads[n] + head
        for v in range(nvar):
            for odd in range(2):
                lev = 2 * i + odd
                share = total_ref[v * levels + lev]
                for t in range(tiles):
                    rows = slice(odd * SUB, (odd + 1) * SUB)
                    tail, head = tails[v * tiles + t][rows], heads[v * tiles + t][rows]
                    ndm_ref[0, v, lev, :, cuts[t]] = base_duals[i][v, odd, :, cuts[t]] - tail
                    ninc_ref[0, v, lev, :, cuts[t]] = (
                        base_incs[i][v, odd, :, cuts[t]] + head + share * tail
                    )


def moved(block, axis, distance, around=False):
    count = lax.axis_size(axis)
    route = [(i, (i + distance) % count) for i in range(count) if around or 0 <= i + distance < count]
    return lax.ppermute(block, axis, route)


def swaps(axis, first):
    route = []
    for i in range(first, lax.axis_size(axis) - 1, 2):
        route += [(i, i + 1), (i + 1, i)]
    return route


def swapped(block, axis, first):
    return lax.ppermute(block, axis, swaps(axis, first))


def body(
    trajectory,
    dual_model,
    increment,
    model_rhs,
    dual_obs,
    innovation,
    coupling,
    error_var,
    obs_var,
    obs_count,
):
    windows, spaces = lax.axis_size("window"), lax.axis_size("space")
    _, steps, nvar, levels, rows, part = trajectory.shape
    columns = dual_model.shape[-1]
    tiles = columns // LANES
    assert trajectory.shape[0] == windows and windows > 1 and rows == SUB and steps == HALF
    assert columns == tiles * LANES == windows * part and levels % 4 == 0
    pairs = levels // 2
    wide = -(-steps * part // LANES) * LANES
    bf16, f32, i16 = jnp.bfloat16, jnp.float32, jnp.int16

    def shape(dims, dtype):
        return jax.ShapeDtypeStruct(dims, dtype)

    block = shape((nvar * levels * wide // LANES + 1, rows, LANES), bf16)
    variances = jnp.pad(error_var[0].T, ((0, SUB - levels), (0, LANES - nvar)))

    blocks = pl.pallas_call(
        lambda *refs: pack_kernel(steps, nvar, levels, part, *refs),
        out_shape=shape((windows,) + block.shape, bf16),
        in_specs=[VMEM, VMEM],
        out_specs=VMEM,
        compiler_params=params(),
    )(variances, trajectory)
    packed, blocks = blocks, lax.all_to_all(blocks, "window", 0, 0, tiled=True)
    order = sorted(range(1, windows), key=lambda d: -d * (windows - d))

    payload = shape((pairs, nvar * tiles + 1, 2 * SUB, LANES), i16)

    counts = [nvar, nvar, steps - 1]
    half_tiles = sum(-(-(count * tiles + 1) // 2) for count in counts)
    halves = shape((pairs, half_tiles, 2 * SUB, LANES), i16)
    near, far, dual = pl.pallas_call(
        half_code_kernel,
        out_shape=[halves, halves, payload],
        in_specs=[VMEM] * 3 + [ANY],
        out_specs=[VMEM] * 3,
        compiler_params=params(),
    )(dual_model, increment, dual_obs, packed)
    far, near = swapped(far, "space", 1), swapped(near, "space", 0)

    *after, totals = pl.pallas_call(
        lambda *refs: around_kernel(windows, nvar, levels, *refs),
        out_shape=[shape((2,) + payload.shape[1:], i16)] * pairs
        + [shape((nvar * levels, rows, LANES), f32)],
        in_specs=[VMEM] * 4,
        out_specs=[VMEM] * (pairs + 1),
        compiler_params=params(),
    )(blocks, dual, near, far)
    after = [moved(piece, "window", -1) for piece in after]

    obs, share, mix = pl.pallas_call(
        lambda *refs: prepare_factor_kernel(steps, nvar, levels, tiles, *refs),
        out_shape=[
            shape((levels, steps, tiles, SUB, LANES), f32),
            shape((levels, steps, SUB, LANES), f32),
            shape((nvar, nvar, SUB, LANES), f32),
        ],
        in_specs=[SMEM] * 2 + [VMEM] * 3,
        out_specs=[VMEM] * 3,
        compiler_params=params(),
    )(obs_count, obs_var, coupling, dual_obs, innovation)

    own, traj_near, traj_far = pl.pallas_call(
        lambda *refs: assemble_kernel(windows, steps, nvar, levels, part, *refs),
        out_shape=[
            shape((steps, nvar * levels, rows, columns), bf16),
            shape((steps, nvar * pairs, rows, columns), bf16),
            shape((far_base(steps, nvar, levels)[1], rows, columns), bf16),
        ],
        in_specs=[VMEM, ANY],
        out_specs=[VMEM] * 3,
        compiler_params=params(),
    )(blocks, mix)
    traj_near, traj_far = swapped(traj_near, "space", 0), swapped(traj_far, "space", 1)

    first = pl.pallas_call(
        lambda *refs: prepare_tangent_kernel(nvar, levels, tiles, *refs),
        out_shape=shape((levels, nvar, tiles, 2 * SUB, LANES), f32),
        in_specs=[VMEM] * 3,
        out_specs=VMEM,
        compiler_params=params(),
    )(near, far, increment)
    new_dual_obs, ends, wide_traj = pl.pallas_call(
        lambda *refs: tangent_kernel(spaces, steps, nvar, levels, tiles, *refs),
        out_shape=[
            shape(dual_obs.shape, f32),
            shape((levels, nvar, tiles, SUB, LANES), f32),
            shape((levels, steps, nvar, tiles, 2 * SUB, LANES), f32),
        ],
        in_specs=[VMEM] * 7,
        out_specs=[VMEM] * 3,
        scratch_shapes=[pltpu.VMEM((2, 2, nvar, tiles, 4 * SUB, LANES), f32)],
        compiler_params=params(),
    )(mix, share, obs, own, traj_near, traj_far, first)

    state = shape((nvar, 2, rows, columns), f32)
    coded = shape((nvar * tiles + 1, 2 * SUB, LANES), i16)
    base_duals, base_incs, sent = [], [], []
    before = ends
    for i in range(pairs):
        last, force = pl.pallas_call(
            lambda *refs, i=i: prepare_adjoint_kernel(i, steps, nvar, tiles, *refs),
            out_shape=[shape((2, n, tiles, 2 * SUB, LANES), f32) for n in (nvar, steps)],
            in_specs=[SMEM] + [VMEM] * 4 + [ANY],
            out_specs=[VMEM] * 2,
            compiler_params=params(),
        )(obs_count, near, far, dual_obs, after[i], before)
        base_dual, base_inc, *payloads = pl.pallas_call(
            lambda *refs, i=i: adjoint_kernel(
                i, windows, spaces, steps, nvar, levels, tiles, *refs
            ),
            out_shape=[state, state] + [coded] * (windows - 1),
            in_specs=[VMEM] * 9,
            out_specs=[VMEM] * (2 + windows - 1),
            scratch_shapes=[
                pltpu.VMEM((2, steps, tiles, 4 * SUB, LANES), f32),
                pltpu.VMEM((2, 2, nvar, tiles, 4 * SUB, LANES), f32),
                pltpu.VMEM((2,) + coded.shape, i16),
            ],
            compiler_params=params(),
        )(mix, totals, wide_traj, last, force, ends, increment, model_rhs, dual_model)
        before = base_dual
        base_duals.append(base_dual)
        base_incs.append(base_inc)
        moving = {d: moved(payloads[d - 1], "window", d, around=True) for d in order}
        sent += [moving[d] for d in range(1, windows)]

    new_dual_model, new_increment = pl.pallas_call(
        lambda *refs: final_kernel(windows, nvar, levels, tiles, *refs),
        out_shape=[shape(dual_model.shape, f32), shape(increment.shape, f32)],
        in_specs=[VMEM] * (len(sent) + 2 * pairs + 1),
        out_specs=[VMEM] * 2,
        compiler_params=params(),
    )(*sent, *base_duals, *base_incs, totals)
    return new_dual_model, new_dual_obs, new_increment


def solution(mesh):
    placed = (
        P("members", None, None, None, "space", "window"),
        P(("members", "window"), None, None, "space", None),
        P(("members", "window"), None, None, "space", None),
        P(("members", "window"), None, None, "space", None),
        P(("members", "window"), None, None, "space", None),
        P(("members", "window"), None, None, "space", None),
        P(),
        P(("members", "window"), None, None),
        P(("members", "window"), None, None),
        P(("members", "window")),
    )
    return jax.shard_map(
        body,
        mesh=mesh,
        in_specs=placed,
        out_specs=(
            P(("members", "window"), None, None, "space", None),
            P(("members", "window"), None, None, "space", None),
            P(("members", "window"), None, None, "space", None),
        ),
        check_vma=False,
    )
```

```python
import jax
import jax.numpy as jnp
from jax import lax
from jax.experimental import pallas as pl
from jax.experimental.pallas import tpu as pltpu
from jax.sharding import PartitionSpec as P

LANES = 128
SUB = 8
HALF = SUB // 2
CODE_MAX = 32766.0
ROUNDER = 12582912.0

diffusion = 0.2
advection = 0.2
coupling_gain = 0.5
keep = 1.0 - 4.0 * diffusion
half_adv = 0.5 * advection

VMEM = pl.BlockSpec(memory_space=pltpu.VMEM)
SMEM = pl.BlockSpec(memory_space=pltpu.SMEM)
ANY = pl.BlockSpec(memory_space=pl.ANY)


def params(mib=24):
    return pltpu.CompilerParams(vmem_limit_bytes=mib * 1024 * 1024)


def lane_index():
    return lax.broadcasted_iota(jnp.int32, (SUB, LANES), 1)


def row_index():
    return lax.broadcasted_iota(jnp.int32, (SUB, LANES), 0)


def tiled(wide):
    short = -wide.shape[1] % LANES
    if short:
        wide = jnp.concatenate([wide, jnp.zeros((wide.shape[0], short), wide.dtype)], 1)
    return [wide[:, i : i + LANES] for i in range(0, wide.shape[1], LANES)]


def place(parts, rolled, lane):
    built = {}
    for key, tiles, first, width, target in parts:
        done = 0
        while done < width:
            a, b = first + done, target + done
            n = min(width - done, LANES - a % LANES, LANES - b % LANES)
            shift = (b - a) % LANES
            name = (key, a // LANES, shift)
            if name not in rolled:
                value = tiles[a // LANES]
                rolled[name] = pltpu.roll(value, shift, 1) if shift else value
            if b % LANES:
                built[b // LANES] = jnp.where(
                    lane >= b % LANES, rolled[name], built[b // LANES]
                )
            else:
                built[b // LANES] = rolled[name]
            done += n
    return [built[i] for i in range(len(built))]


def joined_halves(first, second):
    top = row_index()[:, :1] < HALF
    last = jnp.where(top, pltpu.roll(first, HALF, 0), second)
    start = jnp.where(top, first, pltpu.roll(second, HALF, 0))
    return last, start


def widened(own, near, far, odd, even):
    top = row_index() < HALF
    low, high = jnp.where(even, far, near), jnp.where(even, near, far)
    turned = pltpu.roll(own, HALF, 0)
    low = pltpu.roll(low, HALF, 0) if odd else low
    high = high if odd else pltpu.roll(high, HALF, 0)
    return jnp.where(top, low, turned), jnp.where(top, turned, high)


def row_codes(planes):
    lane = lax.broadcasted_iota(jnp.int32, planes[0][0].shape, 1)
    scales = jnp.zeros(planes[0][0].shape, jnp.float32)
    out = []
    for v, row in enumerate(planes):
        big = jnp.abs(row[0])
        for value in row[1:]:
            big = jnp.maximum(big, jnp.abs(value))
        big = jnp.max(big, axis=1, keepdims=True)
        power = jnp.clip(jnp.ceil(jnp.log2(jnp.maximum(big, 1e-30))), -90.0, 126.0)
        scales = jnp.where(lane == v, power, scales)
        gain = CODE_MAX * jnp.exp2(-power)
        for value in row:
            out.append((value * gain + ROUNDER) - ROUNDER)
    return out, scales


def shorts(value):
    return value.astype(jnp.int32).astype(jnp.int16)


def floats(value):
    return value.astype(jnp.int32).astype(jnp.float32)


def distances(windows):
    return sorted(range(1, windows), key=lambda d: -d * (windows - d))


def pack_kernel(ways, windows, steps, nvar, levels, part, var_ref, traj_ref, *outs):
    me = lax.axis_index("window")
    lane = lane_index()
    variance = var_ref[...]
    high = variance.astype(jnp.bfloat16).astype(jnp.float32)
    middle = (variance - high).astype(jnp.bfloat16).astype(jnp.float32)
    low = variance - high - middle
    split = high + pltpu.roll(middle, HALF, 0) + pltpu.roll(low, LANES // 2, 1)
    split = split.astype(jnp.bfloat16)

    for n, d in enumerate(ways):
        outs[n][outs[n].shape[0] - 1] = split
        target = lax.rem(me + d, windows)

        def variable(v, carry, n=n, target=target):
            for lev in range(levels):
                pieces = [
                    tiled(traj_ref[target, j, v, lev].astype(jnp.float32)) for j in range(steps)
                ]
                parts = [(j, pieces[j], 0, part, j * part) for j in range(steps)]
                placed = place(parts, {}, lane)
                for t, value in enumerate(placed):
                    outs[n][(v * levels + lev) * len(placed) + t] = value.astype(jnp.bfloat16)
            return carry

        lax.fori_loop(0, nvar, variable, 0, unroll=len(ways) == 1)


def even_place():
    return lax.rem(lax.axis_index("space"), 2) == 0


def level_codes(ref, lev, first=0):
    planes = [
        [ref[0, v, lev, :, t : t + LANES] for t in range(0, ref.shape[-1], LANES)]
        for v in range(first, ref.shape[1])
    ]
    values, scales = row_codes(planes)
    return values + [scales]


def half_code_kernel(*refs):
    sources, (near_ref, far_ref, own_ref) = refs[:-3], refs[-3:]
    even = even_place()

    def pair(i, carry):
        near, far = [], []
        for k, ref in enumerate(sources):
            skip = int(k == len(sources) - 1)
            coded = [level_codes(ref, 2 * i + odd, skip) for odd in range(2)]
            for n, (first, second) in enumerate(zip(*coded)):
                if k == 0:
                    own_ref[i, n] = shorts(jnp.concatenate([first, second], 0))
                last, start = joined_halves(first, second)
                near.append(jnp.where(even, last, start))
                far.append(jnp.where(even, start, last))
            if len(near) % 2:
                near.append(jnp.zeros((SUB, LANES), jnp.float32))
                far.append(jnp.zeros((SUB, LANES), jnp.float32))
        for tiles, ref in ((near, near_ref), (far, far_ref)):
            for n in range(0, len(tiles), 2):
                ref[i, n // 2] = shorts(jnp.concatenate(tiles[n : n + 2], 0))
        return carry

    lax.fori_loop(0, near_ref.shape[0], pair, 0)


def half_tile(ref, i, n):
    whole = floats(ref[i, n // 2])
    return whole[SUB:] if n % 2 else whole[:SUB]


def around_kernel(windows, nvar, levels, *refs):
    pieces, (own_ref, near_ref, far_ref) = refs[:windows], refs[windows : windows + 3]
    outs, total_ref = refs[windows + 3 : -1], refs[-1]
    me = lax.axis_index("window")
    even = even_place()
    total = jnp.zeros((SUB, LANES), jnp.float32)
    for d in range(windows):
        split = pieces[d][pieces[d].shape[0] - 1].astype(jnp.float32)
        here = split + pltpu.roll(split, HALF, 0) + pltpu.roll(split, LANES // 2, 1)
        total = total + jnp.where(lax.rem(me - d + windows, windows) <= me, here, 0.0)
    for v in range(nvar):
        for lev in range(levels):
            one = total[lev : lev + 1, v : v + 1]
            total_ref[v * levels + lev] = jnp.broadcast_to(one, (SUB, LANES))
    for i, out_ref in enumerate(outs):
        for n in range(own_ref.shape[1]):
            own = floats(own_ref[i, n])
            near, far = half_tile(near_ref, i, n), half_tile(far_ref, i, n)
            for odd in range(2):
                halves = widened(own[odd * SUB : (odd + 1) * SUB], near, far, odd, even)
                out_ref[odd, n] = shorts(jnp.concatenate(halves, 0))


def decoded(ref, i, first, nvar, tiles):
    scales = jnp.exp2(half_tile(ref, i, first + nvar * tiles)) * (1.0 / CODE_MAX)
    return [
        [half_tile(ref, i, first + v * tiles + t) * scales[:, v : v + 1] for t in range(tiles)]
        for v in range(nvar)
    ]


def is_quarter(j, v, steps):
    return 0 < j < steps - 1 and not (v == 0 and j + 1 > HALF // 2)


def far_base(steps, nvar, levels):
    base, total = {}, 0
    for j in range(steps):
        for v in range(nvar):
            base[j, v] = total
            total += levels // (4 if is_quarter(j, v, steps) else 2)
    return base, total


def joined_quarters(four):
    slot = row_index() // 2
    last, start = pltpu.roll(four[0], 2, 0), four[0]
    for n in range(1, 4):
        last = jnp.where(slot == n, pltpu.roll(four[n], (2 * n + 2) % SUB, 0), last)
        start = jnp.where(slot == n, pltpu.roll(four[n], 2 * n, 0), start)
    return last, start


def assemble_kernel(windows, steps, nvar, levels, part, *refs):
    pieces = refs[:windows]
    own_ref, near_ref, far_ref, stack_ref = refs[windows + 1 :]
    me = lax.axis_index("window")
    even = even_place()
    lane = lane_index()
    count = stack_ref.shape[1]
    packed_tiles = count // (nvar * levels)
    for d in range(windows):
        source = lax.rem(me - d + windows, windows)
        stack_ref[source] = pieces[d][:count]

    pairs = levels // 2
    base, _ = far_base(steps, nvar, levels)

    def variable(v):
        built = {}
        for lev in range(levels):
            plane = v * levels + lev
            sources = [
                [
                    stack_ref[w, plane * packed_tiles + t].astype(jnp.float32)
                    for t in range(packed_tiles)
                ]
                for w in range(windows)
            ]
            rolled = {}
            for j in range(steps):
                parts = [(w, sources[w], j * part, part, w * part) for w in range(windows)]
                built[j, lev] = place(parts, rolled, lane)
                own_ref[j, plane] = jnp.concatenate(built[j, lev], 1).astype(jnp.bfloat16)
        for j in range(steps):
            for i in range(pairs):
                halves = [joined_halves(a, b) for a, b in zip(built[j, 2 * i], built[j, 2 * i + 1])]
                last, start = (jnp.concatenate([h[k] for h in halves], 1) for k in range(2))
                near_ref[j, v * pairs + i] = jnp.where(even, last, start).astype(jnp.bfloat16)
                if not is_quarter(j, v, steps):
                    far_ref[base[j, v] + i] = jnp.where(even, start, last).astype(jnp.bfloat16)
            if is_quarter(j, v, steps):
                for q in range(levels // 4):
                    four = zip(*[built[j, 4 * q + n] for n in range(4)])
                    ends = [joined_quarters(tiles) for tiles in four]
                    last, start = (jnp.concatenate([e[k] for e in ends], 1) for k in range(2))
                    far_ref[base[j, v] + q] = jnp.where(even, start, last).astype(jnp.bfloat16)

    for v in range(nvar):
        variable(v)


def prepare_factor_kernel(
    steps, nvar, levels, tiles,
    count_ref, noise_ref, coupling_ref, dobs_ref, innov_ref, obs_ref, share_ref, mix_ref,
):
    cuts = [slice(t * LANES, (t + 1) * LANES) for t in range(tiles)]
    for v in range(nvar):
        for u in range(nvar):
            one = coupling_gain * coupling_ref[v : v + 1, u : u + 1]
            mix_ref[v, u] = jnp.broadcast_to(one, (SUB, LANES))
    for lev in range(levels):
        for j in range(steps):
            noise = jnp.full((SUB, LANES), noise_ref[0, j, lev])
            share = jnp.where(j < count_ref[0], 1.0, 0.0) / noise
            share_ref[lev, j] = share
            for t in range(tiles):
                gap = innov_ref[0, j, lev, :, cuts[t]] - noise * dobs_ref[0, j, lev, :, cuts[t]]
                obs_ref[lev, j, t] = gap * share


def prepare_tangent_kernel(nvar, levels, tiles, near_ref, far_ref, inc_ref, first_ref):
    even = even_place()
    blocks = [slice(0, SUB), slice(SUB, 2 * SUB)]
    cuts = [slice(t * LANES, (t + 1) * LANES) for t in range(tiles)]
    offset = -(-(nvar * tiles + 1) // 2) * 2
    for i in range(levels // 2):
        fields = [decoded(ref, i, offset, nvar, tiles) for ref in (near_ref, far_ref)]
        for odd in range(2):
            lev = 2 * i + odd
            for t in range(tiles):
                for v in range(nvar):
                    near, far = (side[v][t] for side in fields)
                    halves = widened(inc_ref[0, v, lev, :, cuts[t]], near, far, odd, even)
                    for b in range(2):
                        first_ref[lev, v, t, blocks[b], :] = halves[b]


def prepare_adjoint_kernel(
    i, steps, nvar, tiles, count_ref, near_ref, far_ref, dobs_ref, after_ref, *refs
):
    _, last_ref, force_ref = refs
    even = even_place()
    blocks = [slice(0, SUB), slice(SUB, 2 * SUB)]
    cuts = [slice(t * LANES, (t + 1) * LANES) for t in range(tiles)]
    seen = [jnp.where(j < count_ref[0], 1.0, 0.0) for j in range(steps)]
    offset = -(-(nvar * tiles + 1) // 2) * 2
    none = [[jnp.zeros((SUB, LANES), jnp.float32)] * tiles]
    forces = [none + decoded(ref, i, 2 * offset, steps - 1, tiles) for ref in (near_ref, far_ref)]
    for odd in range(2):
        scales = jnp.exp2(floats(after_ref[odd, nvar * tiles])) * (-1.0 / CODE_MAX)
        for t in range(tiles):
            for v in range(nvar):
                value = floats(after_ref[odd, v * tiles + t])
                last_ref[odd, v, t] = value * scales[:, v : v + 1]
            for j in range(steps):
                near, far = (side[j][t] for side in forces)
                halves = widened(dobs_ref[0, j, 2 * i + odd, :, cuts[t]], near, far, odd, even)
                for b in range(2):
                    force_ref[odd, j, t, blocks[b], :] = seen[j] * halves[b]


def from_north(line, lane):
    turned = [pltpu.roll(value, LANES - 1, 1) for value in line] * 2
    return [jnp.where(lane < LANES - 1, turned[t], turned[t + 1]) for t in range(len(line))]


def from_south(line, lane):
    turned = [pltpu.roll(value, 1, 1) for value in line]
    return [jnp.where(lane > 0, turned[t], turned[t - 1]) for t in range(len(line))]


def masked_last(line, lane):
    return line[:-1] + [jnp.where(lane < LANES - 1, line[-1], 0.0)]


def masked_first(line, lane):
    return [jnp.where(lane > 0, line[0], 0.0)] + line[1:]


def walls(spaces):
    row, place_x = row_index(), lax.axis_index("space")
    low = jnp.where((row == HALF) & (place_x == 0), 0.0, 1.0)
    high = jnp.where((row == HALF - 1) & (place_x == spaces - 1), 0.0, 1.0)

    def walled(block, east, west):
        if block == 0:
            return east, [low * value for value in west]
        return [high * value for value in east], west

    return walled


BLOCKS = [slice(SUB, 2 * SUB), slice(2 * SUB, 3 * SUB)]
UPS = [slice(b.start + 1, b.stop + 1) for b in BLOCKS]
DOWNS = [slice(b.start - 1, b.stop - 1) for b in BLOCKS]
MINE = slice(SUB + HALF, 2 * SUB + HALF)


def tangent_kernel(
    spaces, steps, nvar, levels, tiles,
    mix_ref, share_ref, obs_ref, own_ref, near_ref, far_ref, first_ref,
    ndo_ref, ends_ref, x_ref, s_ref,
):
    lane, row = lane_index(), row_index()
    even = even_place()
    top = row < HALF
    walled = walls(spaces)
    pairs = levels // 2
    cuts = [slice(t * LANES, (t + 1) * LANES) for t in range(tiles)]
    base, _ = far_base(steps, nvar, levels)

    for lev in range(levels):
        i, odd = lev // 2, lev % 2
        for j in range(steps):
            for v in range(nvar):
                for t in range(tiles):
                    own = own_ref[j, v * levels + lev, :, cuts[t]].astype(jnp.float32)
                    near = near_ref[j, v * pairs + i, :, cuts[t]].astype(jnp.float32)
                    quarter = is_quarter(j, v, steps)
                    far = far_ref[base[j, v] + lev // (4 if quarter else 2), :, cuts[t]]
                    far = far.astype(jnp.float32)
                    if quarter:
                        slot = 2 * (lev % 4)
                        low_far = pltpu.roll(far, (HALF - 2 - slot) % SUB, 0)
                        high_far = pltpu.roll(far, (HALF - slot) % SUB, 0)
                    else:
                        low_far = pltpu.roll(far, HALF, 0) if odd else far
                        high_far = far if odd else pltpu.roll(far, HALF, 0)
                    low_near = pltpu.roll(near, HALF, 0) if odd else near
                    high_near = near if odd else pltpu.roll(near, HALF, 0)
                    turned = pltpu.roll(own, HALF, 0)
                    low = jnp.where(even, low_far, low_near)
                    high = jnp.where(even, high_near, high_far)
                    x_ref[lev, j, v, t, :SUB, :] = jnp.where(top, low, turned)
                    x_ref[lev, j, v, t, SUB:, :] = jnp.where(top, turned, high)

    def pair(i, outer):
        for odd in range(2):
            for v in range(nvar):
                for t in range(tiles):
                    s_ref[odd, 0, v, t, SUB : 3 * SUB, :] = first_ref[2 * i + odd, v, t]

        def step(j, carry):
            now = lax.rem(j, 2)
            for odd in range(2):
                lev = 2 * i + odd
                for t in range(tiles):
                    image = share_ref[lev, j] * s_ref[odd, now, 0, t, MINE, :]
                    ndo_ref[0, j, lev, :, cuts[t]] = obs_ref[lev, j, t] - image
                for b in range(2):
                    part = slice(b * SUB, (b + 1) * SUB)
                    here, up, down = BLOCKS[b], UPS[b], DOWNS[b]
                    x = [[x_ref[lev, j, u, t, part, :] for t in range(tiles)] for u in range(nvar)]
                    ce = [diffusion - half_adv * value for value in x[0]]
                    cw = [diffusion + half_adv * value for value in x[0]]
                    ce, cw = walled(b, ce, cw)
                    cn = masked_last([diffusion - half_adv * value for value in x[1]], lane)
                    cs = masked_first([diffusion + half_adv * value for value in x[1]], lane)
                    s = [
                        [s_ref[odd, now, u, t, here, :] for t in range(tiles)] for u in range(nvar)
                    ]
                    xs = [[x[u][t] * s[u][t] for t in range(tiles)] for u in range(nvar)]
                    for v in range(nvar):
                        north, south = from_north(s[v], lane), from_south(s[v], lane)
                        for t in range(tiles):
                            fresh = keep * s[v][t] + ce[t] * s_ref[odd, now, v, t, up, :]
                            fresh = fresh + cw[t] * s_ref[odd, now, v, t, down, :]
                            fresh = fresh + cn[t] * north[t] + cs[t] * south[t]
                            for u in range(nvar):
                                fresh = fresh + mix_ref[v, u] * xs[u][t]
                            s_ref[odd, 1 - now, v, t, here, :] = fresh
            return carry

        lax.fori_loop(0, steps, step, 0)
        for odd in range(2):
            for v in range(nvar):
                for t in range(tiles):
                    ends_ref[2 * i + odd, v, t] = s_ref[odd, steps % 2, v, t, MINE, :]
        return outer

    lax.fori_loop(0, pairs, pair, 0)


def adjoint_kernel(
    i, windows, spaces, steps, nvar, levels, tiles,
    mix_ref, total_ref, x_ref, last_ref, force_ref, ends_ref, inc_ref, rhs_ref, dual_ref,
    ndm_ref, ninc_ref, *rest,
):
    payload_refs = rest[: windows - 1]
    x0_ref, a_ref, q_ref = rest[windows - 1 :]
    me = lax.axis_index("window")
    lane = lane_index()
    walled = walls(spaces)
    cuts = [slice(t * LANES, (t + 1) * LANES) for t in range(tiles)]

    for odd in range(2):
        lev = 2 * i + odd
        for t in range(tiles):
            for j in range(steps):
                x0_ref[odd, j, t, SUB : 3 * SUB, :] = x_ref[lev, j, 0, t]
            for v in range(nvar):
                a_ref[odd, 0, v, t, SUB : 3 * SUB, :] = last_ref[odd, v, t]

    def step(turn, carry):
        now = lax.rem(turn, 2)
        j = steps - 1 - turn
        for odd in range(2):
            lev = 2 * i + odd
            for b in range(2):
                part = slice(b * SUB, (b + 1) * SUB)
                here, up, down = BLOCKS[b], UPS[b], DOWNS[b]
                x = [[x_ref[lev, j, u, t, part, :] for t in range(tiles)] for u in range(nvar)]
                ce = [diffusion + half_adv * x0_ref[odd, j, t, up, :] for t in range(tiles)]
                cw = [diffusion - half_adv * x0_ref[odd, j, t, down, :] for t in range(tiles)]
                ce, cw = walled(b, ce, cw)
                cn = masked_first([diffusion + half_adv * value for value in x[1]], lane)
                cs = masked_last([diffusion - half_adv * value for value in x[1]], lane)
                a = [
                    [a_ref[odd, now, u, t, here, :] for t in range(tiles)] for u in range(nvar)
                ]
                for u in range(nvar):
                    north = from_north([cn[t] * a[u][t] for t in range(tiles)], lane)
                    south = from_south([cs[t] * a[u][t] for t in range(tiles)], lane)
                    for t in range(tiles):
                        fresh = keep * a[u][t] + ce[t] * a_ref[odd, now, u, t, up, :]
                        fresh = fresh + cw[t] * a_ref[odd, now, u, t, down, :]
                        fresh = fresh + north[t] + south[t]
                        pull = mix_ref[0, u] * a[0][t]
                        for v in range(1, nvar):
                            pull = pull + mix_ref[v, u] * a[v][t]
                        fresh = fresh + x[u][t] * pull
                        if u == 0:
                            fresh = fresh + force_ref[odd, j, t, part, :]
                        a_ref[odd, 1 - now, u, t, here, :] = fresh
        return carry

    lax.fori_loop(0, steps, step, 0)

    end = steps % 2
    coded = []
    for odd in range(2):
        lev = 2 * i + odd
        back, ahead = [], []
        for v in range(nvar):
            share = total_ref[v * levels + lev]
            tv, gv = [], []
            for t in range(tiles):
                term = a_ref[odd, end, v, t, MINE, :] - last_ref[odd, v, t, HALF : HALF + SUB, :]
                given = rhs_ref[0, v, lev, :, cuts[t]] - inc_ref[0, v, lev, :, cuts[t]]
                given = given + share * term
                ndm_ref[v, odd, :, cuts[t]] = -(dual_ref[0, v, lev, :, cuts[t]] + term)
                ninc_ref[v, odd, :, cuts[t]] = given
                tv.append(term)
                gv.append(given + ends_ref[lev, v, t])
            back.append(tv)
            ahead.append(gv)
        coded.append((row_codes(back), row_codes(ahead)))
    for kind in range(2):
        first, second = coded[0][kind], coded[1][kind]
        for n, (a, b) in enumerate(zip(first[0] + [first[1]], second[0] + [second[1]])):
            q_ref[kind, n] = shorts(jnp.concatenate([a, b], 0))
    for ref, d in zip(payload_refs, distances(windows)):
        ref[...] = q_ref[jnp.where(me + d >= windows, 0, 1)]


def final_kernel(windows, nvar, levels, tiles, *refs):
    pairs = levels // 2
    cut = pairs * (windows - 1)
    pieces, base_duals, base_incs = refs[:cut], refs[cut : cut + pairs], refs[cut + pairs : -3]
    total_ref, ndm_ref, ninc_ref = refs[-3:]
    me = lax.axis_index("window")
    cuts = [slice(t * LANES, (t + 1) * LANES) for t in range(tiles)]

    for i in range(pairs):
        tails = [None] * (nvar * tiles)
        heads = [None] * (nvar * tiles)
        for n, d in enumerate(distances(windows)):
            piece = pieces[i * (windows - 1) + n]
            later = d > me
            scales = jnp.exp2(floats(piece[nvar * tiles])) * (1.0 / CODE_MAX)
            for v in range(nvar):
                scale = scales[:, v : v + 1]
                for t in range(tiles):
                    k = v * tiles + t
                    value = floats(piece[k]) * scale
                    tail, head = jnp.where(later, value, 0.0), jnp.where(later, 0.0, value)
                    tails[k] = tails[k] + tail if n else tail
                    heads[k] = heads[k] + head if n else head
        for v in range(nvar):
            for odd in range(2):
                lev = 2 * i + odd
                share = total_ref[v * levels + lev]
                for t in range(tiles):
                    rows = slice(odd * SUB, (odd + 1) * SUB)
                    tail, head = tails[v * tiles + t][rows], heads[v * tiles + t][rows]
                    ndm_ref[0, v, lev, :, cuts[t]] = base_duals[i][v, odd, :, cuts[t]] - tail
                    ninc_ref[0, v, lev, :, cuts[t]] = (
                        base_incs[i][v, odd, :, cuts[t]] + head + share * tail
                    )


def moved(block, axis, distance, around=False):
    count = lax.axis_size(axis)
    route = [(i, (i + distance) % count) for i in range(count) if around or 0 <= i + distance < count]
    return lax.ppermute(block, axis, route)


def swaps(axis, first):
    route = []
    for i in range(first, lax.axis_size(axis) - 1, 2):
        route += [(i, i + 1), (i + 1, i)]
    return route


def swapped(block, axis, first):
    return lax.ppermute(block, axis, swaps(axis, first))


def body(
    trajectory,
    dual_model,
    increment,
    model_rhs,
    dual_obs,
    innovation,
    coupling,
    error_var,
    obs_var,
    obs_count,
):
    windows, spaces = lax.axis_size("window"), lax.axis_size("space")
    _, steps, nvar, levels, rows, part = trajectory.shape
    columns = dual_model.shape[-1]
    tiles = columns // LANES
    assert trajectory.shape[0] == windows and windows > 1 and rows == SUB and steps == HALF
    assert columns == tiles * LANES == windows * part and levels % 4 == 0
    pairs = levels // 2
    wide = -(-steps * part // LANES) * LANES
    bf16, f32, i16 = jnp.bfloat16, jnp.float32, jnp.int16

    def shape(dims, dtype):
        return jax.ShapeDtypeStruct(dims, dtype)

    block = shape((nvar * levels * wide // LANES + 1, rows, LANES), bf16)
    variances = jnp.pad(error_var[0].T, ((0, SUB - levels), (0, LANES - nvar)))

    def packed(ways):
        return pl.pallas_call(
            lambda *refs: pack_kernel(ways, windows, steps, nvar, levels, part, *refs),
            out_shape=[block] * len(ways),
            in_specs=[VMEM, VMEM],
            out_specs=[VMEM] * len(ways),
            compiler_params=params(),
        )(variances, trajectory)

    order = distances(windows)
    groups = [[d] for d in order] if windows <= 4 else [order]
    blocks = {}
    for group in groups:
        blocks.update(zip(group, packed(group)))
    arrived = {d: moved(blocks[d], "window", d, around=True) for d in order}
    arrived[0] = packed([0])[0]

    payload = shape((pairs, nvar * tiles + 1, 2 * SUB, LANES), i16)

    counts = [nvar, nvar, steps - 1]
    half_tiles = sum(-(-(count * tiles + 1) // 2) for count in counts)
    halves = shape((pairs, half_tiles, 2 * SUB, LANES), i16)
    near, far, dual = pl.pallas_call(
        half_code_kernel,
        out_shape=[halves, halves, payload],
        in_specs=[VMEM] * 3,
        out_specs=[VMEM] * 3,
        compiler_params=params(),
    )(dual_model, increment, dual_obs)
    far, near = swapped(far, "space", 1), swapped(near, "space", 0)

    blocks_here = [arrived[d] for d in range(windows)]
    *after, totals = pl.pallas_call(
        lambda *refs: around_kernel(windows, nvar, levels, *refs),
        out_shape=[shape((2,) + payload.shape[1:], i16)] * pairs
        + [shape((nvar * levels, rows, LANES), f32)],
        in_specs=[VMEM] * (windows + 3),
        out_specs=[VMEM] * (pairs + 1),
        compiler_params=params(),
    )(*blocks_here, dual, near, far)
    after = [moved(piece, "window", -1) for piece in after]

    obs, share, mix = pl.pallas_call(
        lambda *refs: prepare_factor_kernel(steps, nvar, levels, tiles, *refs),
        out_shape=[
            shape((levels, steps, tiles, SUB, LANES), f32),
            shape((levels, steps, SUB, LANES), f32),
            shape((nvar, nvar, SUB, LANES), f32),
        ],
        in_specs=[SMEM] * 2 + [VMEM] * 3,
        out_specs=[VMEM] * 3,
        compiler_params=params(),
    )(obs_count, obs_var, coupling, dual_obs, innovation)

    own, traj_near, traj_far = pl.pallas_call(
        lambda *refs: assemble_kernel(windows, steps, nvar, levels, part, *refs),
        out_shape=[
            shape((steps, nvar * levels, rows, columns), bf16),
            shape((steps, nvar * pairs, rows, columns), bf16),
            shape((far_base(steps, nvar, levels)[1], rows, columns), bf16),
        ],
        in_specs=[VMEM] * windows + [ANY],
        out_specs=[VMEM] * 3,
        scratch_shapes=[pltpu.VMEM((windows, block.shape[0] - 1, rows, LANES), bf16)],
        compiler_params=params(),
    )(*blocks_here, mix)
    traj_near, traj_far = swapped(traj_near, "space", 0), swapped(traj_far, "space", 1)

    first = pl.pallas_call(
        lambda *refs: prepare_tangent_kernel(nvar, levels, tiles, *refs),
        out_shape=shape((levels, nvar, tiles, 2 * SUB, LANES), f32),
        in_specs=[VMEM] * 3,
        out_specs=VMEM,
        compiler_params=params(),
    )(near, far, increment)
    new_dual_obs, ends, wide_traj = pl.pallas_call(
        lambda *refs: tangent_kernel(spaces, steps, nvar, levels, tiles, *refs),
        out_shape=[
            shape(dual_obs.shape, f32),
            shape((levels, nvar, tiles, SUB, LANES), f32),
            shape((levels, steps, nvar, tiles, 2 * SUB, LANES), f32),
        ],
        in_specs=[VMEM] * 7,
        out_specs=[VMEM] * 3,
        scratch_shapes=[pltpu.VMEM((2, 2, nvar, tiles, 4 * SUB, LANES), f32)],
        compiler_params=params(),
    )(mix, share, obs, own, traj_near, traj_far, first)

    state = shape((nvar, 2, rows, columns), f32)
    coded = shape((nvar * tiles + 1, 2 * SUB, LANES), i16)
    base_duals, base_incs, sent = [], [], []
    before = ends
    for i in range(pairs):
        last, force = pl.pallas_call(
            lambda *refs, i=i: prepare_adjoint_kernel(i, steps, nvar, tiles, *refs),
            out_shape=[shape((2, n, tiles, 2 * SUB, LANES), f32) for n in (nvar, steps)],
            in_specs=[SMEM] + [VMEM] * 4 + [ANY],
            out_specs=[VMEM] * 2,
            compiler_params=params(),
        )(obs_count, near, far, dual_obs, after[i], before)
        base_dual, base_inc, *payloads = pl.pallas_call(
            lambda *refs, i=i: adjoint_kernel(
                i, windows, spaces, steps, nvar, levels, tiles, *refs
            ),
            out_shape=[state, state] + [coded] * (windows - 1),
            in_specs=[VMEM] * 9,
            out_specs=[VMEM] * (2 + windows - 1),
            scratch_shapes=[
                pltpu.VMEM((2, steps, tiles, 4 * SUB, LANES), f32),
                pltpu.VMEM((2, 2, nvar, tiles, 4 * SUB, LANES), f32),
                pltpu.VMEM((2,) + coded.shape, i16),
            ],
            compiler_params=params(),
        )(mix, totals, wide_traj, last, force, ends, increment, model_rhs, dual_model)
        before = base_dual
        base_duals.append(base_dual)
        base_incs.append(base_inc)
        sent += [
            moved(piece, "window", d, around=True) for piece, d in zip(payloads, order)
        ]

    new_dual_model, new_increment = pl.pallas_call(
        lambda *refs: final_kernel(windows, nvar, levels, tiles, *refs),
        out_shape=[shape(dual_model.shape, f32), shape(increment.shape, f32)],
        in_specs=[VMEM] * (len(sent) + 2 * pairs + 1),
        out_specs=[VMEM] * 2,
        compiler_params=params(),
    )(*sent, *base_duals, *base_incs, totals)
    return new_dual_model, new_dual_obs, new_increment


def solution(mesh):
    placed = (
        P("members", None, None, None, "space", "window"),
        P(("members", "window"), None, None, "space", None),
        P(("members", "window"), None, None, "space", None),
        P(("members", "window"), None, None, "space", None),
        P(("members", "window"), None, None, "space", None),
        P(("members", "window"), None, None, "space", None),
        P(),
        P(("members", "window"), None, None),
        P(("members", "window"), None, None),
        P(("members", "window")),
    )
    return jax.shard_map(
        body,
        mesh=mesh,
        in_specs=placed,
        out_specs=(
            P(("members", "window"), None, None, "space", None),
            P(("members", "window"), None, None, "space", None),
            P(("members", "window"), None, None, "space", None),
        ),
        check_vma=False,
    )
```

```python
import jax
import jax.numpy as jnp
from jax import lax
from jax.experimental import pallas as pl
from jax.experimental.pallas import tpu as pltpu
from jax.sharding import PartitionSpec as P

LANES = 128
SUB = 8
HALF = SUB // 2
CODE_MAX = 32000.0
ROUNDER = 12582912.0

diffusion = 0.2
advection = 0.2
coupling_gain = 0.5
keep = 1.0 - 4.0 * diffusion
half_adv = 0.5 * advection

VMEM = pl.BlockSpec(memory_space=pltpu.VMEM)
SMEM = pl.BlockSpec(memory_space=pltpu.SMEM)
ANY = pl.BlockSpec(memory_space=pl.ANY)


def params(mib=24):
    return pltpu.CompilerParams(vmem_limit_bytes=mib * 1024 * 1024)


def lane_index():
    return lax.broadcasted_iota(jnp.int32, (SUB, LANES), 1)


def row_index():
    return lax.broadcasted_iota(jnp.int32, (SUB, LANES), 0)


def tiled(wide):
    short = -wide.shape[1] % LANES
    if short:
        wide = jnp.concatenate([wide, jnp.zeros((wide.shape[0], short), wide.dtype)], 1)
    return [wide[:, i : i + LANES] for i in range(0, wide.shape[1], LANES)]


def place(parts, rolled, lane):
    built = {}
    for key, tiles, first, width, target in parts:
        done = 0
        while done < width:
            a, b = first + done, target + done
            n = min(width - done, LANES - a % LANES, LANES - b % LANES)
            shift = (b - a) % LANES
            name = (key, a // LANES, shift)
            if name not in rolled:
                value = tiles[a // LANES]
                rolled[name] = pltpu.roll(value, shift, 1) if shift else value
            if b % LANES:
                built[b // LANES] = jnp.where(
                    lane >= b % LANES, rolled[name], built[b // LANES]
                )
            else:
                built[b // LANES] = rolled[name]
            done += n
    return [built[i] for i in range(len(built))]


def joined_halves(first, second):
    top = row_index()[:, :1] < HALF
    last = jnp.where(top, pltpu.roll(first, HALF, 0), second)
    start = jnp.where(top, first, pltpu.roll(second, HALF, 0))
    return last, start


def widened(own, near, far, odd, even):
    top = row_index() < HALF
    low, high = jnp.where(even, far, near), jnp.where(even, near, far)
    turned = pltpu.roll(own, HALF, 0)
    low = pltpu.roll(low, HALF, 0) if odd else low
    high = high if odd else pltpu.roll(high, HALF, 0)
    return jnp.where(top, low, turned), jnp.where(top, turned, high)


def row_codes(planes):
    lane = lax.broadcasted_iota(jnp.int32, planes[0][0].shape, 1)
    scales = jnp.zeros(planes[0][0].shape, jnp.float32)
    out = []
    for v, row in enumerate(planes):
        big = jnp.abs(row[0])
        for value in row[1:]:
            big = jnp.maximum(big, jnp.abs(value))
        big = jnp.max(big, axis=1, keepdims=True)
        power = jnp.clip(jnp.ceil(jnp.log2(jnp.maximum(big, 1e-30))), -90.0, 126.0)
        scales = jnp.where(lane == v, power, scales)
        gain = CODE_MAX * jnp.exp2(-power)
        for value in row:
            out.append((value * gain + ROUNDER) - ROUNDER)
    return out, scales


def shorts(value):
    return value.astype(jnp.int32).astype(jnp.int16)


def floats(value):
    return value.astype(jnp.int32).astype(jnp.float32)


def distances(windows):
    return sorted(range(1, windows), key=lambda d: -d * (windows - d))


def pack_kernel(ways, windows, steps, nvar, levels, part, var_ref, traj_ref, *outs):
    me = lax.axis_index("window")
    lane = lane_index()
    variance = var_ref[...]
    high = variance.astype(jnp.bfloat16).astype(jnp.float32)
    middle = (variance - high).astype(jnp.bfloat16).astype(jnp.float32)
    low = variance - high - middle
    split = high + pltpu.roll(middle, HALF, 0) + pltpu.roll(low, LANES // 2, 1)
    split = split.astype(jnp.bfloat16)

    for n, d in enumerate(ways):
        outs[n][outs[n].shape[0] - 1] = split
        target = lax.rem(me + d, windows)

        def variable(v, carry, n=n, target=target):
            for lev in range(levels):
                pieces = [
                    tiled(traj_ref[target, j, v, lev].astype(jnp.float32)) for j in range(steps)
                ]
                parts = [(j, pieces[j], 0, part, j * part) for j in range(steps)]
                placed = place(parts, {}, lane)
                for t, value in enumerate(placed):
                    outs[n][(v * levels + lev) * len(placed) + t] = value.astype(jnp.bfloat16)
            return carry

        lax.fori_loop(0, nvar, variable, 0, unroll=len(ways) == 1)


def even_place():
    return lax.rem(lax.axis_index("space"), 2) == 0


def level_codes(ref, lev, first=0):
    planes = [
        [ref[0, v, lev, :, t : t + LANES] for t in range(0, ref.shape[-1], LANES)]
        for v in range(first, ref.shape[1])
    ]
    values, scales = row_codes(planes)
    return values + [scales]


def half_code_kernel(*refs):
    sources, (near_ref, far_ref, own_ref) = refs[:-3], refs[-3:]
    even = even_place()

    def pair(i, carry):
        near, far = [], []
        for k, ref in enumerate(sources):
            skip = int(k == len(sources) - 1)
            coded = [level_codes(ref, 2 * i + odd, skip) for odd in range(2)]
            for n, (first, second) in enumerate(zip(*coded)):
                if k == 0:
                    own_ref[i, n] = shorts(jnp.concatenate([first, second], 0))
                last, start = joined_halves(first, second)
                near.append(jnp.where(even, last, start))
                far.append(jnp.where(even, start, last))
            if len(near) % 2:
                near.append(jnp.zeros((SUB, LANES), jnp.float32))
                far.append(jnp.zeros((SUB, LANES), jnp.float32))
        for tiles, ref in ((near, near_ref), (far, far_ref)):
            for n in range(0, len(tiles), 2):
                ref[i, n // 2] = shorts(jnp.concatenate(tiles[n : n + 2], 0))
        return carry

    lax.fori_loop(0, near_ref.shape[0], pair, 0)


def half_tile(ref, i, n):
    whole = floats(ref[i, n // 2])
    return whole[SUB:] if n % 2 else whole[:SUB]


def around_kernel(windows, nvar, levels, *refs):
    pieces, (own_ref, near_ref, far_ref) = refs[:windows], refs[windows : windows + 3]
    outs, total_ref = refs[windows + 3 : -1], refs[-1]
    me = lax.axis_index("window")
    even = even_place()
    total = jnp.zeros((SUB, LANES), jnp.float32)
    for d in range(windows):
        split = pieces[d][pieces[d].shape[0] - 1].astype(jnp.float32)
        here = split + pltpu.roll(split, HALF, 0) + pltpu.roll(split, LANES // 2, 1)
        total = total + jnp.where(lax.rem(me - d + windows, windows) <= me, here, 0.0)
    for v in range(nvar):
        for lev in range(levels):
            one = total[lev : lev + 1, v : v + 1]
            total_ref[v * levels + lev] = jnp.broadcast_to(one, (SUB, LANES))
    for i, out_ref in enumerate(outs):
        for n in range(own_ref.shape[1]):
            own = floats(own_ref[i, n])
            near, far = half_tile(near_ref, i, n), half_tile(far_ref, i, n)
            for odd in range(2):
                halves = widened(own[odd * SUB : (odd + 1) * SUB], near, far, odd, even)
                out_ref[odd, n] = shorts(jnp.concatenate(halves, 0))


def decoded(ref, i, first, nvar, tiles):
    scales = jnp.exp2(half_tile(ref, i, first + nvar * tiles)) * (1.0 / CODE_MAX)
    return [
        [half_tile(ref, i, first + v * tiles + t) * scales[:, v : v + 1] for t in range(tiles)]
        for v in range(nvar)
    ]


def is_quarter(j, v, steps):
    return 0 < j < steps - 1 and not (v == 0 and j + 1 > HALF // 2)


def far_base(steps, nvar, levels):
    base, total = {}, 0
    for j in range(steps):
        for v in range(nvar):
            base[j, v] = total
            total += levels // (4 if is_quarter(j, v, steps) else 2)
    return base, total


def joined_quarters(four):
    slot = row_index() // 2
    last, start = pltpu.roll(four[0], 2, 0), four[0]
    for n in range(1, 4):
        last = jnp.where(slot == n, pltpu.roll(four[n], (2 * n + 2) % SUB, 0), last)
        start = jnp.where(slot == n, pltpu.roll(four[n], 2 * n, 0), start)
    return last, start


def assemble_kernel(windows, steps, nvar, levels, part, *refs):
    pieces = refs[:windows]
    own_ref, near_ref, far_ref, stack_ref = refs[windows + 1 :]
    me = lax.axis_index("window")
    even = even_place()
    lane = lane_index()
    count = stack_ref.shape[1]
    packed_tiles = count // (nvar * levels)
    for d in range(windows):
        source = lax.rem(me - d + windows, windows)
        stack_ref[source] = pieces[d][:count]

    pairs = levels // 2
    base, _ = far_base(steps, nvar, levels)

    def variable(v):
        built = {}
        for lev in range(levels):
            plane = v * levels + lev
            sources = [
                [
                    stack_ref[w, plane * packed_tiles + t].astype(jnp.float32)
                    for t in range(packed_tiles)
                ]
                for w in range(windows)
            ]
            rolled = {}
            for j in range(steps):
                parts = [(w, sources[w], j * part, part, w * part) for w in range(windows)]
                built[j, lev] = place(parts, rolled, lane)
                own_ref[j, plane] = jnp.concatenate(built[j, lev], 1).astype(jnp.bfloat16)
        for j in range(steps):
            for i in range(pairs):
                halves = [joined_halves(a, b) for a, b in zip(built[j, 2 * i], built[j, 2 * i + 1])]
                last, start = (jnp.concatenate([h[k] for h in halves], 1) for k in range(2))
                near_ref[j, v * pairs + i] = jnp.where(even, last, start).astype(jnp.bfloat16)
                if not is_quarter(j, v, steps):
                    far_ref[base[j, v] + i] = jnp.where(even, start, last).astype(jnp.bfloat16)
            if is_quarter(j, v, steps):
                for q in range(levels // 4):
                    four = zip(*[built[j, 4 * q + n] for n in range(4)])
                    ends = [joined_quarters(tiles) for tiles in four]
                    last, start = (jnp.concatenate([e[k] for e in ends], 1) for k in range(2))
                    far_ref[base[j, v] + q] = jnp.where(even, start, last).astype(jnp.bfloat16)

    for v in range(nvar):
        variable(v)


def prepare_factor_kernel(
    steps, nvar, levels, tiles,
    count_ref, noise_ref, coupling_ref, dobs_ref, innov_ref, obs_ref, share_ref, mix_ref,
):
    cuts = [slice(t * LANES, (t + 1) * LANES) for t in range(tiles)]
    for v in range(nvar):
        for u in range(nvar):
            one = coupling_gain * coupling_ref[v : v + 1, u : u + 1]
            mix_ref[v, u] = jnp.broadcast_to(one, (SUB, LANES))
    for lev in range(levels):
        for j in range(steps):
            noise = jnp.full((SUB, LANES), noise_ref[0, j, lev])
            share = jnp.where(j < count_ref[0], 1.0, 0.0) / noise
            share_ref[lev, j] = share
            for t in range(tiles):
                gap = innov_ref[0, j, lev, :, cuts[t]] - noise * dobs_ref[0, j, lev, :, cuts[t]]
                obs_ref[lev, j, t] = gap * share


def prepare_tangent_kernel(nvar, levels, tiles, near_ref, far_ref, inc_ref, first_ref):
    even = even_place()
    blocks = [slice(0, SUB), slice(SUB, 2 * SUB)]
    cuts = [slice(t * LANES, (t + 1) * LANES) for t in range(tiles)]
    offset = -(-(nvar * tiles + 1) // 2) * 2
    for i in range(levels // 2):
        fields = [decoded(ref, i, offset, nvar, tiles) for ref in (near_ref, far_ref)]
        for odd in range(2):
            lev = 2 * i + odd
            for t in range(tiles):
                for v in range(nvar):
                    near, far = (side[v][t] for side in fields)
                    halves = widened(inc_ref[0, v, lev, :, cuts[t]], near, far, odd, even)
                    for b in range(2):
                        first_ref[lev, v, t, blocks[b], :] = halves[b]


def prepare_adjoint_kernel(
    i, steps, nvar, tiles, count_ref, near_ref, far_ref, dobs_ref, after_ref, *refs
):
    _, last_ref, force_ref = refs
    even = even_place()
    blocks = [slice(0, SUB), slice(SUB, 2 * SUB)]
    cuts = [slice(t * LANES, (t + 1) * LANES) for t in range(tiles)]
    seen = [jnp.where(j < count_ref[0], 1.0, 0.0) for j in range(steps)]
    offset = -(-(nvar * tiles + 1) // 2) * 2
    none = [[jnp.zeros((SUB, LANES), jnp.float32)] * tiles]
    forces = [none + decoded(ref, i, 2 * offset, steps - 1, tiles) for ref in (near_ref, far_ref)]
    for odd in range(2):
        scales = jnp.exp2(floats(after_ref[odd, nvar * tiles])) * (-1.0 / CODE_MAX)
        for t in range(tiles):
            for v in range(nvar):
                value = floats(after_ref[odd, v * tiles + t])
                last_ref[odd, v, t] = value * scales[:, v : v + 1]
            for j in range(steps):
                near, far = (side[j][t] for side in forces)
                halves = widened(dobs_ref[0, j, 2 * i + odd, :, cuts[t]], near, far, odd, even)
                for b in range(2):
                    force_ref[odd, j, t, blocks[b], :] = seen[j] * halves[b]


def from_north(line, lane):
    turned = [pltpu.roll(value, LANES - 1, 1) for value in line] * 2
    return [jnp.where(lane < LANES - 1, turned[t], turned[t + 1]) for t in range(len(line))]


def from_south(line, lane):
    turned = [pltpu.roll(value, 1, 1) for value in line]
    return [jnp.where(lane > 0, turned[t], turned[t - 1]) for t in range(len(line))]


def masked_last(line, lane):
    return line[:-1] + [jnp.where(lane < LANES - 1, line[-1], 0.0)]


def masked_first(line, lane):
    return [jnp.where(lane > 0, line[0], 0.0)] + line[1:]


def walls(spaces):
    row, place_x = row_index(), lax.axis_index("space")
    low = jnp.where((row == HALF) & (place_x == 0), 0.0, 1.0)
    high = jnp.where((row == HALF - 1) & (place_x == spaces - 1), 0.0, 1.0)

    def walled(block, east, west):
        if block == 0:
            return east, [low * value for value in west]
        return [high * value for value in east], west

    return walled


BLOCKS = [slice(SUB, 2 * SUB), slice(2 * SUB, 3 * SUB)]
UPS = [slice(b.start + 1, b.stop + 1) for b in BLOCKS]
DOWNS = [slice(b.start - 1, b.stop - 1) for b in BLOCKS]
MINE = slice(SUB + HALF, 2 * SUB + HALF)


def tangent_kernel(
    spaces, steps, nvar, levels, tiles,
    mix_ref, share_ref, obs_ref, own_ref, near_ref, far_ref, first_ref,
    ndo_ref, ends_ref, x_ref, s_ref,
):
    lane, row = lane_index(), row_index()
    even = even_place()
    top = row < HALF
    walled = walls(spaces)
    pairs = levels // 2
    cuts = [slice(t * LANES, (t + 1) * LANES) for t in range(tiles)]
    base, _ = far_base(steps, nvar, levels)

    for lev in range(levels):
        i, odd = lev // 2, lev % 2
        for j in range(steps):
            for v in range(nvar):
                for t in range(tiles):
                    own = own_ref[j, v * levels + lev, :, cuts[t]].astype(jnp.float32)
                    near = near_ref[j, v * pairs + i, :, cuts[t]].astype(jnp.float32)
                    quarter = is_quarter(j, v, steps)
                    far = far_ref[base[j, v] + lev // (4 if quarter else 2), :, cuts[t]]
                    far = far.astype(jnp.float32)
                    if quarter:
                        slot = 2 * (lev % 4)
                        low_far = pltpu.roll(far, (HALF - 2 - slot) % SUB, 0)
                        high_far = pltpu.roll(far, (HALF - slot) % SUB, 0)
                    else:
                        low_far = pltpu.roll(far, HALF, 0) if odd else far
                        high_far = far if odd else pltpu.roll(far, HALF, 0)
                    low_near = pltpu.roll(near, HALF, 0) if odd else near
                    high_near = near if odd else pltpu.roll(near, HALF, 0)
                    turned = pltpu.roll(own, HALF, 0)
                    low = jnp.where(even, low_far, low_near)
                    high = jnp.where(even, high_near, high_far)
                    x_ref[lev, j, v, t, :SUB, :] = jnp.where(top, low, turned)
                    x_ref[lev, j, v, t, SUB:, :] = jnp.where(top, turned, high)

    def pair(i, outer):
        for odd in range(2):
            for v in range(nvar):
                for t in range(tiles):
                    s_ref[odd, 0, v, t, SUB : 3 * SUB, :] = first_ref[2 * i + odd, v, t]

        for j in range(steps):
            now = j % 2
            for odd in range(2):
                lev = 2 * i + odd
                for t in range(tiles):
                    image = share_ref[lev, j] * s_ref[odd, now, 0, t, MINE, :]
                    ndo_ref[0, j, lev, :, cuts[t]] = obs_ref[lev, j, t] - image
                for b in range(2):
                    part = slice(b * SUB, (b + 1) * SUB)
                    here, up, down = BLOCKS[b], UPS[b], DOWNS[b]
                    x = [[x_ref[lev, j, u, t, part, :] for t in range(tiles)] for u in range(nvar)]
                    ce = [diffusion - half_adv * value for value in x[0]]
                    cw = [diffusion + half_adv * value for value in x[0]]
                    ce, cw = walled(b, ce, cw)
                    cn = masked_last([diffusion - half_adv * value for value in x[1]], lane)
                    cs = masked_first([diffusion + half_adv * value for value in x[1]], lane)
                    s = [
                        [s_ref[odd, now, u, t, here, :] for t in range(tiles)] for u in range(nvar)
                    ]
                    xs = [[x[u][t] * s[u][t] for t in range(tiles)] for u in range(nvar)]
                    for v in range(nvar):
                        north, south = from_north(s[v], lane), from_south(s[v], lane)
                        for t in range(tiles):
                            fresh = keep * s[v][t] + ce[t] * s_ref[odd, now, v, t, up, :]
                            fresh = fresh + cw[t] * s_ref[odd, now, v, t, down, :]
                            fresh = fresh + cn[t] * north[t] + cs[t] * south[t]
                            for u in range(nvar):
                                fresh = fresh + mix_ref[v, u] * xs[u][t]
                            s_ref[odd, 1 - now, v, t, here, :] = fresh
        for odd in range(2):
            for v in range(nvar):
                for t in range(tiles):
                    ends_ref[2 * i + odd, v, t] = s_ref[odd, steps % 2, v, t, MINE, :]
        return outer

    lax.fori_loop(0, pairs, pair, 0)


def adjoint_kernel(
    i, windows, spaces, steps, nvar, levels, tiles,
    mix_ref, total_ref, x_ref, last_ref, force_ref, ends_ref, inc_ref, rhs_ref, dual_ref,
    ndm_ref, ninc_ref, *rest,
):
    payload_refs = rest[: windows - 1]
    x0_ref, a_ref, q_ref = rest[windows - 1 :]
    me = lax.axis_index("window")
    lane = lane_index()
    walled = walls(spaces)
    cuts = [slice(t * LANES, (t + 1) * LANES) for t in range(tiles)]

    for odd in range(2):
        lev = 2 * i + odd
        for t in range(tiles):
            for j in range(steps):
                x0_ref[odd, j, t, SUB : 3 * SUB, :] = x_ref[lev, j, 0, t]
            for v in range(nvar):
                a_ref[odd, 0, v, t, SUB : 3 * SUB, :] = last_ref[odd, v, t]

    for turn in range(steps):
        now = turn % 2
        j = steps - 1 - turn
        for odd in range(2):
            lev = 2 * i + odd
            for b in range(2):
                part = slice(b * SUB, (b + 1) * SUB)
                here, up, down = BLOCKS[b], UPS[b], DOWNS[b]
                x = [[x_ref[lev, j, u, t, part, :] for t in range(tiles)] for u in range(nvar)]
                ce = [diffusion + half_adv * x0_ref[odd, j, t, up, :] for t in range(tiles)]
                cw = [diffusion - half_adv * x0_ref[odd, j, t, down, :] for t in range(tiles)]
                ce, cw = walled(b, ce, cw)
                cn = masked_first([diffusion + half_adv * value for value in x[1]], lane)
                cs = masked_last([diffusion - half_adv * value for value in x[1]], lane)
                a = [
                    [a_ref[odd, now, u, t, here, :] for t in range(tiles)] for u in range(nvar)
                ]
                for u in range(nvar):
                    north = from_north([cn[t] * a[u][t] for t in range(tiles)], lane)
                    south = from_south([cs[t] * a[u][t] for t in range(tiles)], lane)
                    for t in range(tiles):
                        fresh = keep * a[u][t] + ce[t] * a_ref[odd, now, u, t, up, :]
                        fresh = fresh + cw[t] * a_ref[odd, now, u, t, down, :]
                        fresh = fresh + north[t] + south[t]
                        pull = mix_ref[0, u] * a[0][t]
                        for v in range(1, nvar):
                            pull = pull + mix_ref[v, u] * a[v][t]
                        fresh = fresh + x[u][t] * pull
                        if u == 0:
                            fresh = fresh + force_ref[odd, j, t, part, :]
                        a_ref[odd, 1 - now, u, t, here, :] = fresh
    end = steps % 2
    coded = []
    for odd in range(2):
        lev = 2 * i + odd
        back, ahead = [], []
        for v in range(nvar):
            share = total_ref[v * levels + lev]
            tv, gv = [], []
            for t in range(tiles):
                term = a_ref[odd, end, v, t, MINE, :] - last_ref[odd, v, t, HALF : HALF + SUB, :]
                given = rhs_ref[0, v, lev, :, cuts[t]] - inc_ref[0, v, lev, :, cuts[t]]
                given = given + share * term
                ndm_ref[v, odd, :, cuts[t]] = -(dual_ref[0, v, lev, :, cuts[t]] + term)
                ninc_ref[v, odd, :, cuts[t]] = given
                tv.append(term)
                gv.append(given + ends_ref[lev, v, t])
            back.append(tv)
            ahead.append(gv)
        coded.append((row_codes(back), row_codes(ahead)))
    for kind in range(2):
        first, second = coded[0][kind], coded[1][kind]
        for n, (a, b) in enumerate(zip(first[0] + [first[1]], second[0] + [second[1]])):
            q_ref[kind, n] = shorts(jnp.concatenate([a, b], 0))
    for ref, d in zip(payload_refs, distances(windows)):
        ref[...] = q_ref[jnp.where(me + d >= windows, 0, 1)]


def final_kernel(windows, nvar, levels, tiles, *refs):
    pairs = levels // 2
    cut = pairs * (windows - 1)
    pieces, base_duals, base_incs = refs[:cut], refs[cut : cut + pairs], refs[cut + pairs : -3]
    total_ref, ndm_ref, ninc_ref = refs[-3:]
    me = lax.axis_index("window")
    cuts = [slice(t * LANES, (t + 1) * LANES) for t in range(tiles)]

    for i in range(pairs):
        tails = [None] * (nvar * tiles)
        heads = [None] * (nvar * tiles)
        for n, d in enumerate(distances(windows)):
            piece = pieces[i * (windows - 1) + n]
            later = d > me
            scales = jnp.exp2(floats(piece[nvar * tiles])) * (1.0 / CODE_MAX)
            for v in range(nvar):
                scale = scales[:, v : v + 1]
                for t in range(tiles):
                    k = v * tiles + t
                    value = floats(piece[k]) * scale
                    tail, head = jnp.where(later, value, 0.0), jnp.where(later, 0.0, value)
                    tails[k] = tails[k] + tail if n else tail
                    heads[k] = heads[k] + head if n else head
        for v in range(nvar):
            for odd in range(2):
                lev = 2 * i + odd
                share = total_ref[v * levels + lev]
                for t in range(tiles):
                    rows = slice(odd * SUB, (odd + 1) * SUB)
                    tail, head = tails[v * tiles + t][rows], heads[v * tiles + t][rows]
                    ndm_ref[0, v, lev, :, cuts[t]] = base_duals[i][v, odd, :, cuts[t]] - tail
                    ninc_ref[0, v, lev, :, cuts[t]] = (
                        base_incs[i][v, odd, :, cuts[t]] + head + share * tail
                    )


def moved(block, axis, distance, around=False):
    count = lax.axis_size(axis)
    route = [(i, (i + distance) % count) for i in range(count) if around or 0 <= i + distance < count]
    return lax.ppermute(block, axis, route)


def swaps(axis, first):
    route = []
    for i in range(first, lax.axis_size(axis) - 1, 2):
        route += [(i, i + 1), (i + 1, i)]
    return route


def swapped(block, axis, first):
    return lax.ppermute(block, axis, swaps(axis, first))


def body(
    trajectory,
    dual_model,
    increment,
    model_rhs,
    dual_obs,
    innovation,
    coupling,
    error_var,
    obs_var,
    obs_count,
):
    windows, spaces = lax.axis_size("window"), lax.axis_size("space")
    _, steps, nvar, levels, rows, part = trajectory.shape
    columns = dual_model.shape[-1]
    tiles = columns // LANES
    assert trajectory.shape[0] == windows and windows > 1 and rows == SUB and steps == HALF
    assert columns == tiles * LANES == windows * part and levels % 4 == 0
    pairs = levels // 2
    wide = -(-steps * part // LANES) * LANES
    bf16, f32, i16 = jnp.bfloat16, jnp.float32, jnp.int16

    def shape(dims, dtype):
        return jax.ShapeDtypeStruct(dims, dtype)

    block = shape((nvar * levels * wide // LANES + 1, rows, LANES), bf16)
    variances = jnp.pad(error_var[0].T, ((0, SUB - levels), (0, LANES - nvar)))

    def packed(ways):
        return pl.pallas_call(
            lambda *refs: pack_kernel(ways, windows, steps, nvar, levels, part, *refs),
            out_shape=[block] * len(ways),
            in_specs=[VMEM, VMEM],
            out_specs=[VMEM] * len(ways),
            compiler_params=params(),
        )(variances, trajectory)

    order = distances(windows)
    groups = [[d] for d in order] if windows <= 4 else [order]
    blocks = {}
    for group in groups:
        blocks.update(zip(group, packed(group)))
    arrived = {d: moved(blocks[d], "window", d, around=True) for d in order}
    arrived[0] = packed([0])[0]

    payload = shape((pairs, nvar * tiles + 1, 2 * SUB, LANES), i16)

    counts = [nvar, nvar, steps - 1]
    half_tiles = sum(-(-(count * tiles + 1) // 2) for count in counts)
    halves = shape((pairs, half_tiles, 2 * SUB, LANES), i16)
    near, far, dual = pl.pallas_call(
        half_code_kernel,
        out_shape=[halves, halves, payload],
        in_specs=[VMEM] * 3,
        out_specs=[VMEM] * 3,
        compiler_params=params(),
    )(dual_model, increment, dual_obs)
    far, near = swapped(far, "space", 1), swapped(near, "space", 0)

    blocks_here = [arrived[d] for d in range(windows)]
    *after, totals = pl.pallas_call(
        lambda *refs: around_kernel(windows, nvar, levels, *refs),
        out_shape=[shape((2,) + payload.shape[1:], i16)] * pairs
        + [shape((nvar * levels, rows, LANES), f32)],
        in_specs=[VMEM] * (windows + 3),
        out_specs=[VMEM] * (pairs + 1),
        compiler_params=params(),
    )(*blocks_here, dual, near, far)
    after = [moved(piece, "window", -1) for piece in after]

    obs, share, mix = pl.pallas_call(
        lambda *refs: prepare_factor_kernel(steps, nvar, levels, tiles, *refs),
        out_shape=[
            shape((levels, steps, tiles, SUB, LANES), f32),
            shape((levels, steps, SUB, LANES), f32),
            shape((nvar, nvar, SUB, LANES), f32),
        ],
        in_specs=[SMEM] * 2 + [VMEM] * 3,
        out_specs=[VMEM] * 3,
        compiler_params=params(),
    )(obs_count, obs_var, coupling, dual_obs, innovation)

    own, traj_near, traj_far = pl.pallas_call(
        lambda *refs: assemble_kernel(windows, steps, nvar, levels, part, *refs),
        out_shape=[
            shape((steps, nvar * levels, rows, columns), bf16),
            shape((steps, nvar * pairs, rows, columns), bf16),
            shape((far_base(steps, nvar, levels)[1], rows, columns), bf16),
        ],
        in_specs=[VMEM] * windows + [ANY],
        out_specs=[VMEM] * 3,
        scratch_shapes=[pltpu.VMEM((windows, block.shape[0] - 1, rows, LANES), bf16)],
        compiler_params=params(),
    )(*blocks_here, mix)
    traj_near, traj_far = swapped(traj_near, "space", 0), swapped(traj_far, "space", 1)

    first = pl.pallas_call(
        lambda *refs: prepare_tangent_kernel(nvar, levels, tiles, *refs),
        out_shape=shape((levels, nvar, tiles, 2 * SUB, LANES), f32),
        in_specs=[VMEM] * 3,
        out_specs=VMEM,
        compiler_params=params(),
    )(near, far, increment)
    new_dual_obs, ends, wide_traj = pl.pallas_call(
        lambda *refs: tangent_kernel(spaces, steps, nvar, levels, tiles, *refs),
        out_shape=[
            shape(dual_obs.shape, f32),
            shape((levels, nvar, tiles, SUB, LANES), f32),
            shape((levels, steps, nvar, tiles, 2 * SUB, LANES), f32),
        ],
        in_specs=[VMEM] * 7,
        out_specs=[VMEM] * 3,
        scratch_shapes=[pltpu.VMEM((2, 2, nvar, tiles, 4 * SUB, LANES), f32)],
        compiler_params=params(),
    )(mix, share, obs, own, traj_near, traj_far, first)

    state = shape((nvar, 2, rows, columns), f32)
    coded = shape((nvar * tiles + 1, 2 * SUB, LANES), i16)
    base_duals, base_incs, sent = [], [], []
    before = ends
    for i in range(pairs):
        last, force = pl.pallas_call(
            lambda *refs, i=i: prepare_adjoint_kernel(i, steps, nvar, tiles, *refs),
            out_shape=[shape((2, n, tiles, 2 * SUB, LANES), f32) for n in (nvar, steps)],
            in_specs=[SMEM] + [VMEM] * 4 + [ANY],
            out_specs=[VMEM] * 2,
            compiler_params=params(),
        )(obs_count, near, far, dual_obs, after[i], before)
        base_dual, base_inc, *payloads = pl.pallas_call(
            lambda *refs, i=i: adjoint_kernel(
                i, windows, spaces, steps, nvar, levels, tiles, *refs
            ),
            out_shape=[state, state] + [coded] * (windows - 1),
            in_specs=[VMEM] * 9,
            out_specs=[VMEM] * (2 + windows - 1),
            scratch_shapes=[
                pltpu.VMEM((2, steps, tiles, 4 * SUB, LANES), f32),
                pltpu.VMEM((2, 2, nvar, tiles, 4 * SUB, LANES), f32),
                pltpu.VMEM((2,) + coded.shape, i16),
            ],
            compiler_params=params(),
        )(mix, totals, wide_traj, last, force, ends, increment, model_rhs, dual_model)
        before = base_dual
        base_duals.append(base_dual)
        base_incs.append(base_inc)
        sent += [
            moved(piece, "window", d, around=True) for piece, d in zip(payloads, order)
        ]

    new_dual_model, new_increment = pl.pallas_call(
        lambda *refs: final_kernel(windows, nvar, levels, tiles, *refs),
        out_shape=[shape(dual_model.shape, f32), shape(increment.shape, f32)],
        in_specs=[VMEM] * (len(sent) + 2 * pairs + 1),
        out_specs=[VMEM] * 2,
        compiler_params=params(),
    )(*sent, *base_duals, *base_incs, totals)
    return new_dual_model, new_dual_obs, new_increment


def solution(mesh):
    placed = (
        P("members", None, None, None, "space", "window"),
        P(("members", "window"), None, None, "space", None),
        P(("members", "window"), None, None, "space", None),
        P(("members", "window"), None, None, "space", None),
        P(("members", "window"), None, None, "space", None),
        P(("members", "window"), None, None, "space", None),
        P(),
        P(("members", "window"), None, None),
        P(("members", "window"), None, None),
        P(("members", "window")),
    )
    return jax.shard_map(
        body,
        mesh=mesh,
        in_specs=placed,
        out_specs=(
            P(("members", "window"), None, None, "space", None),
            P(("members", "window"), None, None, "space", None),
            P(("members", "window"), None, None, "space", None),
        ),
        check_vma=False,
    )
```

```python
import jax
import jax.numpy as jnp
from jax import lax
from jax.experimental import pallas as pl
from jax.experimental.pallas import tpu as pltpu
from jax.sharding import PartitionSpec as P

LANES = 128
SUB = 8
HALF = SUB // 2
CODE_MAX = 32000.0
ROUNDER = 12582912.0

diffusion = 0.2
advection = 0.2
coupling_gain = 0.5
keep = 1.0 - 4.0 * diffusion
half_adv = 0.5 * advection

VMEM = pl.BlockSpec(memory_space=pltpu.VMEM)
SMEM = pl.BlockSpec(memory_space=pltpu.SMEM)
ANY = pl.BlockSpec(memory_space=pl.ANY)


def params(mib=24):
    return pltpu.CompilerParams(vmem_limit_bytes=mib * 1024 * 1024)


def lane_index():
    return lax.broadcasted_iota(jnp.int32, (SUB, LANES), 1)


def row_index():
    return lax.broadcasted_iota(jnp.int32, (SUB, LANES), 0)


def tiled(wide):
    short = -wide.shape[1] % LANES
    if short:
        wide = jnp.concatenate([wide, jnp.zeros((wide.shape[0], short), wide.dtype)], 1)
    return [wide[:, i : i + LANES] for i in range(0, wide.shape[1], LANES)]


def place(parts, rolled, lane):
    built = {}
    for key, tiles, first, width, target in parts:
        done = 0
        while done < width:
            a, b = first + done, target + done
            n = min(width - done, LANES - a % LANES, LANES - b % LANES)
            shift = (b - a) % LANES
            name = (key, a // LANES, shift)
            if name not in rolled:
                value = tiles[a // LANES]
                rolled[name] = pltpu.roll(value, shift, 1) if shift else value
            if b % LANES:
                built[b // LANES] = jnp.where(
                    lane >= b % LANES, rolled[name], built[b // LANES]
                )
            else:
                built[b // LANES] = rolled[name]
            done += n
    return [built[i] for i in range(len(built))]


def joined_halves(first, second):
    top = row_index()[:, :1] < HALF
    last = jnp.where(top, pltpu.roll(first, HALF, 0), second)
    start = jnp.where(top, first, pltpu.roll(second, HALF, 0))
    return last, start


def widened(own, near, far, odd, even):
    top = row_index() < HALF
    low, high = jnp.where(even, far, near), jnp.where(even, near, far)
    turned = pltpu.roll(own, HALF, 0)
    low = pltpu.roll(low, HALF, 0) if odd else low
    high = high if odd else pltpu.roll(high, HALF, 0)
    return jnp.where(top, low, turned), jnp.where(top, turned, high)


def row_codes(planes):
    lane = lax.broadcasted_iota(jnp.int32, planes[0][0].shape, 1)
    scales = jnp.zeros(planes[0][0].shape, jnp.float32)
    out = []
    for v, row in enumerate(planes):
        big = jnp.abs(row[0])
        for value in row[1:]:
            big = jnp.maximum(big, jnp.abs(value))
        big = jnp.max(big, axis=1, keepdims=True)
        power = jnp.clip(jnp.ceil(jnp.log2(jnp.maximum(big, 1e-30))), -90.0, 126.0)
        scales = jnp.where(lane == v, power, scales)
        gain = CODE_MAX * jnp.exp2(-power)
        for value in row:
            out.append((value * gain + ROUNDER) - ROUNDER)
    return out, scales


def shorts(value):
    return value.astype(jnp.int32).astype(jnp.int16)


def floats(value):
    return value.astype(jnp.int32).astype(jnp.float32)


def partners(windows):
    return list(range(windows - 1, 0, -1))


def pack_kernel(ways, windows, steps, nvar, levels, part, var_ref, traj_ref, *outs):
    me = lax.axis_index("window")
    lane = lane_index()
    variance = var_ref[...]
    high = variance.astype(jnp.bfloat16).astype(jnp.float32)
    middle = (variance - high).astype(jnp.bfloat16).astype(jnp.float32)
    low = variance - high - middle
    split = high + pltpu.roll(middle, HALF, 0) + pltpu.roll(low, LANES // 2, 1)
    split = split.astype(jnp.bfloat16)

    for n, d in enumerate(ways):
        outs[n][outs[n].shape[0] - 1] = split
        target = me ^ d

        def variable(v, carry, n=n, target=target):
            for lev in range(levels):
                pieces = [
                    tiled(traj_ref[target, j, v, lev].astype(jnp.float32)) for j in range(steps)
                ]
                parts = [(j, pieces[j], 0, part, j * part) for j in range(steps)]
                placed = place(parts, {}, lane)
                for t, value in enumerate(placed):
                    outs[n][(v * levels + lev) * len(placed) + t] = value.astype(jnp.bfloat16)
            return carry

        lax.fori_loop(0, nvar, variable, 0, unroll=len(ways) == 1)


def even_place():
    return lax.rem(lax.axis_index("space"), 2) == 0


def level_codes(ref, lev, first=0):
    planes = [
        [ref[0, v, lev, :, t : t + LANES] for t in range(0, ref.shape[-1], LANES)]
        for v in range(first, ref.shape[1])
    ]
    values, scales = row_codes(planes)
    return values + [scales]


def half_code_kernel(*refs):
    sources, (near_ref, far_ref, own_ref) = refs[:-3], refs[-3:]
    even = even_place()

    def pair(i, carry):
        near, far = [], []
        for k, ref in enumerate(sources):
            skip = int(k == len(sources) - 1)
            coded = [level_codes(ref, 2 * i + odd, skip) for odd in range(2)]
            for n, (first, second) in enumerate(zip(*coded)):
                if k == 0:
                    own_ref[i, n] = shorts(jnp.concatenate([first, second], 0))
                last, start = joined_halves(first, second)
                near.append(jnp.where(even, last, start))
                far.append(jnp.where(even, start, last))
            if len(near) % 2:
                near.append(jnp.zeros((SUB, LANES), jnp.float32))
                far.append(jnp.zeros((SUB, LANES), jnp.float32))
        for tiles, ref in ((near, near_ref), (far, far_ref)):
            for n in range(0, len(tiles), 2):
                ref[i, n // 2] = shorts(jnp.concatenate(tiles[n : n + 2], 0))
        return carry

    lax.fori_loop(0, near_ref.shape[0], pair, 0)


def half_tile(ref, i, n):
    whole = floats(ref[i, n // 2])
    return whole[SUB:] if n % 2 else whole[:SUB]


def around_kernel(windows, nvar, levels, *refs):
    pieces, (own_ref, near_ref, far_ref) = refs[:windows], refs[windows : windows + 3]
    outs, total_ref = refs[windows + 3 : -1], refs[-1]
    me = lax.axis_index("window")
    even = even_place()
    total = jnp.zeros((SUB, LANES), jnp.float32)
    for d in range(windows):
        split = pieces[d][pieces[d].shape[0] - 1].astype(jnp.float32)
        here = split + pltpu.roll(split, HALF, 0) + pltpu.roll(split, LANES // 2, 1)
        total = total + jnp.where((me ^ d) <= me, here, 0.0)
    for v in range(nvar):
        for lev in range(levels):
            one = total[lev : lev + 1, v : v + 1]
            total_ref[v * levels + lev] = jnp.broadcast_to(one, (SUB, LANES))
    for i, out_ref in enumerate(outs):
        for n in range(own_ref.shape[1]):
            own = floats(own_ref[i, n])
            near, far = half_tile(near_ref, i, n), half_tile(far_ref, i, n)
            for odd in range(2):
                halves = widened(own[odd * SUB : (odd + 1) * SUB], near, far, odd, even)
                out_ref[odd, n] = shorts(jnp.concatenate(halves, 0))


def decoded(ref, i, first, nvar, tiles):
    scales = jnp.exp2(half_tile(ref, i, first + nvar * tiles)) * (1.0 / CODE_MAX)
    return [
        [half_tile(ref, i, first + v * tiles + t) * scales[:, v : v + 1] for t in range(tiles)]
        for v in range(nvar)
    ]


def is_quarter(j, v, steps):
    return 0 < j < steps - 1 and not (v == 0 and j + 1 > HALF // 2)


def far_base(steps, nvar, levels):
    base, total = {}, 0
    for j in range(steps):
        for v in range(nvar):
            base[j, v] = total
            total += levels // (4 if is_quarter(j, v, steps) else 2)
    return base, total


def joined_quarters(four):
    slot = row_index() // 2
    last, start = pltpu.roll(four[0], 2, 0), four[0]
    for n in range(1, 4):
        last = jnp.where(slot == n, pltpu.roll(four[n], (2 * n + 2) % SUB, 0), last)
        start = jnp.where(slot == n, pltpu.roll(four[n], 2 * n, 0), start)
    return last, start


def assemble_kernel(windows, steps, nvar, levels, part, *refs):
    pieces = refs[:windows]
    own_ref, near_ref, far_ref, stack_ref = refs[windows + 1 :]
    me = lax.axis_index("window")
    even = even_place()
    lane = lane_index()
    count = stack_ref.shape[1]
    packed_tiles = count // (nvar * levels)
    for d in range(windows):
        stack_ref[me ^ d] = pieces[d][:count]

    pairs = levels // 2
    base, _ = far_base(steps, nvar, levels)

    def variable(v):
        built = {}
        for lev in range(levels):
            plane = v * levels + lev
            sources = [
                [
                    stack_ref[w, plane * packed_tiles + t].astype(jnp.float32)
                    for t in range(packed_tiles)
                ]
                for w in range(windows)
            ]
            rolled = {}
            for j in range(steps):
                parts = [(w, sources[w], j * part, part, w * part) for w in range(windows)]
                built[j, lev] = place(parts, rolled, lane)
                own_ref[j, plane] = jnp.concatenate(built[j, lev], 1).astype(jnp.bfloat16)
        for j in range(steps):
            for i in range(pairs):
                halves = [joined_halves(a, b) for a, b in zip(built[j, 2 * i], built[j, 2 * i + 1])]
                last, start = (jnp.concatenate([h[k] for h in halves], 1) for k in range(2))
                near_ref[j, v * pairs + i] = jnp.where(even, last, start).astype(jnp.bfloat16)
                if not is_quarter(j, v, steps):
                    far_ref[base[j, v] + i] = jnp.where(even, start, last).astype(jnp.bfloat16)
            if is_quarter(j, v, steps):
                for q in range(levels // 4):
                    four = zip(*[built[j, 4 * q + n] for n in range(4)])
                    ends = [joined_quarters(tiles) for tiles in four]
                    last, start = (jnp.concatenate([e[k] for e in ends], 1) for k in range(2))
                    far_ref[base[j, v] + q] = jnp.where(even, start, last).astype(jnp.bfloat16)

    for v in range(nvar):
        variable(v)


def prepare_factor_kernel(
    steps, nvar, levels, tiles,
    count_ref, noise_ref, coupling_ref, dobs_ref, innov_ref, obs_ref, share_ref, mix_ref,
):
    cuts = [slice(t * LANES, (t + 1) * LANES) for t in range(tiles)]
    for v in range(nvar):
        for u in range(nvar):
            one = coupling_gain * coupling_ref[v : v + 1, u : u + 1]
            mix_ref[v, u] = jnp.broadcast_to(one, (SUB, LANES))
    for lev in range(levels):
        for j in range(steps):
            noise = jnp.full((SUB, LANES), noise_ref[0, j, lev])
            share = jnp.where(j < count_ref[0], 1.0, 0.0) / noise
            share_ref[lev, j] = share
            for t in range(tiles):
                gap = innov_ref[0, j, lev, :, cuts[t]] - noise * dobs_ref[0, j, lev, :, cuts[t]]
                obs_ref[lev, j, t] = gap * share


def prepare_tangent_kernel(nvar, levels, tiles, near_ref, far_ref, inc_ref, first_ref):
    even = even_place()
    blocks = [slice(0, SUB), slice(SUB, 2 * SUB)]
    cuts = [slice(t * LANES, (t + 1) * LANES) for t in range(tiles)]
    offset = -(-(nvar * tiles + 1) // 2) * 2
    for i in range(levels // 2):
        fields = [decoded(ref, i, offset, nvar, tiles) for ref in (near_ref, far_ref)]
        for odd in range(2):
            lev = 2 * i + odd
            for t in range(tiles):
                for v in range(nvar):
                    near, far = (side[v][t] for side in fields)
                    halves = widened(inc_ref[0, v, lev, :, cuts[t]], near, far, odd, even)
                    for b in range(2):
                        first_ref[lev, v, t, blocks[b], :] = halves[b]


def prepare_adjoint_kernel(
    i, steps, nvar, tiles, count_ref, near_ref, far_ref, dobs_ref, after_ref, *refs
):
    _, last_ref, force_ref = refs
    even = even_place()
    blocks = [slice(0, SUB), slice(SUB, 2 * SUB)]
    cuts = [slice(t * LANES, (t + 1) * LANES) for t in range(tiles)]
    seen = [jnp.where(j < count_ref[0], 1.0, 0.0) for j in range(steps)]
    offset = -(-(nvar * tiles + 1) // 2) * 2
    none = [[jnp.zeros((SUB, LANES), jnp.float32)] * tiles]
    forces = [none + decoded(ref, i, 2 * offset, steps - 1, tiles) for ref in (near_ref, far_ref)]
    for odd in range(2):
        scales = jnp.exp2(floats(after_ref[odd, nvar * tiles])) * (-1.0 / CODE_MAX)
        for t in range(tiles):
            for v in range(nvar):
                value = floats(after_ref[odd, v * tiles + t])
                last_ref[odd, v, t] = value * scales[:, v : v + 1]
            for j in range(steps):
                near, far = (side[j][t] for side in forces)
                halves = widened(dobs_ref[0, j, 2 * i + odd, :, cuts[t]], near, far, odd, even)
                for b in range(2):
                    force_ref[odd, j, t, blocks[b], :] = seen[j] * halves[b]


def from_north(line, lane):
    turned = [pltpu.roll(value, LANES - 1, 1) for value in line] * 2
    return [jnp.where(lane < LANES - 1, turned[t], turned[t + 1]) for t in range(len(line))]


def from_south(line, lane):
    turned = [pltpu.roll(value, 1, 1) for value in line]
    return [jnp.where(lane > 0, turned[t], turned[t - 1]) for t in range(len(line))]


def masked_last(line, lane):
    return line[:-1] + [jnp.where(lane < LANES - 1, line[-1], 0.0)]


def masked_first(line, lane):
    return [jnp.where(lane > 0, line[0], 0.0)] + line[1:]


def walls(spaces):
    row, place_x = row_index(), lax.axis_index("space")
    low = jnp.where((row == HALF) & (place_x == 0), 0.0, 1.0)
    high = jnp.where((row == HALF - 1) & (place_x == spaces - 1), 0.0, 1.0)

    def walled(block, east, west):
        if block == 0:
            return east, [low * value for value in west]
        return [high * value for value in east], west

    return walled


BLOCKS = [slice(SUB, 2 * SUB), slice(2 * SUB, 3 * SUB)]
UPS = [slice(b.start + 1, b.stop + 1) for b in BLOCKS]
DOWNS = [slice(b.start - 1, b.stop - 1) for b in BLOCKS]
MINE = slice(SUB + HALF, 2 * SUB + HALF)


def tangent_kernel(
    spaces, steps, nvar, levels, tiles,
    mix_ref, share_ref, obs_ref, own_ref, near_ref, far_ref, first_ref,
    ndo_ref, ends_ref, x_ref, s_ref,
):
    lane, row = lane_index(), row_index()
    even = even_place()
    top = row < HALF
    walled = walls(spaces)
    pairs = levels // 2
    cuts = [slice(t * LANES, (t + 1) * LANES) for t in range(tiles)]
    base, _ = far_base(steps, nvar, levels)

    for lev in range(levels):
        i, odd = lev // 2, lev % 2
        for j in range(steps):
            for v in range(nvar):
                for t in range(tiles):
                    own = own_ref[j, v * levels + lev, :, cuts[t]].astype(jnp.float32)
                    near = near_ref[j, v * pairs + i, :, cuts[t]].astype(jnp.float32)
                    quarter = is_quarter(j, v, steps)
                    far = far_ref[base[j, v] + lev // (4 if quarter else 2), :, cuts[t]]
                    far = far.astype(jnp.float32)
                    if quarter:
                        slot = 2 * (lev % 4)
                        low_far = pltpu.roll(far, (HALF - 2 - slot) % SUB, 0)
                        high_far = pltpu.roll(far, (HALF - slot) % SUB, 0)
                    else:
                        low_far = pltpu.roll(far, HALF, 0) if odd else far
                        high_far = far if odd else pltpu.roll(far, HALF, 0)
                    low_near = pltpu.roll(near, HALF, 0) if odd else near
                    high_near = near if odd else pltpu.roll(near, HALF, 0)
                    turned = pltpu.roll(own, HALF, 0)
                    low = jnp.where(even, low_far, low_near)
                    high = jnp.where(even, high_near, high_far)
                    x_ref[lev, j, v, t, :SUB, :] = jnp.where(top, low, turned)
                    x_ref[lev, j, v, t, SUB:, :] = jnp.where(top, turned, high)

    def pair(i, outer):
        for odd in range(2):
            for v in range(nvar):
                for t in range(tiles):
                    s_ref[odd, 0, v, t, SUB : 3 * SUB, :] = first_ref[2 * i + odd, v, t]

        for j in range(steps):
            now = j % 2
            for odd in range(2):
                lev = 2 * i + odd
                for t in range(tiles):
                    image = share_ref[lev, j] * s_ref[odd, now, 0, t, MINE, :]
                    ndo_ref[0, j, lev, :, cuts[t]] = obs_ref[lev, j, t] - image
                for b in range(2):
                    part = slice(b * SUB, (b + 1) * SUB)
                    here, up, down = BLOCKS[b], UPS[b], DOWNS[b]
                    x = [[x_ref[lev, j, u, t, part, :] for t in range(tiles)] for u in range(nvar)]
                    ce = [diffusion - half_adv * value for value in x[0]]
                    cw = [diffusion + half_adv * value for value in x[0]]
                    ce, cw = walled(b, ce, cw)
                    cn = masked_last([diffusion - half_adv * value for value in x[1]], lane)
                    cs = masked_first([diffusion + half_adv * value for value in x[1]], lane)
                    s = [
                        [s_ref[odd, now, u, t, here, :] for t in range(tiles)] for u in range(nvar)
                    ]
                    xs = [[x[u][t] * s[u][t] for t in range(tiles)] for u in range(nvar)]
                    for v in range(nvar):
                        north, south = from_north(s[v], lane), from_south(s[v], lane)
                        for t in range(tiles):
                            fresh = keep * s[v][t] + ce[t] * s_ref[odd, now, v, t, up, :]
                            fresh = fresh + cw[t] * s_ref[odd, now, v, t, down, :]
                            fresh = fresh + cn[t] * north[t] + cs[t] * south[t]
                            for u in range(nvar):
                                fresh = fresh + mix_ref[v, u] * xs[u][t]
                            s_ref[odd, 1 - now, v, t, here, :] = fresh
        for odd in range(2):
            for v in range(nvar):
                for t in range(tiles):
                    ends_ref[2 * i + odd, v, t] = s_ref[odd, steps % 2, v, t, MINE, :]
        return outer

    lax.fori_loop(0, pairs, pair, 0)


def adjoint_kernel(
    i, windows, spaces, steps, nvar, levels, tiles,
    mix_ref, total_ref, x_ref, last_ref, force_ref, ends_ref, inc_ref, rhs_ref, dual_ref,
    ndm_ref, ninc_ref, *rest,
):
    payload_refs = rest[: windows - 1]
    x0_ref, a_ref, q_ref = rest[windows - 1 :]
    me = lax.axis_index("window")
    lane = lane_index()
    walled = walls(spaces)
    cuts = [slice(t * LANES, (t + 1) * LANES) for t in range(tiles)]

    for odd in range(2):
        lev = 2 * i + odd
        for t in range(tiles):
            for j in range(steps):
                x0_ref[odd, j, t, SUB : 3 * SUB, :] = x_ref[lev, j, 0, t]
            for v in range(nvar):
                a_ref[odd, 0, v, t, SUB : 3 * SUB, :] = last_ref[odd, v, t]

    for turn in range(steps):
        now = turn % 2
        j = steps - 1 - turn
        for odd in range(2):
            lev = 2 * i + odd
            for b in range(2):
                part = slice(b * SUB, (b + 1) * SUB)
                here, up, down = BLOCKS[b], UPS[b], DOWNS[b]
                x = [[x_ref[lev, j, u, t, part, :] for t in range(tiles)] for u in range(nvar)]
                ce = [diffusion + half_adv * x0_ref[odd, j, t, up, :] for t in range(tiles)]
                cw = [diffusion - half_adv * x0_ref[odd, j, t, down, :] for t in range(tiles)]
                ce, cw = walled(b, ce, cw)
                cn = masked_first([diffusion + half_adv * value for value in x[1]], lane)
                cs = masked_last([diffusion - half_adv * value for value in x[1]], lane)
                a = [
                    [a_ref[odd, now, u, t, here, :] for t in range(tiles)] for u in range(nvar)
                ]
                for u in range(nvar):
                    north = from_north([cn[t] * a[u][t] for t in range(tiles)], lane)
                    south = from_south([cs[t] * a[u][t] for t in range(tiles)], lane)
                    for t in range(tiles):
                        fresh = keep * a[u][t] + ce[t] * a_ref[odd, now, u, t, up, :]
                        fresh = fresh + cw[t] * a_ref[odd, now, u, t, down, :]
                        fresh = fresh + north[t] + south[t]
                        pull = mix_ref[0, u] * a[0][t]
                        for v in range(1, nvar):
                            pull = pull + mix_ref[v, u] * a[v][t]
                        fresh = fresh + x[u][t] * pull
                        if u == 0:
                            fresh = fresh + force_ref[odd, j, t, part, :]
                        a_ref[odd, 1 - now, u, t, here, :] = fresh
    end = steps % 2
    coded = []
    for odd in range(2):
        lev = 2 * i + odd
        back, ahead = [], []
        for v in range(nvar):
            share = total_ref[v * levels + lev]
            tv, gv = [], []
            for t in range(tiles):
                term = a_ref[odd, end, v, t, MINE, :] - last_ref[odd, v, t, HALF : HALF + SUB, :]
                given = rhs_ref[0, v, lev, :, cuts[t]] - inc_ref[0, v, lev, :, cuts[t]]
                given = given + share * term
                ndm_ref[v, odd, :, cuts[t]] = -(dual_ref[0, v, lev, :, cuts[t]] + term)
                ninc_ref[v, odd, :, cuts[t]] = given
                tv.append(term)
                gv.append(given + ends_ref[lev, v, t])
            back.append(tv)
            ahead.append(gv)
        coded.append((row_codes(back), row_codes(ahead)))
    for kind in range(2):
        first, second = coded[0][kind], coded[1][kind]
        for n, (a, b) in enumerate(zip(first[0] + [first[1]], second[0] + [second[1]])):
            q_ref[kind, n] = shorts(jnp.concatenate([a, b], 0))
    for ref, d in zip(payload_refs, partners(windows)):
        ref[...] = q_ref[jnp.where((me ^ d) < me, 0, 1)]


def final_kernel(windows, nvar, levels, tiles, *refs):
    pairs = levels // 2
    cut = pairs * (windows - 1)
    pieces, base_duals, base_incs = refs[:cut], refs[cut : cut + pairs], refs[cut + pairs : -3]
    total_ref, ndm_ref, ninc_ref = refs[-3:]
    me = lax.axis_index("window")
    cuts = [slice(t * LANES, (t + 1) * LANES) for t in range(tiles)]

    for i in range(pairs):
        tails = [None] * (nvar * tiles)
        heads = [None] * (nvar * tiles)
        for n, d in enumerate(partners(windows)):
            piece = pieces[i * (windows - 1) + n]
            later = (me ^ d) > me
            scales = jnp.exp2(floats(piece[nvar * tiles])) * (1.0 / CODE_MAX)
            for v in range(nvar):
                scale = scales[:, v : v + 1]
                for t in range(tiles):
                    k = v * tiles + t
                    value = floats(piece[k]) * scale
                    tail, head = jnp.where(later, value, 0.0), jnp.where(later, 0.0, value)
                    tails[k] = tails[k] + tail if n else tail
                    heads[k] = heads[k] + head if n else head
        for v in range(nvar):
            for odd in range(2):
                lev = 2 * i + odd
                share = total_ref[v * levels + lev]
                for t in range(tiles):
                    rows = slice(odd * SUB, (odd + 1) * SUB)
                    tail, head = tails[v * tiles + t][rows], heads[v * tiles + t][rows]
                    ndm_ref[0, v, lev, :, cuts[t]] = base_duals[i][v, odd, :, cuts[t]] - tail
                    ninc_ref[0, v, lev, :, cuts[t]] = (
                        base_incs[i][v, odd, :, cuts[t]] + head + share * tail
                    )


def moved(block, axis, distance):
    devices = range(lax.axis_size(axis))
    return lax.ppermute(block, axis, [(i, i + distance) for i in devices if i + distance in devices])


def exchanged(block, axis, mask):
    return lax.ppermute(block, axis, [(i, i ^ mask) for i in range(lax.axis_size(axis))])


def swaps(axis, first):
    route = []
    for i in range(first, lax.axis_size(axis) - 1, 2):
        route += [(i, i + 1), (i + 1, i)]
    return route


def swapped(block, axis, first):
    return lax.ppermute(block, axis, swaps(axis, first))


def body(
    trajectory,
    dual_model,
    increment,
    model_rhs,
    dual_obs,
    innovation,
    coupling,
    error_var,
    obs_var,
    obs_count,
):
    windows, spaces = lax.axis_size("window"), lax.axis_size("space")
    _, steps, nvar, levels, rows, part = trajectory.shape
    columns = dual_model.shape[-1]
    tiles = columns // LANES
    assert trajectory.shape[0] == windows and windows > 1 and rows == SUB and steps == HALF
    assert columns == tiles * LANES == windows * part and levels % 4 == 0
    assert windows & (windows - 1) == 0
    pairs = levels // 2
    wide = -(-steps * part // LANES) * LANES
    bf16, f32, i16 = jnp.bfloat16, jnp.float32, jnp.int16

    def shape(dims, dtype):
        return jax.ShapeDtypeStruct(dims, dtype)

    block = shape((nvar * levels * wide // LANES + 1, rows, LANES), bf16)
    variances = jnp.pad(error_var[0].T, ((0, SUB - levels), (0, LANES - nvar)))

    def packed(ways):
        return pl.pallas_call(
            lambda *refs: pack_kernel(ways, windows, steps, nvar, levels, part, *refs),
            out_shape=[block] * len(ways),
            in_specs=[VMEM, VMEM],
            out_specs=[VMEM] * len(ways),
            compiler_params=params(),
        )(variances, trajectory)

    order = partners(windows)
    groups = [[d] for d in order] if windows <= 4 else [order]
    blocks = {}
    for group in groups:
        blocks.update(zip(group, packed(group)))
    arrived = {d: exchanged(blocks[d], "window", d) for d in order}
    arrived[0] = packed([0])[0]

    payload = shape((pairs, nvar * tiles + 1, 2 * SUB, LANES), i16)

    counts = [nvar, nvar, steps - 1]
    half_tiles = sum(-(-(count * tiles + 1) // 2) for count in counts)
    halves = shape((pairs, half_tiles, 2 * SUB, LANES), i16)
    near, far, dual = pl.pallas_call(
        half_code_kernel,
        out_shape=[halves, halves, payload],
        in_specs=[VMEM] * 3,
        out_specs=[VMEM] * 3,
        compiler_params=params(),
    )(dual_model, increment, dual_obs)
    far, near = swapped(far, "space", 1), swapped(near, "space", 0)

    blocks_here = [arrived[d] for d in range(windows)]
    *after, totals = pl.pallas_call(
        lambda *refs: around_kernel(windows, nvar, levels, *refs),
        out_shape=[shape((2,) + payload.shape[1:], i16)] * pairs
        + [shape((nvar * levels, rows, LANES), f32)],
        in_specs=[VMEM] * (windows + 3),
        out_specs=[VMEM] * (pairs + 1),
        compiler_params=params(),
    )(*blocks_here, dual, near, far)
    after = [moved(piece, "window", -1) for piece in after]

    obs, share, mix = pl.pallas_call(
        lambda *refs: prepare_factor_kernel(steps, nvar, levels, tiles, *refs),
        out_shape=[
            shape((levels, steps, tiles, SUB, LANES), f32),
            shape((levels, steps, SUB, LANES), f32),
            shape((nvar, nvar, SUB, LANES), f32),
        ],
        in_specs=[SMEM] * 2 + [VMEM] * 3,
        out_specs=[VMEM] * 3,
        compiler_params=params(),
    )(obs_count, obs_var, coupling, dual_obs, innovation)

    own, traj_near, traj_far = pl.pallas_call(
        lambda *refs: assemble_kernel(windows, steps, nvar, levels, part, *refs),
        out_shape=[
            shape((steps, nvar * levels, rows, columns), bf16),
            shape((steps, nvar * pairs, rows, columns), bf16),
            shape((far_base(steps, nvar, levels)[1], rows, columns), bf16),
        ],
        in_specs=[VMEM] * windows + [ANY],
        out_specs=[VMEM] * 3,
        scratch_shapes=[pltpu.VMEM((windows, block.shape[0] - 1, rows, LANES), bf16)],
        compiler_params=params(),
    )(*blocks_here, mix)
    traj_near, traj_far = swapped(traj_near, "space", 0), swapped(traj_far, "space", 1)

    first = pl.pallas_call(
        lambda *refs: prepare_tangent_kernel(nvar, levels, tiles, *refs),
        out_shape=shape((levels, nvar, tiles, 2 * SUB, LANES), f32),
        in_specs=[VMEM] * 3,
        out_specs=VMEM,
        compiler_params=params(),
    )(near, far, increment)
    new_dual_obs, ends, wide_traj = pl.pallas_call(
        lambda *refs: tangent_kernel(spaces, steps, nvar, levels, tiles, *refs),
        out_shape=[
            shape(dual_obs.shape, f32),
            shape((levels, nvar, tiles, SUB, LANES), f32),
            shape((levels, steps, nvar, tiles, 2 * SUB, LANES), f32),
        ],
        in_specs=[VMEM] * 7,
        out_specs=[VMEM] * 3,
        scratch_shapes=[pltpu.VMEM((2, 2, nvar, tiles, 4 * SUB, LANES), f32)],
        compiler_params=params(),
    )(mix, share, obs, own, traj_near, traj_far, first)

    state = shape((nvar, 2, rows, columns), f32)
    coded = shape((nvar * tiles + 1, 2 * SUB, LANES), i16)
    base_duals, base_incs, sent = [], [], []
    before = ends
    for i in range(pairs):
        last, force = pl.pallas_call(
            lambda *refs, i=i: prepare_adjoint_kernel(i, steps, nvar, tiles, *refs),
            out_shape=[shape((2, n, tiles, 2 * SUB, LANES), f32) for n in (nvar, steps)],
            in_specs=[SMEM] + [VMEM] * 4 + [ANY],
            out_specs=[VMEM] * 2,
            compiler_params=params(),
        )(obs_count, near, far, dual_obs, after[i], before)
        base_dual, base_inc, *payloads = pl.pallas_call(
            lambda *refs, i=i: adjoint_kernel(
                i, windows, spaces, steps, nvar, levels, tiles, *refs
            ),
            out_shape=[state, state] + [coded] * (windows - 1),
            in_specs=[VMEM] * 9,
            out_specs=[VMEM] * (2 + windows - 1),
            scratch_shapes=[
                pltpu.VMEM((2, steps, tiles, 4 * SUB, LANES), f32),
                pltpu.VMEM((2, 2, nvar, tiles, 4 * SUB, LANES), f32),
                pltpu.VMEM((2,) + coded.shape, i16),
            ],
            compiler_params=params(),
        )(mix, totals, wide_traj, last, force, ends, increment, model_rhs, dual_model)
        before = base_dual
        base_duals.append(base_dual)
        base_incs.append(base_inc)
        sent += [
            exchanged(piece, "window", d) for piece, d in zip(payloads, order)
        ]

    new_dual_model, new_increment = pl.pallas_call(
        lambda *refs: final_kernel(windows, nvar, levels, tiles, *refs),
        out_shape=[shape(dual_model.shape, f32), shape(increment.shape, f32)],
        in_specs=[VMEM] * (len(sent) + 2 * pairs + 1),
        out_specs=[VMEM] * 2,
        compiler_params=params(),
    )(*sent, *base_duals, *base_incs, totals)
    return new_dual_model, new_dual_obs, new_increment


def solution(mesh):
    placed = (
        P("members", None, None, None, "space", "window"),
        P(("members", "window"), None, None, "space", None),
        P(("members", "window"), None, None, "space", None),
        P(("members", "window"), None, None, "space", None),
        P(("members", "window"), None, None, "space", None),
        P(("members", "window"), None, None, "space", None),
        P(),
        P(("members", "window"), None, None),
        P(("members", "window"), None, None),
        P(("members", "window")),
    )
    return jax.shard_map(
        body,
        mesh=mesh,
        in_specs=placed,
        out_specs=(
            P(("members", "window"), None, None, "space", None),
            P(("members", "window"), None, None, "space", None),
            P(("members", "window"), None, None, "space", None),
        ),
        check_vma=False,
    )
```

```python
import jax
import jax.numpy as jnp
from jax import lax
from jax.experimental import pallas as pl
from jax.experimental.pallas import tpu as pltpu
from jax.sharding import PartitionSpec as P

LANES = 128
SUB = 8
HALF = SUB // 2
CODE_MAX = 32000.0
ROUNDER = 12582912.0

diffusion = 0.2
advection = 0.2
coupling_gain = 0.5
keep = 1.0 - 4.0 * diffusion
half_adv = 0.5 * advection

VMEM = pl.BlockSpec(memory_space=pltpu.VMEM)
SMEM = pl.BlockSpec(memory_space=pltpu.SMEM)
ANY = pl.BlockSpec(memory_space=pl.ANY)


def params(mib=24):
    return pltpu.CompilerParams(vmem_limit_bytes=mib * 1024 * 1024)


def lane_index():
    return lax.broadcasted_iota(jnp.int32, (SUB, LANES), 1)


def row_index():
    return lax.broadcasted_iota(jnp.int32, (SUB, LANES), 0)


def tiled(wide):
    short = -wide.shape[1] % LANES
    if short:
        wide = jnp.concatenate([wide, jnp.zeros((wide.shape[0], short), wide.dtype)], 1)
    return [wide[:, i : i + LANES] for i in range(0, wide.shape[1], LANES)]


def place(parts, rolled, lane):
    built = {}
    for key, tiles, first, width, target in parts:
        done = 0
        while done < width:
            a, b = first + done, target + done
            n = min(width - done, LANES - a % LANES, LANES - b % LANES)
            shift = (b - a) % LANES
            name = (key, a // LANES, shift)
            if name not in rolled:
                value = tiles[a // LANES]
                rolled[name] = pltpu.roll(value, shift, 1) if shift else value
            if b % LANES:
                built[b // LANES] = jnp.where(
                    lane >= b % LANES, rolled[name], built[b // LANES]
                )
            else:
                built[b // LANES] = rolled[name]
            done += n
    return [built[i] for i in range(len(built))]


def joined_halves(first, second):
    top = row_index()[:, :1] < HALF
    last = jnp.where(top, pltpu.roll(first, HALF, 0), second)
    start = jnp.where(top, first, pltpu.roll(second, HALF, 0))
    return last, start


def widened(own, near, far, odd, even):
    top = row_index() < HALF
    low, high = jnp.where(even, far, near), jnp.where(even, near, far)
    turned = pltpu.roll(own, HALF, 0)
    low = pltpu.roll(low, HALF, 0) if odd else low
    high = high if odd else pltpu.roll(high, HALF, 0)
    return jnp.where(top, low, turned), jnp.where(top, turned, high)


def row_codes(planes):
    lane = lax.broadcasted_iota(jnp.int32, planes[0][0].shape, 1)
    scales = jnp.zeros(planes[0][0].shape, jnp.float32)
    out = []
    for v, row in enumerate(planes):
        big = jnp.abs(row[0])
        for value in row[1:]:
            big = jnp.maximum(big, jnp.abs(value))
        big = jnp.max(big, axis=1, keepdims=True)
        power = jnp.clip(jnp.ceil(jnp.log2(jnp.maximum(big, 1e-30))), -90.0, 126.0)
        scales = jnp.where(lane == v, power, scales)
        gain = CODE_MAX * jnp.exp2(-power)
        for value in row:
            out.append((value * gain + ROUNDER) - ROUNDER)
    return out, scales


def shorts(value):
    return value.astype(jnp.int32).astype(jnp.int16)


def floats(value):
    return value.astype(jnp.int32).astype(jnp.float32)


def partners(windows):
    return list(range(windows - 1, 0, -1))


def pack_kernel(ways, windows, steps, nvar, levels, part, var_ref, traj_ref, *outs):
    me = lax.axis_index("window")
    lane = lane_index()
    variance = var_ref[...]
    high = variance.astype(jnp.bfloat16).astype(jnp.float32)
    middle = (variance - high).astype(jnp.bfloat16).astype(jnp.float32)
    low = variance - high - middle
    split = high + pltpu.roll(middle, HALF, 0) + pltpu.roll(low, LANES // 2, 1)
    split = split.astype(jnp.bfloat16)

    for n, d in enumerate(ways):
        outs[n][outs[n].shape[0] - 1] = split
        target = me ^ d

        def variable(v, carry, n=n, target=target):
            for lev in range(levels):
                pieces = [
                    tiled(traj_ref[target, j, v, lev].astype(jnp.float32)) for j in range(steps)
                ]
                parts = [(j, pieces[j], 0, part, j * part) for j in range(steps)]
                placed = place(parts, {}, lane)
                for t, value in enumerate(placed):
                    outs[n][(v * levels + lev) * len(placed) + t] = value.astype(jnp.bfloat16)
            return carry

        lax.fori_loop(0, nvar, variable, 0, unroll=len(ways) == 1)


def even_place():
    return lax.rem(lax.axis_index("space"), 2) == 0


def level_codes(ref, lev, first=0):
    planes = [
        [ref[0, v, lev, :, t : t + LANES] for t in range(0, ref.shape[-1], LANES)]
        for v in range(first, ref.shape[1])
    ]
    values, scales = row_codes(planes)
    return values + [scales]


def half_code_kernel(*refs):
    sources, (near_ref, far_ref, own_ref) = refs[:-3], refs[-3:]
    even = even_place()

    def pair(i, carry):
        near, far = [], []
        for k, ref in enumerate(sources):
            skip = int(k == len(sources) - 1)
            coded = [level_codes(ref, 2 * i + odd, skip) for odd in range(2)]
            for n, (first, second) in enumerate(zip(*coded)):
                if k == 0:
                    own_ref[i, n] = shorts(jnp.concatenate([first, second], 0))
                last, start = joined_halves(first, second)
                near.append(jnp.where(even, last, start))
                far.append(jnp.where(even, start, last))
            if len(near) % 2:
                near.append(jnp.zeros((SUB, LANES), jnp.float32))
                far.append(jnp.zeros((SUB, LANES), jnp.float32))
        for tiles, ref in ((near, near_ref), (far, far_ref)):
            for n in range(0, len(tiles), 2):
                ref[i, n // 2] = shorts(jnp.concatenate(tiles[n : n + 2], 0))
        return carry

    lax.fori_loop(0, near_ref.shape[0], pair, 0)


def half_tile(ref, i, n):
    whole = floats(ref[i, n // 2])
    return whole[SUB:] if n % 2 else whole[:SUB]


def around_kernel(windows, nvar, levels, *refs):
    pieces, (own_ref, near_ref, far_ref) = refs[:windows], refs[windows : windows + 3]
    outs, total_ref = refs[windows + 3 : -1], refs[-1]
    me = lax.axis_index("window")
    even = even_place()
    total = jnp.zeros((SUB, LANES), jnp.float32)
    for d in range(windows):
        split = pieces[d][pieces[d].shape[0] - 1].astype(jnp.float32)
        here = split + pltpu.roll(split, HALF, 0) + pltpu.roll(split, LANES // 2, 1)
        total = total + jnp.where((me ^ d) <= me, here, 0.0)
    for v in range(nvar):
        for lev in range(levels):
            one = total[lev : lev + 1, v : v + 1]
            total_ref[v * levels + lev] = jnp.broadcast_to(one, (SUB, LANES))
    for i, out_ref in enumerate(outs):
        for n in range(own_ref.shape[1]):
            own = floats(own_ref[i, n])
            near, far = half_tile(near_ref, i, n), half_tile(far_ref, i, n)
            for odd in range(2):
                halves = widened(own[odd * SUB : (odd + 1) * SUB], near, far, odd, even)
                out_ref[odd, n] = shorts(jnp.concatenate(halves, 0))


def decoded(ref, i, first, nvar, tiles):
    scales = jnp.exp2(half_tile(ref, i, first + nvar * tiles)) * (1.0 / CODE_MAX)
    return [
        [half_tile(ref, i, first + v * tiles + t) * scales[:, v : v + 1] for t in range(tiles)]
        for v in range(nvar)
    ]


def is_quarter(j, v, steps):
    return 0 < j < steps - 1 and not (v == 0 and j + 1 > HALF // 2)


def edge_base(steps, nvar, levels):
    base, total = {}, 0
    for j in range(steps):
        for v in range(nvar):
            base[j, v] = total
            total += levels // (4 if is_quarter(j, v, steps) else 2)
    return base, total


def joined_quarters(four):
    slot = row_index() // 2
    last, start = pltpu.roll(four[0], 2, 0), four[0]
    for n in range(1, 4):
        last = jnp.where(slot == n, pltpu.roll(four[n], (2 * n + 2) % SUB, 0), last)
        start = jnp.where(slot == n, pltpu.roll(four[n], 2 * n, 0), start)
    return last, start


def assemble_kernel(windows, steps, nvar, levels, part, *refs):
    pieces = refs[:windows]
    own_ref, near_ref, far_ref, stack_ref = refs[windows + 1 :]
    me = lax.axis_index("window")
    even = even_place()
    lane = lane_index()
    count = stack_ref.shape[1]
    packed_tiles = count // (nvar * levels)
    for d in range(windows):
        stack_ref[me ^ d] = pieces[d][:count]

    base, _ = edge_base(steps, nvar, levels)

    def variable(v):
        built = {}
        for lev in range(levels):
            plane = v * levels + lev
            sources = [
                [
                    stack_ref[w, plane * packed_tiles + t].astype(jnp.float32)
                    for t in range(packed_tiles)
                ]
                for w in range(windows)
            ]
            rolled = {}
            for j in range(steps):
                parts = [(w, sources[w], j * part, part, w * part) for w in range(windows)]
                built[j, lev] = place(parts, rolled, lane)
                own_ref[j, plane] = jnp.concatenate(built[j, lev], 1).astype(jnp.bfloat16)
        for j in range(steps):
            if is_quarter(j, v, steps):
                groups = [
                    [joined_quarters(four) for four in zip(*[built[j, 4 * q + n] for n in range(4)])]
                    for q in range(levels // 4)
                ]
            else:
                groups = [
                    [joined_halves(a, b) for a, b in zip(built[j, 2 * i], built[j, 2 * i + 1])]
                    for i in range(levels // 2)
                ]
            for n, group in enumerate(groups):
                last, start = (jnp.concatenate([e[k] for e in group], 1) for k in range(2))
                near_ref[base[j, v] + n] = jnp.where(even, last, start).astype(jnp.bfloat16)
                far_ref[base[j, v] + n] = jnp.where(even, start, last).astype(jnp.bfloat16)

    for v in range(nvar):
        variable(v)


def prepare_factor_kernel(
    steps, nvar, levels, tiles,
    count_ref, noise_ref, coupling_ref, dobs_ref, innov_ref, obs_ref, share_ref, mix_ref,
):
    cuts = [slice(t * LANES, (t + 1) * LANES) for t in range(tiles)]
    for v in range(nvar):
        for u in range(nvar):
            one = coupling_gain * coupling_ref[v : v + 1, u : u + 1]
            mix_ref[v, u] = jnp.broadcast_to(one, (SUB, LANES))
    for lev in range(levels):
        for j in range(steps):
            noise = jnp.full((SUB, LANES), noise_ref[0, j, lev])
            share = jnp.where(j < count_ref[0], 1.0, 0.0) / noise
            share_ref[lev, j] = share
            for t in range(tiles):
                gap = innov_ref[0, j, lev, :, cuts[t]] - noise * dobs_ref[0, j, lev, :, cuts[t]]
                obs_ref[lev, j, t] = gap * share


def prepare_tangent_kernel(nvar, levels, tiles, near_ref, far_ref, inc_ref, first_ref):
    even = even_place()
    blocks = [slice(0, SUB), slice(SUB, 2 * SUB)]
    cuts = [slice(t * LANES, (t + 1) * LANES) for t in range(tiles)]
    offset = -(-(nvar * tiles + 1) // 2) * 2
    for i in range(levels // 2):
        fields = [decoded(ref, i, offset, nvar, tiles) for ref in (near_ref, far_ref)]
        for odd in range(2):
            lev = 2 * i + odd
            for t in range(tiles):
                for v in range(nvar):
                    near, far = (side[v][t] for side in fields)
                    halves = widened(inc_ref[0, v, lev, :, cuts[t]], near, far, odd, even)
                    for b in range(2):
                        first_ref[lev, v, t, blocks[b], :] = halves[b]


def prepare_adjoint_kernel(
    i, steps, nvar, tiles, count_ref, near_ref, far_ref, dobs_ref, after_ref, *refs
):
    _, last_ref, force_ref = refs
    even = even_place()
    blocks = [slice(0, SUB), slice(SUB, 2 * SUB)]
    cuts = [slice(t * LANES, (t + 1) * LANES) for t in range(tiles)]
    seen = [jnp.where(j < count_ref[0], 1.0, 0.0) for j in range(steps)]
    offset = -(-(nvar * tiles + 1) // 2) * 2
    none = [[jnp.zeros((SUB, LANES), jnp.float32)] * tiles]
    forces = [none + decoded(ref, i, 2 * offset, steps - 1, tiles) for ref in (near_ref, far_ref)]
    for odd in range(2):
        scales = jnp.exp2(floats(after_ref[odd, nvar * tiles])) * (-1.0 / CODE_MAX)
        for t in range(tiles):
            for v in range(nvar):
                value = floats(after_ref[odd, v * tiles + t])
                last_ref[odd, v, t] = value * scales[:, v : v + 1]
            for j in range(steps):
                near, far = (side[j][t] for side in forces)
                halves = widened(dobs_ref[0, j, 2 * i + odd, :, cuts[t]], near, far, odd, even)
                for b in range(2):
                    force_ref[odd, j, t, blocks[b], :] = seen[j] * halves[b]


def from_north(line, lane):
    turned = [pltpu.roll(value, LANES - 1, 1) for value in line] * 2
    return [jnp.where(lane < LANES - 1, turned[t], turned[t + 1]) for t in range(len(line))]


def from_south(line, lane):
    turned = [pltpu.roll(value, 1, 1) for value in line]
    return [jnp.where(lane > 0, turned[t], turned[t - 1]) for t in range(len(line))]


def masked_last(line, lane):
    return line[:-1] + [jnp.where(lane < LANES - 1, line[-1], 0.0)]


def masked_first(line, lane):
    return [jnp.where(lane > 0, line[0], 0.0)] + line[1:]


def walls(spaces):
    row, place_x = row_index(), lax.axis_index("space")
    low = jnp.where((row == HALF) & (place_x == 0), 0.0, 1.0)
    high = jnp.where((row == HALF - 1) & (place_x == spaces - 1), 0.0, 1.0)

    def walled(block, east, west):
        if block == 0:
            return east, [low * value for value in west]
        return [high * value for value in east], west

    return walled


BLOCKS = [slice(SUB, 2 * SUB), slice(2 * SUB, 3 * SUB)]
UPS = [slice(b.start + 1, b.stop + 1) for b in BLOCKS]
DOWNS = [slice(b.start - 1, b.stop - 1) for b in BLOCKS]
MINE = slice(SUB + HALF, 2 * SUB + HALF)


def tangent_kernel(
    spaces, steps, nvar, levels, tiles,
    mix_ref, share_ref, obs_ref, own_ref, far_ref, near_ref, first_ref,
    ndo_ref, ends_ref, x_ref, s_ref,
):
    lane, row = lane_index(), row_index()
    even = even_place()
    top = row < HALF
    walled = walls(spaces)
    pairs = levels // 2
    cuts = [slice(t * LANES, (t + 1) * LANES) for t in range(tiles)]
    base, _ = edge_base(steps, nvar, levels)

    for lev in range(levels):
        odd = lev % 2
        for j in range(steps):
            for v in range(nvar):
                for t in range(tiles):
                    own = own_ref[j, v * levels + lev, :, cuts[t]].astype(jnp.float32)
                    quarter = is_quarter(j, v, steps)
                    tile = base[j, v] + lev // (4 if quarter else 2)
                    near = near_ref[tile, :, cuts[t]].astype(jnp.float32)
                    far = far_ref[tile, :, cuts[t]].astype(jnp.float32)
                    low, high = jnp.where(even, far, near), jnp.where(even, near, far)
                    if quarter:
                        slot = 2 * (lev % 4)
                        low = pltpu.roll(low, (HALF - 2 - slot) % SUB, 0)
                        high = pltpu.roll(high, (HALF - slot) % SUB, 0)
                    else:
                        low = pltpu.roll(low, HALF, 0) if odd else low
                        high = high if odd else pltpu.roll(high, HALF, 0)
                    turned = pltpu.roll(own, HALF, 0)
                    x_ref[lev, j, v, t, :SUB, :] = jnp.where(top, low, turned)
                    x_ref[lev, j, v, t, SUB:, :] = jnp.where(top, turned, high)

    def pair(i, outer):
        for odd in range(2):
            for v in range(nvar):
                for t in range(tiles):
                    s_ref[odd, 0, v, t, SUB : 3 * SUB, :] = first_ref[2 * i + odd, v, t]

        for j in range(steps):
            now = j % 2
            for odd in range(2):
                lev = 2 * i + odd
                for t in range(tiles):
                    image = share_ref[lev, j] * s_ref[odd, now, 0, t, MINE, :]
                    ndo_ref[0, j, lev, :, cuts[t]] = obs_ref[lev, j, t] - image
                for b in range(2):
                    part = slice(b * SUB, (b + 1) * SUB)
                    here, up, down = BLOCKS[b], UPS[b], DOWNS[b]
                    x = [[x_ref[lev, j, u, t, part, :] for t in range(tiles)] for u in range(nvar)]
                    ce = [diffusion - half_adv * value for value in x[0]]
                    cw = [diffusion + half_adv * value for value in x[0]]
                    ce, cw = walled(b, ce, cw)
                    cn = masked_last([diffusion - half_adv * value for value in x[1]], lane)
                    cs = masked_first([diffusion + half_adv * value for value in x[1]], lane)
                    s = [
                        [s_ref[odd, now, u, t, here, :] for t in range(tiles)] for u in range(nvar)
                    ]
                    xs = [[x[u][t] * s[u][t] for t in range(tiles)] for u in range(nvar)]
                    for v in range(nvar):
                        north, south = from_north(s[v], lane), from_south(s[v], lane)
                        for t in range(tiles):
                            fresh = keep * s[v][t] + ce[t] * s_ref[odd, now, v, t, up, :]
                            fresh = fresh + cw[t] * s_ref[odd, now, v, t, down, :]
                            fresh = fresh + cn[t] * north[t] + cs[t] * south[t]
                            for u in range(nvar):
                                fresh = fresh + mix_ref[v, u] * xs[u][t]
                            s_ref[odd, 1 - now, v, t, here, :] = fresh
        for odd in range(2):
            for v in range(nvar):
                for t in range(tiles):
                    ends_ref[2 * i + odd, v, t] = s_ref[odd, steps % 2, v, t, MINE, :]
        return outer

    lax.fori_loop(0, pairs, pair, 0)


def adjoint_kernel(
    i, windows, spaces, steps, nvar, levels, tiles,
    mix_ref, total_ref, x_ref, last_ref, force_ref, ends_ref, inc_ref, rhs_ref, dual_ref,
    ndm_ref, ninc_ref, *rest,
):
    payload_refs = rest[: windows - 1]
    x0_ref, a_ref, q_ref = rest[windows - 1 :]
    me = lax.axis_index("window")
    lane = lane_index()
    walled = walls(spaces)
    cuts = [slice(t * LANES, (t + 1) * LANES) for t in range(tiles)]

    for odd in range(2):
        lev = 2 * i + odd
        for t in range(tiles):
            for j in range(steps):
                x0_ref[odd, j, t, SUB : 3 * SUB, :] = x_ref[lev, j, 0, t]
            for v in range(nvar):
                a_ref[odd, 0, v, t, SUB : 3 * SUB, :] = last_ref[odd, v, t]

    for turn in range(steps):
        now = turn % 2
        j = steps - 1 - turn
        for odd in range(2):
            lev = 2 * i + odd
            for b in range(2):
                part = slice(b * SUB, (b + 1) * SUB)
                here, up, down = BLOCKS[b], UPS[b], DOWNS[b]
                x = [[x_ref[lev, j, u, t, part, :] for t in range(tiles)] for u in range(nvar)]
                ce = [diffusion + half_adv * x0_ref[odd, j, t, up, :] for t in range(tiles)]
                cw = [diffusion - half_adv * x0_ref[odd, j, t, down, :] for t in range(tiles)]
                ce, cw = walled(b, ce, cw)
                cn = masked_first([diffusion + half_adv * value for value in x[1]], lane)
                cs = masked_last([diffusion - half_adv * value for value in x[1]], lane)
                a = [
                    [a_ref[odd, now, u, t, here, :] for t in range(tiles)] for u in range(nvar)
                ]
                for u in range(nvar):
                    north = from_north([cn[t] * a[u][t] for t in range(tiles)], lane)
                    south = from_south([cs[t] * a[u][t] for t in range(tiles)], lane)
                    for t in range(tiles):
                        fresh = keep * a[u][t] + ce[t] * a_ref[odd, now, u, t, up, :]
                        fresh = fresh + cw[t] * a_ref[odd, now, u, t, down, :]
                        fresh = fresh + north[t] + south[t]
                        pull = mix_ref[0, u] * a[0][t]
                        for v in range(1, nvar):
                            pull = pull + mix_ref[v, u] * a[v][t]
                        fresh = fresh + x[u][t] * pull
                        if u == 0:
                            fresh = fresh + force_ref[odd, j, t, part, :]
                        a_ref[odd, 1 - now, u, t, here, :] = fresh
    end = steps % 2
    coded = []
    for odd in range(2):
        lev = 2 * i + odd
        back, ahead = [], []
        for v in range(nvar):
            share = total_ref[v * levels + lev]
            tv, gv = [], []
            for t in range(tiles):
                term = a_ref[odd, end, v, t, MINE, :] - last_ref[odd, v, t, HALF : HALF + SUB, :]
                given = rhs_ref[0, v, lev, :, cuts[t]] - inc_ref[0, v, lev, :, cuts[t]]
                given = given + share * term
                ndm_ref[v, odd, :, cuts[t]] = -(dual_ref[0, v, lev, :, cuts[t]] + term)
                ninc_ref[v, odd, :, cuts[t]] = given
                tv.append(term)
                gv.append(given + ends_ref[lev, v, t])
            back.append(tv)
            ahead.append(gv)
        coded.append((row_codes(back), row_codes(ahead)))
    for kind in range(2):
        first, second = coded[0][kind], coded[1][kind]
        for n, (a, b) in enumerate(zip(first[0] + [first[1]], second[0] + [second[1]])):
            q_ref[kind, n] = shorts(jnp.concatenate([a, b], 0))
    for ref, d in zip(payload_refs, partners(windows)):
        ref[...] = q_ref[jnp.where((me ^ d) < me, 0, 1)]


def final_kernel(windows, nvar, levels, tiles, *refs):
    pairs = levels // 2
    cut = pairs * (windows - 1)
    pieces, base_duals, base_incs = refs[:cut], refs[cut : cut + pairs], refs[cut + pairs : -3]
    total_ref, ndm_ref, ninc_ref = refs[-3:]
    me = lax.axis_index("window")
    cuts = [slice(t * LANES, (t + 1) * LANES) for t in range(tiles)]

    for i in range(pairs):
        tails = [None] * (nvar * tiles)
        heads = [None] * (nvar * tiles)
        for n, d in enumerate(partners(windows)):
            piece = pieces[i * (windows - 1) + n]
            later = (me ^ d) > me
            scales = jnp.exp2(floats(piece[nvar * tiles])) * (1.0 / CODE_MAX)
            for v in range(nvar):
                scale = scales[:, v : v + 1]
                for t in range(tiles):
                    k = v * tiles + t
                    value = floats(piece[k]) * scale
                    tail, head = jnp.where(later, value, 0.0), jnp.where(later, 0.0, value)
                    tails[k] = tails[k] + tail if n else tail
                    heads[k] = heads[k] + head if n else head
        for v in range(nvar):
            for odd in range(2):
                lev = 2 * i + odd
                share = total_ref[v * levels + lev]
                for t in range(tiles):
                    rows = slice(odd * SUB, (odd + 1) * SUB)
                    tail, head = tails[v * tiles + t][rows], heads[v * tiles + t][rows]
                    ndm_ref[0, v, lev, :, cuts[t]] = base_duals[i][v, odd, :, cuts[t]] - tail
                    ninc_ref[0, v, lev, :, cuts[t]] = (
                        base_incs[i][v, odd, :, cuts[t]] + head + share * tail
                    )


def moved(block, axis, distance):
    devices = range(lax.axis_size(axis))
    return lax.ppermute(block, axis, [(i, i + distance) for i in devices if i + distance in devices])


def exchanged(block, axis, mask):
    return lax.ppermute(block, axis, [(i, i ^ mask) for i in range(lax.axis_size(axis))])


def swaps(axis, first):
    route = []
    for i in range(first, lax.axis_size(axis) - 1, 2):
        route += [(i, i + 1), (i + 1, i)]
    return route


def swapped(block, axis, first):
    return lax.ppermute(block, axis, swaps(axis, first))


def body(
    trajectory,
    dual_model,
    increment,
    model_rhs,
    dual_obs,
    innovation,
    coupling,
    error_var,
    obs_var,
    obs_count,
):
    windows, spaces = lax.axis_size("window"), lax.axis_size("space")
    _, steps, nvar, levels, rows, part = trajectory.shape
    columns = dual_model.shape[-1]
    tiles = columns // LANES
    assert trajectory.shape[0] == windows and windows > 1 and rows == SUB and steps == HALF
    assert columns == tiles * LANES == windows * part and levels % 4 == 0
    assert windows & (windows - 1) == 0
    pairs = levels // 2
    wide = -(-steps * part // LANES) * LANES
    bf16, f32, i16 = jnp.bfloat16, jnp.float32, jnp.int16

    def shape(dims, dtype):
        return jax.ShapeDtypeStruct(dims, dtype)

    block = shape((nvar * levels * wide // LANES + 1, rows, LANES), bf16)
    variances = jnp.pad(error_var[0].T, ((0, SUB - levels), (0, LANES - nvar)))

    def packed(ways):
        return pl.pallas_call(
            lambda *refs: pack_kernel(ways, windows, steps, nvar, levels, part, *refs),
            out_shape=[block] * len(ways),
            in_specs=[VMEM, VMEM],
            out_specs=[VMEM] * len(ways),
            compiler_params=params(),
        )(variances, trajectory)

    order = partners(windows)
    groups = [[d] for d in order] if windows <= 4 else [order]
    blocks = {}
    for group in groups:
        blocks.update(zip(group, packed(group)))
    arrived = {d: exchanged(blocks[d], "window", d) for d in order}
    arrived[0] = packed([0])[0]

    payload = shape((pairs, nvar * tiles + 1, 2 * SUB, LANES), i16)

    counts = [nvar, nvar, steps - 1]
    half_tiles = sum(-(-(count * tiles + 1) // 2) for count in counts)
    halves = shape((pairs, half_tiles, 2 * SUB, LANES), i16)
    near, far, dual = pl.pallas_call(
        half_code_kernel,
        out_shape=[halves, halves, payload],
        in_specs=[VMEM] * 3,
        out_specs=[VMEM] * 3,
        compiler_params=params(),
    )(dual_model, increment, dual_obs)
    far, near = swapped(far, "space", 1), swapped(near, "space", 0)

    blocks_here = [arrived[d] for d in range(windows)]
    *after, totals = pl.pallas_call(
        lambda *refs: around_kernel(windows, nvar, levels, *refs),
        out_shape=[shape((2,) + payload.shape[1:], i16)] * pairs
        + [shape((nvar * levels, rows, LANES), f32)],
        in_specs=[VMEM] * (windows + 3),
        out_specs=[VMEM] * (pairs + 1),
        compiler_params=params(),
    )(*blocks_here, dual, near, far)
    after = [moved(piece, "window", -1) for piece in after]

    obs, share, mix = pl.pallas_call(
        lambda *refs: prepare_factor_kernel(steps, nvar, levels, tiles, *refs),
        out_shape=[
            shape((levels, steps, tiles, SUB, LANES), f32),
            shape((levels, steps, SUB, LANES), f32),
            shape((nvar, nvar, SUB, LANES), f32),
        ],
        in_specs=[SMEM] * 2 + [VMEM] * 3,
        out_specs=[VMEM] * 3,
        compiler_params=params(),
    )(obs_count, obs_var, coupling, dual_obs, innovation)

    own, traj_near, traj_far = pl.pallas_call(
        lambda *refs: assemble_kernel(windows, steps, nvar, levels, part, *refs),
        out_shape=[
            shape((steps, nvar * levels, rows, columns), bf16),
            shape((edge_base(steps, nvar, levels)[1], rows, columns), bf16),
            shape((edge_base(steps, nvar, levels)[1], rows, columns), bf16),
        ],
        in_specs=[VMEM] * windows + [ANY],
        out_specs=[VMEM] * 3,
        scratch_shapes=[pltpu.VMEM((windows, block.shape[0] - 1, rows, LANES), bf16)],
        compiler_params=params(),
    )(*blocks_here, mix)
    traj_far, traj_near = swapped(traj_far, "space", 1), swapped(traj_near, "space", 0)

    first = pl.pallas_call(
        lambda *refs: prepare_tangent_kernel(nvar, levels, tiles, *refs),
        out_shape=shape((levels, nvar, tiles, 2 * SUB, LANES), f32),
        in_specs=[VMEM] * 3,
        out_specs=VMEM,
        compiler_params=params(),
    )(near, far, increment)
    new_dual_obs, ends, wide_traj = pl.pallas_call(
        lambda *refs: tangent_kernel(spaces, steps, nvar, levels, tiles, *refs),
        out_shape=[
            shape(dual_obs.shape, f32),
            shape((levels, nvar, tiles, SUB, LANES), f32),
            shape((levels, steps, nvar, tiles, 2 * SUB, LANES), f32),
        ],
        in_specs=[VMEM] * 7,
        out_specs=[VMEM] * 3,
        scratch_shapes=[pltpu.VMEM((2, 2, nvar, tiles, 4 * SUB, LANES), f32)],
        compiler_params=params(),
    )(mix, share, obs, own, traj_far, traj_near, first)

    state = shape((nvar, 2, rows, columns), f32)
    coded = shape((nvar * tiles + 1, 2 * SUB, LANES), i16)
    base_duals, base_incs, sent = [], [], []
    before = ends
    for i in range(pairs):
        last, force = pl.pallas_call(
            lambda *refs, i=i: prepare_adjoint_kernel(i, steps, nvar, tiles, *refs),
            out_shape=[shape((2, n, tiles, 2 * SUB, LANES), f32) for n in (nvar, steps)],
            in_specs=[SMEM] + [VMEM] * 4 + [ANY],
            out_specs=[VMEM] * 2,
            compiler_params=params(),
        )(obs_count, near, far, dual_obs, after[i], before)
        base_dual, base_inc, *payloads = pl.pallas_call(
            lambda *refs, i=i: adjoint_kernel(
                i, windows, spaces, steps, nvar, levels, tiles, *refs
            ),
            out_shape=[state, state] + [coded] * (windows - 1),
            in_specs=[VMEM] * 9,
            out_specs=[VMEM] * (2 + windows - 1),
            scratch_shapes=[
                pltpu.VMEM((2, steps, tiles, 4 * SUB, LANES), f32),
                pltpu.VMEM((2, 2, nvar, tiles, 4 * SUB, LANES), f32),
                pltpu.VMEM((2,) + coded.shape, i16),
            ],
            compiler_params=params(),
        )(mix, totals, wide_traj, last, force, ends, increment, model_rhs, dual_model)
        before = base_dual
        base_duals.append(base_dual)
        base_incs.append(base_inc)
        sent += [
            exchanged(piece, "window", d) for piece, d in zip(payloads, order)
        ]

    new_dual_model, new_increment = pl.pallas_call(
        lambda *refs: final_kernel(windows, nvar, levels, tiles, *refs),
        out_shape=[shape(dual_model.shape, f32), shape(increment.shape, f32)],
        in_specs=[VMEM] * (len(sent) + 2 * pairs + 1),
        out_specs=[VMEM] * 2,
        compiler_params=params(),
    )(*sent, *base_duals, *base_incs, totals)
    return new_dual_model, new_dual_obs, new_increment


def solution(mesh):
    placed = (
        P("members", None, None, None, "space", "window"),
        P(("members", "window"), None, None, "space", None),
        P(("members", "window"), None, None, "space", None),
        P(("members", "window"), None, None, "space", None),
        P(("members", "window"), None, None, "space", None),
        P(("members", "window"), None, None, "space", None),
        P(),
        P(("members", "window"), None, None),
        P(("members", "window"), None, None),
        P(("members", "window")),
    )
    return jax.shard_map(
        body,
        mesh=mesh,
        in_specs=placed,
        out_specs=(
            P(("members", "window"), None, None, "space", None),
            P(("members", "window"), None, None, "space", None),
            P(("members", "window"), None, None, "space", None),
        ),
        check_vma=False,
    )
```

```python
import jax
import jax.numpy as jnp
from jax import lax
from jax.experimental import pallas as pl
from jax.experimental.pallas import tpu as pltpu
from jax.sharding import PartitionSpec as P

LANES = 128
SUB = 8
HALF = SUB // 2
CODE_MAX = 32000.0
ROUNDER = 12582912.0

diffusion = 0.2
advection = 0.2
coupling_gain = 0.5
keep = 1.0 - 4.0 * diffusion
half_adv = 0.5 * advection

VMEM = pl.BlockSpec(memory_space=pltpu.VMEM)
SMEM = pl.BlockSpec(memory_space=pltpu.SMEM)
ANY = pl.BlockSpec(memory_space=pl.ANY)


def params(mib=24):
    return pltpu.CompilerParams(vmem_limit_bytes=mib * 1024 * 1024)


def lane_index():
    return lax.broadcasted_iota(jnp.int32, (SUB, LANES), 1)


def row_index():
    return lax.broadcasted_iota(jnp.int32, (SUB, LANES), 0)


def tiled(wide):
    short = -wide.shape[1] % LANES
    if short:
        wide = jnp.concatenate([wide, jnp.zeros((wide.shape[0], short), wide.dtype)], 1)
    return [wide[:, i : i + LANES] for i in range(0, wide.shape[1], LANES)]


def place(parts, rolled, lane):
    built = {}
    for key, tiles, first, width, target in parts:
        done = 0
        while done < width:
            a, b = first + done, target + done
            n = min(width - done, LANES - a % LANES, LANES - b % LANES)
            shift = (b - a) % LANES
            name = (key, a // LANES, shift)
            if name not in rolled:
                value = tiles[a // LANES]
                rolled[name] = pltpu.roll(value, shift, 1) if shift else value
            if b % LANES:
                built[b // LANES] = jnp.where(
                    lane >= b % LANES, rolled[name], built[b // LANES]
                )
            else:
                built[b // LANES] = rolled[name]
            done += n
    return [built[i] for i in range(len(built))]


def joined_halves(first, second):
    top = row_index()[:, :1] < HALF
    last = jnp.where(top, pltpu.roll(first, HALF, 0), second)
    start = jnp.where(top, first, pltpu.roll(second, HALF, 0))
    return last, start


def widened(own, near, far, odd, even):
    top = row_index() < HALF
    low, high = jnp.where(even, far, near), jnp.where(even, near, far)
    turned = pltpu.roll(own, HALF, 0)
    low = pltpu.roll(low, HALF, 0) if odd else low
    high = high if odd else pltpu.roll(high, HALF, 0)
    return jnp.where(top, low, turned), jnp.where(top, turned, high)


def row_codes(planes):
    lane = lax.broadcasted_iota(jnp.int32, planes[0][0].shape, 1)
    scales = jnp.zeros(planes[0][0].shape, jnp.float32)
    out = []
    for v, row in enumerate(planes):
        big = jnp.abs(row[0])
        for value in row[1:]:
            big = jnp.maximum(big, jnp.abs(value))
        big = jnp.max(big, axis=1, keepdims=True)
        power = jnp.clip(jnp.ceil(jnp.log2(jnp.maximum(big, 1e-30))), -90.0, 126.0)
        scales = jnp.where(lane == v, power, scales)
        gain = CODE_MAX * jnp.exp2(-power)
        for value in row:
            out.append((value * gain + ROUNDER) - ROUNDER)
    return out, scales


def shorts(value):
    return value.astype(jnp.int32).astype(jnp.int16)


def floats(value):
    return value.astype(jnp.int32).astype(jnp.float32)


def partners(windows):
    return list(range(windows - 1, 0, -1))


def pack_kernel(ways, windows, steps, nvar, levels, part, var_ref, traj_ref, *outs):
    me = lax.axis_index("window")
    lane = lane_index()
    variance = var_ref[...]
    high = variance.astype(jnp.bfloat16).astype(jnp.float32)
    middle = (variance - high).astype(jnp.bfloat16).astype(jnp.float32)
    low = variance - high - middle
    split = high + pltpu.roll(middle, HALF, 0) + pltpu.roll(low, LANES // 2, 1)
    split = split.astype(jnp.bfloat16)

    for n, d in enumerate(ways):
        outs[n][outs[n].shape[0] - 1] = split
        target = lax.rem(me + d, windows)

        def variable(v, carry, n=n, target=target):
            for lev in range(levels):
                pieces = [
                    tiled(traj_ref[target, j, v, lev].astype(jnp.float32)) for j in range(steps)
                ]
                parts = [(j, pieces[j], 0, part, j * part) for j in range(steps)]
                placed = place(parts, {}, lane)
                for t, value in enumerate(placed):
                    outs[n][(v * levels + lev) * len(placed) + t] = value.astype(jnp.bfloat16)
            return carry

        lax.fori_loop(0, nvar, variable, 0, unroll=len(ways) == 1)


def even_place():
    return lax.rem(lax.axis_index("space"), 2) == 0


def level_codes(ref, lev, first=0):
    planes = [
        [ref[0, v, lev, :, t : t + LANES] for t in range(0, ref.shape[-1], LANES)]
        for v in range(first, ref.shape[1])
    ]
    values, scales = row_codes(planes)
    return values + [scales]


def half_code_kernel(*refs):
    sources, (near_ref, far_ref, own_ref) = refs[:-3], refs[-3:]
    even = even_place()

    def pair(i, carry):
        near, far = [], []
        for k, ref in enumerate(sources):
            skip = int(k == len(sources) - 1)
            coded = [level_codes(ref, 2 * i + odd, skip) for odd in range(2)]
            for n, (first, second) in enumerate(zip(*coded)):
                if k == 0:
                    own_ref[i, n] = shorts(jnp.concatenate([first, second], 0))
                last, start = joined_halves(first, second)
                near.append(jnp.where(even, last, start))
                far.append(jnp.where(even, start, last))
            if len(near) % 2:
                near.append(jnp.zeros((SUB, LANES), jnp.float32))
                far.append(jnp.zeros((SUB, LANES), jnp.float32))
        for tiles, ref in ((near, near_ref), (far, far_ref)):
            for n in range(0, len(tiles), 2):
                ref[i, n // 2] = shorts(jnp.concatenate(tiles[n : n + 2], 0))
        return carry

    lax.fori_loop(0, near_ref.shape[0], pair, 0)


def half_tile(ref, i, n):
    whole = floats(ref[i, n // 2])
    return whole[SUB:] if n % 2 else whole[:SUB]


def around_kernel(windows, nvar, levels, *refs):
    pieces, (own_ref, near_ref, far_ref) = refs[:windows], refs[windows : windows + 3]
    outs, total_ref = refs[windows + 3 : -1], refs[-1]
    me = lax.axis_index("window")
    even = even_place()
    total = jnp.zeros((SUB, LANES), jnp.float32)
    for d in range(windows):
        split = pieces[d][pieces[d].shape[0] - 1].astype(jnp.float32)
        here = split + pltpu.roll(split, HALF, 0) + pltpu.roll(split, LANES // 2, 1)
        total = total + jnp.where(lax.rem(me - d + windows, windows) <= me, here, 0.0)
    for v in range(nvar):
        for lev in range(levels):
            one = total[lev : lev + 1, v : v + 1]
            total_ref[v * levels + lev] = jnp.broadcast_to(one, (SUB, LANES))
    for i, out_ref in enumerate(outs):
        for n in range(own_ref.shape[1]):
            own = floats(own_ref[i, n])
            near, far = half_tile(near_ref, i, n), half_tile(far_ref, i, n)
            for odd in range(2):
                halves = widened(own[odd * SUB : (odd + 1) * SUB], near, far, odd, even)
                out_ref[odd, n] = shorts(jnp.concatenate(halves, 0))


def decoded(ref, i, first, nvar, tiles):
    scales = jnp.exp2(half_tile(ref, i, first + nvar * tiles)) * (1.0 / CODE_MAX)
    return [
        [half_tile(ref, i, first + v * tiles + t) * scales[:, v : v + 1] for t in range(tiles)]
        for v in range(nvar)
    ]


def is_quarter(j, v, steps):
    return 0 < j < steps - 1 and not (v == 0 and j + 1 > HALF // 2)


def edge_base(steps, nvar, levels):
    base, total = {}, 0
    for j in range(steps):
        for v in range(nvar):
            base[j, v] = total
            total += levels // (4 if is_quarter(j, v, steps) else 2)
    return base, total


def joined_quarters(four):
    slot = row_index() // 2
    last, start = pltpu.roll(four[0], 2, 0), four[0]
    for n in range(1, 4):
        last = jnp.where(slot == n, pltpu.roll(four[n], (2 * n + 2) % SUB, 0), last)
        start = jnp.where(slot == n, pltpu.roll(four[n], 2 * n, 0), start)
    return last, start


def assemble_kernel(windows, steps, nvar, levels, part, *refs):
    pieces = refs[:windows]
    own_ref, near_ref, far_ref, stack_ref = refs[windows + 1 :]
    me = lax.axis_index("window")
    even = even_place()
    lane = lane_index()
    count = stack_ref.shape[1]
    packed_tiles = count // (nvar * levels)
    for d in range(windows):
        stack_ref[lax.rem(me - d + windows, windows)] = pieces[d][:count]

    base, _ = edge_base(steps, nvar, levels)

    def variable(v):
        built = {}
        for lev in range(levels):
            plane = v * levels + lev
            sources = [
                [
                    stack_ref[w, plane * packed_tiles + t].astype(jnp.float32)
                    for t in range(packed_tiles)
                ]
                for w in range(windows)
            ]
            rolled = {}
            for j in range(steps):
                parts = [(w, sources[w], j * part, part, w * part) for w in range(windows)]
                built[j, lev] = place(parts, rolled, lane)
                own_ref[j, plane] = jnp.concatenate(built[j, lev], 1).astype(jnp.bfloat16)
        for j in range(steps):
            if is_quarter(j, v, steps):
                groups = [
                    [joined_quarters(four) for four in zip(*[built[j, 4 * q + n] for n in range(4)])]
                    for q in range(levels // 4)
                ]
            else:
                groups = [
                    [joined_halves(a, b) for a, b in zip(built[j, 2 * i], built[j, 2 * i + 1])]
                    for i in range(levels // 2)
                ]
            for n, group in enumerate(groups):
                last, start = (jnp.concatenate([e[k] for e in group], 1) for k in range(2))
                near_ref[base[j, v] + n] = jnp.where(even, last, start).astype(jnp.bfloat16)
                far_ref[base[j, v] + n] = jnp.where(even, start, last).astype(jnp.bfloat16)

    for v in range(nvar):
        variable(v)


def prepare_factor_kernel(
    steps, nvar, levels, tiles,
    count_ref, noise_ref, coupling_ref, dobs_ref, innov_ref, obs_ref, share_ref, mix_ref,
):
    cuts = [slice(t * LANES, (t + 1) * LANES) for t in range(tiles)]
    for v in range(nvar):
        for u in range(nvar):
            one = coupling_gain * coupling_ref[v : v + 1, u : u + 1]
            mix_ref[v, u] = jnp.broadcast_to(one, (SUB, LANES))
    for lev in range(levels):
        for j in range(steps):
            noise = jnp.full((SUB, LANES), noise_ref[0, j, lev])
            share = jnp.where(j < count_ref[0], 1.0, 0.0) / noise
            share_ref[lev, j] = share
            for t in range(tiles):
                gap = innov_ref[0, j, lev, :, cuts[t]] - noise * dobs_ref[0, j, lev, :, cuts[t]]
                obs_ref[lev, j, t] = gap * share


def prepare_tangent_kernel(nvar, levels, tiles, near_ref, far_ref, inc_ref, first_ref):
    even = even_place()
    blocks = [slice(0, SUB), slice(SUB, 2 * SUB)]
    cuts = [slice(t * LANES, (t + 1) * LANES) for t in range(tiles)]
    offset = -(-(nvar * tiles + 1) // 2) * 2
    for i in range(levels // 2):
        fields = [decoded(ref, i, offset, nvar, tiles) for ref in (near_ref, far_ref)]
        for odd in range(2):
            lev = 2 * i + odd
            for t in range(tiles):
                for v in range(nvar):
                    near, far = (side[v][t] for side in fields)
                    halves = widened(inc_ref[0, v, lev, :, cuts[t]], near, far, odd, even)
                    for b in range(2):
                        first_ref[lev, v, t, blocks[b], :] = halves[b]


def prepare_adjoint_kernel(
    i, steps, nvar, tiles, count_ref, near_ref, far_ref, dobs_ref, after_ref, *refs
):
    _, last_ref, force_ref = refs
    even = even_place()
    blocks = [slice(0, SUB), slice(SUB, 2 * SUB)]
    cuts = [slice(t * LANES, (t + 1) * LANES) for t in range(tiles)]
    seen = [jnp.where(j < count_ref[0], 1.0, 0.0) for j in range(steps)]
    offset = -(-(nvar * tiles + 1) // 2) * 2
    none = [[jnp.zeros((SUB, LANES), jnp.float32)] * tiles]
    forces = [none + decoded(ref, i, 2 * offset, steps - 1, tiles) for ref in (near_ref, far_ref)]
    for odd in range(2):
        scales = jnp.exp2(floats(after_ref[odd, nvar * tiles])) * (-1.0 / CODE_MAX)
        for t in range(tiles):
            for v in range(nvar):
                value = floats(after_ref[odd, v * tiles + t])
                last_ref[odd, v, t] = value * scales[:, v : v + 1]
            for j in range(steps):
                near, far = (side[j][t] for side in forces)
                halves = widened(dobs_ref[0, j, 2 * i + odd, :, cuts[t]], near, far, odd, even)
                for b in range(2):
                    force_ref[odd, j, t, blocks[b], :] = seen[j] * halves[b]


def from_north(line, lane):
    turned = [pltpu.roll(value, LANES - 1, 1) for value in line] * 2
    return [jnp.where(lane < LANES - 1, turned[t], turned[t + 1]) for t in range(len(line))]


def from_south(line, lane):
    turned = [pltpu.roll(value, 1, 1) for value in line]
    return [jnp.where(lane > 0, turned[t], turned[t - 1]) for t in range(len(line))]


def masked_last(line, lane):
    return line[:-1] + [jnp.where(lane < LANES - 1, line[-1], 0.0)]


def masked_first(line, lane):
    return [jnp.where(lane > 0, line[0], 0.0)] + line[1:]


def walls(spaces):
    row, place_x = row_index(), lax.axis_index("space")
    low = jnp.where((row == HALF) & (place_x == 0), 0.0, 1.0)
    high = jnp.where((row == HALF - 1) & (place_x == spaces - 1), 0.0, 1.0)

    def walled(block, east, west):
        if block == 0:
            return east, [low * value for value in west]
        return [high * value for value in east], west

    return walled


BLOCKS = [slice(SUB, 2 * SUB), slice(2 * SUB, 3 * SUB)]
UPS = [slice(b.start + 1, b.stop + 1) for b in BLOCKS]
DOWNS = [slice(b.start - 1, b.stop - 1) for b in BLOCKS]
MINE = slice(SUB + HALF, 2 * SUB + HALF)


def tangent_kernel(
    spaces, steps, nvar, levels, tiles,
    mix_ref, share_ref, obs_ref, own_ref, near_ref, far_ref, first_ref,
    ndo_ref, ends_ref, x_ref, s_ref,
):
    lane, row = lane_index(), row_index()
    even = even_place()
    top = row < HALF
    walled = walls(spaces)
    pairs = levels // 2
    cuts = [slice(t * LANES, (t + 1) * LANES) for t in range(tiles)]
    base, _ = edge_base(steps, nvar, levels)

    for lev in range(levels):
        odd = lev % 2
        for j in range(steps):
            for v in range(nvar):
                for t in range(tiles):
                    own = own_ref[j, v * levels + lev, :, cuts[t]].astype(jnp.float32)
                    quarter = is_quarter(j, v, steps)
                    tile = base[j, v] + lev // (4 if quarter else 2)
                    near = near_ref[tile, :, cuts[t]].astype(jnp.float32)
                    far = far_ref[tile, :, cuts[t]].astype(jnp.float32)
                    low, high = jnp.where(even, far, near), jnp.where(even, near, far)
                    if quarter:
                        slot = 2 * (lev % 4)
                        low = pltpu.roll(low, (HALF - 2 - slot) % SUB, 0)
                        high = pltpu.roll(high, (HALF - slot) % SUB, 0)
                    else:
                        low = pltpu.roll(low, HALF, 0) if odd else low
                        high = high if odd else pltpu.roll(high, HALF, 0)
                    turned = pltpu.roll(own, HALF, 0)
                    x_ref[lev, j, v, t, :SUB, :] = jnp.where(top, low, turned)
                    x_ref[lev, j, v, t, SUB:, :] = jnp.where(top, turned, high)

    def pair(i, outer):
        for odd in range(2):
            for v in range(nvar):
                for t in range(tiles):
                    s_ref[odd, 0, v, t, SUB : 3 * SUB, :] = first_ref[2 * i + odd, v, t]

        for j in range(steps):
            now = j % 2
            for odd in range(2):
                lev = 2 * i + odd
                for t in range(tiles):
                    image = share_ref[lev, j] * s_ref[odd, now, 0, t, MINE, :]
                    ndo_ref[0, j, lev, :, cuts[t]] = obs_ref[lev, j, t] - image
                for b in range(2):
                    part = slice(b * SUB, (b + 1) * SUB)
                    here, up, down = BLOCKS[b], UPS[b], DOWNS[b]
                    x = [[x_ref[lev, j, u, t, part, :] for t in range(tiles)] for u in range(nvar)]
                    ce = [diffusion - half_adv * value for value in x[0]]
                    cw = [diffusion + half_adv * value for value in x[0]]
                    ce, cw = walled(b, ce, cw)
                    cn = masked_last([diffusion - half_adv * value for value in x[1]], lane)
                    cs = masked_first([diffusion + half_adv * value for value in x[1]], lane)
                    s = [
                        [s_ref[odd, now, u, t, here, :] for t in range(tiles)] for u in range(nvar)
                    ]
                    xs = [[x[u][t] * s[u][t] for t in range(tiles)] for u in range(nvar)]
                    for v in range(nvar):
                        north, south = from_north(s[v], lane), from_south(s[v], lane)
                        for t in range(tiles):
                            fresh = keep * s[v][t] + ce[t] * s_ref[odd, now, v, t, up, :]
                            fresh = fresh + cw[t] * s_ref[odd, now, v, t, down, :]
                            fresh = fresh + cn[t] * north[t] + cs[t] * south[t]
                            for u in range(nvar):
                                fresh = fresh + mix_ref[v, u] * xs[u][t]
                            s_ref[odd, 1 - now, v, t, here, :] = fresh
        for odd in range(2):
            for v in range(nvar):
                for t in range(tiles):
                    ends_ref[2 * i + odd, v, t] = s_ref[odd, steps % 2, v, t, MINE, :]
        return outer

    lax.fori_loop(0, pairs, pair, 0)


def adjoint_kernel(
    i, windows, spaces, steps, nvar, levels, tiles,
    mix_ref, total_ref, x_ref, last_ref, force_ref, ends_ref, inc_ref, rhs_ref, dual_ref,
    ndm_ref, ninc_ref, *rest,
):
    payload_refs = rest[: windows - 1]
    x0_ref, a_ref, q_ref = rest[windows - 1 :]
    me = lax.axis_index("window")
    lane = lane_index()
    walled = walls(spaces)
    cuts = [slice(t * LANES, (t + 1) * LANES) for t in range(tiles)]

    for odd in range(2):
        lev = 2 * i + odd
        for t in range(tiles):
            for j in range(steps):
                x0_ref[odd, j, t, SUB : 3 * SUB, :] = x_ref[lev, j, 0, t]
            for v in range(nvar):
                a_ref[odd, 0, v, t, SUB : 3 * SUB, :] = last_ref[odd, v, t]

    for turn in range(steps):
        now = turn % 2
        j = steps - 1 - turn
        for odd in range(2):
            lev = 2 * i + odd
            for b in range(2):
                part = slice(b * SUB, (b + 1) * SUB)
                here, up, down = BLOCKS[b], UPS[b], DOWNS[b]
                x = [[x_ref[lev, j, u, t, part, :] for t in range(tiles)] for u in range(nvar)]
                ce = [diffusion + half_adv * x0_ref[odd, j, t, up, :] for t in range(tiles)]
                cw = [diffusion - half_adv * x0_ref[odd, j, t, down, :] for t in range(tiles)]
                ce, cw = walled(b, ce, cw)
                cn = masked_first([diffusion + half_adv * value for value in x[1]], lane)
                cs = masked_last([diffusion - half_adv * value for value in x[1]], lane)
                a = [
                    [a_ref[odd, now, u, t, here, :] for t in range(tiles)] for u in range(nvar)
                ]
                for u in range(nvar):
                    north = from_north([cn[t] * a[u][t] for t in range(tiles)], lane)
                    south = from_south([cs[t] * a[u][t] for t in range(tiles)], lane)
                    for t in range(tiles):
                        fresh = keep * a[u][t] + ce[t] * a_ref[odd, now, u, t, up, :]
                        fresh = fresh + cw[t] * a_ref[odd, now, u, t, down, :]
                        fresh = fresh + north[t] + south[t]
                        pull = mix_ref[0, u] * a[0][t]
                        for v in range(1, nvar):
                            pull = pull + mix_ref[v, u] * a[v][t]
                        fresh = fresh + x[u][t] * pull
                        if u == 0:
                            fresh = fresh + force_ref[odd, j, t, part, :]
                        a_ref[odd, 1 - now, u, t, here, :] = fresh
    end = steps % 2
    coded = []
    for odd in range(2):
        lev = 2 * i + odd
        back, ahead = [], []
        for v in range(nvar):
            share = total_ref[v * levels + lev]
            tv, gv = [], []
            for t in range(tiles):
                term = a_ref[odd, end, v, t, MINE, :] - last_ref[odd, v, t, HALF : HALF + SUB, :]
                given = rhs_ref[0, v, lev, :, cuts[t]] - inc_ref[0, v, lev, :, cuts[t]]
                given = given + share * term
                ndm_ref[v, odd, :, cuts[t]] = -(dual_ref[0, v, lev, :, cuts[t]] + term)
                ninc_ref[v, odd, :, cuts[t]] = given
                tv.append(term)
                gv.append(given + ends_ref[lev, v, t])
            back.append(tv)
            ahead.append(gv)
        coded.append((row_codes(back), row_codes(ahead)))
    for kind in range(2):
        first, second = coded[0][kind], coded[1][kind]
        for n, (a, b) in enumerate(zip(first[0] + [first[1]], second[0] + [second[1]])):
            q_ref[kind, n] = shorts(jnp.concatenate([a, b], 0))
    for ref, d in zip(payload_refs, partners(windows)):
        ref[...] = q_ref[jnp.where((me ^ d) < me, 0, 1)]


def final_kernel(windows, nvar, levels, tiles, *refs):
    pairs = levels // 2
    cut = pairs * (windows - 1)
    pieces, base_duals, base_incs = refs[:cut], refs[cut : cut + pairs], refs[cut + pairs : -3]
    total_ref, ndm_ref, ninc_ref = refs[-3:]
    me = lax.axis_index("window")
    cuts = [slice(t * LANES, (t + 1) * LANES) for t in range(tiles)]

    for i in range(pairs):
        tails = [None] * (nvar * tiles)
        heads = [None] * (nvar * tiles)
        for n, d in enumerate(partners(windows)):
            piece = pieces[i * (windows - 1) + n]
            later = (me ^ d) > me
            scales = jnp.exp2(floats(piece[nvar * tiles])) * (1.0 / CODE_MAX)
            for v in range(nvar):
                scale = scales[:, v : v + 1]
                for t in range(tiles):
                    k = v * tiles + t
                    value = floats(piece[k]) * scale
                    tail, head = jnp.where(later, value, 0.0), jnp.where(later, 0.0, value)
                    tails[k] = tails[k] + tail if n else tail
                    heads[k] = heads[k] + head if n else head
        for v in range(nvar):
            for odd in range(2):
                lev = 2 * i + odd
                share = total_ref[v * levels + lev]
                for t in range(tiles):
                    rows = slice(odd * SUB, (odd + 1) * SUB)
                    tail, head = tails[v * tiles + t][rows], heads[v * tiles + t][rows]
                    ndm_ref[0, v, lev, :, cuts[t]] = base_duals[i][v, odd, :, cuts[t]] - tail
                    ninc_ref[0, v, lev, :, cuts[t]] = (
                        base_incs[i][v, odd, :, cuts[t]] + head + share * tail
                    )


def moved(block, axis, distance):
    devices = range(lax.axis_size(axis))
    return lax.ppermute(block, axis, [(i, i + distance) for i in devices if i + distance in devices])


def rotated(block, axis, distance):
    count = lax.axis_size(axis)
    return lax.ppermute(block, axis, [(i, (i + distance) % count) for i in range(count)])


def exchanged(block, axis, mask):
    return lax.ppermute(block, axis, [(i, i ^ mask) for i in range(lax.axis_size(axis))])


def swaps(axis, first):
    route = []
    for i in range(first, lax.axis_size(axis) - 1, 2):
        route += [(i, i + 1), (i + 1, i)]
    return route


def swapped(block, axis, first):
    return lax.ppermute(block, axis, swaps(axis, first))


def body(
    trajectory,
    dual_model,
    increment,
    model_rhs,
    dual_obs,
    innovation,
    coupling,
    error_var,
    obs_var,
    obs_count,
):
    windows, spaces = lax.axis_size("window"), lax.axis_size("space")
    _, steps, nvar, levels, rows, part = trajectory.shape
    columns = dual_model.shape[-1]
    tiles = columns // LANES
    assert trajectory.shape[0] == windows and windows > 1 and rows == SUB and steps == HALF
    assert columns == tiles * LANES == windows * part and levels % 4 == 0
    assert windows & (windows - 1) == 0
    pairs = levels // 2
    wide = -(-steps * part // LANES) * LANES
    bf16, f32, i16 = jnp.bfloat16, jnp.float32, jnp.int16

    def shape(dims, dtype):
        return jax.ShapeDtypeStruct(dims, dtype)

    block = shape((nvar * levels * wide // LANES + 1, rows, LANES), bf16)
    variances = jnp.pad(error_var[0].T, ((0, SUB - levels), (0, LANES - nvar)))

    def packed(ways):
        return pl.pallas_call(
            lambda *refs: pack_kernel(ways, windows, steps, nvar, levels, part, *refs),
            out_shape=[block] * len(ways),
            in_specs=[VMEM, VMEM],
            out_specs=[VMEM] * len(ways),
            compiler_params=params(),
        )(variances, trajectory)

    order = list(range(1, windows))
    groups = [[d] for d in order] if windows <= 4 else [order]
    blocks = {}
    for group in groups:
        blocks.update(zip(group, packed(group)))
    arrived = {d: rotated(blocks[d], "window", d) for d in order}
    arrived[0] = packed([0])[0]

    payload = shape((pairs, nvar * tiles + 1, 2 * SUB, LANES), i16)

    counts = [nvar, nvar, steps - 1]
    half_tiles = sum(-(-(count * tiles + 1) // 2) for count in counts)
    halves = shape((pairs, half_tiles, 2 * SUB, LANES), i16)
    near, far, dual = pl.pallas_call(
        half_code_kernel,
        out_shape=[halves, halves, payload],
        in_specs=[VMEM] * 3,
        out_specs=[VMEM] * 3,
        compiler_params=params(),
    )(dual_model, increment, dual_obs)
    far, near = swapped(far, "space", 1), swapped(near, "space", 0)

    blocks_here = [arrived[d] for d in range(windows)]
    *after, totals = pl.pallas_call(
        lambda *refs: around_kernel(windows, nvar, levels, *refs),
        out_shape=[shape((2,) + payload.shape[1:], i16)] * pairs
        + [shape((nvar * levels, rows, LANES), f32)],
        in_specs=[VMEM] * (windows + 3),
        out_specs=[VMEM] * (pairs + 1),
        compiler_params=params(),
    )(*blocks_here, dual, near, far)
    after = [moved(piece, "window", -1) for piece in after]

    obs, share, mix = pl.pallas_call(
        lambda *refs: prepare_factor_kernel(steps, nvar, levels, tiles, *refs),
        out_shape=[
            shape((levels, steps, tiles, SUB, LANES), f32),
            shape((levels, steps, SUB, LANES), f32),
            shape((nvar, nvar, SUB, LANES), f32),
        ],
        in_specs=[SMEM] * 2 + [VMEM] * 3,
        out_specs=[VMEM] * 3,
        compiler_params=params(),
    )(obs_count, obs_var, coupling, dual_obs, innovation)

    own, traj_near, traj_far = pl.pallas_call(
        lambda *refs: assemble_kernel(windows, steps, nvar, levels, part, *refs),
        out_shape=[
            shape((steps, nvar * levels, rows, columns), bf16),
            shape((edge_base(steps, nvar, levels)[1], rows, columns), bf16),
            shape((edge_base(steps, nvar, levels)[1], rows, columns), bf16),
        ],
        in_specs=[VMEM] * windows + [ANY],
        out_specs=[VMEM] * 3,
        scratch_shapes=[pltpu.VMEM((windows, block.shape[0] - 1, rows, LANES), bf16)],
        compiler_params=params(),
    )(*blocks_here, mix)
    traj_far, traj_near = swapped(traj_far, "space", 1), swapped(traj_near, "space", 0)

    first = pl.pallas_call(
        lambda *refs: prepare_tangent_kernel(nvar, levels, tiles, *refs),
        out_shape=shape((levels, nvar, tiles, 2 * SUB, LANES), f32),
        in_specs=[VMEM] * 3,
        out_specs=VMEM,
        compiler_params=params(),
    )(near, far, increment)
    new_dual_obs, ends, wide_traj = pl.pallas_call(
        lambda *refs: tangent_kernel(spaces, steps, nvar, levels, tiles, *refs),
        out_shape=[
            shape(dual_obs.shape, f32),
            shape((levels, nvar, tiles, SUB, LANES), f32),
            shape((levels, steps, nvar, tiles, 2 * SUB, LANES), f32),
        ],
        in_specs=[VMEM] * 7,
        out_specs=[VMEM] * 3,
        scratch_shapes=[pltpu.VMEM((2, 2, nvar, tiles, 4 * SUB, LANES), f32)],
        compiler_params=params(),
    )(mix, share, obs, own, traj_near, traj_far, first)

    state = shape((nvar, 2, rows, columns), f32)
    coded = shape((nvar * tiles + 1, 2 * SUB, LANES), i16)
    base_duals, base_incs, sent = [], [], []
    before = ends
    for i in range(pairs):
        last, force = pl.pallas_call(
            lambda *refs, i=i: prepare_adjoint_kernel(i, steps, nvar, tiles, *refs),
            out_shape=[shape((2, n, tiles, 2 * SUB, LANES), f32) for n in (nvar, steps)],
            in_specs=[SMEM] + [VMEM] * 4 + [ANY],
            out_specs=[VMEM] * 2,
            compiler_params=params(),
        )(obs_count, near, far, dual_obs, after[i], before)
        base_dual, base_inc, *payloads = pl.pallas_call(
            lambda *refs, i=i: adjoint_kernel(
                i, windows, spaces, steps, nvar, levels, tiles, *refs
            ),
            out_shape=[state, state] + [coded] * (windows - 1),
            in_specs=[VMEM] * 9,
            out_specs=[VMEM] * (2 + windows - 1),
            scratch_shapes=[
                pltpu.VMEM((2, steps, tiles, 4 * SUB, LANES), f32),
                pltpu.VMEM((2, 2, nvar, tiles, 4 * SUB, LANES), f32),
                pltpu.VMEM((2,) + coded.shape, i16),
            ],
            compiler_params=params(),
        )(mix, totals, wide_traj, last, force, ends, increment, model_rhs, dual_model)
        before = base_dual
        base_duals.append(base_dual)
        base_incs.append(base_inc)
        sent += [
            exchanged(piece, "window", mask)
            for piece, mask in zip(payloads, partners(windows))
        ]

    new_dual_model, new_increment = pl.pallas_call(
        lambda *refs: final_kernel(windows, nvar, levels, tiles, *refs),
        out_shape=[shape(dual_model.shape, f32), shape(increment.shape, f32)],
        in_specs=[VMEM] * (len(sent) + 2 * pairs + 1),
        out_specs=[VMEM] * 2,
        compiler_params=params(),
    )(*sent, *base_duals, *base_incs, totals)
    return new_dual_model, new_dual_obs, new_increment


def solution(mesh):
    placed = (
        P("members", None, None, None, "space", "window"),
        P(("members", "window"), None, None, "space", None),
        P(("members", "window"), None, None, "space", None),
        P(("members", "window"), None, None, "space", None),
        P(("members", "window"), None, None, "space", None),
        P(("members", "window"), None, None, "space", None),
        P(),
        P(("members", "window"), None, None),
        P(("members", "window"), None, None),
        P(("members", "window")),
    )
    return jax.shard_map(
        body,
        mesh=mesh,
        in_specs=placed,
        out_specs=(
            P(("members", "window"), None, None, "space", None),
            P(("members", "window"), None, None, "space", None),
            P(("members", "window"), None, None, "space", None),
        ),
        check_vma=False,
    )
```

```python
import jax
import jax.numpy as jnp
from jax import lax
from jax.experimental import pallas as pl
from jax.experimental.pallas import tpu as pltpu
from jax.sharding import PartitionSpec as P

LANES = 128
SUB = 8
HALF = SUB // 2
CODE_MAX = 32000.0
ROUNDER = 12582912.0

diffusion = 0.2
advection = 0.2
coupling_gain = 0.5
keep = 1.0 - 4.0 * diffusion
half_adv = 0.5 * advection

VMEM = pl.BlockSpec(memory_space=pltpu.VMEM)
SMEM = pl.BlockSpec(memory_space=pltpu.SMEM)
ANY = pl.BlockSpec(memory_space=pl.ANY)


def params(mib=24):
    return pltpu.CompilerParams(vmem_limit_bytes=mib * 1024 * 1024)


def lane_index():
    return lax.broadcasted_iota(jnp.int32, (SUB, LANES), 1)


def row_index():
    return lax.broadcasted_iota(jnp.int32, (SUB, LANES), 0)


def tiled(wide):
    short = -wide.shape[1] % LANES
    if short:
        wide = jnp.concatenate([wide, jnp.zeros((wide.shape[0], short), wide.dtype)], 1)
    return [wide[:, i : i + LANES] for i in range(0, wide.shape[1], LANES)]


def place(parts, rolled, lane):
    built = {}
    for key, tiles, first, width, target in parts:
        done = 0
        while done < width:
            a, b = first + done, target + done
            n = min(width - done, LANES - a % LANES, LANES - b % LANES)
            shift = (b - a) % LANES
            name = (key, a // LANES, shift)
            if name not in rolled:
                value = tiles[a // LANES]
                rolled[name] = pltpu.roll(value, shift, 1) if shift else value
            if b % LANES:
                built[b // LANES] = jnp.where(
                    lane >= b % LANES, rolled[name], built[b // LANES]
                )
            else:
                built[b // LANES] = rolled[name]
            done += n
    return [built[i] for i in range(len(built))]


def joined_halves(first, second):
    top = row_index()[:, :1] < HALF
    last = jnp.where(top, pltpu.roll(first, HALF, 0), second)
    start = jnp.where(top, first, pltpu.roll(second, HALF, 0))
    return last, start


def widened(own, near, far, odd, even):
    top = row_index() < HALF
    low, high = jnp.where(even, far, near), jnp.where(even, near, far)
    turned = pltpu.roll(own, HALF, 0)
    low = pltpu.roll(low, HALF, 0) if odd else low
    high = high if odd else pltpu.roll(high, HALF, 0)
    return jnp.where(top, low, turned), jnp.where(top, turned, high)


def row_codes(planes):
    lane = lax.broadcasted_iota(jnp.int32, planes[0][0].shape, 1)
    scales = jnp.zeros(planes[0][0].shape, jnp.float32)
    out = []
    for v, row in enumerate(planes):
        big = jnp.abs(row[0])
        for value in row[1:]:
            big = jnp.maximum(big, jnp.abs(value))
        big = jnp.max(big, axis=1, keepdims=True)
        power = jnp.clip(jnp.ceil(jnp.log2(jnp.maximum(big, 1e-30))), -90.0, 126.0)
        scales = jnp.where(lane == v, power, scales)
        gain = CODE_MAX * jnp.exp2(-power)
        for value in row:
            out.append((value * gain + ROUNDER) - ROUNDER)
    return out, scales


def shorts(value):
    return value.astype(jnp.int32).astype(jnp.int16)


def floats(value):
    return value.astype(jnp.int32).astype(jnp.float32)


def partners(windows):
    return list(range(1, windows))


def pack_kernel(ways, windows, steps, nvar, levels, part, var_ref, traj_ref, *outs):
    me = lax.axis_index("window")
    lane = lane_index()
    variance = var_ref[...]
    high = variance.astype(jnp.bfloat16).astype(jnp.float32)
    middle = (variance - high).astype(jnp.bfloat16).astype(jnp.float32)
    low = variance - high - middle
    split = high + pltpu.roll(middle, HALF, 0) + pltpu.roll(low, LANES // 2, 1)
    split = split.astype(jnp.bfloat16)

    for n, d in enumerate(ways):
        outs[n][outs[n].shape[0] - 1] = split
        target = lax.rem(me + d, windows)

        def variable(v, carry, n=n, target=target):
            for lev in range(levels):
                pieces = [
                    tiled(traj_ref[target, j, v, lev].astype(jnp.float32)) for j in range(steps)
                ]
                parts = [(j, pieces[j], 0, part, j * part) for j in range(steps)]
                placed = place(parts, {}, lane)
                for t, value in enumerate(placed):
                    outs[n][(v * levels + lev) * len(placed) + t] = value.astype(jnp.bfloat16)
            return carry

        lax.fori_loop(0, nvar, variable, 0, unroll=len(ways) == 1)


def even_place():
    return lax.rem(lax.axis_index("space"), 2) == 0


def level_codes(ref, lev, first=0):
    planes = [
        [ref[0, v, lev, :, t : t + LANES] for t in range(0, ref.shape[-1], LANES)]
        for v in range(first, ref.shape[1])
    ]
    values, scales = row_codes(planes)
    return values + [scales]


def half_code_kernel(*refs):
    sources, (near_ref, far_ref, own_ref) = refs[:-3], refs[-3:]
    even = even_place()

    def pair(i, carry):
        near, far = [], []
        for k, ref in enumerate(sources):
            skip = int(k == len(sources) - 1)
            coded = [level_codes(ref, 2 * i + odd, skip) for odd in range(2)]
            for n, (first, second) in enumerate(zip(*coded)):
                if k == 0:
                    own_ref[i, n] = shorts(jnp.concatenate([first, second], 0))
                last, start = joined_halves(first, second)
                near.append(jnp.where(even, last, start))
                far.append(jnp.where(even, start, last))
            if len(near) % 2:
                near.append(jnp.zeros((SUB, LANES), jnp.float32))
                far.append(jnp.zeros((SUB, LANES), jnp.float32))
        for tiles, ref in ((near, near_ref), (far, far_ref)):
            for n in range(0, len(tiles), 2):
                ref[i, n // 2] = shorts(jnp.concatenate(tiles[n : n + 2], 0))
        return carry

    lax.fori_loop(0, near_ref.shape[0], pair, 0)


def half_tile(ref, i, n):
    whole = floats(ref[i, n // 2])
    return whole[SUB:] if n % 2 else whole[:SUB]


def around_kernel(windows, nvar, levels, *refs):
    pieces, (own_ref, near_ref, far_ref) = refs[:windows], refs[windows : windows + 3]
    outs, total_ref = refs[windows + 3 : -1], refs[-1]
    me = lax.axis_index("window")
    even = even_place()
    total = jnp.zeros((SUB, LANES), jnp.float32)
    for d in range(windows):
        split = pieces[d][pieces[d].shape[0] - 1].astype(jnp.float32)
        here = split + pltpu.roll(split, HALF, 0) + pltpu.roll(split, LANES // 2, 1)
        total = total + jnp.where(lax.rem(me - d + windows, windows) <= me, here, 0.0)
    for v in range(nvar):
        for lev in range(levels):
            one = total[lev : lev + 1, v : v + 1]
            total_ref[v * levels + lev] = jnp.broadcast_to(one, (SUB, LANES))
    for i, out_ref in enumerate(outs):
        for n in range(own_ref.shape[1]):
            own = floats(own_ref[i, n])
            near, far = half_tile(near_ref, i, n), half_tile(far_ref, i, n)
            for odd in range(2):
                halves = widened(own[odd * SUB : (odd + 1) * SUB], near, far, odd, even)
                out_ref[odd, n] = shorts(jnp.concatenate(halves, 0))


def decoded(ref, i, first, nvar, tiles):
    scales = jnp.exp2(half_tile(ref, i, first + nvar * tiles)) * (1.0 / CODE_MAX)
    return [
        [half_tile(ref, i, first + v * tiles + t) * scales[:, v : v + 1] for t in range(tiles)]
        for v in range(nvar)
    ]


def is_quarter(j, v, steps):
    return 0 < j < steps - 1 and not (v == 0 and j + 1 > HALF // 2)


def edge_base(steps, nvar, levels):
    base, total = {}, 0
    for j in range(steps):
        for v in range(nvar):
            base[j, v] = total
            total += levels // (4 if is_quarter(j, v, steps) else 2)
    return base, total


def joined_quarters(four):
    slot = row_index() // 2
    last, start = pltpu.roll(four[0], 2, 0), four[0]
    for n in range(1, 4):
        last = jnp.where(slot == n, pltpu.roll(four[n], (2 * n + 2) % SUB, 0), last)
        start = jnp.where(slot == n, pltpu.roll(four[n], 2 * n, 0), start)
    return last, start


def assemble_kernel(windows, steps, nvar, levels, part, *refs):
    pieces = refs[:windows]
    own_ref, near_ref, far_ref, stack_ref = refs[windows + 1 :]
    me = lax.axis_index("window")
    even = even_place()
    lane = lane_index()
    count = stack_ref.shape[1]
    packed_tiles = count // (nvar * levels)
    for d in range(windows):
        stack_ref[lax.rem(me - d + windows, windows)] = pieces[d][:count]

    base, _ = edge_base(steps, nvar, levels)

    def variable(v):
        built = {}
        for lev in range(levels):
            plane = v * levels + lev
            sources = [
                [
                    stack_ref[w, plane * packed_tiles + t].astype(jnp.float32)
                    for t in range(packed_tiles)
                ]
                for w in range(windows)
            ]
            rolled = {}
            for j in range(steps):
                parts = [(w, sources[w], j * part, part, w * part) for w in range(windows)]
                built[j, lev] = place(parts, rolled, lane)
                own_ref[j, plane] = jnp.concatenate(built[j, lev], 1).astype(jnp.bfloat16)
        for j in range(steps):
            if is_quarter(j, v, steps):
                groups = [
                    [joined_quarters(four) for four in zip(*[built[j, 4 * q + n] for n in range(4)])]
                    for q in range(levels // 4)
                ]
            else:
                groups = [
                    [joined_halves(a, b) for a, b in zip(built[j, 2 * i], built[j, 2 * i + 1])]
                    for i in range(levels // 2)
                ]
            for n, group in enumerate(groups):
                last, start = (jnp.concatenate([e[k] for e in group], 1) for k in range(2))
                near_ref[base[j, v] + n] = jnp.where(even, last, start).astype(jnp.bfloat16)
                far_ref[base[j, v] + n] = jnp.where(even, start, last).astype(jnp.bfloat16)

    for v in range(nvar):
        variable(v)


def prepare_factor_kernel(
    steps, nvar, levels, tiles,
    count_ref, noise_ref, coupling_ref, dobs_ref, innov_ref, obs_ref, share_ref, mix_ref,
):
    cuts = [slice(t * LANES, (t + 1) * LANES) for t in range(tiles)]
    for v in range(nvar):
        for u in range(nvar):
            one = coupling_gain * coupling_ref[v : v + 1, u : u + 1]
            mix_ref[v, u] = jnp.broadcast_to(one, (SUB, LANES))
    for lev in range(levels):
        for j in range(steps):
            noise = jnp.full((SUB, LANES), noise_ref[0, j, lev])
            share = jnp.where(j < count_ref[0], 1.0, 0.0) / noise
            share_ref[lev, j] = share
            for t in range(tiles):
                gap = innov_ref[0, j, lev, :, cuts[t]] - noise * dobs_ref[0, j, lev, :, cuts[t]]
                obs_ref[lev, j, t] = gap * share


def prepare_tangent_kernel(nvar, levels, tiles, near_ref, far_ref, inc_ref, first_ref):
    even = even_place()
    blocks = [slice(0, SUB), slice(SUB, 2 * SUB)]
    cuts = [slice(t * LANES, (t + 1) * LANES) for t in range(tiles)]
    offset = -(-(nvar * tiles + 1) // 2) * 2
    for i in range(levels // 2):
        fields = [decoded(ref, i, offset, nvar, tiles) for ref in (near_ref, far_ref)]
        for odd in range(2):
            lev = 2 * i + odd
            for t in range(tiles):
                for v in range(nvar):
                    near, far = (side[v][t] for side in fields)
                    halves = widened(inc_ref[0, v, lev, :, cuts[t]], near, far, odd, even)
                    for b in range(2):
                        first_ref[lev, v, t, blocks[b], :] = halves[b]


def prepare_adjoint_kernel(
    i, steps, nvar, tiles, count_ref, near_ref, far_ref, dobs_ref, after_ref, *refs
):
    _, last_ref, force_ref = refs
    even = even_place()
    blocks = [slice(0, SUB), slice(SUB, 2 * SUB)]
    cuts = [slice(t * LANES, (t + 1) * LANES) for t in range(tiles)]
    seen = [jnp.where(j < count_ref[0], 1.0, 0.0) for j in range(steps)]
    offset = -(-(nvar * tiles + 1) // 2) * 2
    none = [[jnp.zeros((SUB, LANES), jnp.float32)] * tiles]
    forces = [none + decoded(ref, i, 2 * offset, steps - 1, tiles) for ref in (near_ref, far_ref)]
    for odd in range(2):
        scales = jnp.exp2(floats(after_ref[odd, nvar * tiles])) * (-1.0 / CODE_MAX)
        for t in range(tiles):
            for v in range(nvar):
                value = floats(after_ref[odd, v * tiles + t])
                last_ref[odd, v, t] = value * scales[:, v : v + 1]
            for j in range(steps):
                near, far = (side[j][t] for side in forces)
                halves = widened(dobs_ref[0, j, 2 * i + odd, :, cuts[t]], near, far, odd, even)
                for b in range(2):
                    force_ref[odd, j, t, blocks[b], :] = seen[j] * halves[b]


def from_north(line, lane):
    turned = [pltpu.roll(value, LANES - 1, 1) for value in line] * 2
    return [jnp.where(lane < LANES - 1, turned[t], turned[t + 1]) for t in range(len(line))]


def from_south(line, lane):
    turned = [pltpu.roll(value, 1, 1) for value in line]
    return [jnp.where(lane > 0, turned[t], turned[t - 1]) for t in range(len(line))]


def masked_last(line, lane):
    return line[:-1] + [jnp.where(lane < LANES - 1, line[-1], 0.0)]


def masked_first(line, lane):
    return [jnp.where(lane > 0, line[0], 0.0)] + line[1:]


def walls(spaces):
    row, place_x = row_index(), lax.axis_index("space")
    low = jnp.where((row == HALF) & (place_x == 0), 0.0, 1.0)
    high = jnp.where((row == HALF - 1) & (place_x == spaces - 1), 0.0, 1.0)

    def walled(block, east, west):
        if block == 0:
            return east, [low * value for value in west]
        return [high * value for value in east], west

    return walled


BLOCKS = [slice(SUB, 2 * SUB), slice(2 * SUB, 3 * SUB)]
UPS = [slice(b.start + 1, b.stop + 1) for b in BLOCKS]
DOWNS = [slice(b.start - 1, b.stop - 1) for b in BLOCKS]
MINE = slice(SUB + HALF, 2 * SUB + HALF)


def tangent_kernel(
    spaces, steps, nvar, levels, tiles,
    mix_ref, share_ref, obs_ref, own_ref, near_ref, far_ref, first_ref,
    ndo_ref, ends_ref, x_ref, s_ref,
):
    lane, row = lane_index(), row_index()
    even = even_place()
    top = row < HALF
    walled = walls(spaces)
    pairs = levels // 2
    cuts = [slice(t * LANES, (t + 1) * LANES) for t in range(tiles)]
    base, _ = edge_base(steps, nvar, levels)

    for lev in range(levels):
        odd = lev % 2
        for j in range(steps):
            for v in range(nvar):
                for t in range(tiles):
                    own = own_ref[j, v * levels + lev, :, cuts[t]].astype(jnp.float32)
                    quarter = is_quarter(j, v, steps)
                    tile = base[j, v] + lev // (4 if quarter else 2)
                    near = near_ref[tile, :, cuts[t]].astype(jnp.float32)
                    far = far_ref[tile, :, cuts[t]].astype(jnp.float32)
                    low, high = jnp.where(even, far, near), jnp.where(even, near, far)
                    if quarter:
                        slot = 2 * (lev % 4)
                        low = pltpu.roll(low, (HALF - 2 - slot) % SUB, 0)
                        high = pltpu.roll(high, (HALF - slot) % SUB, 0)
                    else:
                        low = pltpu.roll(low, HALF, 0) if odd else low
                        high = high if odd else pltpu.roll(high, HALF, 0)
                    turned = pltpu.roll(own, HALF, 0)
                    x_ref[lev, j, v, t, :SUB, :] = jnp.where(top, low, turned)
                    x_ref[lev, j, v, t, SUB:, :] = jnp.where(top, turned, high)

    def pair(i, outer):
        for odd in range(2):
            for v in range(nvar):
                for t in range(tiles):
                    s_ref[odd, 0, v, t, SUB : 3 * SUB, :] = first_ref[2 * i + odd, v, t]

        for j in range(steps):
            now = j % 2
            for odd in range(2):
                lev = 2 * i + odd
                for t in range(tiles):
                    image = share_ref[lev, j] * s_ref[odd, now, 0, t, MINE, :]
                    ndo_ref[0, j, lev, :, cuts[t]] = obs_ref[lev, j, t] - image
                for b in range(2):
                    part = slice(b * SUB, (b + 1) * SUB)
                    here, up, down = BLOCKS[b], UPS[b], DOWNS[b]
                    x = [[x_ref[lev, j, u, t, part, :] for t in range(tiles)] for u in range(nvar)]
                    ce = [diffusion - half_adv * value for value in x[0]]
                    cw = [diffusion + half_adv * value for value in x[0]]
                    ce, cw = walled(b, ce, cw)
                    cn = masked_last([diffusion - half_adv * value for value in x[1]], lane)
                    cs = masked_first([diffusion + half_adv * value for value in x[1]], lane)
                    s = [
                        [s_ref[odd, now, u, t, here, :] for t in range(tiles)] for u in range(nvar)
                    ]
                    xs = [[x[u][t] * s[u][t] for t in range(tiles)] for u in range(nvar)]
                    for v in range(nvar):
                        north, south = from_north(s[v], lane), from_south(s[v], lane)
                        for t in range(tiles):
                            fresh = keep * s[v][t] + ce[t] * s_ref[odd, now, v, t, up, :]
                            fresh = fresh + cw[t] * s_ref[odd, now, v, t, down, :]
                            fresh = fresh + cn[t] * north[t] + cs[t] * south[t]
                            for u in range(nvar):
                                fresh = fresh + mix_ref[v, u] * xs[u][t]
                            s_ref[odd, 1 - now, v, t, here, :] = fresh
        for odd in range(2):
            for v in range(nvar):
                for t in range(tiles):
                    ends_ref[2 * i + odd, v, t] = s_ref[odd, steps % 2, v, t, MINE, :]
        return outer

    lax.fori_loop(0, pairs, pair, 0)


def adjoint_kernel(
    i, windows, spaces, steps, nvar, levels, tiles,
    mix_ref, total_ref, x_ref, last_ref, force_ref, ends_ref, inc_ref, rhs_ref, dual_ref,
    ndm_ref, ninc_ref, *rest,
):
    payload_refs = rest[: windows - 1]
    x0_ref, a_ref, q_ref = rest[windows - 1 :]
    me = lax.axis_index("window")
    lane = lane_index()
    walled = walls(spaces)
    cuts = [slice(t * LANES, (t + 1) * LANES) for t in range(tiles)]

    for odd in range(2):
        lev = 2 * i + odd
        for t in range(tiles):
            for j in range(steps):
                x0_ref[odd, j, t, SUB : 3 * SUB, :] = x_ref[lev, j, 0, t]
            for v in range(nvar):
                a_ref[odd, 0, v, t, SUB : 3 * SUB, :] = last_ref[odd, v, t]

    for turn in range(steps):
        now = turn % 2
        j = steps - 1 - turn
        for odd in range(2):
            lev = 2 * i + odd
            for b in range(2):
                part = slice(b * SUB, (b + 1) * SUB)
                here, up, down = BLOCKS[b], UPS[b], DOWNS[b]
                x = [[x_ref[lev, j, u, t, part, :] for t in range(tiles)] for u in range(nvar)]
                ce = [diffusion + half_adv * x0_ref[odd, j, t, up, :] for t in range(tiles)]
                cw = [diffusion - half_adv * x0_ref[odd, j, t, down, :] for t in range(tiles)]
                ce, cw = walled(b, ce, cw)
                cn = masked_first([diffusion + half_adv * value for value in x[1]], lane)
                cs = masked_last([diffusion - half_adv * value for value in x[1]], lane)
                a = [
                    [a_ref[odd, now, u, t, here, :] for t in range(tiles)] for u in range(nvar)
                ]
                for u in range(nvar):
                    north = from_north([cn[t] * a[u][t] for t in range(tiles)], lane)
                    south = from_south([cs[t] * a[u][t] for t in range(tiles)], lane)
                    for t in range(tiles):
                        fresh = keep * a[u][t] + ce[t] * a_ref[odd, now, u, t, up, :]
                        fresh = fresh + cw[t] * a_ref[odd, now, u, t, down, :]
                        fresh = fresh + north[t] + south[t]
                        pull = mix_ref[0, u] * a[0][t]
                        for v in range(1, nvar):
                            pull = pull + mix_ref[v, u] * a[v][t]
                        fresh = fresh + x[u][t] * pull
                        if u == 0:
                            fresh = fresh + force_ref[odd, j, t, part, :]
                        a_ref[odd, 1 - now, u, t, here, :] = fresh
    end = steps % 2
    coded = []
    for odd in range(2):
        lev = 2 * i + odd
        back, ahead = [], []
        for v in range(nvar):
            share = total_ref[v * levels + lev]
            tv, gv = [], []
            for t in range(tiles):
                term = a_ref[odd, end, v, t, MINE, :] - last_ref[odd, v, t, HALF : HALF + SUB, :]
                given = rhs_ref[0, v, lev, :, cuts[t]] - inc_ref[0, v, lev, :, cuts[t]]
                given = given + share * term
                ndm_ref[v, odd, :, cuts[t]] = -(dual_ref[0, v, lev, :, cuts[t]] + term)
                ninc_ref[v, odd, :, cuts[t]] = given
                tv.append(term)
                gv.append(given + ends_ref[lev, v, t])
            back.append(tv)
            ahead.append(gv)
        coded.append((row_codes(back), row_codes(ahead)))
    for kind in range(2):
        first, second = coded[0][kind], coded[1][kind]
        for n, (a, b) in enumerate(zip(first[0] + [first[1]], second[0] + [second[1]])):
            q_ref[kind, n] = shorts(jnp.concatenate([a, b], 0))
    for ref, d in zip(payload_refs, partners(windows)):
        ref[...] = q_ref[jnp.where((me ^ d) < me, 0, 1)]


def final_kernel(windows, nvar, levels, tiles, *refs):
    pairs = levels // 2
    cut = pairs * (windows - 1)
    pieces, base_duals, base_incs = refs[:cut], refs[cut : cut + pairs], refs[cut + pairs : -3]
    total_ref, ndm_ref, ninc_ref = refs[-3:]
    me = lax.axis_index("window")
    cuts = [slice(t * LANES, (t + 1) * LANES) for t in range(tiles)]

    for i in range(pairs):
        tails = [None] * (nvar * tiles)
        heads = [None] * (nvar * tiles)
        for n, d in enumerate(partners(windows)):
            piece = pieces[i * (windows - 1) + n]
            later = (me ^ d) > me
            scales = jnp.exp2(floats(piece[nvar * tiles])) * (1.0 / CODE_MAX)
            for v in range(nvar):
                scale = scales[:, v : v + 1]
                for t in range(tiles):
                    k = v * tiles + t
                    value = floats(piece[k]) * scale
                    tail, head = jnp.where(later, value, 0.0), jnp.where(later, 0.0, value)
                    tails[k] = tails[k] + tail if n else tail
                    heads[k] = heads[k] + head if n else head
        for v in range(nvar):
            for odd in range(2):
                lev = 2 * i + odd
                share = total_ref[v * levels + lev]
                for t in range(tiles):
                    rows = slice(odd * SUB, (odd + 1) * SUB)
                    tail, head = tails[v * tiles + t][rows], heads[v * tiles + t][rows]
                    ndm_ref[0, v, lev, :, cuts[t]] = base_duals[i][v, odd, :, cuts[t]] - tail
                    ninc_ref[0, v, lev, :, cuts[t]] = (
                        base_incs[i][v, odd, :, cuts[t]] + head + share * tail
                    )


def moved(block, axis, distance):
    devices = range(lax.axis_size(axis))
    return lax.ppermute(block, axis, [(i, i + distance) for i in devices if i + distance in devices])


def rotated(block, axis, distance):
    count = lax.axis_size(axis)
    return lax.ppermute(block, axis, [(i, (i + distance) % count) for i in range(count)])


def exchanged(block, axis, mask):
    return lax.ppermute(block, axis, [(i, i ^ mask) for i in range(lax.axis_size(axis))])


def swaps(axis, first):
    route = []
    for i in range(first, lax.axis_size(axis) - 1, 2):
        route += [(i, i + 1), (i + 1, i)]
    return route


def swapped(block, axis, first):
    return lax.ppermute(block, axis, swaps(axis, first))


def body(
    trajectory,
    dual_model,
    increment,
    model_rhs,
    dual_obs,
    innovation,
    coupling,
    error_var,
    obs_var,
    obs_count,
):
    windows, spaces = lax.axis_size("window"), lax.axis_size("space")
    _, steps, nvar, levels, rows, part = trajectory.shape
    columns = dual_model.shape[-1]
    tiles = columns // LANES
    assert trajectory.shape[0] == windows and windows > 1 and rows == SUB and steps == HALF
    assert columns == tiles * LANES == windows * part and levels % 4 == 0
    assert windows & (windows - 1) == 0
    pairs = levels // 2
    wide = -(-steps * part // LANES) * LANES
    bf16, f32, i16 = jnp.bfloat16, jnp.float32, jnp.int16

    def shape(dims, dtype):
        return jax.ShapeDtypeStruct(dims, dtype)

    block = shape((nvar * levels * wide // LANES + 1, rows, LANES), bf16)
    variances = jnp.pad(error_var[0].T, ((0, SUB - levels), (0, LANES - nvar)))

    def packed(ways):
        return pl.pallas_call(
            lambda *refs: pack_kernel(ways, windows, steps, nvar, levels, part, *refs),
            out_shape=[block] * len(ways),
            in_specs=[VMEM, VMEM],
            out_specs=[VMEM] * len(ways),
            compiler_params=params(),
        )(variances, trajectory)

    order = list(range(1, windows))
    groups = [[d] for d in order] if windows <= 4 else [order]
    blocks = {}
    for group in groups:
        blocks.update(zip(group, packed(group)))
    arrived = {d: rotated(blocks[d], "window", d) for d in order}
    arrived[0] = packed([0])[0]

    payload = shape((pairs, nvar * tiles + 1, 2 * SUB, LANES), i16)

    counts = [nvar, nvar, steps - 1]
    half_tiles = sum(-(-(count * tiles + 1) // 2) for count in counts)
    halves = shape((pairs, half_tiles, 2 * SUB, LANES), i16)
    near, far, dual = pl.pallas_call(
        half_code_kernel,
        out_shape=[halves, halves, payload],
        in_specs=[VMEM] * 3,
        out_specs=[VMEM] * 3,
        compiler_params=params(),
    )(dual_model, increment, dual_obs)
    far, near = swapped(far, "space", 1), swapped(near, "space", 0)

    blocks_here = [arrived[d] for d in range(windows)]
    *after, totals = pl.pallas_call(
        lambda *refs: around_kernel(windows, nvar, levels, *refs),
        out_shape=[shape((2,) + payload.shape[1:], i16)] * pairs
        + [shape((nvar * levels, rows, LANES), f32)],
        in_specs=[VMEM] * (windows + 3),
        out_specs=[VMEM] * (pairs + 1),
        compiler_params=params(),
    )(*blocks_here, dual, near, far)
    after = [moved(piece, "window", -1) for piece in after]

    obs, share, mix = pl.pallas_call(
        lambda *refs: prepare_factor_kernel(steps, nvar, levels, tiles, *refs),
        out_shape=[
            shape((levels, steps, tiles, SUB, LANES), f32),
            shape((levels, steps, SUB, LANES), f32),
            shape((nvar, nvar, SUB, LANES), f32),
        ],
        in_specs=[SMEM] * 2 + [VMEM] * 3,
        out_specs=[VMEM] * 3,
        compiler_params=params(),
    )(obs_count, obs_var, coupling, dual_obs, innovation)

    own, traj_near, traj_far = pl.pallas_call(
        lambda *refs: assemble_kernel(windows, steps, nvar, levels, part, *refs),
        out_shape=[
            shape((steps, nvar * levels, rows, columns), bf16),
            shape((edge_base(steps, nvar, levels)[1], rows, columns), bf16),
            shape((edge_base(steps, nvar, levels)[1], rows, columns), bf16),
        ],
        in_specs=[VMEM] * windows + [ANY],
        out_specs=[VMEM] * 3,
        scratch_shapes=[pltpu.VMEM((windows, block.shape[0] - 1, rows, LANES), bf16)],
        compiler_params=params(),
    )(*blocks_here, mix)
    traj_far, traj_near = swapped(traj_far, "space", 1), swapped(traj_near, "space", 0)

    first = pl.pallas_call(
        lambda *refs: prepare_tangent_kernel(nvar, levels, tiles, *refs),
        out_shape=shape((levels, nvar, tiles, 2 * SUB, LANES), f32),
        in_specs=[VMEM] * 3,
        out_specs=VMEM,
        compiler_params=params(),
    )(near, far, increment)
    new_dual_obs, ends, wide_traj = pl.pallas_call(
        lambda *refs: tangent_kernel(spaces, steps, nvar, levels, tiles, *refs),
        out_shape=[
            shape(dual_obs.shape, f32),
            shape((levels, nvar, tiles, SUB, LANES), f32),
            shape((levels, steps, nvar, tiles, 2 * SUB, LANES), f32),
        ],
        in_specs=[VMEM] * 7,
        out_specs=[VMEM] * 3,
        scratch_shapes=[pltpu.VMEM((2, 2, nvar, tiles, 4 * SUB, LANES), f32)],
        compiler_params=params(),
    )(mix, share, obs, own, traj_near, traj_far, first)

    state = shape((nvar, 2, rows, columns), f32)
    coded = shape((nvar * tiles + 1, 2 * SUB, LANES), i16)
    base_duals, base_incs, sent = [], [], []
    before = ends
    for i in range(pairs):
        last, force = pl.pallas_call(
            lambda *refs, i=i: prepare_adjoint_kernel(i, steps, nvar, tiles, *refs),
            out_shape=[shape((2, n, tiles, 2 * SUB, LANES), f32) for n in (nvar, steps)],
            in_specs=[SMEM] + [VMEM] * 4 + [ANY],
            out_specs=[VMEM] * 2,
            compiler_params=params(),
        )(obs_count, near, far, dual_obs, after[i], before)
        base_dual, base_inc, *payloads = pl.pallas_call(
            lambda *refs, i=i: adjoint_kernel(
                i, windows, spaces, steps, nvar, levels, tiles, *refs
            ),
            out_shape=[state, state] + [coded] * (windows - 1),
            in_specs=[VMEM] * 9,
            out_specs=[VMEM] * (2 + windows - 1),
            scratch_shapes=[
                pltpu.VMEM((2, steps, tiles, 4 * SUB, LANES), f32),
                pltpu.VMEM((2, 2, nvar, tiles, 4 * SUB, LANES), f32),
                pltpu.VMEM((2,) + coded.shape, i16),
            ],
            compiler_params=params(),
        )(mix, totals, wide_traj, last, force, ends, increment, model_rhs, dual_model)
        before = base_dual
        base_duals.append(base_dual)
        base_incs.append(base_inc)
        sent += [
            exchanged(piece, "window", mask)
            for piece, mask in zip(payloads, partners(windows))
        ]

    new_dual_model, new_increment = pl.pallas_call(
        lambda *refs: final_kernel(windows, nvar, levels, tiles, *refs),
        out_shape=[shape(dual_model.shape, f32), shape(increment.shape, f32)],
        in_specs=[VMEM] * (len(sent) + 2 * pairs + 1),
        out_specs=[VMEM] * 2,
        compiler_params=params(),
    )(*sent, *base_duals, *base_incs, totals)
    return new_dual_model, new_dual_obs, new_increment


def solution(mesh):
    placed = (
        P("members", None, None, None, "space", "window"),
        P(("members", "window"), None, None, "space", None),
        P(("members", "window"), None, None, "space", None),
        P(("members", "window"), None, None, "space", None),
        P(("members", "window"), None, None, "space", None),
        P(("members", "window"), None, None, "space", None),
        P(),
        P(("members", "window"), None, None),
        P(("members", "window"), None, None),
        P(("members", "window")),
    )
    return jax.shard_map(
        body,
        mesh=mesh,
        in_specs=placed,
        out_specs=(
            P(("members", "window"), None, None, "space", None),
            P(("members", "window"), None, None, "space", None),
            P(("members", "window"), None, None, "space", None),
        ),
        check_vma=False,
    )
```

```python
import jax
import jax.numpy as jnp
from jax import lax
from jax.experimental import pallas as pl
from jax.experimental.pallas import tpu as pltpu
from jax.sharding import PartitionSpec as P

LANES = 128
SUB = 8
HALF = SUB // 2
CODE_MAX = 32000.0
ROUNDER = 12582912.0

diffusion = 0.2
advection = 0.2
coupling_gain = 0.5
keep = 1.0 - 4.0 * diffusion
half_adv = 0.5 * advection

VMEM = pl.BlockSpec(memory_space=pltpu.VMEM)
SMEM = pl.BlockSpec(memory_space=pltpu.SMEM)
ANY = pl.BlockSpec(memory_space=pl.ANY)


def params(mib=24):
    return pltpu.CompilerParams(vmem_limit_bytes=mib * 1024 * 1024)


def lane_index():
    return lax.broadcasted_iota(jnp.int32, (SUB, LANES), 1)


def row_index():
    return lax.broadcasted_iota(jnp.int32, (SUB, LANES), 0)


def tiled(wide):
    short = -wide.shape[1] % LANES
    if short:
        wide = jnp.concatenate([wide, jnp.zeros((wide.shape[0], short), wide.dtype)], 1)
    return [wide[:, i : i + LANES] for i in range(0, wide.shape[1], LANES)]


def place(parts, rolled, lane):
    built = {}
    for key, tiles, first, width, target in parts:
        done = 0
        while done < width:
            a, b = first + done, target + done
            n = min(width - done, LANES - a % LANES, LANES - b % LANES)
            shift = (b - a) % LANES
            name = (key, a // LANES, shift)
            if name not in rolled:
                value = tiles[a // LANES]
                rolled[name] = pltpu.roll(value, shift, 1) if shift else value
            if b % LANES:
                built[b // LANES] = jnp.where(
                    lane >= b % LANES, rolled[name], built[b // LANES]
                )
            else:
                built[b // LANES] = rolled[name]
            done += n
    return [built[i] for i in range(len(built))]


def joined_halves(first, second):
    top = row_index()[:, :1] < HALF
    last = jnp.where(top, pltpu.roll(first, HALF, 0), second)
    start = jnp.where(top, first, pltpu.roll(second, HALF, 0))
    return last, start


def widened(own, near, far, odd, even):
    top = row_index() < HALF
    low, high = jnp.where(even, far, near), jnp.where(even, near, far)
    turned = pltpu.roll(own, HALF, 0)
    low = pltpu.roll(low, HALF, 0) if odd else low
    high = high if odd else pltpu.roll(high, HALF, 0)
    return jnp.where(top, low, turned), jnp.where(top, turned, high)


def row_codes(planes):
    lane = lax.broadcasted_iota(jnp.int32, planes[0][0].shape, 1)
    scales = jnp.zeros(planes[0][0].shape, jnp.float32)
    out = []
    for v, row in enumerate(planes):
        big = jnp.abs(row[0])
        for value in row[1:]:
            big = jnp.maximum(big, jnp.abs(value))
        big = jnp.max(big, axis=1, keepdims=True)
        power = jnp.clip(jnp.ceil(jnp.log2(jnp.maximum(big, 1e-30))), -90.0, 126.0)
        scales = jnp.where(lane == v, power, scales)
        gain = CODE_MAX * jnp.exp2(-power)
        for value in row:
            out.append((value * gain + ROUNDER) - ROUNDER)
    return out, scales


def shorts(value):
    return value.astype(jnp.int32).astype(jnp.int16)


def floats(value):
    return value.astype(jnp.int32).astype(jnp.float32)


def partners(windows):
    return list(range(windows - 1, 0, -1))


def pack_kernel(ways, windows, steps, nvar, levels, part, var_ref, traj_ref, *outs):
    me = lax.axis_index("window")
    lane = lane_index()
    variance = var_ref[...]
    high = variance.astype(jnp.bfloat16).astype(jnp.float32)
    middle = (variance - high).astype(jnp.bfloat16).astype(jnp.float32)
    low = variance - high - middle
    split = high + pltpu.roll(middle, HALF, 0) + pltpu.roll(low, LANES // 2, 1)
    split = split.astype(jnp.bfloat16)

    for n, d in enumerate(ways):
        outs[n][outs[n].shape[0] - 1] = split
        target = lax.rem(me + d, windows)

        def variable(v, carry, n=n, target=target):
            for lev in range(levels):
                pieces = [
                    tiled(traj_ref[target, j, v, lev].astype(jnp.float32)) for j in range(steps)
                ]
                parts = [(j, pieces[j], 0, part, j * part) for j in range(steps)]
                placed = place(parts, {}, lane)
                for t, value in enumerate(placed):
                    outs[n][(v * levels + lev) * len(placed) + t] = value.astype(jnp.bfloat16)
            return carry

        lax.fori_loop(0, nvar, variable, 0, unroll=len(ways) == 1)


def even_place():
    return lax.rem(lax.axis_index("space"), 2) == 0


def level_codes(ref, lev, first=0):
    planes = [
        [ref[0, v, lev, :, t : t + LANES] for t in range(0, ref.shape[-1], LANES)]
        for v in range(first, ref.shape[1])
    ]
    values, scales = row_codes(planes)
    return values + [scales]


def half_code_kernel(*refs):
    sources, (near_ref, far_ref, own_ref) = refs[:-3], refs[-3:]
    even = even_place()

    def pair(i, carry):
        near, far = [], []
        for k, ref in enumerate(sources):
            skip = int(k == len(sources) - 1)
            coded = [level_codes(ref, 2 * i + odd, skip) for odd in range(2)]
            for n, (first, second) in enumerate(zip(*coded)):
                if k == 0:
                    own_ref[i, n] = shorts(jnp.concatenate([first, second], 0))
                last, start = joined_halves(first, second)
                near.append(jnp.where(even, last, start))
                far.append(jnp.where(even, start, last))
            if len(near) % 2:
                near.append(jnp.zeros((SUB, LANES), jnp.float32))
                far.append(jnp.zeros((SUB, LANES), jnp.float32))
        for tiles, ref in ((near, near_ref), (far, far_ref)):
            for n in range(0, len(tiles), 2):
                ref[i, n // 2] = shorts(jnp.concatenate(tiles[n : n + 2], 0))
        return carry

    lax.fori_loop(0, near_ref.shape[0], pair, 0)


def half_tile(ref, i, n):
    whole = floats(ref[i, n // 2])
    return whole[SUB:] if n % 2 else whole[:SUB]


def around_kernel(i, own_ref, near_ref, far_ref, *refs):
    out_ref = refs[-1]
    even = even_place()
    for n in range(own_ref.shape[1]):
        own = floats(own_ref[i, n])
        near, far = half_tile(near_ref, i, n), half_tile(far_ref, i, n)
        for odd in range(2):
            halves = widened(own[odd * SUB : (odd + 1) * SUB], near, far, odd, even)
            out_ref[odd, n] = shorts(jnp.concatenate(halves, 0))


def total_kernel(windows, nvar, levels, *refs):
    pieces, total_ref = refs[:windows], refs[-1]
    me = lax.axis_index("window")
    total = jnp.zeros((SUB, LANES), jnp.float32)
    for d in range(windows):
        split = pieces[d][pieces[d].shape[0] - 1].astype(jnp.float32)
        here = split + pltpu.roll(split, HALF, 0) + pltpu.roll(split, LANES // 2, 1)
        total = total + jnp.where(lax.rem(me - d + windows, windows) <= me, here, 0.0)
    for v in range(nvar):
        for lev in range(levels):
            one = total[lev : lev + 1, v : v + 1]
            total_ref[v * levels + lev] = jnp.broadcast_to(one, (SUB, LANES))


def decoded(ref, i, first, nvar, tiles):
    scales = jnp.exp2(half_tile(ref, i, first + nvar * tiles)) * (1.0 / CODE_MAX)
    return [
        [half_tile(ref, i, first + v * tiles + t) * scales[:, v : v + 1] for t in range(tiles)]
        for v in range(nvar)
    ]


def is_quarter(j, v, steps):
    return 0 < j < steps - 1 and not (v == 0 and j + 1 > HALF // 2)


def edge_base(steps, nvar, levels):
    base, total = {}, 0
    for j in range(steps):
        for v in range(nvar):
            base[j, v] = total
            total += levels // (4 if is_quarter(j, v, steps) else 2)
    return base, total


def joined_quarters(four):
    slot = row_index() // 2
    last, start = pltpu.roll(four[0], 2, 0), four[0]
    for n in range(1, 4):
        last = jnp.where(slot == n, pltpu.roll(four[n], (2 * n + 2) % SUB, 0), last)
        start = jnp.where(slot == n, pltpu.roll(four[n], 2 * n, 0), start)
    return last, start


def assemble_kernel(windows, steps, nvar, levels, part, *refs):
    pieces = refs[:windows]
    own_ref, near_ref, far_ref, stack_ref = refs[windows + 1 :]
    me = lax.axis_index("window")
    even = even_place()
    lane = lane_index()
    count = stack_ref.shape[1]
    packed_tiles = count // (nvar * levels)
    for d in range(windows):
        stack_ref[lax.rem(me - d + windows, windows)] = pieces[d][:count]

    base, _ = edge_base(steps, nvar, levels)

    def variable(v):
        built = {}
        for lev in range(levels):
            plane = v * levels + lev
            sources = [
                [
                    stack_ref[w, plane * packed_tiles + t].astype(jnp.float32)
                    for t in range(packed_tiles)
                ]
                for w in range(windows)
            ]
            rolled = {}
            for j in range(steps):
                parts = [(w, sources[w], j * part, part, w * part) for w in range(windows)]
                built[j, lev] = place(parts, rolled, lane)
                own_ref[j, plane] = jnp.concatenate(built[j, lev], 1).astype(jnp.bfloat16)
        for j in range(steps):
            if is_quarter(j, v, steps):
                groups = [
                    [joined_quarters(four) for four in zip(*[built[j, 4 * q + n] for n in range(4)])]
                    for q in range(levels // 4)
                ]
            else:
                groups = [
                    [joined_halves(a, b) for a, b in zip(built[j, 2 * i], built[j, 2 * i + 1])]
                    for i in range(levels // 2)
                ]
            for n, group in enumerate(groups):
                last, start = (jnp.concatenate([e[k] for e in group], 1) for k in range(2))
                near_ref[base[j, v] + n] = jnp.where(even, last, start).astype(jnp.bfloat16)
                far_ref[base[j, v] + n] = jnp.where(even, start, last).astype(jnp.bfloat16)

    for v in range(nvar):
        variable(v)


def prepare_factor_kernel(
    steps, nvar, levels, tiles,
    count_ref, noise_ref, coupling_ref, dobs_ref, innov_ref, obs_ref, share_ref, mix_ref,
):
    cuts = [slice(t * LANES, (t + 1) * LANES) for t in range(tiles)]
    for v in range(nvar):
        for u in range(nvar):
            one = coupling_gain * coupling_ref[v : v + 1, u : u + 1]
            mix_ref[v, u] = jnp.broadcast_to(one, (SUB, LANES))
    for lev in range(levels):
        for j in range(steps):
            noise = jnp.full((SUB, LANES), noise_ref[0, j, lev])
            share = jnp.where(j < count_ref[0], 1.0, 0.0) / noise
            share_ref[lev, j] = share
            for t in range(tiles):
                gap = innov_ref[0, j, lev, :, cuts[t]] - noise * dobs_ref[0, j, lev, :, cuts[t]]
                obs_ref[lev, j, t] = gap * share


def prepare_tangent_kernel(nvar, levels, tiles, near_ref, far_ref, inc_ref, first_ref):
    even = even_place()
    blocks = [slice(0, SUB), slice(SUB, 2 * SUB)]
    cuts = [slice(t * LANES, (t + 1) * LANES) for t in range(tiles)]
    offset = -(-(nvar * tiles + 1) // 2) * 2
    for i in range(levels // 2):
        fields = [decoded(ref, i, offset, nvar, tiles) for ref in (near_ref, far_ref)]
        for odd in range(2):
            lev = 2 * i + odd
            for t in range(tiles):
                for v in range(nvar):
                    near, far = (side[v][t] for side in fields)
                    halves = widened(inc_ref[0, v, lev, :, cuts[t]], near, far, odd, even)
                    for b in range(2):
                        first_ref[lev, v, t, blocks[b], :] = halves[b]


def prepare_adjoint_kernel(
    i, steps, nvar, tiles, count_ref, near_ref, far_ref, dobs_ref, after_ref, *refs
):
    _, last_ref, force_ref = refs
    even = even_place()
    blocks = [slice(0, SUB), slice(SUB, 2 * SUB)]
    cuts = [slice(t * LANES, (t + 1) * LANES) for t in range(tiles)]
    seen = [jnp.where(j < count_ref[0], 1.0, 0.0) for j in range(steps)]
    offset = -(-(nvar * tiles + 1) // 2) * 2
    none = [[jnp.zeros((SUB, LANES), jnp.float32)] * tiles]
    forces = [none + decoded(ref, i, 2 * offset, steps - 1, tiles) for ref in (near_ref, far_ref)]
    for odd in range(2):
        scales = jnp.exp2(floats(after_ref[odd, nvar * tiles])) * (-1.0 / CODE_MAX)
        for t in range(tiles):
            for v in range(nvar):
                value = floats(after_ref[odd, v * tiles + t])
                last_ref[odd, v, t] = value * scales[:, v : v + 1]
            for j in range(steps):
                near, far = (side[j][t] for side in forces)
                halves = widened(dobs_ref[0, j, 2 * i + odd, :, cuts[t]], near, far, odd, even)
                for b in range(2):
                    force_ref[odd, j, t, blocks[b], :] = seen[j] * halves[b]


def from_north(line, lane):
    turned = [pltpu.roll(value, LANES - 1, 1) for value in line] * 2
    return [jnp.where(lane < LANES - 1, turned[t], turned[t + 1]) for t in range(len(line))]


def from_south(line, lane):
    turned = [pltpu.roll(value, 1, 1) for value in line]
    return [jnp.where(lane > 0, turned[t], turned[t - 1]) for t in range(len(line))]


def masked_last(line, lane):
    return line[:-1] + [jnp.where(lane < LANES - 1, line[-1], 0.0)]


def masked_first(line, lane):
    return [jnp.where(lane > 0, line[0], 0.0)] + line[1:]


def walls(spaces):
    row, place_x = row_index(), lax.axis_index("space")
    low = jnp.where((row == HALF) & (place_x == 0), 0.0, 1.0)
    high = jnp.where((row == HALF - 1) & (place_x == spaces - 1), 0.0, 1.0)

    def walled(block, east, west):
        if block == 0:
            return east, [low * value for value in west]
        return [high * value for value in east], west

    return walled


BLOCKS = [slice(SUB, 2 * SUB), slice(2 * SUB, 3 * SUB)]
UPS = [slice(b.start + 1, b.stop + 1) for b in BLOCKS]
DOWNS = [slice(b.start - 1, b.stop - 1) for b in BLOCKS]
MINE = slice(SUB + HALF, 2 * SUB + HALF)


def tangent_kernel(
    spaces, steps, nvar, levels, tiles,
    mix_ref, share_ref, obs_ref, own_ref, near_ref, far_ref, first_ref,
    ndo_ref, ends_ref, x_ref, s_ref,
):
    lane, row = lane_index(), row_index()
    even = even_place()
    top = row < HALF
    walled = walls(spaces)
    pairs = levels // 2
    cuts = [slice(t * LANES, (t + 1) * LANES) for t in range(tiles)]
    base, _ = edge_base(steps, nvar, levels)

    for lev in range(levels):
        odd = lev % 2
        for j in range(steps):
            for v in range(nvar):
                for t in range(tiles):
                    own = own_ref[j, v * levels + lev, :, cuts[t]].astype(jnp.float32)
                    quarter = is_quarter(j, v, steps)
                    tile = base[j, v] + lev // (4 if quarter else 2)
                    near = near_ref[tile, :, cuts[t]].astype(jnp.float32)
                    far = far_ref[tile, :, cuts[t]].astype(jnp.float32)
                    low, high = jnp.where(even, far, near), jnp.where(even, near, far)
                    if quarter:
                        slot = 2 * (lev % 4)
                        low = pltpu.roll(low, (HALF - 2 - slot) % SUB, 0)
                        high = pltpu.roll(high, (HALF - slot) % SUB, 0)
                    else:
                        low = pltpu.roll(low, HALF, 0) if odd else low
                        high = high if odd else pltpu.roll(high, HALF, 0)
                    turned = pltpu.roll(own, HALF, 0)
                    x_ref[lev, j, v, t, :SUB, :] = jnp.where(top, low, turned)
                    x_ref[lev, j, v, t, SUB:, :] = jnp.where(top, turned, high)

    def pair(i, outer):
        for odd in range(2):
            for v in range(nvar):
                for t in range(tiles):
                    s_ref[odd, 0, v, t, SUB : 3 * SUB, :] = first_ref[2 * i + odd, v, t]

        for j in range(steps):
            now = j % 2
            for odd in range(2):
                lev = 2 * i + odd
                for t in range(tiles):
                    image = share_ref[lev, j] * s_ref[odd, now, 0, t, MINE, :]
                    ndo_ref[0, j, lev, :, cuts[t]] = obs_ref[lev, j, t] - image
                for b in range(2):
                    part = slice(b * SUB, (b + 1) * SUB)
                    here, up, down = BLOCKS[b], UPS[b], DOWNS[b]
                    x = [[x_ref[lev, j, u, t, part, :] for t in range(tiles)] for u in range(nvar)]
                    ce = [diffusion - half_adv * value for value in x[0]]
                    cw = [diffusion + half_adv * value for value in x[0]]
                    ce, cw = walled(b, ce, cw)
                    cn = masked_last([diffusion - half_adv * value for value in x[1]], lane)
                    cs = masked_first([diffusion + half_adv * value for value in x[1]], lane)
                    s = [
                        [s_ref[odd, now, u, t, here, :] for t in range(tiles)] for u in range(nvar)
                    ]
                    xs = [[x[u][t] * s[u][t] for t in range(tiles)] for u in range(nvar)]
                    for v in range(nvar):
                        north, south = from_north(s[v], lane), from_south(s[v], lane)
                        for t in range(tiles):
                            fresh = keep * s[v][t] + ce[t] * s_ref[odd, now, v, t, up, :]
                            fresh = fresh + cw[t] * s_ref[odd, now, v, t, down, :]
                            fresh = fresh + cn[t] * north[t] + cs[t] * south[t]
                            for u in range(nvar):
                                fresh = fresh + mix_ref[v, u] * xs[u][t]
                            s_ref[odd, 1 - now, v, t, here, :] = fresh
        for odd in range(2):
            for v in range(nvar):
                for t in range(tiles):
                    ends_ref[2 * i + odd, v, t] = s_ref[odd, steps % 2, v, t, MINE, :]
        return outer

    lax.fori_loop(0, pairs, pair, 0)


def adjoint_kernel(
    i, windows, spaces, steps, nvar, levels, tiles,
    mix_ref, total_ref, x_ref, last_ref, force_ref, ends_ref, inc_ref, rhs_ref, dual_ref,
    ndm_ref, ninc_ref, *rest,
):
    payload_refs = rest[: windows - 1]
    x0_ref, a_ref, q_ref = rest[windows - 1 :]
    me = lax.axis_index("window")
    lane = lane_index()
    walled = walls(spaces)
    cuts = [slice(t * LANES, (t + 1) * LANES) for t in range(tiles)]

    for odd in range(2):
        lev = 2 * i + odd
        for t in range(tiles):
            for j in range(steps):
                x0_ref[odd, j, t, SUB : 3 * SUB, :] = x_ref[lev, j, 0, t]
            for v in range(nvar):
                a_ref[odd, 0, v, t, SUB : 3 * SUB, :] = last_ref[odd, v, t]

    for turn in range(steps):
        now = turn % 2
        j = steps - 1 - turn
        for odd in range(2):
            lev = 2 * i + odd
            for b in range(2):
                part = slice(b * SUB, (b + 1) * SUB)
                here, up, down = BLOCKS[b], UPS[b], DOWNS[b]
                x = [[x_ref[lev, j, u, t, part, :] for t in range(tiles)] for u in range(nvar)]
                ce = [diffusion + half_adv * x0_ref[odd, j, t, up, :] for t in range(tiles)]
                cw = [diffusion - half_adv * x0_ref[odd, j, t, down, :] for t in range(tiles)]
                ce, cw = walled(b, ce, cw)
                cn = masked_first([diffusion + half_adv * value for value in x[1]], lane)
                cs = masked_last([diffusion - half_adv * value for value in x[1]], lane)
                a = [
                    [a_ref[odd, now, u, t, here, :] for t in range(tiles)] for u in range(nvar)
                ]
                for u in range(nvar):
                    north = from_north([cn[t] * a[u][t] for t in range(tiles)], lane)
                    south = from_south([cs[t] * a[u][t] for t in range(tiles)], lane)
                    for t in range(tiles):
                        fresh = keep * a[u][t] + ce[t] * a_ref[odd, now, u, t, up, :]
                        fresh = fresh + cw[t] * a_ref[odd, now, u, t, down, :]
                        fresh = fresh + north[t] + south[t]
                        pull = mix_ref[0, u] * a[0][t]
                        for v in range(1, nvar):
                            pull = pull + mix_ref[v, u] * a[v][t]
                        fresh = fresh + x[u][t] * pull
                        if u == 0:
                            fresh = fresh + force_ref[odd, j, t, part, :]
                        a_ref[odd, 1 - now, u, t, here, :] = fresh
    end = steps % 2
    coded = []
    for odd in range(2):
        lev = 2 * i + odd
        back, ahead = [], []
        for v in range(nvar):
            share = total_ref[v * levels + lev]
            tv, gv = [], []
            for t in range(tiles):
                term = a_ref[odd, end, v, t, MINE, :] - last_ref[odd, v, t, HALF : HALF + SUB, :]
                given = rhs_ref[0, v, lev, :, cuts[t]] - inc_ref[0, v, lev, :, cuts[t]]
                given = given + share * term
                ndm_ref[v, odd, :, cuts[t]] = -(dual_ref[0, v, lev, :, cuts[t]] + term)
                ninc_ref[v, odd, :, cuts[t]] = given
                tv.append(term)
                gv.append(given + ends_ref[lev, v, t])
            back.append(tv)
            ahead.append(gv)
        coded.append((row_codes(back), row_codes(ahead)))
    for kind in range(2):
        first, second = coded[0][kind], coded[1][kind]
        for n, (a, b) in enumerate(zip(first[0] + [first[1]], second[0] + [second[1]])):
            q_ref[kind, n] = shorts(jnp.concatenate([a, b], 0))
    for ref, d in zip(payload_refs, partners(windows)):
        ref[...] = q_ref[jnp.where((me ^ d) < me, 0, 1)]


def final_kernel(windows, nvar, levels, tiles, *refs):
    pairs = levels // 2
    cut = pairs * (windows - 1)
    pieces, base_duals, base_incs = refs[:cut], refs[cut : cut + pairs], refs[cut + pairs : -3]
    total_ref, ndm_ref, ninc_ref = refs[-3:]
    me = lax.axis_index("window")
    cuts = [slice(t * LANES, (t + 1) * LANES) for t in range(tiles)]

    for i in range(pairs):
        tails = [None] * (nvar * tiles)
        heads = [None] * (nvar * tiles)
        for n, d in enumerate(partners(windows)):
            piece = pieces[i * (windows - 1) + n]
            later = (me ^ d) > me
            scales = jnp.exp2(floats(piece[nvar * tiles])) * (1.0 / CODE_MAX)
            for v in range(nvar):
                scale = scales[:, v : v + 1]
                for t in range(tiles):
                    k = v * tiles + t
                    value = floats(piece[k]) * scale
                    tail, head = jnp.where(later, value, 0.0), jnp.where(later, 0.0, value)
                    tails[k] = tails[k] + tail if n else tail
                    heads[k] = heads[k] + head if n else head
        for v in range(nvar):
            for odd in range(2):
                lev = 2 * i + odd
                share = total_ref[v * levels + lev]
                for t in range(tiles):
                    rows = slice(odd * SUB, (odd + 1) * SUB)
                    tail, head = tails[v * tiles + t][rows], heads[v * tiles + t][rows]
                    ndm_ref[0, v, lev, :, cuts[t]] = base_duals[i][v, odd, :, cuts[t]] - tail
                    ninc_ref[0, v, lev, :, cuts[t]] = (
                        base_incs[i][v, odd, :, cuts[t]] + head + share * tail
                    )


def moved(block, axis, distance):
    devices = range(lax.axis_size(axis))
    return lax.ppermute(block, axis, [(i, i + distance) for i in devices if i + distance in devices])


def rotated(block, axis, distance):
    count = lax.axis_size(axis)
    return lax.ppermute(block, axis, [(i, (i + distance) % count) for i in range(count)])


def exchanged(block, axis, mask):
    return lax.ppermute(block, axis, [(i, i ^ mask) for i in range(lax.axis_size(axis))])


def swaps(axis, first):
    route = []
    for i in range(first, lax.axis_size(axis) - 1, 2):
        route += [(i, i + 1), (i + 1, i)]
    return route


def swapped(block, axis, first):
    return lax.ppermute(block, axis, swaps(axis, first))


def body(
    trajectory,
    dual_model,
    increment,
    model_rhs,
    dual_obs,
    innovation,
    coupling,
    error_var,
    obs_var,
    obs_count,
):
    windows, spaces = lax.axis_size("window"), lax.axis_size("space")
    _, steps, nvar, levels, rows, part = trajectory.shape
    columns = dual_model.shape[-1]
    tiles = columns // LANES
    assert trajectory.shape[0] == windows and windows > 1 and rows == SUB and steps == HALF
    assert columns == tiles * LANES == windows * part and levels % 4 == 0
    assert windows & (windows - 1) == 0
    pairs = levels // 2
    wide = -(-steps * part // LANES) * LANES
    bf16, f32, i16 = jnp.bfloat16, jnp.float32, jnp.int16

    def shape(dims, dtype):
        return jax.ShapeDtypeStruct(dims, dtype)

    block = shape((nvar * levels * wide // LANES + 1, rows, LANES), bf16)
    variances = jnp.pad(error_var[0].T, ((0, SUB - levels), (0, LANES - nvar)))

    def packed(ways):
        return pl.pallas_call(
            lambda *refs: pack_kernel(ways, windows, steps, nvar, levels, part, *refs),
            out_shape=[block] * len(ways),
            in_specs=[VMEM, VMEM],
            out_specs=[VMEM] * len(ways),
            compiler_params=params(),
        )(variances, trajectory)

    order = list(range(1, windows))
    groups = [[d] for d in order] if windows <= 4 else [order]
    blocks = {}
    for group in groups:
        blocks.update(zip(group, packed(group)))
    arrived = {d: rotated(blocks[d], "window", d) for d in order}
    arrived[0] = packed([0])[0]

    payload = shape((pairs, nvar * tiles + 1, 2 * SUB, LANES), i16)

    counts = [nvar, nvar, steps - 1]
    half_tiles = sum(-(-(count * tiles + 1) // 2) for count in counts)
    halves = shape((pairs, half_tiles, 2 * SUB, LANES), i16)
    near, far, dual = pl.pallas_call(
        half_code_kernel,
        out_shape=[halves, halves, payload],
        in_specs=[VMEM] * 3,
        out_specs=[VMEM] * 3,
        compiler_params=params(),
    )(dual_model, increment, dual_obs)
    far, near = swapped(far, "space", 1), swapped(near, "space", 0)

    blocks_here = [arrived[d] for d in range(windows)]

    def shifted(i, before):
        codes = pl.pallas_call(
            lambda *refs: around_kernel(i, *refs),
            out_shape=shape((2,) + payload.shape[1:], i16),
            in_specs=[VMEM] * 3 + [ANY],
            out_specs=VMEM,
            compiler_params=params(),
        )(dual, near, far, before)
        return moved(codes, "window", -1)

    totals = pl.pallas_call(
        lambda *refs: total_kernel(windows, nvar, levels, *refs),
        out_shape=shape((nvar * levels, rows, LANES), f32),
        in_specs=[VMEM] * windows,
        out_specs=VMEM,
        compiler_params=params(),
    )(*blocks_here)
    obs, share, mix = pl.pallas_call(
        lambda *refs: prepare_factor_kernel(steps, nvar, levels, tiles, *refs),
        out_shape=[
            shape((levels, steps, tiles, SUB, LANES), f32),
            shape((levels, steps, SUB, LANES), f32),
            shape((nvar, nvar, SUB, LANES), f32),
        ],
        in_specs=[SMEM] * 2 + [VMEM] * 3,
        out_specs=[VMEM] * 3,
        compiler_params=params(),
    )(obs_count, obs_var, coupling, dual_obs, innovation)

    own, traj_near, traj_far = pl.pallas_call(
        lambda *refs: assemble_kernel(windows, steps, nvar, levels, part, *refs),
        out_shape=[
            shape((steps, nvar * levels, rows, columns), bf16),
            shape((edge_base(steps, nvar, levels)[1], rows, columns), bf16),
            shape((edge_base(steps, nvar, levels)[1], rows, columns), bf16),
        ],
        in_specs=[VMEM] * windows + [ANY],
        out_specs=[VMEM] * 3,
        scratch_shapes=[pltpu.VMEM((windows, block.shape[0] - 1, rows, LANES), bf16)],
        compiler_params=params(),
    )(*blocks_here, mix)
    traj_far, traj_near = swapped(traj_far, "space", 1), swapped(traj_near, "space", 0)

    first = pl.pallas_call(
        lambda *refs: prepare_tangent_kernel(nvar, levels, tiles, *refs),
        out_shape=shape((levels, nvar, tiles, 2 * SUB, LANES), f32),
        in_specs=[VMEM] * 3,
        out_specs=VMEM,
        compiler_params=params(),
    )(near, far, increment)
    new_dual_obs, ends, wide_traj = pl.pallas_call(
        lambda *refs: tangent_kernel(spaces, steps, nvar, levels, tiles, *refs),
        out_shape=[
            shape(dual_obs.shape, f32),
            shape((levels, nvar, tiles, SUB, LANES), f32),
            shape((levels, steps, nvar, tiles, 2 * SUB, LANES), f32),
        ],
        in_specs=[VMEM] * 7,
        out_specs=[VMEM] * 3,
        scratch_shapes=[pltpu.VMEM((2, 2, nvar, tiles, 4 * SUB, LANES), f32)],
        compiler_params=params(),
    )(mix, share, obs, own, traj_near, traj_far, first)

    after = [shifted(i, ends if i else own) for i in range(pairs)]
    state = shape((nvar, 2, rows, columns), f32)
    coded = shape((nvar * tiles + 1, 2 * SUB, LANES), i16)
    base_duals, base_incs, sent = [], [], []
    before = ends
    for i in range(pairs):
        last, force = pl.pallas_call(
            lambda *refs, i=i: prepare_adjoint_kernel(i, steps, nvar, tiles, *refs),
            out_shape=[shape((2, n, tiles, 2 * SUB, LANES), f32) for n in (nvar, steps)],
            in_specs=[SMEM] + [VMEM] * 4 + [ANY],
            out_specs=[VMEM] * 2,
            compiler_params=params(),
        )(obs_count, near, far, dual_obs, after[i], before)
        base_dual, base_inc, *payloads = pl.pallas_call(
            lambda *refs, i=i: adjoint_kernel(
                i, windows, spaces, steps, nvar, levels, tiles, *refs
            ),
            out_shape=[state, state] + [coded] * (windows - 1),
            in_specs=[VMEM] * 9,
            out_specs=[VMEM] * (2 + windows - 1),
            scratch_shapes=[
                pltpu.VMEM((2, steps, tiles, 4 * SUB, LANES), f32),
                pltpu.VMEM((2, 2, nvar, tiles, 4 * SUB, LANES), f32),
                pltpu.VMEM((2,) + coded.shape, i16),
            ],
            compiler_params=params(),
        )(mix, totals, wide_traj, last, force, ends, increment, model_rhs, dual_model)
        before = base_dual
        base_duals.append(base_dual)
        base_incs.append(base_inc)
        sent += [
            exchanged(piece, "window", mask)
            for piece, mask in zip(payloads, partners(windows))
        ]

    new_dual_model, new_increment = pl.pallas_call(
        lambda *refs: final_kernel(windows, nvar, levels, tiles, *refs),
        out_shape=[shape(dual_model.shape, f32), shape(increment.shape, f32)],
        in_specs=[VMEM] * (len(sent) + 2 * pairs + 1),
        out_specs=[VMEM] * 2,
        compiler_params=params(),
    )(*sent, *base_duals, *base_incs, totals)
    return new_dual_model, new_dual_obs, new_increment


def solution(mesh):
    placed = (
        P("members", None, None, None, "space", "window"),
        P(("members", "window"), None, None, "space", None),
        P(("members", "window"), None, None, "space", None),
        P(("members", "window"), None, None, "space", None),
        P(("members", "window"), None, None, "space", None),
        P(("members", "window"), None, None, "space", None),
        P(),
        P(("members", "window"), None, None),
        P(("members", "window"), None, None),
        P(("members", "window")),
    )
    return jax.shard_map(
        body,
        mesh=mesh,
        in_specs=placed,
        out_specs=(
            P(("members", "window"), None, None, "space", None),
            P(("members", "window"), None, None, "space", None),
            P(("members", "window"), None, None, "space", None),
        ),
        check_vma=False,
    )
```

```python
import jax
import jax.numpy as jnp
from jax import lax
from jax.experimental import pallas as pl
from jax.experimental.pallas import tpu as pltpu
from jax.sharding import PartitionSpec as P

LANES = 128
SUB = 8
HALF = SUB // 2
CODE_MAX = 32000.0
ROUNDER = 12582912.0

diffusion = 0.2
advection = 0.2
coupling_gain = 0.5
keep = 1.0 - 4.0 * diffusion
half_adv = 0.5 * advection

VMEM = pl.BlockSpec(memory_space=pltpu.VMEM)
SMEM = pl.BlockSpec(memory_space=pltpu.SMEM)
ANY = pl.BlockSpec(memory_space=pl.ANY)


def params(mib=24):
    return pltpu.CompilerParams(vmem_limit_bytes=mib * 1024 * 1024)


def lane_index():
    return lax.broadcasted_iota(jnp.int32, (SUB, LANES), 1)


def row_index():
    return lax.broadcasted_iota(jnp.int32, (SUB, LANES), 0)


def tiled(wide):
    short = -wide.shape[1] % LANES
    if short:
        wide = jnp.concatenate([wide, jnp.zeros((wide.shape[0], short), wide.dtype)], 1)
    return [wide[:, i : i + LANES] for i in range(0, wide.shape[1], LANES)]


def place(parts, rolled, lane):
    built = {}
    for key, tiles, first, width, target in parts:
        done = 0
        while done < width:
            a, b = first + done, target + done
            n = min(width - done, LANES - a % LANES, LANES - b % LANES)
            shift = (b - a) % LANES
            name = (key, a // LANES, shift)
            if name not in rolled:
                value = tiles[a // LANES]
                rolled[name] = pltpu.roll(value, shift, 1) if shift else value
            if b % LANES:
                built[b // LANES] = jnp.where(
                    lane >= b % LANES, rolled[name], built[b // LANES]
                )
            else:
                built[b // LANES] = rolled[name]
            done += n
    return [built[i] for i in range(len(built))]


def joined_halves(first, second):
    top = row_index()[:, :1] < HALF
    last = jnp.where(top, pltpu.roll(first, HALF, 0), second)
    start = jnp.where(top, first, pltpu.roll(second, HALF, 0))
    return last, start


def widened(own, near, far, odd, even):
    top = row_index() < HALF
    low, high = jnp.where(even, far, near), jnp.where(even, near, far)
    turned = pltpu.roll(own, HALF, 0)
    low = pltpu.roll(low, HALF, 0) if odd else low
    high = high if odd else pltpu.roll(high, HALF, 0)
    return jnp.where(top, low, turned), jnp.where(top, turned, high)


def row_codes(planes):
    lane = lax.broadcasted_iota(jnp.int32, planes[0][0].shape, 1)
    scales = jnp.zeros(planes[0][0].shape, jnp.float32)
    out = []
    for v, row in enumerate(planes):
        big = jnp.abs(row[0])
        for value in row[1:]:
            big = jnp.maximum(big, jnp.abs(value))
        big = jnp.max(big, axis=1, keepdims=True)
        power = jnp.clip(jnp.ceil(jnp.log2(jnp.maximum(big, 1e-30))), -90.0, 126.0)
        scales = jnp.where(lane == v, power, scales)
        gain = CODE_MAX * jnp.exp2(-power)
        for value in row:
            out.append((value * gain + ROUNDER) - ROUNDER)
    return out, scales


def shorts(value):
    return value.astype(jnp.int32).astype(jnp.int16)


def floats(value):
    return value.astype(jnp.int32).astype(jnp.float32)


def partners(windows):
    return list(range(windows - 1, 0, -1))


def pack_kernel(ways, windows, steps, nvar, levels, part, var_ref, traj_ref, *outs):
    me = lax.axis_index("window")
    lane = lane_index()
    variance = var_ref[...]
    high = variance.astype(jnp.bfloat16).astype(jnp.float32)
    middle = (variance - high).astype(jnp.bfloat16).astype(jnp.float32)
    low = variance - high - middle
    split = high + pltpu.roll(middle, HALF, 0) + pltpu.roll(low, LANES // 2, 1)
    split = split.astype(jnp.bfloat16)

    for n, d in enumerate(ways):
        outs[n][outs[n].shape[0] - 1] = split
        target = lax.rem(me + d, windows)

        def variable(v, carry, n=n, target=target):
            for lev in range(levels):
                pieces = [
                    tiled(traj_ref[target, j, v, lev].astype(jnp.float32)) for j in range(steps)
                ]
                parts = [(j, pieces[j], 0, part, j * part) for j in range(steps)]
                placed = place(parts, {}, lane)
                for t, value in enumerate(placed):
                    outs[n][(v * levels + lev) * len(placed) + t] = value.astype(jnp.bfloat16)
            return carry

        lax.fori_loop(0, nvar, variable, 0, unroll=len(ways) == 1)


def even_place():
    return lax.rem(lax.axis_index("space"), 2) == 0


def level_codes(ref, lev, first=0):
    planes = [
        [ref[0, v, lev, :, t : t + LANES] for t in range(0, ref.shape[-1], LANES)]
        for v in range(first, ref.shape[1])
    ]
    values, scales = row_codes(planes)
    return values + [scales]


def half_code_kernel(*refs):
    sources, (near_ref, far_ref, own_ref) = refs[:-3], refs[-3:]
    even = even_place()

    def pair(i, carry):
        near, far = [], []
        for k, ref in enumerate(sources):
            skip = int(k == len(sources) - 1)
            coded = [level_codes(ref, 2 * i + odd, skip) for odd in range(2)]
            for n, (first, second) in enumerate(zip(*coded)):
                if k == 0:
                    own_ref[i, n] = shorts(jnp.concatenate([first, second], 0))
                last, start = joined_halves(first, second)
                near.append(jnp.where(even, last, start))
                far.append(jnp.where(even, start, last))
            if len(near) % 2:
                near.append(jnp.zeros((SUB, LANES), jnp.float32))
                far.append(jnp.zeros((SUB, LANES), jnp.float32))
        for tiles, ref in ((near, near_ref), (far, far_ref)):
            for n in range(0, len(tiles), 2):
                ref[i, n // 2] = shorts(jnp.concatenate(tiles[n : n + 2], 0))
        return carry

    lax.fori_loop(0, near_ref.shape[0], pair, 0)


def half_tile(ref, i, n):
    whole = floats(ref[i, n // 2])
    return whole[SUB:] if n % 2 else whole[:SUB]


def around_kernel(windows, nvar, levels, *refs):
    pieces, (own_ref, near_ref, far_ref) = refs[:windows], refs[windows : windows + 3]
    outs, total_ref = refs[windows + 3 : -1], refs[-1]
    me = lax.axis_index("window")
    even = even_place()
    total = jnp.zeros((SUB, LANES), jnp.float32)
    for d in range(windows):
        split = pieces[d][pieces[d].shape[0] - 1].astype(jnp.float32)
        here = split + pltpu.roll(split, HALF, 0) + pltpu.roll(split, LANES // 2, 1)
        total = total + jnp.where(lax.rem(me - d + windows, windows) <= me, here, 0.0)
    for v in range(nvar):
        for lev in range(levels):
            one = total[lev : lev + 1, v : v + 1]
            total_ref[v * levels + lev] = jnp.broadcast_to(one, (SUB, LANES))
    lev = 0
    for out_ref in outs:
        for k in range(out_ref.shape[0]):
            i, odd = lev // 2, lev % 2
            for n in range(own_ref.shape[1]):
                own = floats(own_ref[i, n])[odd * SUB : (odd + 1) * SUB]
                near, far = half_tile(near_ref, i, n), half_tile(far_ref, i, n)
                halves = widened(own, near, far, odd, even)
                out_ref[k, n] = shorts(jnp.concatenate(halves, 0))
            lev += 1


def decoded(ref, i, first, nvar, tiles):
    scales = jnp.exp2(half_tile(ref, i, first + nvar * tiles)) * (1.0 / CODE_MAX)
    return [
        [half_tile(ref, i, first + v * tiles + t) * scales[:, v : v + 1] for t in range(tiles)]
        for v in range(nvar)
    ]


def is_quarter(j, v, steps):
    return 0 < j < steps - 1 and not (v == 0 and j + 1 > HALF // 2)


def edge_base(steps, nvar, levels):
    base, total = {}, 0
    for j in range(steps):
        for v in range(nvar):
            base[j, v] = total
            total += levels // (4 if is_quarter(j, v, steps) else 2)
    return base, total


def joined_quarters(four):
    slot = row_index() // 2
    last, start = pltpu.roll(four[0], 2, 0), four[0]
    for n in range(1, 4):
        last = jnp.where(slot == n, pltpu.roll(four[n], (2 * n + 2) % SUB, 0), last)
        start = jnp.where(slot == n, pltpu.roll(four[n], 2 * n, 0), start)
    return last, start


def assemble_kernel(windows, steps, nvar, levels, part, *refs):
    pieces = refs[:windows]
    own_ref, near_ref, far_ref, stack_ref = refs[windows + 1 :]
    me = lax.axis_index("window")
    even = even_place()
    lane = lane_index()
    count = stack_ref.shape[1]
    packed_tiles = count // (nvar * levels)
    for d in range(windows):
        stack_ref[lax.rem(me - d + windows, windows)] = pieces[d][:count]

    base, _ = edge_base(steps, nvar, levels)

    def variable(v):
        built = {}
        for lev in range(levels):
            plane = v * levels + lev
            sources = [
                [
                    stack_ref[w, plane * packed_tiles + t].astype(jnp.float32)
                    for t in range(packed_tiles)
                ]
                for w in range(windows)
            ]
            rolled = {}
            for j in range(steps):
                parts = [(w, sources[w], j * part, part, w * part) for w in range(windows)]
                built[j, lev] = place(parts, rolled, lane)
                own_ref[j, plane] = jnp.concatenate(built[j, lev], 1).astype(jnp.bfloat16)
        for j in range(steps):
            if is_quarter(j, v, steps):
                groups = [
                    [joined_quarters(four) for four in zip(*[built[j, 4 * q + n] for n in range(4)])]
                    for q in range(levels // 4)
                ]
            else:
                groups = [
                    [joined_halves(a, b) for a, b in zip(built[j, 2 * i], built[j, 2 * i + 1])]
                    for i in range(levels // 2)
                ]
            for n, group in enumerate(groups):
                last, start = (jnp.concatenate([e[k] for e in group], 1) for k in range(2))
                near_ref[base[j, v] + n] = jnp.where(even, last, start).astype(jnp.bfloat16)
                far_ref[base[j, v] + n] = jnp.where(even, start, last).astype(jnp.bfloat16)

    for v in range(nvar):
        variable(v)


def prepare_factor_kernel(
    steps, nvar, levels, tiles,
    count_ref, noise_ref, coupling_ref, dobs_ref, innov_ref, obs_ref, share_ref, mix_ref,
):
    cuts = [slice(t * LANES, (t + 1) * LANES) for t in range(tiles)]
    for v in range(nvar):
        for u in range(nvar):
            one = coupling_gain * coupling_ref[v : v + 1, u : u + 1]
            mix_ref[v, u] = jnp.broadcast_to(one, (SUB, LANES))
    for lev in range(levels):
        for j in range(steps):
            noise = jnp.full((SUB, LANES), noise_ref[0, j, lev])
            share = jnp.where(j < count_ref[0], 1.0, 0.0) / noise
            share_ref[lev, j] = share
            for t in range(tiles):
                gap = innov_ref[0, j, lev, :, cuts[t]] - noise * dobs_ref[0, j, lev, :, cuts[t]]
                obs_ref[lev, j, t] = gap * share


def prepare_tangent_kernel(nvar, levels, tiles, near_ref, far_ref, inc_ref, first_ref):
    even = even_place()
    blocks = [slice(0, SUB), slice(SUB, 2 * SUB)]
    cuts = [slice(t * LANES, (t + 1) * LANES) for t in range(tiles)]
    offset = -(-(nvar * tiles + 1) // 2) * 2
    for i in range(levels // 2):
        fields = [decoded(ref, i, offset, nvar, tiles) for ref in (near_ref, far_ref)]
        for odd in range(2):
            lev = 2 * i + odd
            for t in range(tiles):
                for v in range(nvar):
                    near, far = (side[v][t] for side in fields)
                    halves = widened(inc_ref[0, v, lev, :, cuts[t]], near, far, odd, even)
                    for b in range(2):
                        first_ref[lev, v, t, blocks[b], :] = halves[b]


def prepare_adjoint_kernel(
    i, steps, nvar, tiles, count_ref, near_ref, far_ref, dobs_ref, *refs
):
    after_refs, (_, last_ref, force_ref) = refs[:-3], refs[-3:]
    even = even_place()
    blocks = [slice(0, SUB), slice(SUB, 2 * SUB)]
    cuts = [slice(t * LANES, (t + 1) * LANES) for t in range(tiles)]
    seen = [jnp.where(j < count_ref[0], 1.0, 0.0) for j in range(steps)]
    offset = -(-(nvar * tiles + 1) // 2) * 2
    none = [[jnp.zeros((SUB, LANES), jnp.float32)] * tiles]
    forces = [none + decoded(ref, i, 2 * offset, steps - 1, tiles) for ref in (near_ref, far_ref)]
    for odd in range(2):
        after_ref, k = (after_refs[odd], 0) if len(after_refs) == 2 else (after_refs[0], odd)
        scales = jnp.exp2(floats(after_ref[k, nvar * tiles])) * (-1.0 / CODE_MAX)
        for t in range(tiles):
            for v in range(nvar):
                value = floats(after_ref[k, v * tiles + t])
                last_ref[odd, v, t] = value * scales[:, v : v + 1]
            for j in range(steps):
                near, far = (side[j][t] for side in forces)
                halves = widened(dobs_ref[0, j, 2 * i + odd, :, cuts[t]], near, far, odd, even)
                for b in range(2):
                    force_ref[odd, j, t, blocks[b], :] = seen[j] * halves[b]


def from_north(line, lane):
    turned = [pltpu.roll(value, LANES - 1, 1) for value in line] * 2
    return [jnp.where(lane < LANES - 1, turned[t], turned[t + 1]) for t in range(len(line))]


def from_south(line, lane):
    turned = [pltpu.roll(value, 1, 1) for value in line]
    return [jnp.where(lane > 0, turned[t], turned[t - 1]) for t in range(len(line))]


def masked_last(line, lane):
    return line[:-1] + [jnp.where(lane < LANES - 1, line[-1], 0.0)]


def masked_first(line, lane):
    return [jnp.where(lane > 0, line[0], 0.0)] + line[1:]


def walls(spaces):
    row, place_x = row_index(), lax.axis_index("space")
    low = jnp.where((row == HALF) & (place_x == 0), 0.0, 1.0)
    high = jnp.where((row == HALF - 1) & (place_x == spaces - 1), 0.0, 1.0)

    def walled(block, east, west):
        if block == 0:
            return east, [low * value for value in west]
        return [high * value for value in east], west

    return walled


BLOCKS = [slice(SUB, 2 * SUB), slice(2 * SUB, 3 * SUB)]
UPS = [slice(b.start + 1, b.stop + 1) for b in BLOCKS]
DOWNS = [slice(b.start - 1, b.stop - 1) for b in BLOCKS]
MINE = slice(SUB + HALF, 2 * SUB + HALF)


def tangent_kernel(
    spaces, steps, nvar, levels, tiles,
    mix_ref, share_ref, obs_ref, own_ref, near_ref, far_ref, first_ref,
    ndo_ref, ends_ref, x_ref, s_ref,
):
    lane, row = lane_index(), row_index()
    even = even_place()
    top = row < HALF
    walled = walls(spaces)
    pairs = levels // 2
    cuts = [slice(t * LANES, (t + 1) * LANES) for t in range(tiles)]
    base, _ = edge_base(steps, nvar, levels)

    for lev in range(levels):
        odd = lev % 2
        for j in range(steps):
            for v in range(nvar):
                for t in range(tiles):
                    own = own_ref[j, v * levels + lev, :, cuts[t]].astype(jnp.float32)
                    quarter = is_quarter(j, v, steps)
                    tile = base[j, v] + lev // (4 if quarter else 2)
                    near = near_ref[tile, :, cuts[t]].astype(jnp.float32)
                    far = far_ref[tile, :, cuts[t]].astype(jnp.float32)
                    low, high = jnp.where(even, far, near), jnp.where(even, near, far)
                    if quarter:
                        slot = 2 * (lev % 4)
                        low = pltpu.roll(low, (HALF - 2 - slot) % SUB, 0)
                        high = pltpu.roll(high, (HALF - slot) % SUB, 0)
                    else:
                        low = pltpu.roll(low, HALF, 0) if odd else low
                        high = high if odd else pltpu.roll(high, HALF, 0)
                    turned = pltpu.roll(own, HALF, 0)
                    x_ref[lev, j, v, t, :SUB, :] = jnp.where(top, low, turned)
                    x_ref[lev, j, v, t, SUB:, :] = jnp.where(top, turned, high)

    def pair(i, outer):
        for odd in range(2):
            for v in range(nvar):
                for t in range(tiles):
                    s_ref[odd, 0, v, t, SUB : 3 * SUB, :] = first_ref[2 * i + odd, v, t]

        for j in range(steps):
            now = j % 2
            for odd in range(2):
                lev = 2 * i + odd
                for t in range(tiles):
                    image = share_ref[lev, j] * s_ref[odd, now, 0, t, MINE, :]
                    ndo_ref[0, j, lev, :, cuts[t]] = obs_ref[lev, j, t] - image
                for b in range(2):
                    part = slice(b * SUB, (b + 1) * SUB)
                    here, up, down = BLOCKS[b], UPS[b], DOWNS[b]
                    x = [[x_ref[lev, j, u, t, part, :] for t in range(tiles)] for u in range(nvar)]
                    ce = [diffusion - half_adv * value for value in x[0]]
                    cw = [diffusion + half_adv * value for value in x[0]]
                    ce, cw = walled(b, ce, cw)
                    cn = masked_last([diffusion - half_adv * value for value in x[1]], lane)
                    cs = masked_first([diffusion + half_adv * value for value in x[1]], lane)
                    s = [
                        [s_ref[odd, now, u, t, here, :] for t in range(tiles)] for u in range(nvar)
                    ]
                    xs = [[x[u][t] * s[u][t] for t in range(tiles)] for u in range(nvar)]
                    for v in range(nvar):
                        north, south = from_north(s[v], lane), from_south(s[v], lane)
                        for t in range(tiles):
                            fresh = keep * s[v][t] + ce[t] * s_ref[odd, now, v, t, up, :]
                            fresh = fresh + cw[t] * s_ref[odd, now, v, t, down, :]
                            fresh = fresh + cn[t] * north[t] + cs[t] * south[t]
                            for u in range(nvar):
                                fresh = fresh + mix_ref[v, u] * xs[u][t]
                            s_ref[odd, 1 - now, v, t, here, :] = fresh
        for odd in range(2):
            for v in range(nvar):
                for t in range(tiles):
                    ends_ref[2 * i + odd, v, t] = s_ref[odd, steps % 2, v, t, MINE, :]
        return outer

    lax.fori_loop(0, pairs, pair, 0)


def adjoint_kernel(
    i, windows, spaces, steps, nvar, levels, tiles,
    mix_ref, total_ref, x_ref, last_ref, force_ref, ends_ref, inc_ref, rhs_ref, dual_ref,
    ndm_ref, ninc_ref, *rest,
):
    payload_refs = rest[: windows - 1]
    x0_ref, a_ref, q_ref = rest[windows - 1 :]
    me = lax.axis_index("window")
    lane = lane_index()
    walled = walls(spaces)
    cuts = [slice(t * LANES, (t + 1) * LANES) for t in range(tiles)]

    for odd in range(2):
        lev = 2 * i + odd
        for t in range(tiles):
            for j in range(steps):
                x0_ref[odd, j, t, SUB : 3 * SUB, :] = x_ref[lev, j, 0, t]
            for v in range(nvar):
                a_ref[odd, 0, v, t, SUB : 3 * SUB, :] = last_ref[odd, v, t]

    for turn in range(steps):
        now = turn % 2
        j = steps - 1 - turn
        for odd in range(2):
            lev = 2 * i + odd
            for b in range(2):
                part = slice(b * SUB, (b + 1) * SUB)
                here, up, down = BLOCKS[b], UPS[b], DOWNS[b]
                x = [[x_ref[lev, j, u, t, part, :] for t in range(tiles)] for u in range(nvar)]
                ce = [diffusion + half_adv * x0_ref[odd, j, t, up, :] for t in range(tiles)]
                cw = [diffusion - half_adv * x0_ref[odd, j, t, down, :] for t in range(tiles)]
                ce, cw = walled(b, ce, cw)
                cn = masked_first([diffusion + half_adv * value for value in x[1]], lane)
                cs = masked_last([diffusion - half_adv * value for value in x[1]], lane)
                a = [
                    [a_ref[odd, now, u, t, here, :] for t in range(tiles)] for u in range(nvar)
                ]
                for u in range(nvar):
                    north = from_north([cn[t] * a[u][t] for t in range(tiles)], lane)
                    south = from_south([cs[t] * a[u][t] for t in range(tiles)], lane)
                    for t in range(tiles):
                        fresh = keep * a[u][t] + ce[t] * a_ref[odd, now, u, t, up, :]
                        fresh = fresh + cw[t] * a_ref[odd, now, u, t, down, :]
                        fresh = fresh + north[t] + south[t]
                        pull = mix_ref[0, u] * a[0][t]
                        for v in range(1, nvar):
                            pull = pull + mix_ref[v, u] * a[v][t]
                        fresh = fresh + x[u][t] * pull
                        if u == 0:
                            fresh = fresh + force_ref[odd, j, t, part, :]
                        a_ref[odd, 1 - now, u, t, here, :] = fresh
    end = steps % 2
    coded = []
    for odd in range(2):
        lev = 2 * i + odd
        back, ahead = [], []
        for v in range(nvar):
            share = total_ref[v * levels + lev]
            tv, gv = [], []
            for t in range(tiles):
                term = a_ref[odd, end, v, t, MINE, :] - last_ref[odd, v, t, HALF : HALF + SUB, :]
                given = rhs_ref[0, v, lev, :, cuts[t]] - inc_ref[0, v, lev, :, cuts[t]]
                given = given + share * term
                ndm_ref[v, odd, :, cuts[t]] = -(dual_ref[0, v, lev, :, cuts[t]] + term)
                ninc_ref[v, odd, :, cuts[t]] = given
                tv.append(term)
                gv.append(given + ends_ref[lev, v, t])
            back.append(tv)
            ahead.append(gv)
        coded.append((row_codes(back), row_codes(ahead)))
    for kind in range(2):
        first, second = coded[0][kind], coded[1][kind]
        for n, (a, b) in enumerate(zip(first[0] + [first[1]], second[0] + [second[1]])):
            q_ref[kind, n] = shorts(jnp.concatenate([a, b], 0))
    for ref, d in zip(payload_refs, partners(windows)):
        ref[...] = q_ref[jnp.where((me ^ d) < me, 0, 1)]


def final_kernel(windows, nvar, levels, tiles, *refs):
    pairs = levels // 2
    cut = pairs * (windows - 1)
    pieces, base_duals, base_incs = refs[:cut], refs[cut : cut + pairs], refs[cut + pairs : -3]
    total_ref, ndm_ref, ninc_ref = refs[-3:]
    me = lax.axis_index("window")
    cuts = [slice(t * LANES, (t + 1) * LANES) for t in range(tiles)]

    for i in range(pairs):
        tails = [None] * (nvar * tiles)
        heads = [None] * (nvar * tiles)
        for n, d in enumerate(partners(windows)):
            piece = pieces[i * (windows - 1) + n]
            later = (me ^ d) > me
            scales = jnp.exp2(floats(piece[nvar * tiles])) * (1.0 / CODE_MAX)
            for v in range(nvar):
                scale = scales[:, v : v + 1]
                for t in range(tiles):
                    k = v * tiles + t
                    value = floats(piece[k]) * scale
                    tail, head = jnp.where(later, value, 0.0), jnp.where(later, 0.0, value)
                    tails[k] = tails[k] + tail if n else tail
                    heads[k] = heads[k] + head if n else head
        for v in range(nvar):
            for odd in range(2):
                lev = 2 * i + odd
                share = total_ref[v * levels + lev]
                for t in range(tiles):
                    rows = slice(odd * SUB, (odd + 1) * SUB)
                    tail, head = tails[v * tiles + t][rows], heads[v * tiles + t][rows]
                    ndm_ref[0, v, lev, :, cuts[t]] = base_duals[i][v, odd, :, cuts[t]] - tail
                    ninc_ref[0, v, lev, :, cuts[t]] = (
                        base_incs[i][v, odd, :, cuts[t]] + head + share * tail
                    )


def moved(block, axis, distance):
    devices = range(lax.axis_size(axis))
    return lax.ppermute(block, axis, [(i, i + distance) for i in devices if i + distance in devices])


def rotated(block, axis, distance):
    count = lax.axis_size(axis)
    return lax.ppermute(block, axis, [(i, (i + distance) % count) for i in range(count)])


def exchanged(block, axis, mask):
    return lax.ppermute(block, axis, [(i, i ^ mask) for i in range(lax.axis_size(axis))])


def swaps(axis, first):
    route = []
    for i in range(first, lax.axis_size(axis) - 1, 2):
        route += [(i, i + 1), (i + 1, i)]
    return route


def swapped(block, axis, first):
    return lax.ppermute(block, axis, swaps(axis, first))


def body(
    trajectory,
    dual_model,
    increment,
    model_rhs,
    dual_obs,
    innovation,
    coupling,
    error_var,
    obs_var,
    obs_count,
):
    windows, spaces = lax.axis_size("window"), lax.axis_size("space")
    _, steps, nvar, levels, rows, part = trajectory.shape
    columns = dual_model.shape[-1]
    tiles = columns // LANES
    assert trajectory.shape[0] == windows and windows > 1 and rows == SUB and steps == HALF
    assert columns == tiles * LANES == windows * part and levels % 4 == 0
    assert windows & (windows - 1) == 0
    pairs = levels // 2
    wide = -(-steps * part // LANES) * LANES
    bf16, f32, i16 = jnp.bfloat16, jnp.float32, jnp.int16

    def shape(dims, dtype):
        return jax.ShapeDtypeStruct(dims, dtype)

    block = shape((nvar * levels * wide // LANES + 1, rows, LANES), bf16)
    variances = jnp.pad(error_var[0].T, ((0, SUB - levels), (0, LANES - nvar)))

    def packed(ways):
        return pl.pallas_call(
            lambda *refs: pack_kernel(ways, windows, steps, nvar, levels, part, *refs),
            out_shape=[block] * len(ways),
            in_specs=[VMEM, VMEM],
            out_specs=[VMEM] * len(ways),
            compiler_params=params(),
        )(variances, trajectory)

    order = list(range(1, windows))
    groups = [[d] for d in order] if windows <= 4 else [order]
    blocks = {}
    for group in groups:
        blocks.update(zip(group, packed(group)))
    arrived = {d: rotated(blocks[d], "window", d) for d in order}
    arrived[0] = packed([0])[0]

    payload = shape((pairs, nvar * tiles + 1, 2 * SUB, LANES), i16)

    counts = [nvar, nvar, steps - 1]
    half_tiles = sum(-(-(count * tiles + 1) // 2) for count in counts)
    halves = shape((pairs, half_tiles, 2 * SUB, LANES), i16)
    near, far, dual = pl.pallas_call(
        half_code_kernel,
        out_shape=[halves, halves, payload],
        in_specs=[VMEM] * 3,
        out_specs=[VMEM] * 3,
        compiler_params=params(),
    )(dual_model, increment, dual_obs)
    far, near = swapped(far, "space", 1), swapped(near, "space", 0)

    blocks_here = [arrived[d] for d in range(windows)]
    flows = [1, 1] + [2] * (pairs - 1)
    *after, totals = pl.pallas_call(
        lambda *refs: around_kernel(windows, nvar, levels, *refs),
        out_shape=[shape((count,) + payload.shape[1:], i16) for count in flows]
        + [shape((nvar * levels, rows, LANES), f32)],
        in_specs=[VMEM] * (windows + 3),
        out_specs=[VMEM] * (len(flows) + 1),
        compiler_params=params(),
    )(*blocks_here, dual, near, far)
    after = [moved(piece, "window", -1) for piece in after]
    after = [after[:2]] + [[piece] for piece in after[2:]]

    obs, share, mix = pl.pallas_call(
        lambda *refs: prepare_factor_kernel(steps, nvar, levels, tiles, *refs),
        out_shape=[
            shape((levels, steps, tiles, SUB, LANES), f32),
            shape((levels, steps, SUB, LANES), f32),
            shape((nvar, nvar, SUB, LANES), f32),
        ],
        in_specs=[SMEM] * 2 + [VMEM] * 3,
        out_specs=[VMEM] * 3,
        compiler_params=params(),
    )(obs_count, obs_var, coupling, dual_obs, innovation)

    own, traj_near, traj_far = pl.pallas_call(
        lambda *refs: assemble_kernel(windows, steps, nvar, levels, part, *refs),
        out_shape=[
            shape((steps, nvar * levels, rows, columns), bf16),
            shape((edge_base(steps, nvar, levels)[1], rows, columns), bf16),
            shape((edge_base(steps, nvar, levels)[1], rows, columns), bf16),
        ],
        in_specs=[VMEM] * windows + [ANY],
        out_specs=[VMEM] * 3,
        scratch_shapes=[pltpu.VMEM((windows, block.shape[0] - 1, rows, LANES), bf16)],
        compiler_params=params(),
    )(*blocks_here, mix)
    traj_far, traj_near = swapped(traj_far, "space", 1), swapped(traj_near, "space", 0)

    first = pl.pallas_call(
        lambda *refs: prepare_tangent_kernel(nvar, levels, tiles, *refs),
        out_shape=shape((levels, nvar, tiles, 2 * SUB, LANES), f32),
        in_specs=[VMEM] * 3,
        out_specs=VMEM,
        compiler_params=params(),
    )(near, far, increment)
    new_dual_obs, ends, wide_traj = pl.pallas_call(
        lambda *refs: tangent_kernel(spaces, steps, nvar, levels, tiles, *refs),
        out_shape=[
            shape(dual_obs.shape, f32),
            shape((levels, nvar, tiles, SUB, LANES), f32),
            shape((levels, steps, nvar, tiles, 2 * SUB, LANES), f32),
        ],
        in_specs=[VMEM] * 7,
        out_specs=[VMEM] * 3,
        scratch_shapes=[pltpu.VMEM((2, 2, nvar, tiles, 4 * SUB, LANES), f32)],
        compiler_params=params(),
    )(mix, share, obs, own, traj_near, traj_far, first)

    state = shape((nvar, 2, rows, columns), f32)
    coded = shape((nvar * tiles + 1, 2 * SUB, LANES), i16)
    base_duals, base_incs, sent = [], [], []
    before = ends
    for i in range(pairs):
        last, force = pl.pallas_call(
            lambda *refs, i=i: prepare_adjoint_kernel(i, steps, nvar, tiles, *refs),
            out_shape=[shape((2, n, tiles, 2 * SUB, LANES), f32) for n in (nvar, steps)],
            in_specs=[SMEM] + [VMEM] * (3 + len(after[i])) + [ANY],
            out_specs=[VMEM] * 2,
            compiler_params=params(),
        )(obs_count, near, far, dual_obs, *after[i], before)
        base_dual, base_inc, *payloads = pl.pallas_call(
            lambda *refs, i=i: adjoint_kernel(
                i, windows, spaces, steps, nvar, levels, tiles, *refs
            ),
            out_shape=[state, state] + [coded] * (windows - 1),
            in_specs=[VMEM] * 9,
            out_specs=[VMEM] * (2 + windows - 1),
            scratch_shapes=[
                pltpu.VMEM((2, steps, tiles, 4 * SUB, LANES), f32),
                pltpu.VMEM((2, 2, nvar, tiles, 4 * SUB, LANES), f32),
                pltpu.VMEM((2,) + coded.shape, i16),
            ],
            compiler_params=params(),
        )(mix, totals, wide_traj, last, force, ends, increment, model_rhs, dual_model)
        before = base_dual
        base_duals.append(base_dual)
        base_incs.append(base_inc)
        sent += [
            exchanged(piece, "window", mask)
            for piece, mask in zip(payloads, partners(windows))
        ]

    new_dual_model, new_increment = pl.pallas_call(
        lambda *refs: final_kernel(windows, nvar, levels, tiles, *refs),
        out_shape=[shape(dual_model.shape, f32), shape(increment.shape, f32)],
        in_specs=[VMEM] * (len(sent) + 2 * pairs + 1),
        out_specs=[VMEM] * 2,
        compiler_params=params(),
    )(*sent, *base_duals, *base_incs, totals)
    return new_dual_model, new_dual_obs, new_increment


def solution(mesh):
    placed = (
        P("members", None, None, None, "space", "window"),
        P(("members", "window"), None, None, "space", None),
        P(("members", "window"), None, None, "space", None),
        P(("members", "window"), None, None, "space", None),
        P(("members", "window"), None, None, "space", None),
        P(("members", "window"), None, None, "space", None),
        P(),
        P(("members", "window"), None, None),
        P(("members", "window"), None, None),
        P(("members", "window")),
    )
    return jax.shard_map(
        body,
        mesh=mesh,
        in_specs=placed,
        out_specs=(
            P(("members", "window"), None, None, "space", None),
            P(("members", "window"), None, None, "space", None),
            P(("members", "window"), None, None, "space", None),
        ),
        check_vma=False,
    )
```

```python
import jax
import jax.numpy as jnp
from jax import lax
from jax.experimental import pallas as pl
from jax.experimental.pallas import tpu as pltpu
from jax.sharding import PartitionSpec as P

LANES = 128
SUB = 8
HALF = SUB // 2
CODE_MAX = 32000.0
ROUNDER = 12582912.0

diffusion = 0.2
advection = 0.2
coupling_gain = 0.5
keep = 1.0 - 4.0 * diffusion
half_adv = 0.5 * advection

VMEM = pl.BlockSpec(memory_space=pltpu.VMEM)
SMEM = pl.BlockSpec(memory_space=pltpu.SMEM)
ANY = pl.BlockSpec(memory_space=pl.ANY)


def params(mib=24):
    return pltpu.CompilerParams(vmem_limit_bytes=mib * 1024 * 1024)


def lane_index():
    return lax.broadcasted_iota(jnp.int32, (SUB, LANES), 1)


def row_index():
    return lax.broadcasted_iota(jnp.int32, (SUB, LANES), 0)


def tiled(wide):
    short = -wide.shape[1] % LANES
    if short:
        wide = jnp.concatenate([wide, jnp.zeros((wide.shape[0], short), wide.dtype)], 1)
    return [wide[:, i : i + LANES] for i in range(0, wide.shape[1], LANES)]


def place(parts, rolled, lane):
    built = {}
    for key, tiles, first, width, target in parts:
        done = 0
        while done < width:
            a, b = first + done, target + done
            n = min(width - done, LANES - a % LANES, LANES - b % LANES)
            shift = (b - a) % LANES
            name = (key, a // LANES, shift)
            if name not in rolled:
                value = tiles[a // LANES]
                rolled[name] = pltpu.roll(value, shift, 1) if shift else value
            if b % LANES:
                built[b // LANES] = jnp.where(
                    lane >= b % LANES, rolled[name], built[b // LANES]
                )
            else:
                built[b // LANES] = rolled[name]
            done += n
    return [built[i] for i in range(len(built))]


def joined_halves(first, second):
    top = row_index()[:, :1] < HALF
    last = jnp.where(top, pltpu.roll(first, HALF, 0), second)
    start = jnp.where(top, first, pltpu.roll(second, HALF, 0))
    return last, start


def widened(own, near, far, odd, even):
    top = row_index() < HALF
    low, high = jnp.where(even, far, near), jnp.where(even, near, far)
    turned = pltpu.roll(own, HALF, 0)
    low = pltpu.roll(low, HALF, 0) if odd else low
    high = high if odd else pltpu.roll(high, HALF, 0)
    return jnp.where(top, low, turned), jnp.where(top, turned, high)


def row_codes(planes):
    lane = lax.broadcasted_iota(jnp.int32, planes[0][0].shape, 1)
    scales = jnp.zeros(planes[0][0].shape, jnp.float32)
    out = []
    for v, row in enumerate(planes):
        big = jnp.abs(row[0])
        for value in row[1:]:
            big = jnp.maximum(big, jnp.abs(value))
        big = jnp.max(big, axis=1, keepdims=True)
        power = jnp.clip(jnp.ceil(jnp.log2(jnp.maximum(big, 1e-30))), -90.0, 126.0)
        scales = jnp.where(lane == v, power, scales)
        gain = CODE_MAX * jnp.exp2(-power)
        for value in row:
            out.append((value * gain + ROUNDER) - ROUNDER)
    return out, scales


def shorts(value):
    return value.astype(jnp.int32).astype(jnp.int16)


def floats(value):
    return value.astype(jnp.int32).astype(jnp.float32)


def partners(windows):
    return list(range(windows - 1, 0, -1))


def pack_kernel(ways, windows, steps, nvar, levels, part, var_ref, traj_ref, *outs):
    me = lax.axis_index("window")
    lane = lane_index()
    variance = var_ref[...]
    high = variance.astype(jnp.bfloat16).astype(jnp.float32)
    middle = (variance - high).astype(jnp.bfloat16).astype(jnp.float32)
    low = variance - high - middle
    split = high + pltpu.roll(middle, HALF, 0) + pltpu.roll(low, LANES // 2, 1)
    split = split.astype(jnp.bfloat16)

    for n, d in enumerate(ways):
        outs[n][outs[n].shape[0] - 1] = split
        target = lax.rem(me + d, windows)

        def variable(v, carry, n=n, target=target):
            for lev in range(levels):
                pieces = [
                    tiled(traj_ref[target, j, v, lev].astype(jnp.float32)) for j in range(steps)
                ]
                parts = [(j, pieces[j], 0, part, j * part) for j in range(steps)]
                placed = place(parts, {}, lane)
                for t, value in enumerate(placed):
                    outs[n][(v * levels + lev) * len(placed) + t] = value.astype(jnp.bfloat16)
            return carry

        lax.fori_loop(0, nvar, variable, 0, unroll=len(ways) == 1)


def even_place():
    return lax.rem(lax.axis_index("space"), 2) == 0


def level_codes(ref, lev, first=0):
    planes = [
        [ref[0, v, lev, :, t : t + LANES] for t in range(0, ref.shape[-1], LANES)]
        for v in range(first, ref.shape[1])
    ]
    values, scales = row_codes(planes)
    return values + [scales]


def half_code_kernel(*refs):
    sources, (near_ref, far_ref, own_ref) = refs[:-3], refs[-3:]
    even = even_place()

    def pair(i, carry):
        near, far = [], []
        for k, ref in enumerate(sources):
            skip = int(k == len(sources) - 1)
            coded = [level_codes(ref, 2 * i + odd, skip) for odd in range(2)]
            for n, (first, second) in enumerate(zip(*coded)):
                if k == 0:
                    own_ref[i, n] = shorts(jnp.concatenate([first, second], 0))
                last, start = joined_halves(first, second)
                near.append(jnp.where(even, last, start))
                far.append(jnp.where(even, start, last))
            if len(near) % 2:
                near.append(jnp.zeros((SUB, LANES), jnp.float32))
                far.append(jnp.zeros((SUB, LANES), jnp.float32))
        for tiles, ref in ((near, near_ref), (far, far_ref)):
            for n in range(0, len(tiles), 2):
                ref[i, n // 2] = shorts(jnp.concatenate(tiles[n : n + 2], 0))
        return carry

    lax.fori_loop(0, near_ref.shape[0], pair, 0)


def half_tile(ref, i, n):
    whole = floats(ref[i, n // 2])
    return whole[SUB:] if n % 2 else whole[:SUB]


def around_kernel(windows, nvar, levels, *refs):
    pieces, (own_ref, near_ref, far_ref) = refs[:windows], refs[windows : windows + 3]
    outs, total_ref = refs[windows + 3 : -1], refs[-1]
    me = lax.axis_index("window")
    even = even_place()
    total = jnp.zeros((SUB, LANES), jnp.float32)
    for d in range(windows):
        split = pieces[d][pieces[d].shape[0] - 1].astype(jnp.float32)
        here = split + pltpu.roll(split, HALF, 0) + pltpu.roll(split, LANES // 2, 1)
        total = total + jnp.where(lax.rem(me - d + windows, windows) <= me, here, 0.0)
    for v in range(nvar):
        for lev in range(levels):
            one = total[lev : lev + 1, v : v + 1]
            total_ref[v * levels + lev] = jnp.broadcast_to(one, (SUB, LANES))
    for i, out_ref in enumerate(outs):
        for n in range(own_ref.shape[1]):
            own = floats(own_ref[i, n])
            near, far = half_tile(near_ref, i, n), half_tile(far_ref, i, n)
            for odd in range(2):
                halves = widened(own[odd * SUB : (odd + 1) * SUB], near, far, odd, even)
                out_ref[odd, n] = shorts(jnp.concatenate(halves, 0))


def decoded(ref, i, first, nvar, tiles):
    scales = jnp.exp2(half_tile(ref, i, first + nvar * tiles)) * (1.0 / CODE_MAX)
    return [
        [half_tile(ref, i, first + v * tiles + t) * scales[:, v : v + 1] for t in range(tiles)]
        for v in range(nvar)
    ]


def is_quarter(j, v, steps):
    return 0 < j < steps - 1 and not (v == 0 and j + 1 > HALF // 2)


def edge_base(steps, nvar, levels):
    base, total = {}, 0
    for j in range(steps):
        for v in range(nvar):
            base[j, v] = total
            total += levels // (4 if is_quarter(j, v, steps) else 2)
    return base, total


def joined_quarters(four):
    slot = row_index() // 2
    last, start = pltpu.roll(four[0], 2, 0), four[0]
    for n in range(1, 4):
        last = jnp.where(slot == n, pltpu.roll(four[n], (2 * n + 2) % SUB, 0), last)
        start = jnp.where(slot == n, pltpu.roll(four[n], 2 * n, 0), start)
    return last, start


def assemble_kernel(windows, steps, nvar, levels, part, *refs):
    pieces = refs[:windows]
    own_ref, near_ref, far_ref, stack_ref = refs[windows + 1 :]
    me = lax.axis_index("window")
    even = even_place()
    lane = lane_index()
    count = stack_ref.shape[1]
    packed_tiles = count // (nvar * levels)
    for d in range(windows):
        stack_ref[lax.rem(me - d + windows, windows)] = pieces[d][:count]

    base, _ = edge_base(steps, nvar, levels)

    def variable(v):
        built = {}
        for lev in range(levels):
            plane = v * levels + lev
            sources = [
                [
                    stack_ref[w, plane * packed_tiles + t].astype(jnp.float32)
                    for t in range(packed_tiles)
                ]
                for w in range(windows)
            ]
            rolled = {}
            for j in range(steps):
                parts = [(w, sources[w], j * part, part, w * part) for w in range(windows)]
                built[j, lev] = place(parts, rolled, lane)
                own_ref[j, plane] = jnp.concatenate(built[j, lev], 1).astype(jnp.bfloat16)
        for j in range(steps):
            if is_quarter(j, v, steps):
                groups = [
                    [joined_quarters(four) for four in zip(*[built[j, 4 * q + n] for n in range(4)])]
                    for q in range(levels // 4)
                ]
            else:
                groups = [
                    [joined_halves(a, b) for a, b in zip(built[j, 2 * i], built[j, 2 * i + 1])]
                    for i in range(levels // 2)
                ]
            for n, group in enumerate(groups):
                last, start = (jnp.concatenate([e[k] for e in group], 1) for k in range(2))
                near_ref[base[j, v] + n] = jnp.where(even, last, start).astype(jnp.bfloat16)
                far_ref[base[j, v] + n] = jnp.where(even, start, last).astype(jnp.bfloat16)

    for v in range(nvar):
        variable(v)


def prepare_factor_kernel(
    steps, nvar, levels, tiles,
    count_ref, noise_ref, coupling_ref, dobs_ref, innov_ref, obs_ref, share_ref, mix_ref,
):
    cuts = [slice(t * LANES, (t + 1) * LANES) for t in range(tiles)]
    for v in range(nvar):
        for u in range(nvar):
            one = coupling_gain * coupling_ref[v : v + 1, u : u + 1]
            mix_ref[v, u] = jnp.broadcast_to(one, (SUB, LANES))
    for lev in range(levels):
        for j in range(steps):
            noise = jnp.full((SUB, LANES), noise_ref[0, j, lev])
            share = jnp.where(j < count_ref[0], 1.0, 0.0) / noise
            share_ref[lev, j] = share
            for t in range(tiles):
                gap = innov_ref[0, j, lev, :, cuts[t]] - noise * dobs_ref[0, j, lev, :, cuts[t]]
                obs_ref[lev, j, t] = gap * share


def prepare_tangent_kernel(nvar, levels, tiles, near_ref, far_ref, inc_ref, first_ref):
    even = even_place()
    blocks = [slice(0, SUB), slice(SUB, 2 * SUB)]
    cuts = [slice(t * LANES, (t + 1) * LANES) for t in range(tiles)]
    offset = -(-(nvar * tiles + 1) // 2) * 2
    for i in range(levels // 2):
        fields = [decoded(ref, i, offset, nvar, tiles) for ref in (near_ref, far_ref)]
        for odd in range(2):
            lev = 2 * i + odd
            for t in range(tiles):
                for v in range(nvar):
                    near, far = (side[v][t] for side in fields)
                    halves = widened(inc_ref[0, v, lev, :, cuts[t]], near, far, odd, even)
                    for b in range(2):
                        first_ref[lev, v, t, blocks[b], :] = halves[b]


def prepare_adjoint_kernel(
    i, steps, nvar, tiles, count_ref, near_ref, far_ref, dobs_ref, after_ref, *refs
):
    _, last_ref, force_ref = refs
    even = even_place()
    blocks = [slice(0, SUB), slice(SUB, 2 * SUB)]
    cuts = [slice(t * LANES, (t + 1) * LANES) for t in range(tiles)]
    seen = [jnp.where(j < count_ref[0], 1.0, 0.0) for j in range(steps)]
    offset = -(-(nvar * tiles + 1) // 2) * 2
    none = [[jnp.zeros((SUB, LANES), jnp.float32)] * tiles]
    forces = [none + decoded(ref, i, 2 * offset, steps - 1, tiles) for ref in (near_ref, far_ref)]
    for odd in range(2):
        scales = jnp.exp2(floats(after_ref[odd, nvar * tiles])) * (-1.0 / CODE_MAX)
        for t in range(tiles):
            for v in range(nvar):
                value = floats(after_ref[odd, v * tiles + t])
                last_ref[odd, v, t] = value * scales[:, v : v + 1]
            for j in range(steps):
                near, far = (side[j][t] for side in forces)
                halves = widened(dobs_ref[0, j, 2 * i + odd, :, cuts[t]], near, far, odd, even)
                for b in range(2):
                    force_ref[odd, j, t, blocks[b], :] = seen[j] * halves[b]


def from_north(line, lane):
    turned = [pltpu.roll(value, LANES - 1, 1) for value in line] * 2
    return [jnp.where(lane < LANES - 1, turned[t], turned[t + 1]) for t in range(len(line))]


def from_south(line, lane):
    turned = [pltpu.roll(value, 1, 1) for value in line]
    return [jnp.where(lane > 0, turned[t], turned[t - 1]) for t in range(len(line))]


def masked_last(line, lane):
    return line[:-1] + [jnp.where(lane < LANES - 1, line[-1], 0.0)]


def masked_first(line, lane):
    return [jnp.where(lane > 0, line[0], 0.0)] + line[1:]


def walls(spaces):
    row, place_x = row_index(), lax.axis_index("space")
    low = jnp.where((row == HALF) & (place_x == 0), 0.0, 1.0)
    high = jnp.where((row == HALF - 1) & (place_x == spaces - 1), 0.0, 1.0)

    def walled(block, east, west):
        if block == 0:
            return east, [low * value for value in west]
        return [high * value for value in east], west

    return walled


BLOCKS = [slice(SUB, 2 * SUB), slice(2 * SUB, 3 * SUB)]
UPS = [slice(b.start + 1, b.stop + 1) for b in BLOCKS]
DOWNS = [slice(b.start - 1, b.stop - 1) for b in BLOCKS]
MINE = slice(SUB + HALF, 2 * SUB + HALF)


def tangent_kernel(
    spaces, steps, nvar, levels, tiles,
    mix_ref, share_ref, obs_ref, own_ref, near_ref, far_ref, first_ref,
    ndo_ref, ends_ref, x_ref, s_ref,
):
    lane, row = lane_index(), row_index()
    even = even_place()
    top = row < HALF
    walled = walls(spaces)
    pairs = levels // 2
    cuts = [slice(t * LANES, (t + 1) * LANES) for t in range(tiles)]
    base, _ = edge_base(steps, nvar, levels)

    for lev in range(levels):
        odd = lev % 2
        for j in range(steps):
            for v in range(nvar):
                for t in range(tiles):
                    own = own_ref[j, v * levels + lev, :, cuts[t]].astype(jnp.float32)
                    quarter = is_quarter(j, v, steps)
                    tile = base[j, v] + lev // (4 if quarter else 2)
                    near = near_ref[tile, :, cuts[t]].astype(jnp.float32)
                    far = far_ref[tile, :, cuts[t]].astype(jnp.float32)
                    low, high = jnp.where(even, far, near), jnp.where(even, near, far)
                    if quarter:
                        slot = 2 * (lev % 4)
                        low = pltpu.roll(low, (HALF - 2 - slot) % SUB, 0)
                        high = pltpu.roll(high, (HALF - slot) % SUB, 0)
                    else:
                        low = pltpu.roll(low, HALF, 0) if odd else low
                        high = high if odd else pltpu.roll(high, HALF, 0)
                    turned = pltpu.roll(own, HALF, 0)
                    x_ref[lev, j, v, t, :SUB, :] = jnp.where(top, low, turned)
                    x_ref[lev, j, v, t, SUB:, :] = jnp.where(top, turned, high)

    def pair(i, outer):
        for odd in range(2):
            for v in range(nvar):
                for t in range(tiles):
                    s_ref[odd, 0, v, t, SUB : 3 * SUB, :] = first_ref[2 * i + odd, v, t]

        for j in range(steps):
            now = j % 2
            for odd in range(2):
                lev = 2 * i + odd
                for t in range(tiles):
                    image = share_ref[lev, j] * s_ref[odd, now, 0, t, MINE, :]
                    ndo_ref[0, j, lev, :, cuts[t]] = obs_ref[lev, j, t] - image
                for b in range(2):
                    part = slice(b * SUB, (b + 1) * SUB)
                    here, up, down = BLOCKS[b], UPS[b], DOWNS[b]
                    x = [[x_ref[lev, j, u, t, part, :] for t in range(tiles)] for u in range(nvar)]
                    ce = [diffusion - half_adv * value for value in x[0]]
                    cw = [diffusion + half_adv * value for value in x[0]]
                    ce, cw = walled(b, ce, cw)
                    cn = masked_last([diffusion - half_adv * value for value in x[1]], lane)
                    cs = masked_first([diffusion + half_adv * value for value in x[1]], lane)
                    s = [
                        [s_ref[odd, now, u, t, here, :] for t in range(tiles)] for u in range(nvar)
                    ]
                    xs = [[x[u][t] * s[u][t] for t in range(tiles)] for u in range(nvar)]
                    for v in range(nvar):
                        north, south = from_north(s[v], lane), from_south(s[v], lane)
                        for t in range(tiles):
                            fresh = keep * s[v][t] + ce[t] * s_ref[odd, now, v, t, up, :]
                            fresh = fresh + cw[t] * s_ref[odd, now, v, t, down, :]
                            fresh = fresh + cn[t] * north[t] + cs[t] * south[t]
                            for u in range(nvar):
                                fresh = fresh + mix_ref[v, u] * xs[u][t]
                            s_ref[odd, 1 - now, v, t, here, :] = fresh
        for odd in range(2):
            for v in range(nvar):
                for t in range(tiles):
                    ends_ref[2 * i + odd, v, t] = s_ref[odd, steps % 2, v, t, MINE, :]
        return outer

    lax.fori_loop(0, pairs, pair, 0)


def adjoint_kernel(
    i, windows, spaces, steps, nvar, levels, tiles,
    mix_ref, total_ref, x_ref, last_ref, force_ref, ends_ref, inc_ref, rhs_ref, dual_ref,
    ndm_ref, ninc_ref, *rest,
):
    payload_refs = rest[: windows - 1]
    x0_ref, a_ref, q_ref = rest[windows - 1 :]
    me = lax.axis_index("window")
    lane = lane_index()
    walled = walls(spaces)
    cuts = [slice(t * LANES, (t + 1) * LANES) for t in range(tiles)]

    for odd in range(2):
        lev = 2 * i + odd
        for t in range(tiles):
            for j in range(steps):
                x0_ref[odd, j, t, SUB : 3 * SUB, :] = x_ref[lev, j, 0, t]
            for v in range(nvar):
                a_ref[odd, 0, v, t, SUB : 3 * SUB, :] = last_ref[odd, v, t]

    for turn in range(steps):
        now = turn % 2
        j = steps - 1 - turn
        for odd in range(2):
            lev = 2 * i + odd
            for b in range(2):
                part = slice(b * SUB, (b + 1) * SUB)
                here, up, down = BLOCKS[b], UPS[b], DOWNS[b]
                x = [[x_ref[lev, j, u, t, part, :] for t in range(tiles)] for u in range(nvar)]
                ce = [diffusion + half_adv * x0_ref[odd, j, t, up, :] for t in range(tiles)]
                cw = [diffusion - half_adv * x0_ref[odd, j, t, down, :] for t in range(tiles)]
                ce, cw = walled(b, ce, cw)
                cn = masked_first([diffusion + half_adv * value for value in x[1]], lane)
                cs = masked_last([diffusion - half_adv * value for value in x[1]], lane)
                a = [
                    [a_ref[odd, now, u, t, here, :] for t in range(tiles)] for u in range(nvar)
                ]
                for u in range(nvar):
                    north = from_north([cn[t] * a[u][t] for t in range(tiles)], lane)
                    south = from_south([cs[t] * a[u][t] for t in range(tiles)], lane)
                    for t in range(tiles):
                        fresh = keep * a[u][t] + ce[t] * a_ref[odd, now, u, t, up, :]
                        fresh = fresh + cw[t] * a_ref[odd, now, u, t, down, :]
                        fresh = fresh + north[t] + south[t]
                        pull = mix_ref[0, u] * a[0][t]
                        for v in range(1, nvar):
                            pull = pull + mix_ref[v, u] * a[v][t]
                        fresh = fresh + x[u][t] * pull
                        if u == 0:
                            fresh = fresh + force_ref[odd, j, t, part, :]
                        a_ref[odd, 1 - now, u, t, here, :] = fresh
    end = steps % 2
    coded = []
    for odd in range(2):
        lev = 2 * i + odd
        back, ahead = [], []
        for v in range(nvar):
            share = total_ref[v * levels + lev]
            tv, gv = [], []
            for t in range(tiles):
                term = a_ref[odd, end, v, t, MINE, :] - last_ref[odd, v, t, HALF : HALF + SUB, :]
                given = rhs_ref[0, v, lev, :, cuts[t]] - inc_ref[0, v, lev, :, cuts[t]]
                given = given + share * term
                ndm_ref[v, odd, :, cuts[t]] = -(dual_ref[0, v, lev, :, cuts[t]] + term)
                ninc_ref[v, odd, :, cuts[t]] = given
                tv.append(term)
                gv.append(given + ends_ref[lev, v, t])
            back.append(tv)
            ahead.append(gv)
        coded.append((row_codes(back), row_codes(ahead)))
    for kind in range(2):
        first, second = coded[0][kind], coded[1][kind]
        for n, (a, b) in enumerate(zip(first[0] + [first[1]], second[0] + [second[1]])):
            q_ref[kind, n] = shorts(jnp.concatenate([a, b], 0))
    for ref, d in zip(payload_refs, partners(windows)):
        ref[...] = q_ref[jnp.where((me ^ d) < me, 0, 1)]


def add_pair(i, windows, nvar, levels, tiles, pieces, base_dual_ref, base_inc_ref, total_ref, write):
    me = lax.axis_index("window")
    cuts = [slice(t * LANES, (t + 1) * LANES) for t in range(tiles)]
    tails = [None] * (nvar * tiles)
    heads = [None] * (nvar * tiles)
    for n, d in enumerate(partners(windows)):
        piece = pieces[n]
        later = (me ^ d) > me
        scales = jnp.exp2(floats(piece[nvar * tiles])) * (1.0 / CODE_MAX)
        for v in range(nvar):
            scale = scales[:, v : v + 1]
            for t in range(tiles):
                k = v * tiles + t
                value = floats(piece[k]) * scale
                tail, head = jnp.where(later, value, 0.0), jnp.where(later, 0.0, value)
                tails[k] = tails[k] + tail if n else tail
                heads[k] = heads[k] + head if n else head
    for v in range(nvar):
        for odd in range(2):
            share = total_ref[v * levels + 2 * i + odd]
            for t in range(tiles):
                rows = slice(odd * SUB, (odd + 1) * SUB)
                tail, head = tails[v * tiles + t][rows], heads[v * tiles + t][rows]
                dual = base_dual_ref[v, odd, :, cuts[t]] - tail
                write(v, odd, cuts[t], dual, base_inc_ref[v, odd, :, cuts[t]] + head + share * tail)


def early_kernel(i, windows, nvar, levels, tiles, *refs):
    pieces, (base_dual_ref, base_inc_ref, total_ref, dual_ref, inc_ref) = refs[:-5], refs[-5:]

    def write(v, odd, cut, dual, inc):
        dual_ref[v, odd, :, cut] = dual
        inc_ref[v, odd, :, cut] = inc

    add_pair(
        i, windows, nvar, levels, tiles, pieces, base_dual_ref, base_inc_ref, total_ref, write
    )


def final_kernel(windows, nvar, levels, tiles, *refs):
    last = levels // 2 - 1
    pieces, done = refs[: windows - 1], refs[windows - 1 : windows - 1 + 2 * last]
    base_dual_ref, base_inc_ref, total_ref, ndm_ref, ninc_ref = refs[-5:]
    for i in range(last):
        for odd in range(2):
            ndm_ref[0, :, 2 * i + odd] = done[2 * i][:, odd]
            ninc_ref[0, :, 2 * i + odd] = done[2 * i + 1][:, odd]

    def write(v, odd, cut, dual, inc):
        ndm_ref[0, v, 2 * last + odd, :, cut] = dual
        ninc_ref[0, v, 2 * last + odd, :, cut] = inc

    add_pair(
        last, windows, nvar, levels, tiles, pieces, base_dual_ref, base_inc_ref, total_ref, write
    )


def moved(block, axis, distance):
    devices = range(lax.axis_size(axis))
    return lax.ppermute(block, axis, [(i, i + distance) for i in devices if i + distance in devices])


def rotated(block, axis, distance):
    count = lax.axis_size(axis)
    return lax.ppermute(block, axis, [(i, (i + distance) % count) for i in range(count)])


def exchanged(block, axis, mask):
    return lax.ppermute(block, axis, [(i, i ^ mask) for i in range(lax.axis_size(axis))])


def swaps(axis, first):
    route = []
    for i in range(first, lax.axis_size(axis) - 1, 2):
        route += [(i, i + 1), (i + 1, i)]
    return route


def swapped(block, axis, first):
    return lax.ppermute(block, axis, swaps(axis, first))


def body(
    trajectory,
    dual_model,
    increment,
    model_rhs,
    dual_obs,
    innovation,
    coupling,
    error_var,
    obs_var,
    obs_count,
):
    windows, spaces = lax.axis_size("window"), lax.axis_size("space")
    _, steps, nvar, levels, rows, part = trajectory.shape
    columns = dual_model.shape[-1]
    tiles = columns // LANES
    assert trajectory.shape[0] == windows and windows > 1 and rows == SUB and steps == HALF
    assert columns == tiles * LANES == windows * part and levels % 4 == 0
    assert windows & (windows - 1) == 0
    pairs = levels // 2
    wide = -(-steps * part // LANES) * LANES
    bf16, f32, i16 = jnp.bfloat16, jnp.float32, jnp.int16

    def shape(dims, dtype):
        return jax.ShapeDtypeStruct(dims, dtype)

    block = shape((nvar * levels * wide // LANES + 1, rows, LANES), bf16)
    variances = jnp.pad(error_var[0].T, ((0, SUB - levels), (0, LANES - nvar)))

    def packed(ways):
        return pl.pallas_call(
            lambda *refs: pack_kernel(ways, windows, steps, nvar, levels, part, *refs),
            out_shape=[block] * len(ways),
            in_specs=[VMEM, VMEM],
            out_specs=[VMEM] * len(ways),
            compiler_params=params(),
        )(variances, trajectory)

    order = list(range(1, windows))
    groups = [[d] for d in order] if windows <= 4 else [order]
    blocks = {}
    for group in groups:
        blocks.update(zip(group, packed(group)))
    arrived = {d: rotated(blocks[d], "window", d) for d in order}
    arrived[0] = packed([0])[0]

    payload = shape((pairs, nvar * tiles + 1, 2 * SUB, LANES), i16)

    counts = [nvar, nvar, steps - 1]
    half_tiles = sum(-(-(count * tiles + 1) // 2) for count in counts)
    halves = shape((pairs, half_tiles, 2 * SUB, LANES), i16)
    near, far, dual = pl.pallas_call(
        half_code_kernel,
        out_shape=[halves, halves, payload],
        in_specs=[VMEM] * 3,
        out_specs=[VMEM] * 3,
        compiler_params=params(),
    )(dual_model, increment, dual_obs)
    far, near = swapped(far, "space", 1), swapped(near, "space", 0)

    blocks_here = [arrived[d] for d in range(windows)]
    *after, totals = pl.pallas_call(
        lambda *refs: around_kernel(windows, nvar, levels, *refs),
        out_shape=[shape((2,) + payload.shape[1:], i16)] * pairs
        + [shape((nvar * levels, rows, LANES), f32)],
        in_specs=[VMEM] * (windows + 3),
        out_specs=[VMEM] * (pairs + 1),
        compiler_params=params(),
    )(*blocks_here, dual, near, far)
    after = [moved(piece, "window", -1) for piece in after]

    obs, share, mix = pl.pallas_call(
        lambda *refs: prepare_factor_kernel(steps, nvar, levels, tiles, *refs),
        out_shape=[
            shape((levels, steps, tiles, SUB, LANES), f32),
            shape((levels, steps, SUB, LANES), f32),
            shape((nvar, nvar, SUB, LANES), f32),
        ],
        in_specs=[SMEM] * 2 + [VMEM] * 3,
        out_specs=[VMEM] * 3,
        compiler_params=params(),
    )(obs_count, obs_var, coupling, dual_obs, innovation)

    own, traj_near, traj_far = pl.pallas_call(
        lambda *refs: assemble_kernel(windows, steps, nvar, levels, part, *refs),
        out_shape=[
            shape((steps, nvar * levels, rows, columns), bf16),
            shape((edge_base(steps, nvar, levels)[1], rows, columns), bf16),
            shape((edge_base(steps, nvar, levels)[1], rows, columns), bf16),
        ],
        in_specs=[VMEM] * windows + [ANY],
        out_specs=[VMEM] * 3,
        scratch_shapes=[pltpu.VMEM((windows, block.shape[0] - 1, rows, LANES), bf16)],
        compiler_params=params(),
    )(*blocks_here, mix)
    traj_far, traj_near = swapped(traj_far, "space", 1), swapped(traj_near, "space", 0)

    first = pl.pallas_call(
        lambda *refs: prepare_tangent_kernel(nvar, levels, tiles, *refs),
        out_shape=shape((levels, nvar, tiles, 2 * SUB, LANES), f32),
        in_specs=[VMEM] * 3,
        out_specs=VMEM,
        compiler_params=params(),
    )(near, far, increment)
    new_dual_obs, ends, wide_traj = pl.pallas_call(
        lambda *refs: tangent_kernel(spaces, steps, nvar, levels, tiles, *refs),
        out_shape=[
            shape(dual_obs.shape, f32),
            shape((levels, nvar, tiles, SUB, LANES), f32),
            shape((levels, steps, nvar, tiles, 2 * SUB, LANES), f32),
        ],
        in_specs=[VMEM] * 7,
        out_specs=[VMEM] * 3,
        scratch_shapes=[pltpu.VMEM((2, 2, nvar, tiles, 4 * SUB, LANES), f32)],
        compiler_params=params(),
    )(mix, share, obs, own, traj_near, traj_far, first)

    state = shape((nvar, 2, rows, columns), f32)
    coded = shape((nvar * tiles + 1, 2 * SUB, LANES), i16)
    done = []
    before = ends
    for i in range(pairs):
        last, force = pl.pallas_call(
            lambda *refs, i=i: prepare_adjoint_kernel(i, steps, nvar, tiles, *refs),
            out_shape=[shape((2, n, tiles, 2 * SUB, LANES), f32) for n in (nvar, steps)],
            in_specs=[SMEM] + [VMEM] * 4 + [ANY],
            out_specs=[VMEM] * 2,
            compiler_params=params(),
        )(obs_count, near, far, dual_obs, after[i], before)
        base_dual, base_inc, *payloads = pl.pallas_call(
            lambda *refs, i=i: adjoint_kernel(
                i, windows, spaces, steps, nvar, levels, tiles, *refs
            ),
            out_shape=[state, state] + [coded] * (windows - 1),
            in_specs=[VMEM] * 9,
            out_specs=[VMEM] * (2 + windows - 1),
            scratch_shapes=[
                pltpu.VMEM((2, steps, tiles, 4 * SUB, LANES), f32),
                pltpu.VMEM((2, 2, nvar, tiles, 4 * SUB, LANES), f32),
                pltpu.VMEM((2,) + coded.shape, i16),
            ],
            compiler_params=params(),
        )(mix, totals, wide_traj, last, force, ends, increment, model_rhs, dual_model)
        before = base_dual
        sent = [
            exchanged(piece, "window", mask)
            for piece, mask in zip(payloads, partners(windows))
        ]
        if i < pairs - 1:
            done += pl.pallas_call(
                lambda *refs, i=i: early_kernel(i, windows, nvar, levels, tiles, *refs),
                out_shape=[state, state],
                in_specs=[VMEM] * (windows + 2),
                out_specs=[VMEM] * 2,
                compiler_params=params(),
            )(*sent, base_dual, base_inc, totals)

    new_dual_model, new_increment = pl.pallas_call(
        lambda *refs: final_kernel(windows, nvar, levels, tiles, *refs),
        out_shape=[shape(dual_model.shape, f32), shape(increment.shape, f32)],
        in_specs=[VMEM] * (windows + 2 + len(done)),
        out_specs=[VMEM] * 2,
        compiler_params=params(),
    )(*sent, *done, base_dual, base_inc, totals)
    return new_dual_model, new_dual_obs, new_increment


def solution(mesh):
    placed = (
        P("members", None, None, None, "space", "window"),
        P(("members", "window"), None, None, "space", None),
        P(("members", "window"), None, None, "space", None),
        P(("members", "window"), None, None, "space", None),
        P(("members", "window"), None, None, "space", None),
        P(("members", "window"), None, None, "space", None),
        P(),
        P(("members", "window"), None, None),
        P(("members", "window"), None, None),
        P(("members", "window")),
    )
    return jax.shard_map(
        body,
        mesh=mesh,
        in_specs=placed,
        out_specs=(
            P(("members", "window"), None, None, "space", None),
            P(("members", "window"), None, None, "space", None),
            P(("members", "window"), None, None, "space", None),
        ),
        check_vma=False,
    )
```
